32 devices in a mesh: dp: 8 (over z, y), expert: 4 (over x, core).
Axes of the slice: x: 2, y: 2, z: 4, core: 2. Of those that a mesh axis runs over, the one named last changes fastest.
Arguments:
- tokens: bfloat16 [8192, 768], P(('expert', 'dp')), may hold values from -6 to 6
- lengths: int32 [8], replicated, may hold values from 256 to 1024, as said below
- expert_ids: int32 [8192, 1], P(('expert', 'dp')), may hold values from 0 to 7; in each aligned block of 256 rows (0 to 255, 256 to 511, ...) at most 48 rows name the same one
- gain_one: bfloat16 [768], replicated, may hold values from 0.5 to 1.5
- w_query: bfloat16 [768, 768], replicated, may hold values from -0.02734375 to 0.02734375
- w_key: bfloat16 [768, 768], replicated, may hold values from -0.21875 to 0.21875
- w_value: bfloat16 [768, 768], replicated, may hold values from -0.21875 to 0.21875
- w_output: bfloat16 [768, 768], replicated, may hold values from -2.5 to 2.5
- bias_table: bfloat16 [32, 12], replicated, may hold values from -4 to 4
- gain_two: bfloat16 [768], replicated, may hold values from 0.5 to 1.5
- w_router: bfloat16 [768, 8], replicated, may hold values from -0.15625 to 0.15625
- w_in: bfloat16 [8, 768, 3072], P('expert'), may hold values from -0.21875 to 0.21875
- w_out: bfloat16 [8, 3072, 768], P('expert'), may hold values from -1.75 to 1.75
- cotangent: bfloat16 [8192, 768], P(('expert', 'dp')), may hold values from -6 to 6
Outputs:
- output: bfloat16 [8192, 768], P(('expert', 'dp'))
- d_tokens: float32 [8192, 768], P(('expert', 'dp'))
- d_gain_one: float32 [768], replicated
- d_query: float32 [768, 768], replicated
- d_key: float32 [768, 768], replicated
- d_value: float32 [768, 768], replicated
- d_output: float32 [768, 768], replicated
- d_table: float32 [32, 12], replicated
- d_gain_two: float32 [768], replicated
- d_router: float32 [768, 8], replicated
- d_in: float32 [8, 768, 3072], P('expert', 'dp')
- d_out: float32 [8, 3072, 768], P('expert', 'dp')
The draws below stay inside these ranges and needn't reach their ends.
Inputs may be any that keep to these rules, and one draw needn't show every extreme that they name: `lengths`: one sequence of every 2 consecutive ones has length 1024. `expert_ids`: in the rows of one device (aligned blocks of 256 rows) no expert is chosen more than 48 times.
All inputs are finite; a program needn't handle non-finite values.
Results may differ from the reference program's by a relative error of at most 0.015.
Values may be sent and summed in bfloat16 or wider, within the bound.
A program may use at most 512 MiB of HBM per device.

```python
import math
import jax
import jax.numpy as jnp
import numpy as np
from jax import lax

D = 768
H = 12
HD = 64
FF = 3072
BUCKETS = 32
EXACT = 8
TOK_DEV = 256
SPAN = 4
SEQ = 1024
SEQS = 8
TOKENS = 8192
EXPERTS = 8
SLOTS = 48
CAP = 160
N_DP = 8
N_EXPERT = 4


def draw_lengths(key, part):
    key = jax.random.fold_in(key, 7)
    first_key, second_key = jax.random.split(key)
    drawn_lengths = jax.random.randint(first_key, (SEQS,), SEQ // 4, SEQ + 1)
    per_column = N_DP // SPAN
    full_pick = jax.random.randint(second_key, (N_EXPERT,), 0, per_column)
    column_pick = jnp.repeat(full_pick, per_column, total_repeat_length=SEQS)
    full_length = jnp.arange(SEQS) % per_column == column_pick
    return jnp.where(full_length, SEQ, drawn_lengths).astype(jnp.int32)


def level_of(stream_key, dims, cuts, smallest, high):
    level, own = 1.0, jax.random.fold_in(stream_key, 6)
    for position, shards_of in cuts:
        draws = jnp.exp(jax.random.uniform(jax.random.fold_in(own, position), (shards_of,), jnp.float32, smallest / len(cuts), high / len(cuts)))
        level = level * jnp.repeat(draws, dims[position] // shards_of).reshape([-1 if axis == position else 1 for axis in range(len(dims))])
    return level


def shared_out(stream_key, own, number, rows, number_of, top, limit, skew):
    sequence = jax.random.permutation(stream_key, number_of)
    crowded, ordinary = portions_of(number_of, rows * top, limit, skew, True), portions_of(number_of, rows * top, limit, skew, False)
    places = jnp.arange(number_of)

    def named(sizes, turn):
        used = int((sizes > 0).sum())
        fixed = max(1, used // 4)
        passed = fixed + (places - fixed + turn * (used - fixed)) % max(1, number_of - fixed)
        return jnp.zeros((number_of,), jnp.int32).at[sequence[jnp.where(places < fixed, places, passed)]].set(jnp.asarray(sizes, jnp.int32))

    sizes = jnp.where(number % 4 == 0, named(crowded, number // 4), named(ordinary, number - number // 4 - 1))
    mixed = jax.random.permutation(jax.random.fold_in(own, 3), number_of)
    giver, receiver = mixed[0:number_of // 2 * 2:2], mixed[1:number_of // 2 * 2:2]
    room = jnp.minimum(sizes[giver] - 1, limit - sizes[receiver]) // 2
    room = jnp.where((giver == sequence[0]) | (receiver == sequence[0]) | (sizes[receiver] == 0), 0, jnp.maximum(room, 0))
    passed = jax.random.randint(jax.random.fold_in(own, 4), (number_of // 2,), 0, 1 << 20) % (room + 1)
    sizes = sizes.at[giver].add(-passed).at[receiver].add(passed)
    members = jnp.searchsorted(jnp.cumsum(sizes), jnp.arange(rows * top), side="right").astype(jnp.int32)
    table = members.reshape(top, rows).T
    table = table[jax.random.permutation(jax.random.fold_in(own, 1), rows)]
    turn = jax.random.randint(jax.random.fold_in(own, 2), (rows, 1), 0, top)
    return jnp.take_along_axis(table, (jnp.arange(top)[None, :] + turn) % top, axis=1)


def portions_of(count, total, bound, lean, full):
    weights = [(1 << 20) // math.isqrt(grade ** lean) + 1 for grade in range(1, count + 1)]
    largest = bound if full else min(bound, max(-(-total // count), total * weights[0] // sum(weights)))
    least = 1 if total - largest >= count - 1 else 0
    holding, surplus = [largest] + [least] * (count - 1), total - largest - least * (count - 1)
    while surplus > 0:
        candidates = [i for i in range(1, count) if holding[i] < largest] or [i for i in range(1, count) if holding[i] < bound]
        mass, budget = sum([weights[i] for i in candidates]), surplus
        for i in candidates:
            extra = min(bound - holding[i], max(1, budget * weights[i] // mass), surplus)
            holding[i] = holding[i] + extra
            surplus = surplus - extra
    return np.array(holding)


def normal_values(rng, dims, scale, reach, pieces=(), kind=jnp.bfloat16):
    loudness = level_of(rng, dims, pieces, -0.22, 0.18) if pieces else 1.0
    array = jax.random.normal(rng, dims, jnp.float32) * scale * loudness
    return jnp.minimum(jnp.maximum(array, -reach), reach).astype(kind)


def setup_inputs(seed: int = 0) -> dict:
    arg_keys = jax.random.split(jax.random.key(seed), 15)
    tokens = normal_values(arg_keys[0], (TOKENS, D), 1.0, 6.0, ((0, 32),))
    lengths = draw_lengths(jax.random.fold_in(arg_keys[14], 71), 0)
    expert_ids_keys = jax.random.split(jax.random.fold_in(arg_keys[2], 1), TOKENS // TOK_DEV)
    expert_ids_turns = jax.random.permutation(jax.random.fold_in(arg_keys[2], 3), TOKENS // TOK_DEV)
    expert_ids = jax.vmap(lambda own, number: shared_out(jax.random.fold_in(arg_keys[2], 2), own, number, TOK_DEV, EXPERTS, 1, SLOTS, 2))(expert_ids_keys, expert_ids_turns).reshape((TOKENS, 1))
    gain_one = jnp.clip(1.0 + 0.1 * jax.random.normal(arg_keys[3], (D,), jnp.float32), 0.5, 1.5).astype(jnp.bfloat16)
    w_query = normal_values(arg_keys[4], (D, D), (D * HD) ** -0.5, 0.02734375)
    w_key = normal_values(arg_keys[5], (D, D), D ** -0.5, 0.21875)
    w_value = normal_values(arg_keys[6], (D, D), D ** -0.5, 0.21875)
    w_output = normal_values(arg_keys[7], (D, D), (max(D // 128, 1)) ** -0.5, 2.5)
    bias_table = normal_values(arg_keys[8], (BUCKETS, H), 1.0, 4.0)
    gain_two = jnp.clip(1.0 + 0.1 * jax.random.normal(arg_keys[9], (D,), jnp.float32), 0.5, 1.5).astype(jnp.bfloat16)
    w_router = normal_values(arg_keys[10], (D, EXPERTS), (2 * D) ** -0.5, 0.15625)
    w_in = normal_values(arg_keys[11], (EXPERTS, D, FF), D ** -0.5, 0.21875, ((0, 4),))
    w_out = normal_values(arg_keys[12], (EXPERTS, FF, D), (max(FF // 256, 1)) ** -0.5, 1.75, ((0, 4),))
    cotangent = normal_values(arg_keys[13], (TOKENS, D), 1.0, 6.0, ((0, 32),))
    return {"tokens": tokens, "lengths": lengths, "expert_ids": expert_ids, "gain_one": gain_one, "w_query": w_query, "w_key": w_key, "w_value": w_value, "w_output": w_output, "bias_table": bias_table, "gain_two": gain_two, "w_router": w_router, "w_in": w_in, "w_out": w_out, "cotangent": cotangent}


@jax.custom_vjp
def low(v):
    return lax.optimization_barrier(v.astype(jnp.bfloat16)).astype(jnp.float32)

@jax.custom_vjp
def low_back(v):
    return v

def low_keep(v):
    return (low(v), None)

def low_pass(kept, grad):
    return (grad,)

def back_keep(v):
    return (v, None)

def back_low(kept, grad):
    return (low(grad),)
low.defvjp(low_keep, low_pass)
low_back.defvjp(back_keep, back_low)

def bucket_of(relative):
    distance = jnp.abs(relative)
    beyond = jnp.full(relative.shape, EXACT, jnp.int32)
    for level_step in range(1, BUCKETS // 2 - EXACT):
        boundary = math.isqrt(EXACT * EXACT * (1 << level_step) - 1) + 1
        beyond = beyond + (distance >= boundary).astype(jnp.int32)
    nearby = jnp.where(distance < EXACT, distance, beyond)
    return nearby + jnp.where(relative > 0, BUCKETS // 2, 0).astype(jnp.int32)

def rms_scale(values, gain):
    return values * lax.rsqrt(lax.optimization_barrier(jnp.mean(values * values, axis=-1, keepdims=True)) + 1e-06) * gain

def highest(left_side, right_side):
    return jnp.dot(left_side, right_side, precision=lax.Precision.HIGHEST)

def regroup(values):
    shaped = values.reshape((N_EXPERT, N_DP, TOK_DEV) + values.shape[1:])
    return jnp.swapaxes(shaped, 0, 1).reshape((N_DP, N_EXPERT * TOK_DEV) + values.shape[1:])

def ungroup(values):
    shaped = values.reshape((N_DP, N_EXPERT, TOK_DEV) + values.shape[2:])
    return jnp.swapaxes(shaped, 0, 1).reshape((TOKENS,) + values.shape[2:])

def sequence_attend(operands, bias_rows, score_grid):
    query_seq, key_seq, value_seq, key_valid = operands

    def head_attend(head_operands):
        query_head, key_head, value_head, column = head_operands
        scores = highest(query_head, key_head.T) + column[score_grid]
        scores = low_back(jnp.where(key_valid[None, :], scores, -1000000000.0))
        weights = low(jax.nn.softmax(scores, axis=-1))
        return highest(weights, value_head)
    heads_out = lax.map(jax.checkpoint(head_attend), (jnp.swapaxes(query_seq, 0, 1), jnp.swapaxes(key_seq, 0, 1), jnp.swapaxes(value_seq, 0, 1), bias_rows.T))
    return jnp.swapaxes(heads_out, 0, 1)

def expert_group(operands, inner_w, outer_w):
    group_rows, slot_index = operands
    buffer = jnp.zeros((EXPERTS * CAP + 1, D), jnp.float32).at[slot_index].add(group_rows)
    buffer = low_back(buffer[:-1].reshape(EXPERTS, CAP, D))
    inner_act = low_back(jnp.einsum('ecd,edf->ecf', buffer, inner_w, precision=lax.Precision.HIGHEST))
    active = low(jax.nn.gelu(inner_act))
    result = low_back(low(jnp.einsum('ecf,efd->ecd', active, outer_w, precision=lax.Precision.HIGHEST)))
    flat_rows = jnp.concatenate([result.reshape(EXPERTS * CAP, D), jnp.zeros((1, D), jnp.float32)], axis=0)
    return flat_rows[slot_index]

def reference(tokens, lengths, expert_ids, gain_one, w_query, w_key, w_value, w_output, bias_table, gain_two, w_router, w_in, w_out, cotangent):
    positions_all = jnp.arange(TOKENS, dtype=jnp.int32)
    valid_mask = positions_all % SEQ < lengths[positions_all // SEQ]
    chosen = expert_ids[:, 0]
    expert_hits = ((chosen[:, None] == jnp.arange(EXPERTS, dtype=jnp.int32)[None, :]) & valid_mask[:, None]).astype(jnp.int32)
    grouped = regroup(expert_hits)
    before = jnp.cumsum(grouped, axis=1) - grouped
    token_rank = ungroup(lax.optimization_barrier(jnp.sum(before * grouped, axis=-1)))
    kept_mask = valid_mask & (token_rank < CAP)
    slot_index = jnp.where(kept_mask, chosen * CAP + token_rank, EXPERTS * CAP).astype(jnp.int32)
    slot_groups = regroup(slot_index)
    valid_f = valid_mask.astype(jnp.float32)[:, None]
    kept_f = kept_mask.astype(jnp.float32)
    seq_positions = jnp.arange(SEQ, dtype=jnp.int32)
    score_grid = bucket_of(seq_positions[None, :] - seq_positions[:, None])
    key_valid = valid_mask.reshape(SEQS, SEQ)

    def forward(token_f, gain_a, query_w, key_w, value_w, output_w, bias_rows, gain_b, router_w, inner_w, outer_w):
        normed = low(rms_scale(token_f, gain_a))
        queries = low_back(low(highest(normed, query_w)))
        keys = low_back(low(highest(normed, key_w)))
        values = low_back(low(highest(normed, value_w)))
        seq_shape = (SEQS, SEQ, H, HD)
        attended = lax.map(jax.checkpoint(lambda operands: sequence_attend(operands, bias_rows, score_grid)), (queries.reshape(seq_shape), keys.reshape(seq_shape), values.reshape(seq_shape), key_valid))
        attended = low_back(low(attended.reshape(TOKENS, D)))
        residual = token_f + highest(attended, output_w)
        routed = low(rms_scale(residual, gain_b))
        router = jax.nn.softmax(highest(routed, router_w), axis=-1)
        gate_value = jnp.take_along_axis(router, chosen[:, None], axis=1)[:, 0] * kept_f
        returned = lax.map(jax.checkpoint(lambda operands: expert_group(operands, inner_w, outer_w)), (regroup(routed), slot_groups))
        return valid_f * (residual + gate_value[:, None] * ungroup(returned))
    primal = tuple((entry.astype(jnp.float32) for entry in (tokens, gain_one, w_query, w_key, w_value, w_output, bias_table, gain_two, w_router, w_in, w_out)))
    output, pullback = jax.vjp(forward, *primal)
    gradients = pullback(cotangent.astype(jnp.float32))
    return (output.astype(jnp.bfloat16), gradients[0], gradients[1], gradients[2], gradients[3], gradients[4], gradients[5], gradients[6], gradients[7], gradients[8], gradients[9], gradients[10])
```

```python
import functools
import math

import jax
import jax.numpy as jnp
from jax import lax
from jax.experimental import pallas as pl
from jax.experimental.pallas import tpu as pltpu
from jax.sharding import PartitionSpec as P

BUCKETS = 32
EXACT = 8
MASKED = -1000000000.0
F32 = jnp.float32
BF16 = jnp.bfloat16
VMEM_BYTES = 56 * 1024 * 1024


def bucket_of(relative):
    distance = jnp.abs(relative)
    beyond = jnp.full(relative.shape, EXACT, jnp.int32)
    for level_step in range(1, BUCKETS // 2 - EXACT):
        boundary = math.isqrt(EXACT * EXACT * (1 << level_step) - 1) + 1
        beyond = beyond + (distance >= boundary).astype(jnp.int32)
    nearby = jnp.where(distance < EXACT, distance, beyond)
    return nearby + jnp.where(relative > 0, BUCKETS // 2, 0).astype(jnp.int32)


def normalize(values, gain):
    inverse = lax.rsqrt(jnp.mean(values * values, axis=-1, keepdims=True) + 1e-06)
    return (values * inverse * gain, inverse)


def norm_back(values, inverse, gain, upstream):
    scaled_up = upstream * gain
    d_gain = jnp.sum(upstream * values * inverse, axis=0)
    cubed = inverse * inverse * inverse
    d_values = inverse * scaled_up - values * cubed * jnp.mean(
        values * scaled_up, axis=-1, keepdims=True
    )
    return (d_values, d_gain)


def dot(left_side, right_side):
    return jnp.dot(left_side, right_side, preferred_element_type=F32)


def dot_t(left_side, right_side):
    return lax.dot_general(
        left_side, right_side, (((1,), (1,)), ((), ())), preferred_element_type=F32
    )


def t_dot(left_side, right_side):
    return lax.dot_general(
        left_side, right_side, (((0,), (0,)), ((), ())), preferred_element_type=F32
    )


def gelu_parts(value):
    scale = math.sqrt(2.0 / math.pi)
    square = value * value
    tanh = jnp.tanh(scale * (value + 0.044715 * value * square))
    half = 0.5 * (1.0 + tanh)
    slope = half + 0.5 * value * (1.0 - tanh * tanh) * scale * (1.0 + 3 * 0.044715 * square)
    return (value * half, slope)


def build_bias(win_ref, bias_ref):
    count, block, _ = bias_ref.shape

    @pl.loop(0, count)
    def _(index):
        row = win_ref[0, pl.ds(index, 1), :]
        wide = jnp.broadcast_to(row, (block, 2 * block))
        bias_ref[index] = pltpu.roll(wide, 0, 1, stride=1, stride_axis=0)[:, :block]


def attend_kernel(length_ref, win_ref, q_ref, k_ref, v_ref, o_ref, lse_ref, bias_ref):
    block = bias_ref.shape[1]
    q_blocks = q_ref.shape[1] // block
    k_blocks = k_ref.shape[1] // block
    build_bias(win_ref, bias_ref)
    length = length_ref[0]

    @pl.loop(0, q_blocks)
    def _(i):
        rows = pl.ds(pl.multiple_of(i * block, block), block)
        query = q_ref[0, rows, :]
        scores = []
        for j in range(k_blocks):
            part = dot_t(k_ref[0, j * block : (j + 1) * block, :], query)
            part = part + bias_ref[j - i + q_blocks - 1]
            position = lax.broadcasted_iota(jnp.int32, (block, 1), 0) + j * block
            scores.append(jnp.where(position < length, part, MASKED))
        top = functools.reduce(jnp.maximum, [jnp.max(s, axis=0, keepdims=True) for s in scores])
        total = jnp.zeros((1, block), F32)
        out = jnp.zeros((v_ref.shape[2], block), F32)
        for j in range(k_blocks):
            scaled = jnp.exp(scores[j] - top)
            total = total + jnp.sum(scaled, axis=0, keepdims=True)
            out = out + t_dot(v_ref[0, j * block : (j + 1) * block, :], scaled.astype(BF16))
        out = out * (1.0 / total)
        o_ref[0, rows, :] = out.T.astype(BF16)
        lse_ref[0, pl.ds(i, 1), :] = top + jnp.log(total)


def attend_back_kernel(
    length_ref, win_ref, q_ref, k_ref, v_ref, g_ref, lse_ref,
    dq_ref, dk_ref, dv_ref, dwin_ref, bias_ref, dbias_ref,
):
    block = bias_ref.shape[1]
    q_blocks = q_ref.shape[1] // block
    k_blocks = k_ref.shape[1] // block
    build_bias(win_ref, bias_ref)
    length = length_ref[0]
    dk_ref[...] = jnp.zeros_like(dk_ref)
    dv_ref[...] = jnp.zeros_like(dv_ref)
    dbias_ref[...] = jnp.zeros_like(dbias_ref)

    @pl.loop(0, q_blocks)
    def _(i):
        rows = pl.ds(pl.multiple_of(i * block, block), block)
        query = q_ref[0, rows, :]
        grad = g_ref[0, rows, :]
        log_norm = lse_ref[0, pl.ds(i, 1), :]
        probs, d_probs = [], []
        spread = jnp.zeros((1, block), F32)
        for j in range(k_blocks):
            keys = slice(j * block, (j + 1) * block)
            part = dot_t(k_ref[0, keys, :], query)
            part = part + bias_ref[j - i + q_blocks - 1]
            position = lax.broadcasted_iota(jnp.int32, (block, 1), 0) + j * block
            part = jnp.where(position < length, part, MASKED)
            prob = jnp.exp(part - log_norm)
            d_prob = dot_t(v_ref[0, keys, :], grad)
            spread = spread + jnp.sum(prob * d_prob, axis=0, keepdims=True)
            dv_ref[0, keys, :] += dot(prob.astype(BF16), grad)
            probs.append(prob)
            d_probs.append(d_prob)
        d_query = jnp.zeros((q_ref.shape[2], block), F32)
        for j in range(k_blocks):
            keys = slice(j * block, (j + 1) * block)
            d_score = probs[j] * (d_probs[j] - spread)
            dbias_ref[j - i + q_blocks - 1] += d_score
            low = d_score.astype(BF16)
            dk_ref[0, keys, :] += dot(low, query)
            d_query = d_query + t_dot(k_ref[0, keys, :], low)
        dq_ref[0, rows, :] = d_query.T.astype(BF16)

    @pl.loop(0, dbias_ref.shape[0])
    def _(index):
        wide = jnp.concatenate([dbias_ref[index], jnp.zeros((block, block), F32)], axis=1)
        half = block // 2
        while half:
            wide = wide[:half] + pltpu.roll(wide[half:], 2 * block - half, 1)
            half //= 2
        dwin_ref[0, pl.ds(index, 1), :] = wide


def head_block(rows, width):
    return pl.BlockSpec((1, rows, width), lambda h: (h, 0, 0))


def attend(length, window, query, key, value):
    heads, q_rows, width = query.shape
    k_rows = key.shape[1]
    count, block = window.shape[1], window.shape[2] // 2
    return pl.pallas_call(
        attend_kernel,
        grid=(heads,),
        in_specs=[
            pl.BlockSpec(memory_space=pltpu.SMEM),
            head_block(count, 2 * block),
            head_block(q_rows, width),
            head_block(k_rows, width),
            head_block(k_rows, width),
        ],
        out_specs=[head_block(q_rows, width), head_block(q_rows // block, block)],
        out_shape=[
            jax.ShapeDtypeStruct((heads, q_rows, width), BF16),
            jax.ShapeDtypeStruct((heads, q_rows // block, block), F32),
        ],
        scratch_shapes=[pltpu.VMEM((count, block, block), F32)],
        compiler_params=pltpu.CompilerParams(vmem_limit_bytes=VMEM_BYTES),
        name="attend",
    )(length, window, query, key, value)


def attend_back(length, window, query, key, value, grad, log_norm):
    heads, q_rows, width = query.shape
    k_rows = key.shape[1]
    count, block = window.shape[1], window.shape[2] // 2
    return pl.pallas_call(
        attend_back_kernel,
        grid=(heads,),
        in_specs=[
            pl.BlockSpec(memory_space=pltpu.SMEM),
            head_block(count, 2 * block),
            head_block(q_rows, width),
            head_block(k_rows, width),
            head_block(k_rows, width),
            head_block(q_rows, width),
            head_block(q_rows // block, block),
        ],
        out_specs=[
            head_block(q_rows, width),
            head_block(k_rows, width),
            head_block(k_rows, width),
            head_block(count, 2 * block),
        ],
        out_shape=[
            jax.ShapeDtypeStruct((heads, q_rows, width), BF16),
            jax.ShapeDtypeStruct((heads, k_rows, width), F32),
            jax.ShapeDtypeStruct((heads, k_rows, width), F32),
            jax.ShapeDtypeStruct((heads, count, 2 * block), F32),
        ],
        scratch_shapes=[pltpu.VMEM((count, block, block), F32) for _ in range(2)],
        compiler_params=pltpu.CompilerParams(vmem_limit_bytes=VMEM_BYTES),
        name="attend_back",
    )(length, window, query, key, value, grad, log_norm)


def experts_kernel(rows_ref, w_in_ref, w_out_ref, out_ref, acc_ref, back_ref):
    width = w_in_ref.shape[1]
    step = pl.program_id(1)

    @pl.when(step == 0)
    def _():
        acc_ref[...] = jnp.zeros_like(acc_ref)
        back_ref[...] = jnp.zeros_like(back_ref)

    inner = dot(rows_ref[0, :, :width], w_in_ref[0])
    active, slope = gelu_parts(inner)
    acc_ref[...] += dot(active.astype(BF16), w_out_ref[0])
    d_active = dot_t(rows_ref[0, :, width:], w_out_ref[0])
    d_inner = (d_active * slope).astype(BF16)
    back_ref[...] += dot_t(d_inner, w_in_ref[0])

    @pl.when(step == pl.num_programs(1) - 1)
    def _():
        out_ref[0, :, :width] = acc_ref[...].astype(BF16)
        out_ref[0, :, width:] = back_ref[...].astype(BF16)


def experts(rows, w_in, w_out):
    local, count, double = rows.shape
    width, hidden = w_in.shape[1:]
    piece = 512
    return pl.pallas_call(
        experts_kernel,
        grid=(local, hidden // piece),
        in_specs=[
            pl.BlockSpec((1, count, double), lambda e, f: (e, 0, 0)),
            pl.BlockSpec((1, width, piece), lambda e, f: (e, 0, f)),
            pl.BlockSpec((1, piece, width), lambda e, f: (e, f, 0)),
        ],
        out_specs=pl.BlockSpec((1, count, double), lambda e, f: (e, 0, 0)),
        out_shape=jax.ShapeDtypeStruct((local, count, double), BF16),
        scratch_shapes=[pltpu.VMEM((count, width), F32) for _ in range(2)],
        compiler_params=pltpu.CompilerParams(vmem_limit_bytes=VMEM_BYTES),
        name="experts",
    )(rows, w_in, w_out)


def weight_grads_kernel(rows_ref, w_in_ref, w_out_ref, d_in_ref, d_out_ref, acc_ref):
    width = w_in_ref.shape[1]
    step = pl.program_id(1)
    rows = rows_ref[...].reshape(rows_ref.shape[0] * rows_ref.shape[2], 2 * width)

    @pl.when(step == 0)
    def _():
        acc_ref[...] = jnp.zeros_like(acc_ref)
        d_out_ref[...] = jnp.zeros_like(d_out_ref)

    inner = dot(rows[:, :width], w_in_ref[0])
    active, slope = gelu_parts(inner)
    d_active = dot_t(rows[:, width:], w_out_ref[0])
    d_inner = (d_active * slope).astype(BF16)
    d_out_ref[0] += t_dot(active.astype(BF16), rows[:, width:])
    acc_ref[...] += t_dot(rows[:, :width], d_inner)

    @pl.when(step == pl.num_programs(1) - 1)
    def _():
        d_in_ref[0] = acc_ref[...].astype(BF16)


def weight_grads(rows, w_in, w_out):
    groups, local, count, double = rows.shape
    width, piece = w_in.shape[1:]
    together = 4
    return pl.pallas_call(
        weight_grads_kernel,
        grid=(local, groups // together),
        in_specs=[
            pl.BlockSpec((together, 1, count, double), lambda e, g: (g, e, 0, 0)),
            pl.BlockSpec((1, width, piece), lambda e, g: (e, 0, 0)),
            pl.BlockSpec((1, piece, width), lambda e, g: (e, 0, 0)),
        ],
        out_specs=[
            pl.BlockSpec((1, width, piece), lambda e, g: (e, 0, 0)),
            pl.BlockSpec((1, piece, width), lambda e, g: (e, 0, 0)),
        ],
        out_shape=[
            jax.ShapeDtypeStruct((local, width, piece), BF16),
            jax.ShapeDtypeStruct((local, piece, width), F32),
        ],
        scratch_shapes=[pltpu.VMEM((width, piece), F32)],
        compiler_params=pltpu.CompilerParams(vmem_limit_bytes=VMEM_BYTES),
        name="weight_grads",
    )(rows, w_in, w_out)


def all_to_all(array, axis, groups=None):
    return lax.all_to_all(
        array, axis, split_axis=0, concat_axis=0, tiled=True, axis_index_groups=groups
    )


def to_experts(received, local):
    total, slots, width = received.shape
    shaped = received.reshape(total // local, local, slots, width)
    return jnp.swapaxes(shaped, 0, 1).reshape(local, total // local * slots, width)


def to_sources(by_expert, sources):
    local, total, width = by_expert.shape
    shaped = by_expert.reshape(local, sources, total // sources, width)
    return jnp.swapaxes(shaped, 0, 1).reshape(sources * local, total // sources, width)


def per_device(
    tokens, lengths, expert_ids, gain_one, w_query, w_key, w_value, w_output,
    bias_table, gain_two, w_router, w_in, w_out, cotangent,
):
    tok_rows, width = tokens.shape
    head_count = bias_table.shape[1]
    head_width = width // head_count
    expert_count = w_router.shape[1]
    local = w_in.shape[0]
    hidden = w_in.shape[2]
    dp_count, ex_count = lax.axis_size("dp"), lax.axis_size("expert")
    dp_index, ex_index = lax.axis_index("dp"), lax.axis_index("expert")
    span = dp_count // 2
    quad = math.gcd(span, head_count)
    heads = head_count // quad
    part = heads * head_width
    q_rows = quad * tok_rows
    q_parts = span // quad
    place = dp_index % span
    mine, q_part = place % quad, place // quad
    quads = [[i * quad + j for j in range(quad)] for i in range(dp_count // quad)]
    spans = [[i * span + j for j in range(span)] for i in range(dp_count // span)]
    seq_id = ex_index * (dp_count // span) + dp_index // span
    start_row = place * tok_rows

    length = jnp.sum(jnp.where(jnp.arange(lengths.shape[0], dtype=jnp.int32) == seq_id, lengths, 0))
    valid_mask = start_row + jnp.arange(tok_rows, dtype=jnp.int32) < length
    valid_f = valid_mask.astype(F32)
    length_arg = length.reshape(1)

    if q_parts == 1:
        tokens_all = all_to_all(
            jnp.broadcast_to(tokens[None], (quad, tok_rows, width)), "dp", quads
        ).reshape(q_rows, width)
        tokens_q = tokens_all
    else:
        tokens_all = lax.all_gather(tokens, "dp", axis_index_groups=spans, tiled=True)
        tokens_q = lax.dynamic_slice_in_dim(tokens_all, q_part * q_rows, q_rows, 0)
    gain_a = gain_one.astype(F32)
    normed_all = normalize(tokens_all.astype(F32), gain_a)[0].astype(BF16)
    normed_q = normalize(tokens_q.astype(F32), gain_a)[0].astype(BF16)

    table = lax.dynamic_slice_in_dim(bias_table.astype(F32), mine * heads, heads, 1)
    counts = span * tok_rows // tok_rows + quad - 1
    offset = jnp.arange(2 * tok_rows, dtype=jnp.int32)
    offset = jnp.where(offset < tok_rows, offset, offset - 2 * tok_rows)
    codes = (
        jnp.arange(counts, dtype=jnp.int32)[:, None] * tok_rows
        - offset[None, :]
        - (q_rows - tok_rows)
        - q_part * q_rows
    )
    window_hot = (
        bucket_of(codes)[:, :, None] == jnp.arange(table.shape[0], dtype=jnp.int32)
    ).astype(BF16)
    window = jnp.einsum("amb,bh->ham", window_hot, table.astype(BF16), preferred_element_type=F32)

    def my_columns(weight):
        return lax.dynamic_slice_in_dim(weight, mine * part, part, 1).reshape(
            width, heads, head_width
        )

    def project(rows, weight):
        return jnp.einsum(
            "sd,dhc->hsc", rows, my_columns(weight), preferred_element_type=F32
        ).astype(BF16)

    query = project(normed_q, w_query)
    key = project(normed_all, w_key)
    value = project(normed_all, w_value)
    attended_heads, log_norm = attend(length_arg, window, query, key, value)
    attended = all_to_all(
        jnp.transpose(
            attended_heads.reshape(heads, quad, tok_rows, head_width), (1, 2, 0, 3)
        ).reshape(quad, tok_rows, part),
        "dp",
        quads,
    )
    attended = jnp.swapaxes(attended, 0, 1).reshape(tok_rows, width)

    token_f = tokens.astype(F32)
    residual = token_f + dot(attended, w_output)
    gain_b = gain_two.astype(F32)
    routed_f, inverse_two = normalize(residual, gain_b)
    routed = routed_f.astype(BF16)
    router = jax.nn.softmax(dot(routed, w_router), axis=-1)

    chosen = expert_ids[:, 0]
    chosen_hot = chosen[:, None] == jnp.arange(expert_count, dtype=jnp.int32)[None, :]
    valid_hits = (chosen_hot & valid_mask[:, None]).astype(jnp.int32)
    per_source = lax.all_gather(jnp.sum(valid_hits, axis=0), "expert")
    earlier = jnp.arange(ex_count, dtype=jnp.int32)[:, None] < ex_index
    offsets = jnp.sum(jnp.where(earlier, per_source, 0), axis=0)
    local_rank = jnp.sum((jnp.cumsum(valid_hits, axis=0) - valid_hits) * valid_hits, axis=1)
    group_rank = local_rank + jnp.sum(valid_hits * offsets[None, :], axis=1)
    capacity = 5 * tok_rows // (4 * local)
    slots = 3 * tok_rows // (2 * expert_count)
    kept_mask = valid_mask & (group_rank < capacity)
    kept_f = kept_mask.astype(F32)
    target = jnp.where(kept_mask, chosen * slots + local_rank, -1)
    placing = (
        jnp.arange(expert_count * slots, dtype=jnp.int32)[:, None] == target[None, :]
    ).astype(BF16)
    chosen_f = chosen_hot.astype(F32)
    chosen_prob = jnp.sum(router * chosen_f, axis=1)
    gate = chosen_prob * kept_f
    upstream = cotangent.astype(F32) * valid_f[:, None]
    d_expert = (gate[:, None] * upstream).astype(BF16)

    sending = dot(placing, jnp.concatenate([routed, d_expert], axis=1)).astype(BF16)
    expert_rows = to_experts(
        all_to_all(sending.reshape(expert_count, slots, 2 * width), "expert"), local
    )
    group_rows = lax.all_gather(expert_rows, "dp")
    results = experts(expert_rows, w_in, w_out)
    returned = all_to_all(to_sources(results, ex_count), "expert")
    gathered = t_dot(placing, returned.reshape(expert_count * slots, 2 * width))
    expert_out, d_routed = gathered[:, :width], gathered[:, width:]

    output = (valid_f[:, None] * (residual + gate[:, None] * expert_out)).astype(BF16)
    d_gate = jnp.sum(upstream * expert_out, axis=1) * kept_f
    d_logits = router * (chosen_f - chosen_prob[:, None]) * d_gate[:, None]
    d_router = t_dot(routed, d_logits.astype(BF16))
    d_routed = d_routed + dot_t(d_logits.astype(BF16), w_router)
    d_norm_two, d_gain_two = norm_back(residual, inverse_two, gain_b, d_routed)
    d_residual = upstream + d_norm_two
    low_residual = d_residual.astype(BF16)
    d_attended = dot_t(low_residual, w_output).astype(BF16)
    d_output = t_dot(attended, low_residual)

    grad = all_to_all(
        jnp.swapaxes(d_attended.reshape(tok_rows, quad, part), 0, 1), "dp", quads
    ).reshape(q_rows, heads, head_width)
    grad = jnp.swapaxes(grad, 0, 1)
    d_query_rows, d_key_rows, d_value_rows, d_window = attend_back(
        length_arg, window, query, key, value, grad, log_norm
    )
    if q_parts > 1:
        strided = [
            [i * span + j + quad * n for n in range(q_parts)]
            for i in range(dp_count // span)
            for j in range(quad)
        ]
        d_key_rows, d_value_rows = [
            lax.psum_scatter(
                rows, "dp", scatter_dimension=1, axis_index_groups=strided, tiled=True
            )
            for rows in (d_key_rows, d_value_rows)
        ]
    d_rows = jnp.stack([d_query_rows, d_key_rows.astype(BF16), d_value_rows.astype(BF16)])
    d_parts = jnp.einsum("sd,khsc->dkhc", normed_q, d_rows, preferred_element_type=F32)
    d_table = jnp.einsum("amb,ham->bh", window_hot.astype(F32), d_window, precision="highest")
    d_mine = all_to_all(
        jnp.transpose(
            d_rows.reshape(3, heads, quad, tok_rows, head_width), (2, 3, 0, 1, 4)
        ).reshape(quad, tok_rows, 3 * part),
        "dp",
        quads,
    ).reshape(quad, tok_rows, 3, part)
    d_mine = jnp.transpose(d_mine, (2, 1, 0, 3)).reshape(3, tok_rows, width)
    d_normed = dot_t(d_mine[0], w_query) + dot_t(d_mine[1], w_key) + dot_t(d_mine[2], w_value)
    inverse_one = normalize(token_f, gain_a)[1]
    d_norm_one, d_gain_one = norm_back(token_f, inverse_one, gain_a, d_normed)
    d_tokens = d_residual + d_norm_one

    piece = hidden // dp_count
    my_in = lax.dynamic_slice_in_dim(w_in, dp_index * piece, piece, 2)
    my_out = lax.dynamic_slice_in_dim(w_out, dp_index * piece, piece, 1)
    d_in_piece, d_out = weight_grads(group_rows, my_in, my_out)
    d_in = all_to_all(
        jnp.swapaxes(d_in_piece.reshape(local, dp_count, width // dp_count, piece), 0, 1), "dp"
    )
    d_in = (
        jnp.transpose(d_in, (1, 2, 0, 3)).reshape(local, width // dp_count, hidden).astype(F32)
    )

    def spread(array, axis):
        wide = jnp.zeros(array.shape[:axis] + (array.shape[axis] * quad,) + array.shape[axis + 1 :], F32)
        return lax.dynamic_update_slice_in_dim(wide, array, mine * array.shape[axis], axis)

    d_parts = d_parts.reshape(width, 3, part)
    big = jnp.stack([spread(d_parts[:, n], 1) for n in range(3)] + [d_output])
    summed = lax.psum(big.astype(BF16), ("dp", "expert")).astype(F32)
    small = lax.psum(
        (d_gain_one, spread(d_table, 1), d_gain_two, d_router), ("dp", "expert")
    )
    return (
        output, d_tokens, small[0], summed[0], summed[1], summed[2], summed[3],
        small[1], small[2], small[3], d_in, d_out,
    )


def solution(mesh):
    rows = P(("expert", "dp"), None)
    owned = P("expert", None, None)
    return jax.shard_map(
        per_device,
        mesh=mesh,
        in_specs=(
            rows, P(), rows, P(), P(), P(), P(), P(), P(), P(), P(), owned, owned, rows,
        ),
        out_specs=(
            rows, rows, P(), P(), P(), P(), P(), P(), P(), P(),
            P("expert", "dp", None), P("expert", "dp", None),
        ),
        check_vma=False,
    )
```

```python
import functools
import math

import jax
import jax.numpy as jnp
from jax import lax
from jax.experimental import pallas as pl
from jax.experimental.pallas import tpu as pltpu
from jax.sharding import PartitionSpec as P

BUCKETS = 32
EXACT = 8
MASKED = -1000000000.0
F32 = jnp.float32
BF16 = jnp.bfloat16
VMEM_BYTES = 56 * 1024 * 1024


def bucket_of(relative):
    distance = jnp.abs(relative)
    beyond = jnp.full(relative.shape, EXACT, jnp.int32)
    for level_step in range(1, BUCKETS // 2 - EXACT):
        boundary = math.isqrt(EXACT * EXACT * (1 << level_step) - 1) + 1
        beyond = beyond + (distance >= boundary).astype(jnp.int32)
    nearby = jnp.where(distance < EXACT, distance, beyond)
    return nearby + jnp.where(relative > 0, BUCKETS // 2, 0).astype(jnp.int32)


def normalize(values, gain):
    inverse = lax.rsqrt(jnp.mean(values * values, axis=-1, keepdims=True) + 1e-06)
    return (values * inverse * gain, inverse)


def norm_back(values, inverse, gain, upstream):
    scaled_up = upstream * gain
    d_gain = jnp.sum(upstream * values * inverse, axis=0)
    cubed = inverse * inverse * inverse
    d_values = inverse * scaled_up - values * cubed * jnp.mean(
        values * scaled_up, axis=-1, keepdims=True
    )
    return (d_values, d_gain)


def dot(left_side, right_side):
    return jnp.dot(left_side, right_side, preferred_element_type=F32)


def dot_t(left_side, right_side):
    return lax.dot_general(
        left_side, right_side, (((1,), (1,)), ((), ())), preferred_element_type=F32
    )


def t_dot(left_side, right_side):
    return lax.dot_general(
        left_side, right_side, (((0,), (0,)), ((), ())), preferred_element_type=F32
    )


def gelu_parts(value):
    scale = math.sqrt(2.0 / math.pi)
    square = value * value
    tanh = jnp.tanh(scale * (value + 0.044715 * value * square))
    half = 0.5 * (1.0 + tanh)
    slope = half + 0.5 * value * (1.0 - tanh * tanh) * scale * (1.0 + 3 * 0.044715 * square)
    return (value * half, slope)


def build_bias(win_ref, bias_ref):
    count, block, _ = bias_ref.shape

    @pl.loop(0, count)
    def _(index):
        row = win_ref[0, pl.ds(index, 1), :]
        wide = jnp.broadcast_to(row, (block, 2 * block))
        bias_ref[index] = pltpu.roll(wide, 0, 1, stride=1, stride_axis=0)[:, :block]


def attend_kernel(length_ref, win_ref, q_ref, k_ref, v_ref, o_ref, lse_ref, bias_ref):
    block = bias_ref.shape[1]
    q_blocks = q_ref.shape[1] // block
    k_blocks = k_ref.shape[1] // block
    build_bias(win_ref, bias_ref)
    length = length_ref[0]

    @pl.loop(0, q_blocks)
    def _(i):
        rows = pl.ds(pl.multiple_of(i * block, block), block)
        query = q_ref[0, rows, :]
        scores = []
        for j in range(k_blocks):
            part = dot_t(k_ref[0, j * block : (j + 1) * block, :], query)
            part = part + bias_ref[j - i + q_blocks - 1]
            position = lax.broadcasted_iota(jnp.int32, (block, 1), 0) + j * block
            scores.append(jnp.where(position < length, part, MASKED))
        top = functools.reduce(jnp.maximum, [jnp.max(s, axis=0, keepdims=True) for s in scores])
        total = jnp.zeros((1, block), F32)
        out = jnp.zeros((v_ref.shape[2], block), F32)
        for j in range(k_blocks):
            scaled = jnp.exp(scores[j] - top)
            total = total + jnp.sum(scaled, axis=0, keepdims=True)
            out = out + t_dot(v_ref[0, j * block : (j + 1) * block, :], scaled.astype(BF16))
        out = out * (1.0 / total)
        o_ref[0, rows, :] = out.T.astype(BF16)
        lse_ref[0, pl.ds(i, 1), :] = top + jnp.log(total)


def attend_back_kernel(
    length_ref, win_ref, q_ref, k_ref, v_ref, g_ref, lse_ref,
    dq_ref, dk_ref, dv_ref, dwin_ref, bias_ref, dbias_ref,
):
    block = bias_ref.shape[1]
    q_blocks = q_ref.shape[1] // block
    k_blocks = k_ref.shape[1] // block
    build_bias(win_ref, bias_ref)
    length = length_ref[0]
    dk_ref[...] = jnp.zeros_like(dk_ref)
    dv_ref[...] = jnp.zeros_like(dv_ref)
    dbias_ref[...] = jnp.zeros_like(dbias_ref)

    @pl.loop(0, q_blocks)
    def _(i):
        rows = pl.ds(pl.multiple_of(i * block, block), block)
        query = q_ref[0, rows, :]
        grad = g_ref[0, rows, :]
        log_norm = lse_ref[0, pl.ds(i, 1), :]
        probs, d_probs = [], []
        spread = jnp.zeros((1, block), F32)
        for j in range(k_blocks):
            keys = slice(j * block, (j + 1) * block)
            part = dot_t(k_ref[0, keys, :], query)
            part = part + bias_ref[j - i + q_blocks - 1]
            position = lax.broadcasted_iota(jnp.int32, (block, 1), 0) + j * block
            part = jnp.where(position < length, part, MASKED)
            prob = jnp.exp(part - log_norm)
            d_prob = dot_t(v_ref[0, keys, :], grad)
            spread = spread + jnp.sum(prob * d_prob, axis=0, keepdims=True)
            dv_ref[0, keys, :] += dot(prob.astype(BF16), grad)
            probs.append(prob)
            d_probs.append(d_prob)
        d_query = jnp.zeros((q_ref.shape[2], block), F32)
        for j in range(k_blocks):
            keys = slice(j * block, (j + 1) * block)
            d_score = probs[j] * (d_probs[j] - spread)
            dbias_ref[j - i + q_blocks - 1] += d_score
            low = d_score.astype(BF16)
            dk_ref[0, keys, :] += dot(low, query)
            d_query = d_query + t_dot(k_ref[0, keys, :], low)
        dq_ref[0, rows, :] = d_query.T.astype(BF16)

    @pl.loop(0, dbias_ref.shape[0])
    def _(index):
        wide = jnp.concatenate([dbias_ref[index], jnp.zeros((block, block), F32)], axis=1)
        half = block // 2
        while half:
            wide = wide[:half] + pltpu.roll(wide[half:], 2 * block - half, 1)
            half //= 2
        dwin_ref[0, pl.ds(index, 1), :] = wide


def head_block(rows, width):
    return pl.BlockSpec((1, rows, width), lambda h: (h, 0, 0))


def attend(length, window, query, key, value):
    heads, q_rows, width = query.shape
    k_rows = key.shape[1]
    count, block = window.shape[1], window.shape[2] // 2
    return pl.pallas_call(
        attend_kernel,
        grid=(heads,),
        in_specs=[
            pl.BlockSpec(memory_space=pltpu.SMEM),
            head_block(count, 2 * block),
            head_block(q_rows, width),
            head_block(k_rows, width),
            head_block(k_rows, width),
        ],
        out_specs=[head_block(q_rows, width), head_block(q_rows // block, block)],
        out_shape=[
            jax.ShapeDtypeStruct((heads, q_rows, width), BF16),
            jax.ShapeDtypeStruct((heads, q_rows // block, block), F32),
        ],
        scratch_shapes=[pltpu.VMEM((count, block, block), F32)],
        compiler_params=pltpu.CompilerParams(vmem_limit_bytes=VMEM_BYTES),
        name="attend",
    )(length, window, query, key, value)


def attend_back(length, window, query, key, value, grad, log_norm):
    heads, q_rows, width = query.shape
    k_rows = key.shape[1]
    count, block = window.shape[1], window.shape[2] // 2
    return pl.pallas_call(
        attend_back_kernel,
        grid=(heads,),
        in_specs=[
            pl.BlockSpec(memory_space=pltpu.SMEM),
            head_block(count, 2 * block),
            head_block(q_rows, width),
            head_block(k_rows, width),
            head_block(k_rows, width),
            head_block(q_rows, width),
            head_block(q_rows // block, block),
        ],
        out_specs=[
            head_block(q_rows, width),
            head_block(k_rows, width),
            head_block(k_rows, width),
            head_block(count, 2 * block),
        ],
        out_shape=[
            jax.ShapeDtypeStruct((heads, q_rows, width), BF16),
            jax.ShapeDtypeStruct((heads, k_rows, width), F32),
            jax.ShapeDtypeStruct((heads, k_rows, width), F32),
            jax.ShapeDtypeStruct((heads, count, 2 * block), F32),
        ],
        scratch_shapes=[pltpu.VMEM((count, block, block), F32) for _ in range(2)],
        compiler_params=pltpu.CompilerParams(vmem_limit_bytes=VMEM_BYTES),
        name="attend_back",
    )(length, window, query, key, value, grad, log_norm)


def experts_kernel(rows_ref, w_in_ref, w_out_ref, out_ref, acc_ref, back_ref):
    width = w_in_ref.shape[1]
    step = pl.program_id(1)

    @pl.when(step == 0)
    def _():
        acc_ref[...] = jnp.zeros_like(acc_ref)
        back_ref[...] = jnp.zeros_like(back_ref)

    inner = dot(rows_ref[0, :, :width], w_in_ref[0])
    active, slope = gelu_parts(inner)
    acc_ref[...] += dot(active.astype(BF16), w_out_ref[0])
    d_active = dot_t(rows_ref[0, :, width:], w_out_ref[0])
    d_inner = (d_active * slope).astype(BF16)
    back_ref[...] += dot_t(d_inner, w_in_ref[0])

    @pl.when(step == pl.num_programs(1) - 1)
    def _():
        out_ref[0, :, :width] = acc_ref[...].astype(BF16)
        out_ref[0, :, width:] = back_ref[...].astype(BF16)


def experts(rows, w_in, w_out):
    local, count, double = rows.shape
    width, hidden = w_in.shape[1:]
    piece = 512
    return pl.pallas_call(
        experts_kernel,
        grid=(local, hidden // piece),
        in_specs=[
            pl.BlockSpec((1, count, double), lambda e, f: (e, 0, 0)),
            pl.BlockSpec((1, width, piece), lambda e, f: (e, 0, f)),
            pl.BlockSpec((1, piece, width), lambda e, f: (e, f, 0)),
        ],
        out_specs=pl.BlockSpec((1, count, double), lambda e, f: (e, 0, 0)),
        out_shape=jax.ShapeDtypeStruct((local, count, double), BF16),
        scratch_shapes=[pltpu.VMEM((count, width), F32) for _ in range(2)],
        compiler_params=pltpu.CompilerParams(vmem_limit_bytes=VMEM_BYTES),
        name="experts",
    )(rows, w_in, w_out)


def weight_grads_kernel(rows_ref, w_in_ref, w_out_ref, d_in_ref, d_out_ref, acc_ref):
    width = w_in_ref.shape[1]
    step = pl.program_id(1)
    rows = rows_ref[...].reshape(rows_ref.shape[0] * rows_ref.shape[2], 2 * width)

    @pl.when(step == 0)
    def _():
        acc_ref[...] = jnp.zeros_like(acc_ref)
        d_out_ref[...] = jnp.zeros_like(d_out_ref)

    inner = dot(rows[:, :width], w_in_ref[0])
    active, slope = gelu_parts(inner)
    d_active = dot_t(rows[:, width:], w_out_ref[0])
    d_inner = (d_active * slope).astype(BF16)
    d_out_ref[0] += t_dot(active.astype(BF16), rows[:, width:])
    acc_ref[...] += t_dot(rows[:, :width], d_inner)

    @pl.when(step == pl.num_programs(1) - 1)
    def _():
        d_in_ref[0] = acc_ref[...].astype(BF16)


def weight_grads(rows, w_in, w_out):
    groups, local, count, double = rows.shape
    width, piece = w_in.shape[1:]
    together = 4
    return pl.pallas_call(
        weight_grads_kernel,
        grid=(local, groups // together),
        in_specs=[
            pl.BlockSpec((together, 1, count, double), lambda e, g: (g, e, 0, 0)),
            pl.BlockSpec((1, width, piece), lambda e, g: (e, 0, 0)),
            pl.BlockSpec((1, piece, width), lambda e, g: (e, 0, 0)),
        ],
        out_specs=[
            pl.BlockSpec((1, width, piece), lambda e, g: (e, 0, 0)),
            pl.BlockSpec((1, piece, width), lambda e, g: (e, 0, 0)),
        ],
        out_shape=[
            jax.ShapeDtypeStruct((local, width, piece), BF16),
            jax.ShapeDtypeStruct((local, piece, width), F32),
        ],
        scratch_shapes=[pltpu.VMEM((width, piece), F32)],
        compiler_params=pltpu.CompilerParams(vmem_limit_bytes=VMEM_BYTES),
        name="weight_grads",
    )(rows, w_in, w_out)


class Place:
    def __init__(self):
        dp, ex = lax.axis_index("dp"), lax.axis_index("expert")
        self.y = lax.rem(dp, 2)
        self.z_lo = lax.rem(lax.div(dp, 2), 2)
        self.z_hi = lax.div(dp, 4)
        self.core = lax.rem(ex, 2)
        self.x = lax.div(ex, 2)

    def member(self):
        return self.z_lo * 2 + self.y

    def flip(self, **bits):
        c = {n: getattr(self, n) for n in ("y", "z_lo", "z_hi", "core", "x")}
        for name in bits:
            c[name] = 1 - c[name]
        return (c["z_hi"] * 4 + c["z_lo"] * 2 + c["y"], c["x"] * 2 + c["core"])

    def relation(self, r):
        bits = {}
        if r % 2:
            bits["y"] = 1
        if r // 2:
            bits["z_lo"] = 1
        y = 1 - self.y if r % 2 else self.y
        z_lo = 1 - self.z_lo if r // 2 else self.z_lo
        return self.flip(**bits), z_lo * 2 + y


def send(src, dst, send_sem, recv_sem, device):
    copy = pltpu.make_async_remote_copy(
        src_ref=src, dst_ref=dst, send_sem=send_sem, recv_sem=recv_sem,
        device_id=device, device_id_type=pl.DeviceIdType.MESH,
    )
    copy.start()
    return copy


def greet(devices):
    barrier = pltpu.get_barrier_semaphore()
    for device in devices:
        pl.semaphore_signal(barrier, inc=1, device_id=device, device_id_type=pl.DeviceIdType.MESH)
    pl.semaphore_wait(barrier, len(devices))


def attend_quad_kernel(length_ref, win_ref, qkv_ref, o_ref, lse_ref, bias_ref):
    heads = win_ref.shape[0]
    block = bias_ref.shape[1]
    part = qkv_ref.shape[1] // 3
    width = part // heads
    blocks = qkv_ref.shape[0] // block
    length = length_ref[0]
    for h in range(heads):
        fill_bias(win_ref, h, bias_ref)
        cols = slice(h * width, (h + 1) * width)
        key = qkv_ref[:, part + h * width : part + (h + 1) * width]
        value = qkv_ref[:, 2 * part + h * width : 2 * part + (h + 1) * width]

        @pl.loop(0, blocks)
        def _(i):
            rows = pl.ds(pl.multiple_of(i * block, block), block)
            query = qkv_ref[rows, cols]
            scores = []
            for j in range(blocks):
                piece = dot_t(key[j * block : (j + 1) * block], query)
                piece = piece + bias_ref[j - i + blocks - 1]
                position = lax.broadcasted_iota(jnp.int32, (block, 1), 0) + j * block
                scores.append(jnp.where(position < length, piece, MASKED))
            top = functools.reduce(
                jnp.maximum, [jnp.max(s, axis=0, keepdims=True) for s in scores]
            )
            total = jnp.zeros((1, block), F32)
            out = jnp.zeros((width, block), F32)
            for j in range(blocks):
                scaled = jnp.exp(scores[j] - top)
                total = total + jnp.sum(scaled, axis=0, keepdims=True)
                out = out + t_dot(value[j * block : (j + 1) * block], scaled.astype(BF16))
            out = out * (1.0 / total)
            o_ref[rows, cols] = out.T.astype(BF16)
            lse_ref[h, pl.ds(i, 1), :] = top + jnp.log(total)


def fill_bias(win_ref, h, bias_ref):
    count, block, _ = bias_ref.shape

    @pl.loop(0, count)
    def _(index):
        wide = jnp.broadcast_to(win_ref[h, pl.ds(index, 1), :], (block, 2 * block))
        bias_ref[index] = pltpu.roll(wide, 0, 1, stride=1, stride_axis=0)[:, :block]


def attend_quad(length, window, qkv):
    heads, count, double = window.shape
    block = double // 2
    rows, triple = qkv.shape
    return pl.pallas_call(
        attend_quad_kernel,
        in_specs=[pl.BlockSpec(memory_space=pltpu.SMEM)] + [pl.BlockSpec(memory_space=pltpu.VMEM)] * 2,
        out_specs=[pl.BlockSpec(memory_space=pltpu.VMEM)] * 2,
        out_shape=[
            jax.ShapeDtypeStruct((rows, triple // 3), BF16),
            jax.ShapeDtypeStruct((heads, rows // block, block), F32),
        ],
        scratch_shapes=[pltpu.VMEM((count, block, block), F32)],
        compiler_params=pltpu.CompilerParams(vmem_limit_bytes=VMEM_BYTES),
        name="attend_quad",
    )(length, window, qkv)


def back_kernel(
    length_ref, win_ref, hot_ref, qkv_ref, lse_ref, attended_ref, normed_ref, token_ref,
    gain_ref, residual_ref, w_output_ref, w_quad_ref, small_ref,
    d_tokens_ref, d_weights_ref, total_ref,
    grad_ref, grad_send, low_ref, bias_ref, dbias_ref, dkey_ref, dvalue_ref, dqkv_ref,
    dmine_ref, load_ref, first_ref, second_ref, third_ref, sum_one_ref, sum_two_ref, all_ref,
    small_send, small_recv,
    grad_sems, low_sems, mine_sems, first_sems, second_sems, third_sems, ring_sems, core_sems,
    small_sems,
):
    place = Place()
    mine = place.member()
    heads = win_ref.shape[0]
    block = bias_ref.shape[1]
    part = qkv_ref.shape[1] // 3
    width = part // heads
    blocks = qkv_ref.shape[0] // block
    quad = blocks
    full = normed_ref.shape[1]
    length = length_ref[0]

    def my_rows(index):
        return pl.ds(pl.multiple_of(index * block, block), block)

    others = [place.relation(r) for r in (1, 2, 3)]
    greet(
        [device for device, _ in others]
        + [place.flip(core=1), place.flip(x=1), place.flip(z_hi=1)]
    )

    low = residual_ref[...].astype(BF16)
    low_ref[my_rows(mine), :] = low
    d_attended = dot_t(low, w_output_ref[...]).astype(BF16)
    for m in range(quad):
        grad_send[m] = d_attended[:, m * part : (m + 1) * part]
    copies = []
    for n, (device, member) in enumerate(others):
        copies.append(
            send(grad_send.at[member], grad_ref.at[my_rows(mine)], grad_sems.at[0, n], grad_sems.at[1, n], device)
        )
    low_copies = []
    for n, (device, member) in enumerate(others):
        low_copies.append(
            send(low_ref.at[my_rows(mine)], low_ref.at[my_rows(mine)], low_sems.at[0, n], low_sems.at[1, n], device)
        )
    grad_ref[my_rows(mine), :] = grad_send[mine]
    fill_bias(win_ref, 0, bias_ref)
    for copy in copies:
        copy.wait()

    for h in range(heads):
        if h:
            fill_bias(win_ref, h, bias_ref)
        cols = slice(h * width, (h + 1) * width)
        key = qkv_ref[:, part + h * width : part + (h + 1) * width]
        value = qkv_ref[:, 2 * part + h * width : 2 * part + (h + 1) * width]
        dkey_ref[...] = jnp.zeros_like(dkey_ref)
        dvalue_ref[...] = jnp.zeros_like(dvalue_ref)
        dbias_ref[...] = jnp.zeros_like(dbias_ref)

        @pl.loop(0, blocks)
        def _(i):
            rows = my_rows(i)
            query = qkv_ref[rows, cols]
            grad = grad_ref[rows, cols]
            log_norm = lse_ref[h, pl.ds(i, 1), :]
            probs, d_probs = [], []
            spread = jnp.zeros((1, block), F32)
            for j in range(blocks):
                keys = slice(j * block, (j + 1) * block)
                piece = dot_t(key[keys], query)
                piece = piece + bias_ref[j - i + blocks - 1]
                position = lax.broadcasted_iota(jnp.int32, (block, 1), 0) + j * block
                piece = jnp.where(position < length, piece, MASKED)
                prob = jnp.exp(piece - log_norm)
                d_prob = dot_t(value[keys], grad)
                spread = spread + jnp.sum(prob * d_prob, axis=0, keepdims=True)
                dvalue_ref[keys, :] += dot(prob.astype(BF16), grad)
                probs.append(prob)
                d_probs.append(d_prob)
            d_query = jnp.zeros((width, block), F32)
            for j in range(blocks):
                keys = slice(j * block, (j + 1) * block)
                d_score = probs[j] * (d_probs[j] - spread)
                dbias_ref[j - i + blocks - 1] += d_score
                low_score = d_score.astype(BF16)
                dkey_ref[keys, :] += dot(low_score, query)
                d_query = d_query + t_dot(key[keys], low_score)
            dqkv_ref[rows, cols] = d_query.T.astype(BF16)

        dqkv_ref[:, part + h * width : part + (h + 1) * width] = dkey_ref[...].astype(BF16)
        dqkv_ref[:, 2 * part + h * width : 2 * part + (h + 1) * width] = dvalue_ref[...].astype(BF16)
        table_row = jnp.zeros((1, hot_ref.shape[2]), F32)
        for a in range(dbias_ref.shape[0]):
            wide = jnp.concatenate([dbias_ref[a], jnp.zeros((block, block), F32)], axis=1)
            half = block // 2
            while half:
                wide = wide[:half] + pltpu.roll(wide[half:], 2 * block - half, 1)
                half //= 2
            table_row = table_row + jnp.dot(
                wide, hot_ref[a], precision=lax.Precision.HIGHEST, preferred_element_type=F32
            )
        if h == 0:
            small_send[0] = small_ref[...]
        for m in range(quad):
            row = 12 + m * heads + h
            small_send[0, row : row + 1, : hot_ref.shape[2]] = jnp.where(mine == m, table_row, 0.0)

    mine_copies = []
    for n, (device, member) in enumerate(others):
        mine_copies.append(
            send(dqkv_ref.at[my_rows(member)], dmine_ref.at[mine], mine_sems.at[0, n], mine_sems.at[1, n], device)
        )
    dmine_ref[mine] = dqkv_ref[my_rows(mine), :]

    d_parts = t_dot(normed_ref[...], dqkv_ref[...])
    d_gain = lax.dot_general(
        jnp.ones((8, 3 * part), F32), d_parts * w_quad_ref[mine].astype(F32), (((1,), (1,)), ((), ())),
        precision=lax.Precision.HIGHEST, preferred_element_type=F32,
    )
    load_ref[:, : 3 * part] = d_parts.astype(BF16)
    gain = gain_ref[...]
    small_send[0, 0:1, :] = d_gain[0:1] / gain
    for copy in low_copies:
        copy.wait()
    d_output = t_dot(attended_ref[...], low_ref[...]).astype(BF16)
    for m in range(quad):
        load_ref[m * part : (m + 1) * part, 3 * part :] = d_output[:, m * part : (m + 1) * part]

    core, x = place.core, place.x
    quarter = load_ref.shape[0] // 4

    def chunk(c, b):
        return pl.ds(pl.multiple_of((c * 2 + b) * quarter, quarter), quarter)

    core_device, x_device, z_device = (
        place.flip(core=1), place.flip(x=1), place.flip(z_hi=1),
    )
    one = [
        send(load_ref.at[chunk(1 - core, 1 - x)], first_ref.at[0], first_sems.at[0, 0], first_sems.at[1, 0], core_device),
        send(load_ref.at[chunk(1 - core, x)], first_ref.at[1], first_sems.at[0, 1], first_sems.at[1, 1], core_device),
    ]
    small_devices = [core_device, x_device, z_device, others[0][0], others[1][0]]
    small_copies = []

    def small_start(n):
        small_copies.append(
            send(small_send.at[n], small_recv.at[n], small_sems.at[0, n], small_sems.at[1, n], small_devices[n])
        )

    def small_end(n):
        small_copies[n].wait()
        total = small_send[n] + small_recv[n]
        if n + 1 < len(small_devices):
            small_send[n + 1] = total
        else:
            total_ref[...] = total

    small_start(0)

    for copy in mine_copies:
        copy.wait()
    d_normed = dot_t(dmine_ref[0], w_quad_ref[0])
    for m in range(1, quad):
        d_normed = d_normed + dot_t(dmine_ref[m], w_quad_ref[m])

    one[0].wait()
    sum_one_ref[...] = (load_ref[chunk(core, 1 - x), :].astype(F32) + first_ref[0].astype(F32)).astype(BF16)
    two = send(sum_one_ref, second_ref, second_sems.at[0], second_sems.at[1], x_device)
    small_end(0)
    small_start(1)
    token = token_ref[...].astype(F32)
    inverse = lax.rsqrt(jnp.mean(token * token, axis=-1, keepdims=True) + 1e-06)
    scaled = d_normed * gain
    cubed = inverse * inverse * inverse
    d_tokens_ref[...] = residual_ref[...] + inverse * scaled - token * cubed * jnp.mean(
        token * scaled, axis=-1, keepdims=True
    )
    one[1].wait()
    two.wait()
    sum_two_ref[...] = (
        load_ref[chunk(core, x), :].astype(F32) + first_ref[1].astype(F32) + second_ref[...].astype(F32)
    ).astype(BF16)
    three = send(sum_two_ref, third_ref, third_sems.at[0], third_sems.at[1], z_device)
    small_end(1)
    small_start(2)
    three.wait()
    all_ref[mine, chunk(core, x), :] = (sum_two_ref[...].astype(F32) + third_ref[...].astype(F32)).astype(BF16)

    thirds = 3
    third = quarter // thirds
    steps = {"x": x_device, "y": others[0][0], "z": others[1][0]}

    def spot(axes, t):
        y = 1 - place.y if "y" in axes else place.y
        z_lo = 1 - place.z_lo if "z" in axes else place.z_lo
        xx = 1 - x if "x" in axes else x
        row = pl.multiple_of((core * 2 + xx) * quarter + t * third, third)
        return all_ref.at[z_lo * 2 + y, pl.ds(row, third)]

    orders = ("xyz", "yzx", "zxy")
    passed = []

    def to_core(axes, t, n):
        where = spot(axes, t)
        passed.append(send(where, where, core_sems.at[0, t, n], core_sems.at[1, t, n], core_device))

    rings = {}

    def forward(axes, t, axis, n):
        where = spot(axes, t)
        rings[t, n] = send(where, where, ring_sems.at[0, t, n], ring_sems.at[1, t, n], steps[axis])

    for t, (a, b, c) in enumerate(orders):
        forward("", t, a, 0)
        forward("", t, b, 1)
        forward("", t, c, 3)
        to_core("", t, 0)
    small_end(2)
    small_start(3)
    for t, (a, b, c) in enumerate(orders):
        rings[t, 0].wait_recv()
        forward(a, t, b, 2)
        forward(a, t, c, 4)
        to_core(a, t, 1)
    small_end(3)
    small_start(4)
    for t, (a, b, c) in enumerate(orders):
        rings[t, 1].wait_recv()
        forward(b, t, c, 5)
        to_core(b, t, 2)
        rings[t, 2].wait_recv()
        forward(a + b, t, c, 6)
        to_core(a + b, t, 3)
    small_end(4)
    for t, (a, b, c) in enumerate(orders):
        for n, axes in ((3, c), (4, a + c), (5, b + c), (6, a + b + c)):
            rings[t, n].wait_recv()
            to_core(axes, t, n + 1)
    for t in range(thirds):
        for n in range(7):
            rings[t, n].wait_send()
    for copy in passed:
        copy.wait()

    @pl.loop(0, full // 64)
    def _(i):
        rows = pl.ds(pl.multiple_of(i * 64, 64), 64)
        for kind in range(3):
            d_weights_ref[kind, rows, :] = jnp.concatenate(
                [all_ref[m, rows, kind * part : (kind + 1) * part].astype(F32) for m in range(quad)], axis=1
            )

    for m in range(quad):
        d_weights_ref[3, m * part : (m + 1) * part, :] = jnp.concatenate(
            [all_ref[m, n * part : (n + 1) * part, 3 * part :].astype(F32) for n in range(quad)], axis=1
        )


def back(length, window, hot, qkv, log_norm, attended, normed, tokens, gain, residual, w_output, w_quad, small):
    heads, count, double = window.shape
    block = double // 2
    rows, triple = qkv.shape
    part = triple // 3
    full = normed.shape[1]
    width = part // heads
    quad = rows // block
    quarter = full // 4
    vmem = pl.BlockSpec(memory_space=pltpu.VMEM)
    dma = pltpu.SemaphoreType.DMA
    return pl.pallas_call(
        back_kernel,
        in_specs=[pl.BlockSpec(memory_space=pltpu.SMEM)] + [vmem] * 12,
        out_specs=[vmem] * 3,
        out_shape=[
            jax.ShapeDtypeStruct((block, full), F32),
            jax.ShapeDtypeStruct((4, full, full), F32),
            jax.ShapeDtypeStruct(small.shape, F32),
        ],
        scratch_shapes=[
            pltpu.VMEM((rows, part), BF16),
            pltpu.VMEM((quad, block, part), BF16),
            pltpu.VMEM((rows, full), BF16),
            pltpu.VMEM((count, block, block), F32),
            pltpu.VMEM((count, block, block), F32),
            pltpu.VMEM((rows, width), F32),
            pltpu.VMEM((rows, width), F32),
            pltpu.VMEM((rows, triple), BF16),
            pltpu.VMEM((quad, block, triple), BF16),
            pltpu.VMEM((full, full), BF16),
            pltpu.VMEM((2, quarter, full), BF16),
            pltpu.VMEM((quarter, full), BF16),
            pltpu.VMEM((quarter, full), BF16),
            pltpu.VMEM((quarter, full), BF16),
            pltpu.VMEM((quarter, full), BF16),
            pltpu.VMEM((quad, full, full), BF16),
            pltpu.VMEM((5,) + small.shape, F32),
            pltpu.VMEM((5,) + small.shape, F32),
            dma((2, 3)), dma((2, 3)), dma((2, 3)), dma((2, 2)), dma((2,)), dma((2,)),
            dma((2, 3, 7)), dma((2, 3, 8)), dma((2, 5)),
        ],
        compiler_params=pltpu.CompilerParams(
            vmem_limit_bytes=VMEM_BYTES, collective_id=0, has_side_effects=True
        ),
        name="back",
    )(length, window, hot, qkv, log_norm, attended, normed, tokens, gain, residual, w_output, w_quad, small)


def all_to_all(array, axis, groups=None):
    return lax.all_to_all(
        array, axis, split_axis=0, concat_axis=0, tiled=True, axis_index_groups=groups
    )


def to_experts(received, local):
    total, slots, width = received.shape
    shaped = received.reshape(total // local, local, slots, width)
    return jnp.swapaxes(shaped, 0, 1).reshape(local, total // local * slots, width)


def to_sources(by_expert, sources):
    local, total, width = by_expert.shape
    shaped = by_expert.reshape(local, sources, total // sources, width)
    return jnp.swapaxes(shaped, 0, 1).reshape(sources * local, total // sources, width)


def per_device(
    tokens, lengths, expert_ids, gain_one, w_query, w_key, w_value, w_output,
    bias_table, gain_two, w_router, w_in, w_out, cotangent,
):
    tok_rows, width = tokens.shape
    head_count = bias_table.shape[1]
    head_width = width // head_count
    expert_count = w_router.shape[1]
    local = w_in.shape[0]
    hidden = w_in.shape[2]
    dp_count, ex_count = lax.axis_size("dp"), lax.axis_size("expert")
    dp_index, ex_index = lax.axis_index("dp"), lax.axis_index("expert")
    span = dp_count // 2
    quad = math.gcd(span, head_count)
    heads = head_count // quad
    part = heads * head_width
    q_rows = quad * tok_rows
    q_parts = span // quad
    place = dp_index % span
    mine, q_part = place % quad, place // quad
    quads = [[i * quad + j for j in range(quad)] for i in range(dp_count // quad)]
    spans = [[i * span + j for j in range(span)] for i in range(dp_count // span)]
    seq_id = ex_index * (dp_count // span) + dp_index // span
    start_row = place * tok_rows

    length = jnp.sum(jnp.where(jnp.arange(lengths.shape[0], dtype=jnp.int32) == seq_id, lengths, 0))
    valid_mask = start_row + jnp.arange(tok_rows, dtype=jnp.int32) < length
    valid_f = valid_mask.astype(F32)
    length_arg = length.reshape(1)

    if q_parts == 1:
        tokens_all = all_to_all(
            jnp.broadcast_to(tokens[None], (quad, tok_rows, width)), "dp", quads
        ).reshape(q_rows, width)
        tokens_q = tokens_all
    else:
        tokens_all = lax.all_gather(tokens, "dp", axis_index_groups=spans, tiled=True)
        tokens_q = lax.dynamic_slice_in_dim(tokens_all, q_part * q_rows, q_rows, 0)
    gain_a = gain_one.astype(F32)
    normed_all = normalize(tokens_all.astype(F32), gain_a)[0].astype(BF16)
    normed_q = normalize(tokens_q.astype(F32), gain_a)[0].astype(BF16)

    table = lax.dynamic_slice_in_dim(bias_table.astype(F32), mine * heads, heads, 1)
    counts = span * tok_rows // tok_rows + quad - 1
    offset = jnp.arange(2 * tok_rows, dtype=jnp.int32)
    offset = jnp.where(offset < tok_rows, offset, offset - 2 * tok_rows)
    codes = (
        jnp.arange(counts, dtype=jnp.int32)[:, None] * tok_rows
        - offset[None, :]
        - (q_rows - tok_rows)
        - q_part * q_rows
    )
    window_hot = (
        bucket_of(codes)[:, :, None] == jnp.arange(table.shape[0], dtype=jnp.int32)
    ).astype(BF16)
    window = jnp.einsum("amb,bh->ham", window_hot, table.astype(BF16), preferred_element_type=F32)

    def my_columns(weight):
        return lax.dynamic_slice_in_dim(weight, mine * part, part, 1).reshape(
            width, heads, head_width
        )

    def project(rows, weight):
        return jnp.einsum(
            "sd,dhc->hsc", rows, my_columns(weight), preferred_element_type=F32
        ).astype(BF16)

    query = project(normed_q, w_query)
    key = project(normed_all, w_key)
    value = project(normed_all, w_value)
    attended_heads, log_norm = attend(length_arg, window, query, key, value)
    attended = all_to_all(
        jnp.transpose(
            attended_heads.reshape(heads, quad, tok_rows, head_width), (1, 2, 0, 3)
        ).reshape(quad, tok_rows, part),
        "dp",
        quads,
    )
    attended = jnp.swapaxes(attended, 0, 1).reshape(tok_rows, width)

    token_f = tokens.astype(F32)
    residual = token_f + dot(attended, w_output)
    gain_b = gain_two.astype(F32)
    routed_f, inverse_two = normalize(residual, gain_b)
    routed = routed_f.astype(BF16)
    router = jax.nn.softmax(dot(routed, w_router), axis=-1)

    chosen = expert_ids[:, 0]
    chosen_hot = chosen[:, None] == jnp.arange(expert_count, dtype=jnp.int32)[None, :]
    valid_hits = (chosen_hot & valid_mask[:, None]).astype(jnp.int32)
    per_source = lax.all_gather(jnp.sum(valid_hits, axis=0), "expert")
    earlier = jnp.arange(ex_count, dtype=jnp.int32)[:, None] < ex_index
    offsets = jnp.sum(jnp.where(earlier, per_source, 0), axis=0)
    local_rank = jnp.sum((jnp.cumsum(valid_hits, axis=0) - valid_hits) * valid_hits, axis=1)
    group_rank = local_rank + jnp.sum(valid_hits * offsets[None, :], axis=1)
    capacity = 5 * tok_rows // (4 * local)
    slots = 3 * tok_rows // (2 * expert_count)
    kept_mask = valid_mask & (group_rank < capacity)
    kept_f = kept_mask.astype(F32)
    target = jnp.where(kept_mask, chosen * slots + local_rank, -1)
    placing = (
        jnp.arange(expert_count * slots, dtype=jnp.int32)[:, None] == target[None, :]
    ).astype(BF16)
    chosen_f = chosen_hot.astype(F32)
    chosen_prob = jnp.sum(router * chosen_f, axis=1)
    gate = chosen_prob * kept_f
    upstream = cotangent.astype(F32) * valid_f[:, None]
    d_expert = (gate[:, None] * upstream).astype(BF16)

    sending = dot(placing, jnp.concatenate([routed, d_expert], axis=1)).astype(BF16)
    expert_rows = to_experts(
        all_to_all(sending.reshape(expert_count, slots, 2 * width), "expert"), local
    )
    group_rows = lax.all_gather(expert_rows, "dp")
    results = experts(expert_rows, w_in, w_out)
    returned = all_to_all(to_sources(results, ex_count), "expert")
    gathered = t_dot(placing, returned.reshape(expert_count * slots, 2 * width))
    expert_out, d_routed = gathered[:, :width], gathered[:, width:]

    output = (valid_f[:, None] * (residual + gate[:, None] * expert_out)).astype(BF16)
    d_gate = jnp.sum(upstream * expert_out, axis=1) * kept_f
    d_logits = router * (chosen_f - chosen_prob[:, None]) * d_gate[:, None]
    d_router = t_dot(routed, d_logits.astype(BF16))
    d_routed = d_routed + dot_t(d_logits.astype(BF16), w_router)
    d_norm_two, d_gain_two = norm_back(residual, inverse_two, gain_b, d_routed)
    d_residual = upstream + d_norm_two
    low_residual = d_residual.astype(BF16)
    d_attended = dot_t(low_residual, w_output).astype(BF16)
    d_output = t_dot(attended, low_residual)

    grad = all_to_all(
        jnp.swapaxes(d_attended.reshape(tok_rows, quad, part), 0, 1), "dp", quads
    ).reshape(q_rows, heads, head_width)
    grad = jnp.swapaxes(grad, 0, 1)
    d_query_rows, d_key_rows, d_value_rows, d_window = attend_back(
        length_arg, window, query, key, value, grad, log_norm
    )
    if q_parts > 1:
        strided = [
            [i * span + j + quad * n for n in range(q_parts)]
            for i in range(dp_count // span)
            for j in range(quad)
        ]
        d_key_rows, d_value_rows = [
            lax.psum_scatter(
                rows, "dp", scatter_dimension=1, axis_index_groups=strided, tiled=True
            )
            for rows in (d_key_rows, d_value_rows)
        ]
    d_rows = jnp.stack([d_query_rows, d_key_rows.astype(BF16), d_value_rows.astype(BF16)])
    d_parts = jnp.einsum("sd,khsc->dkhc", normed_q, d_rows, preferred_element_type=F32)
    d_table = jnp.einsum("amb,ham->bh", window_hot.astype(F32), d_window, precision="highest")
    d_mine = all_to_all(
        jnp.transpose(
            d_rows.reshape(3, heads, quad, tok_rows, head_width), (2, 3, 0, 1, 4)
        ).reshape(quad, tok_rows, 3 * part),
        "dp",
        quads,
    ).reshape(quad, tok_rows, 3, part)
    d_mine = jnp.transpose(d_mine, (2, 1, 0, 3)).reshape(3, tok_rows, width)
    d_normed = dot_t(d_mine[0], w_query) + dot_t(d_mine[1], w_key) + dot_t(d_mine[2], w_value)
    inverse_one = normalize(token_f, gain_a)[1]
    d_norm_one, d_gain_one = norm_back(token_f, inverse_one, gain_a, d_normed)
    d_tokens = d_residual + d_norm_one

    piece = hidden // dp_count
    my_in = lax.dynamic_slice_in_dim(w_in, dp_index * piece, piece, 2)
    my_out = lax.dynamic_slice_in_dim(w_out, dp_index * piece, piece, 1)
    d_in_piece, d_out = weight_grads(group_rows, my_in, my_out)
    d_in = all_to_all(
        jnp.swapaxes(d_in_piece.reshape(local, dp_count, width // dp_count, piece), 0, 1), "dp"
    )
    d_in = (
        jnp.transpose(d_in, (1, 2, 0, 3)).reshape(local, width // dp_count, hidden).astype(F32)
    )

    def spread(array, axis):
        wide = jnp.zeros(array.shape[:axis] + (array.shape[axis] * quad,) + array.shape[axis + 1 :], F32)
        return lax.dynamic_update_slice_in_dim(wide, array, mine * array.shape[axis], axis)

    d_parts = d_parts.reshape(width, 3, part)
    big = jnp.stack([spread(d_parts[:, n], 1) for n in range(3)] + [d_output])
    summed = lax.psum(big.astype(BF16), ("dp", "expert")).astype(F32)
    small = lax.psum(
        (d_gain_one, spread(d_table, 1), d_gain_two, d_router), ("dp", "expert")
    )
    return (
        output, d_tokens, small[0], summed[0], summed[1], summed[2], summed[3],
        small[1], small[2], small[3], d_in, d_out,
    )


def per_device_quad(
    tokens, lengths, expert_ids, gain_one, w_query, w_key, w_value, w_output,
    bias_table, gain_two, w_router, w_in, w_out, cotangent,
):
    tok_rows, width = tokens.shape
    head_count = bias_table.shape[1]
    expert_count = w_router.shape[1]
    local = w_in.shape[0]
    hidden = w_in.shape[2]
    dp_count, ex_count = lax.axis_size("dp"), lax.axis_size("expert")
    dp_index, ex_index = lax.axis_index("dp"), lax.axis_index("expert")
    quad = dp_count // 2
    heads = head_count // quad
    part = width // quad
    q_rows = quad * tok_rows
    mine = dp_index % quad
    quads = [[i * quad + j for j in range(quad)] for i in range(dp_count // quad)]
    seq_id = ex_index * 2 + dp_index // quad
    start_row = mine * tok_rows

    length = jnp.sum(jnp.where(jnp.arange(lengths.shape[0], dtype=jnp.int32) == seq_id, lengths, 0))
    valid_mask = start_row + jnp.arange(tok_rows, dtype=jnp.int32) < length
    valid_f = valid_mask.astype(F32)
    length_arg = length.reshape(1)

    tokens_all = all_to_all(
        jnp.broadcast_to(tokens[None], (quad, tok_rows, width)), "dp", quads
    ).reshape(q_rows, width)
    gain_a = gain_one.astype(F32)
    normed = normalize(tokens_all.astype(F32), gain_a)[0].astype(BF16)

    table = lax.dynamic_slice_in_dim(bias_table, mine * heads, heads, 1)
    counts = 2 * quad - 1
    offset = jnp.arange(2 * tok_rows, dtype=jnp.int32)
    offset = jnp.where(offset < tok_rows, offset, offset - 2 * tok_rows)
    codes = (
        jnp.arange(counts, dtype=jnp.int32)[:, None] * tok_rows
        - offset[None, :]
        - (q_rows - tok_rows)
    )
    window_hot = (
        bucket_of(codes)[:, :, None] == jnp.arange(table.shape[0], dtype=jnp.int32)
    ).astype(F32)
    window = jnp.einsum(
        "amb,bh->ham", window_hot.astype(BF16), table, preferred_element_type=F32
    )

    w_quad = jnp.transpose(
        jnp.stack([w.reshape(width, quad, part) for w in (w_query, w_key, w_value)], axis=1),
        (2, 0, 1, 3),
    ).reshape(quad, width, 3 * part)
    w_mine = lax.dynamic_index_in_dim(w_quad, mine, 0, keepdims=False)
    qkv = dot(normed, w_mine).astype(BF16)
    attended_heads, log_norm = attend_quad(length_arg, window, qkv)
    attended = all_to_all(attended_heads.reshape(quad, tok_rows, part), "dp", quads)
    attended = jnp.swapaxes(attended, 0, 1).reshape(tok_rows, width)

    token_f = tokens.astype(F32)
    residual = token_f + dot(attended, w_output)
    gain_b = gain_two.astype(F32)
    routed_f, inverse_two = normalize(residual, gain_b)
    routed = routed_f.astype(BF16)
    router = jax.nn.softmax(dot(routed, w_router), axis=-1)

    chosen = expert_ids[:, 0]
    chosen_hot = chosen[:, None] == jnp.arange(expert_count, dtype=jnp.int32)[None, :]
    valid_hits = (chosen_hot & valid_mask[:, None]).astype(jnp.int32)
    per_source = lax.all_gather(jnp.sum(valid_hits, axis=0), "expert")
    earlier = jnp.arange(ex_count, dtype=jnp.int32)[:, None] < ex_index
    offsets = jnp.sum(jnp.where(earlier, per_source, 0), axis=0)
    local_rank = jnp.sum((jnp.cumsum(valid_hits, axis=0) - valid_hits) * valid_hits, axis=1)
    group_rank = local_rank + jnp.sum(valid_hits * offsets[None, :], axis=1)
    capacity = 5 * tok_rows // (4 * local)
    slots = 3 * tok_rows // (2 * expert_count)
    kept_mask = valid_mask & (group_rank < capacity)
    kept_f = kept_mask.astype(F32)
    target = jnp.where(kept_mask, chosen * slots + local_rank, -1)
    placing = (
        jnp.arange(expert_count * slots, dtype=jnp.int32)[:, None] == target[None, :]
    ).astype(BF16)
    chosen_f = chosen_hot.astype(F32)
    chosen_prob = jnp.sum(router * chosen_f, axis=1)
    gate = chosen_prob * kept_f
    upstream = cotangent.astype(F32) * valid_f[:, None]
    d_expert = (gate[:, None] * upstream).astype(BF16)

    sending = dot(placing, jnp.concatenate([routed, d_expert], axis=1)).astype(BF16)
    expert_rows = to_experts(
        all_to_all(sending.reshape(expert_count, slots, 2 * width), "expert"), local
    )
    group_rows = lax.all_gather(expert_rows, "dp")
    results = experts(expert_rows, w_in, w_out)
    returned = all_to_all(to_sources(results, ex_count), "expert")
    gathered = t_dot(placing, returned.reshape(expert_count * slots, 2 * width))
    expert_out, d_routed = gathered[:, :width], gathered[:, width:]

    output = (valid_f[:, None] * (residual + gate[:, None] * expert_out)).astype(BF16)
    d_gate = jnp.sum(upstream * expert_out, axis=1) * kept_f
    d_logits = (router * (chosen_f - chosen_prob[:, None]) * d_gate[:, None]).astype(BF16)
    d_router = t_dot(d_logits, routed)
    d_routed = d_routed + dot_t(d_logits, w_router)
    d_norm_two, d_gain_two = norm_back(residual, inverse_two, gain_b, d_routed)
    d_residual = upstream + d_norm_two
    blank = jnp.zeros((1, width), F32)
    small = jnp.concatenate([blank, d_gain_two[None], d_router] + [blank] * (2 + head_count))

    d_tokens, d_weights, total = back(
        length_arg, window, window_hot, qkv, log_norm, attended_heads, normed, tokens,
        gain_a[None], d_residual, w_output, w_quad, small,
    )

    piece = hidden // dp_count
    my_in = lax.dynamic_slice_in_dim(w_in, dp_index * piece, piece, 2)
    my_out = lax.dynamic_slice_in_dim(w_out, dp_index * piece, piece, 1)
    group_rows, d_tokens = lax.optimization_barrier((group_rows, d_tokens))
    d_in_piece, d_out = weight_grads(group_rows, my_in, my_out)
    d_in = all_to_all(
        jnp.swapaxes(d_in_piece.reshape(local, dp_count, width // dp_count, piece), 0, 1), "dp"
    )
    d_in = (
        jnp.transpose(d_in, (1, 2, 0, 3)).reshape(local, width // dp_count, hidden).astype(F32)
    )
    return (
        output, d_tokens, total[0], d_weights[0], d_weights[1], d_weights[2], d_weights[3],
        total[12:, : table.shape[0]].T, total[1], total[2 : 2 + expert_count].T, d_in, d_out,
    )


def solution(mesh):
    rows = P(("expert", "dp"), None)
    owned = P("expert", None, None)
    return jax.shard_map(
        per_device_quad if dict(mesh.shape) == {"dp": 8, "expert": 4} else per_device,
        mesh=mesh,
        in_specs=(
            rows, P(), rows, P(), P(), P(), P(), P(), P(), P(), P(), owned, owned, rows,
        ),
        out_specs=(
            rows, rows, P(), P(), P(), P(), P(), P(), P(), P(),
            P("expert", "dp", None), P("expert", "dp", None),
        ),
        check_vma=False,
    )
```

```python
import functools
import math

import jax
import jax.numpy as jnp
from jax import lax
from jax.experimental import pallas as pl
from jax.experimental.pallas import tpu as pltpu
from jax.sharding import PartitionSpec as P

BUCKETS = 32
EXACT = 8
MASKED = -1000000000.0
F32 = jnp.float32
BF16 = jnp.bfloat16
VMEM_BYTES = 56 * 1024 * 1024


def bucket_of(relative):
    distance = jnp.abs(relative)
    beyond = jnp.full(relative.shape, EXACT, jnp.int32)
    for level_step in range(1, BUCKETS // 2 - EXACT):
        boundary = math.isqrt(EXACT * EXACT * (1 << level_step) - 1) + 1
        beyond = beyond + (distance >= boundary).astype(jnp.int32)
    nearby = jnp.where(distance < EXACT, distance, beyond)
    return nearby + jnp.where(relative > 0, BUCKETS // 2, 0).astype(jnp.int32)


def normalize(values, gain):
    inverse = lax.rsqrt(jnp.mean(values * values, axis=-1, keepdims=True) + 1e-06)
    return (values * inverse * gain, inverse)


def norm_back(values, inverse, gain, upstream):
    scaled_up = upstream * gain
    d_gain = jnp.sum(upstream * values * inverse, axis=0)
    cubed = inverse * inverse * inverse
    d_values = inverse * scaled_up - values * cubed * jnp.mean(
        values * scaled_up, axis=-1, keepdims=True
    )
    return (d_values, d_gain)


def dot(left_side, right_side):
    return jnp.dot(left_side, right_side, preferred_element_type=F32)


def dot_t(left_side, right_side):
    return lax.dot_general(
        left_side, right_side, (((1,), (1,)), ((), ())), preferred_element_type=F32
    )


def t_dot(left_side, right_side):
    return lax.dot_general(
        left_side, right_side, (((0,), (0,)), ((), ())), preferred_element_type=F32
    )


def gelu_parts(value):
    scale = math.sqrt(2.0 / math.pi)
    square = value * value
    tanh = jnp.tanh(scale * (value + 0.044715 * value * square))
    half = 0.5 * (1.0 + tanh)
    slope = half + 0.5 * value * (1.0 - tanh * tanh) * scale * (1.0 + 3 * 0.044715 * square)
    return (value * half, slope)


def build_bias(win_ref, bias_ref):
    count, block, _ = bias_ref.shape

    @pl.loop(0, count)
    def _(index):
        row = win_ref[0, pl.ds(index, 1), :]
        wide = jnp.broadcast_to(row, (block, 2 * block))
        bias_ref[index] = pltpu.roll(wide, 0, 1, stride=1, stride_axis=0)[:, :block]


def attend_kernel(length_ref, win_ref, q_ref, k_ref, v_ref, o_ref, lse_ref, bias_ref):
    block = bias_ref.shape[1]
    q_blocks = q_ref.shape[1] // block
    k_blocks = k_ref.shape[1] // block
    build_bias(win_ref, bias_ref)
    length = length_ref[0]

    @pl.loop(0, q_blocks)
    def _(i):
        rows = pl.ds(pl.multiple_of(i * block, block), block)
        query = q_ref[0, rows, :]
        scores = []
        for j in range(k_blocks):
            part = dot_t(k_ref[0, j * block : (j + 1) * block, :], query)
            part = part + bias_ref[j - i + q_blocks - 1]
            position = lax.broadcasted_iota(jnp.int32, (block, 1), 0) + j * block
            scores.append(jnp.where(position < length, part, MASKED))
        top = functools.reduce(jnp.maximum, [jnp.max(s, axis=0, keepdims=True) for s in scores])
        total = jnp.zeros((1, block), F32)
        out = jnp.zeros((v_ref.shape[2], block), F32)
        for j in range(k_blocks):
            scaled = jnp.exp(scores[j] - top)
            total = total + jnp.sum(scaled, axis=0, keepdims=True)
            out = out + t_dot(v_ref[0, j * block : (j + 1) * block, :], scaled.astype(BF16))
        out = out * (1.0 / total)
        o_ref[0, rows, :] = out.T.astype(BF16)
        lse_ref[0, pl.ds(i, 1), :] = top + jnp.log(total)


def attend_back_kernel(
    length_ref, win_ref, q_ref, k_ref, v_ref, g_ref, lse_ref,
    dq_ref, dk_ref, dv_ref, dwin_ref, bias_ref, dbias_ref,
):
    block = bias_ref.shape[1]
    q_blocks = q_ref.shape[1] // block
    k_blocks = k_ref.shape[1] // block
    build_bias(win_ref, bias_ref)
    length = length_ref[0]
    dk_ref[...] = jnp.zeros_like(dk_ref)
    dv_ref[...] = jnp.zeros_like(dv_ref)
    dbias_ref[...] = jnp.zeros_like(dbias_ref)

    @pl.loop(0, q_blocks)
    def _(i):
        rows = pl.ds(pl.multiple_of(i * block, block), block)
        query = q_ref[0, rows, :]
        grad = g_ref[0, rows, :]
        log_norm = lse_ref[0, pl.ds(i, 1), :]
        probs, d_probs = [], []
        spread = jnp.zeros((1, block), F32)
        for j in range(k_blocks):
            keys = slice(j * block, (j + 1) * block)
            part = dot_t(k_ref[0, keys, :], query)
            part = part + bias_ref[j - i + q_blocks - 1]
            position = lax.broadcasted_iota(jnp.int32, (block, 1), 0) + j * block
            part = jnp.where(position < length, part, MASKED)
            prob = jnp.exp(part - log_norm)
            d_prob = dot_t(v_ref[0, keys, :], grad)
            spread = spread + jnp.sum(prob * d_prob, axis=0, keepdims=True)
            dv_ref[0, keys, :] += dot(prob.astype(BF16), grad)
            probs.append(prob)
            d_probs.append(d_prob)
        d_query = jnp.zeros((q_ref.shape[2], block), F32)
        for j in range(k_blocks):
            keys = slice(j * block, (j + 1) * block)
            d_score = probs[j] * (d_probs[j] - spread)
            dbias_ref[j - i + q_blocks - 1] += d_score
            low = d_score.astype(BF16)
            dk_ref[0, keys, :] += dot(low, query)
            d_query = d_query + t_dot(k_ref[0, keys, :], low)
        dq_ref[0, rows, :] = d_query.T.astype(BF16)

    @pl.loop(0, dbias_ref.shape[0])
    def _(index):
        wide = jnp.concatenate([dbias_ref[index], jnp.zeros((block, block), F32)], axis=1)
        half = block // 2
        while half:
            wide = wide[:half] + pltpu.roll(wide[half:], 2 * block - half, 1)
            half //= 2
        dwin_ref[0, pl.ds(index, 1), :] = wide


def head_block(rows, width):
    return pl.BlockSpec((1, rows, width), lambda h: (h, 0, 0))


def attend(length, window, query, key, value):
    heads, q_rows, width = query.shape
    k_rows = key.shape[1]
    count, block = window.shape[1], window.shape[2] // 2
    return pl.pallas_call(
        attend_kernel,
        grid=(heads,),
        in_specs=[
            pl.BlockSpec(memory_space=pltpu.SMEM),
            head_block(count, 2 * block),
            head_block(q_rows, width),
            head_block(k_rows, width),
            head_block(k_rows, width),
        ],
        out_specs=[head_block(q_rows, width), head_block(q_rows // block, block)],
        out_shape=[
            jax.ShapeDtypeStruct((heads, q_rows, width), BF16),
            jax.ShapeDtypeStruct((heads, q_rows // block, block), F32),
        ],
        scratch_shapes=[pltpu.VMEM((count, block, block), F32)],
        compiler_params=pltpu.CompilerParams(vmem_limit_bytes=VMEM_BYTES),
        name="attend",
    )(length, window, query, key, value)


def attend_back(length, window, query, key, value, grad, log_norm):
    heads, q_rows, width = query.shape
    k_rows = key.shape[1]
    count, block = window.shape[1], window.shape[2] // 2
    return pl.pallas_call(
        attend_back_kernel,
        grid=(heads,),
        in_specs=[
            pl.BlockSpec(memory_space=pltpu.SMEM),
            head_block(count, 2 * block),
            head_block(q_rows, width),
            head_block(k_rows, width),
            head_block(k_rows, width),
            head_block(q_rows, width),
            head_block(q_rows // block, block),
        ],
        out_specs=[
            head_block(q_rows, width),
            head_block(k_rows, width),
            head_block(k_rows, width),
            head_block(count, 2 * block),
        ],
        out_shape=[
            jax.ShapeDtypeStruct((heads, q_rows, width), BF16),
            jax.ShapeDtypeStruct((heads, k_rows, width), F32),
            jax.ShapeDtypeStruct((heads, k_rows, width), F32),
            jax.ShapeDtypeStruct((heads, count, 2 * block), F32),
        ],
        scratch_shapes=[pltpu.VMEM((count, block, block), F32) for _ in range(2)],
        compiler_params=pltpu.CompilerParams(vmem_limit_bytes=VMEM_BYTES),
        name="attend_back",
    )(length, window, query, key, value, grad, log_norm)


def experts_kernel(rows_ref, w_in_ref, w_out_ref, out_ref, acc_ref, back_ref):
    width = w_in_ref.shape[1]
    step = pl.program_id(1)

    @pl.when(step == 0)
    def _():
        acc_ref[...] = jnp.zeros_like(acc_ref)
        back_ref[...] = jnp.zeros_like(back_ref)

    inner = dot(rows_ref[0, :, :width], w_in_ref[0])
    active, slope = gelu_parts(inner)
    acc_ref[...] += dot(active.astype(BF16), w_out_ref[0])
    d_active = dot_t(rows_ref[0, :, width:], w_out_ref[0])
    d_inner = (d_active * slope).astype(BF16)
    back_ref[...] += dot_t(d_inner, w_in_ref[0])

    @pl.when(step == pl.num_programs(1) - 1)
    def _():
        out_ref[0, :, :width] = acc_ref[...].astype(BF16)
        out_ref[0, :, width:] = back_ref[...].astype(BF16)


def experts(rows, w_in, w_out):
    local, count, double = rows.shape
    width, hidden = w_in.shape[1:]
    piece = 512
    return pl.pallas_call(
        experts_kernel,
        grid=(local, hidden // piece),
        in_specs=[
            pl.BlockSpec((1, count, double), lambda e, f: (e, 0, 0)),
            pl.BlockSpec((1, width, piece), lambda e, f: (e, 0, f)),
            pl.BlockSpec((1, piece, width), lambda e, f: (e, f, 0)),
        ],
        out_specs=pl.BlockSpec((1, count, double), lambda e, f: (e, 0, 0)),
        out_shape=jax.ShapeDtypeStruct((local, count, double), BF16),
        scratch_shapes=[pltpu.VMEM((count, width), F32) for _ in range(2)],
        compiler_params=pltpu.CompilerParams(vmem_limit_bytes=VMEM_BYTES),
        name="experts",
    )(rows, w_in, w_out)


def weight_grads_kernel(rows_ref, w_in_ref, w_out_ref, d_in_ref, d_out_ref, acc_ref):
    width = w_in_ref.shape[1]
    step = pl.program_id(1)
    rows = rows_ref[...].reshape(rows_ref.shape[0] * rows_ref.shape[2], 2 * width)

    @pl.when(step == 0)
    def _():
        acc_ref[...] = jnp.zeros_like(acc_ref)
        d_out_ref[...] = jnp.zeros_like(d_out_ref)

    inner = dot(rows[:, :width], w_in_ref[0])
    active, slope = gelu_parts(inner)
    d_active = dot_t(rows[:, width:], w_out_ref[0])
    d_inner = (d_active * slope).astype(BF16)
    d_out_ref[0] += t_dot(active.astype(BF16), rows[:, width:])
    acc_ref[...] += t_dot(rows[:, :width], d_inner)

    @pl.when(step == pl.num_programs(1) - 1)
    def _():
        d_in_ref[0] = acc_ref[...].astype(BF16)


def weight_grads(rows, w_in, w_out):
    groups, local, count, double = rows.shape
    width, piece = w_in.shape[1:]
    together = 4
    return pl.pallas_call(
        weight_grads_kernel,
        grid=(local, groups // together),
        in_specs=[
            pl.BlockSpec((together, 1, count, double), lambda e, g: (g, e, 0, 0)),
            pl.BlockSpec((1, width, piece), lambda e, g: (e, 0, 0)),
            pl.BlockSpec((1, piece, width), lambda e, g: (e, 0, 0)),
        ],
        out_specs=[
            pl.BlockSpec((1, width, piece), lambda e, g: (e, 0, 0)),
            pl.BlockSpec((1, piece, width), lambda e, g: (e, 0, 0)),
        ],
        out_shape=[
            jax.ShapeDtypeStruct((local, width, piece), BF16),
            jax.ShapeDtypeStruct((local, piece, width), F32),
        ],
        scratch_shapes=[pltpu.VMEM((width, piece), F32)],
        compiler_params=pltpu.CompilerParams(vmem_limit_bytes=VMEM_BYTES),
        name="weight_grads",
    )(rows, w_in, w_out)


class Place:
    def __init__(self):
        self.dp, self.ex = lax.axis_index("dp"), lax.axis_index("expert")
        self.y = lax.rem(self.dp, 2)
        self.z = lax.div(self.dp, 2)
        self.z_lo = lax.rem(self.z, 2)
        self.z_hi = lax.div(self.dp, 4)
        self.core = lax.rem(self.ex, 2)
        self.x = lax.div(self.ex, 2)
        self.member = self.z_lo * 2 + self.y

    def flip(self, *names):
        c = {n: getattr(self, n) for n in ("y", "z_lo", "z_hi", "core", "x")}
        for name in names:
            c[name] = 1 - c[name]
        return (c["z_hi"] * 4 + c["z_lo"] * 2 + c["y"], c["x"] * 2 + c["core"])

    def quad_others(self):
        found = []
        for names in (("y",), ("z_lo",), ("y", "z_lo")):
            device = self.flip(*names)
            found.append((device, lax.rem(device[0], 4)))
        return found

    def expert_others(self):
        return [self.flip(*names) for names in (("core",), ("x",), ("core", "x"))]

    def dp_others(self):
        names = (("y",), ("z_lo",), ("y", "z_lo"), ("z_hi",), ("z_hi", "y"), ("z_hi", "z_lo"), ("z_hi", "y", "z_lo"))
        return [self.flip(*n) for n in names]


def remote(src, dst, sems, index, device):
    return pltpu.make_async_remote_copy(
        src_ref=src, dst_ref=dst, send_sem=sems.at[(0,) + index], recv_sem=sems.at[(1,) + index],
        device_id=device, device_id_type=pl.DeviceIdType.MESH,
    )


def send(src, dst, sems, index, device):
    copy = remote(src, dst, sems, index, device)
    copy.start()
    return copy


def greet(devices):
    barrier = pltpu.get_barrier_semaphore()
    for device in devices:
        pl.semaphore_signal(barrier, inc=1, device_id=device, device_id_type=pl.DeviceIdType.MESH)
    pl.semaphore_wait(barrier, len(devices))


def fill_bias(win_ref, h, bias_ref):
    count, block, _ = bias_ref.shape

    @pl.loop(0, count)
    def _(index):
        wide = jnp.broadcast_to(win_ref[h, pl.ds(index, 1), :], (block, 2 * block))
        bias_ref[index] = pltpu.roll(wide, 0, 1, stride=1, stride_axis=0)[:, :block]


def attend_quad_kernel(length_ref, win_ref, qkv_ref, o_ref, lse_ref, bias_ref):
    heads = win_ref.shape[0]
    block = bias_ref.shape[1]
    part = qkv_ref.shape[1] // 3
    width = part // heads
    blocks = qkv_ref.shape[0] // block
    length = length_ref[0]
    for h in range(heads):
        fill_bias(win_ref, h, bias_ref)
        cols = slice(h * width, (h + 1) * width)
        key = qkv_ref[:, part + h * width : part + (h + 1) * width]
        value = qkv_ref[:, 2 * part + h * width : 2 * part + (h + 1) * width]

        @pl.loop(0, blocks)
        def _(i):
            rows = pl.ds(pl.multiple_of(i * block, block), block)
            query = qkv_ref[rows, cols]
            scores = []
            for j in range(blocks):
                piece = dot_t(key[j * block : (j + 1) * block], query)
                piece = piece + bias_ref[j - i + blocks - 1]
                position = lax.broadcasted_iota(jnp.int32, (block, 1), 0) + j * block
                scores.append(jnp.where(position < length, piece, MASKED))
            top = functools.reduce(
                jnp.maximum, [jnp.max(s, axis=0, keepdims=True) for s in scores]
            )
            total = jnp.zeros((1, block), F32)
            out = jnp.zeros((width, block), F32)
            for j in range(blocks):
                scaled = jnp.exp(scores[j] - top)
                total = total + jnp.sum(scaled, axis=0, keepdims=True)
                out = out + t_dot(value[j * block : (j + 1) * block], scaled.astype(BF16))
            out = out * (1.0 / total)
            o_ref[rows, cols] = out.T.astype(BF16)
            lse_ref[h, pl.ds(i, 1), :] = top + jnp.log(total)


def attend_quad(length, window, qkv):
    heads, count, double = window.shape
    block = double // 2
    rows, triple = qkv.shape
    vmem = pl.BlockSpec(memory_space=pltpu.VMEM)
    return pl.pallas_call(
        attend_quad_kernel,
        in_specs=[pl.BlockSpec(memory_space=pltpu.SMEM), vmem, vmem],
        out_specs=[vmem] * 2,
        out_shape=[
            jax.ShapeDtypeStruct((rows, triple // 3), BF16),
            jax.ShapeDtypeStruct((heads, rows // block, block), F32),
        ],
        scratch_shapes=[pltpu.VMEM((count, block, block), F32)],
        compiler_params=pltpu.CompilerParams(vmem_limit_bytes=VMEM_BYTES),
        name="attend_quad",
    )(length, window, qkv)


def rest_kernel(
    length_ref, sending_ref, pack_ref, placing_ref, columns_ref, residual_ref, routed_ref, cotangent_ref,
    gain_two_ref, w_router_ref, win_ref, hot_ref, qkv_ref, lse_ref, attended_ref, normed_ref,
    token_ref, gain_ref, w_output_ref, w_quad_ref, w_in_ref, w_out_ref,
    output_ref, d_tokens_ref, d_weights_ref, total_ref, d_out_ref, d_in_ref,
    arrive_ref, rows_ref, in_buf, out_buf, result_ref, back_send, back_ref,
    grad_ref, grad_send, low_ref, bias_ref, dbias_ref, dkey_ref, dvalue_ref, dqkv_ref,
    dmine_ref, load_ref, first_ref, second_ref, third_ref, sum_one_ref, sum_two_ref,
    small_send, small_recv, active_ref, inner_ref, d_in_send, d_residual_ref,
    go_sems, weight_sems, line_sems, cross_sems, back_sems,
    grad_sems, low_sems, mine_sems, first_sems, second_sems, third_sems, ring_sems, core_sems,
    small_sems, d_in_sems, block_sems,
):
    place = Place()
    mine, ex, dp, z = place.member, place.ex, place.dp, place.z
    heads = win_ref.shape[0]
    block = bias_ref.shape[1]
    part = qkv_ref.shape[1] // 3
    head_width = part // heads
    blocks = quad = qkv_ref.shape[0] // block
    width = normed_ref.shape[1]
    local, slots = arrive_ref.shape[1:3]
    sources = arrive_ref.shape[0]
    capacity = rows_ref.shape[2]
    experts_count = local * sources
    length = length_ref[0]
    piece = in_buf.shape[2]
    pieces = w_in_ref.shape[2] // piece
    depth = in_buf.shape[0]

    def my_rows(index):
        return pl.ds(pl.multiple_of(index * block, block), block)

    quad_others = place.quad_others()
    expert_others = place.expert_others()
    dp_others = place.dp_others()

    def weight_copies(n):
        e, f, slot = n // pieces, n % pieces, n % depth
        return (
            pltpu.make_async_copy(
                w_in_ref.at[e, :, f * piece : (f + 1) * piece], in_buf.at[slot], weight_sems.at[0, slot]
            ),
            pltpu.make_async_copy(
                w_out_ref.at[e, f * piece : (f + 1) * piece, :], out_buf.at[slot], weight_sems.at[1, slot]
            ),
        )

    hidden = active_ref.shape[2]
    my_hidden = pl.ds(pl.multiple_of(dp * hidden, hidden), hidden)

    def block_copies(e):
        return (
            pltpu.make_async_copy(w_in_ref.at[e, :, my_hidden], in_buf.at[e, :, :hidden], block_sems.at[0, e]),
            pltpu.make_async_copy(w_out_ref.at[e, my_hidden, :], out_buf.at[e, :hidden, :], block_sems.at[1, e]),
        )

    for n in range(depth):
        for copy in weight_copies(n):
            copy.start()

    greet(dp_others + expert_others)

    going = []
    for n, device in enumerate(expert_others):
        going.append(
            send(sending_ref.at[pl.ds(device[1] * local, local)], arrive_ref.at[ex], go_sems, (n,), device)
        )
    arrive_ref[ex] = sending_ref[pl.ds(ex * local, local)]
    for copy in going:
        copy.wait()
    for e in range(local):
        slots_rows = arrive_ref[:, e].reshape(sources * slots, 2 * width)
        rows_ref[dp, e] = dot(pack_ref[e], slots_rows).astype(BF16)

    across = place.flip("y")
    left = (dp - 2, ex)
    right = (dp + 2, ex)

    def block_of(offset):
        return rows_ref.at[dp + 2 * offset]

    def along(direction, step, offset):
        return remote(block_of(offset), block_of(offset), line_sems, (direction, step), right if direction else left)

    def over(index, offset):
        return remote(block_of(offset), block_of(offset), cross_sems, (index,), across)

    over(0, 0).start()

    @pl.when(z < 3)
    def _():
        along(1, 0, 0).start()

    @pl.when(z > 0)
    def _():
        along(0, 0, 0).start()

    def relay(k):
        @pl.when(z >= k)
        def _():
            along(1, k - 1, -k).wait_recv()
            over(k, -k).start()
            if k < 3:

                @pl.when(z < 3)
                def _():
                    along(1, k, -k).start()

        @pl.when(z + k <= 3)
        def _():
            along(0, k - 1, k).wait_recv()
            over(3 + k, k).start()
            if k < 3:

                @pl.when(z > 0)
                def _():
                    along(0, k, k).start()

    def relay_end():
        over(0, 0).wait()
        for k in (1, 2, 3):

            @pl.when(z >= k)
            def _():
                over(k, -k).wait()

            @pl.when(z + k <= 3)
            def _():
                over(3 + k, k).wait()

        for k in (0, 1, 2):

            @pl.when((z >= k) & (z < 3))
            def _():
                along(1, k, -k).wait_send()

            @pl.when((z + k <= 3) & (z > 0))
            def _():
                along(0, k, k).wait_send()

    backs = []
    for e in range(local):
        rows = rows_ref[dp, e, :, :width]
        d_rows = rows_ref[dp, e, :, width:]
        for f in range(pieces):
            n = e * pieces + f
            for copy in weight_copies(n):
                copy.wait()
            weight_in = in_buf[n % depth]
            weight_out = out_buf[n % depth]
            active, slope = gelu_parts(dot(rows, weight_in))
            forward = dot(active.astype(BF16), weight_out)
            d_inner = (dot_t(d_rows, weight_out) * slope).astype(BF16)
            backward = dot_t(d_inner, weight_in)
            if f == 0:
                result_ref[:, :width] = forward
                result_ref[:, width:] = backward
            else:
                result_ref[:, :width] += forward
                result_ref[:, width:] += backward
            if n + depth < local * pieces:
                for copy in weight_copies(n + depth):
                    copy.start()
        spread_rows = t_dot(pack_ref[e], result_ref[...].astype(BF16)).astype(BF16)
        back_send[:, e] = spread_rows.reshape(sources, slots, 2 * width)
        for n, device in enumerate(expert_others):
            backs.append(
                send(back_send.at[device[1], e], back_ref.at[ex * local + e], back_sems, (e, n), device)
            )
        back_ref[ex * local + e] = back_send[ex, e]
    for e in range(local):
        for copy in block_copies(e):
            copy.start()
    fill_bias(win_ref, 0, bias_ref)
    for copy in backs:
        copy.wait()

    gathered = t_dot(placing_ref[...], back_ref[...].reshape(experts_count * slots, 2 * width))
    expert_out = gathered[:, :width]
    columns = columns_ref[...]
    gate = columns[:, 8:9]
    valid = columns[:, 9:10]
    kept = columns[:, 10:11]
    residual = residual_ref[...]
    output_ref[...] = (valid * (residual + gate * expert_out)).astype(BF16)
    upstream = cotangent_ref[...].astype(F32) * valid
    d_gate = jnp.sum(upstream * expert_out, axis=1, keepdims=True) * kept
    d_logits = (columns[:, :8] * d_gate).astype(BF16)
    small_send[0] = jnp.zeros(small_send.shape[1:], F32)
    small_send[0, 2:10, :] = t_dot(d_logits, routed_ref[...])
    d_routed = gathered[:, width:] + dot_t(d_logits, w_router_ref[...])
    inverse = lax.rsqrt(jnp.mean(residual * residual, axis=-1, keepdims=True) + 1e-06)
    small_send[0, 1:2, :] = jnp.sum(d_routed * residual * inverse, axis=0, keepdims=True)
    scaled = d_routed * gain_two_ref[...]
    cubed = inverse * inverse * inverse
    d_residual = upstream + inverse * scaled - residual * cubed * jnp.mean(
        residual * scaled, axis=-1, keepdims=True
    )
    d_residual_ref[...] = d_residual

    low = d_residual.astype(BF16)
    low_ref[my_rows(mine), :] = low
    d_attended = dot_t(low, w_output_ref[...]).astype(BF16)
    for m in range(quad):
        grad_send[m] = d_attended[:, m * part : (m + 1) * part]
    copies = []
    for n, (device, member) in enumerate(quad_others):
        copies.append(
            send(grad_send.at[member], grad_ref.at[my_rows(mine)], grad_sems, (n,), device)
        )
    low_copies = []
    for n, (device, member) in enumerate(quad_others):
        low_copies.append(
            send(low_ref.at[my_rows(mine)], low_ref.at[my_rows(mine)], low_sems, (n,), device)
        )
    grad_ref[my_rows(mine), :] = grad_send[mine]
    relay(1)
    for copy in copies:
        copy.wait()

    for h in range(heads):
        if h:
            fill_bias(win_ref, h, bias_ref)
        cols = slice(h * head_width, (h + 1) * head_width)
        key = qkv_ref[:, part + h * head_width : part + (h + 1) * head_width]
        value = qkv_ref[:, 2 * part + h * head_width : 2 * part + (h + 1) * head_width]
        dkey_ref[...] = jnp.zeros_like(dkey_ref)
        dvalue_ref[...] = jnp.zeros_like(dvalue_ref)
        dbias_ref[...] = jnp.zeros_like(dbias_ref)

        @pl.loop(0, blocks)
        def _(i):
            rows = my_rows(i)
            query = qkv_ref[rows, cols]
            grad = grad_ref[rows, cols]
            log_norm = lse_ref[h, pl.ds(i, 1), :]
            probs, d_probs = [], []
            spread = jnp.zeros((1, block), F32)
            for j in range(blocks):
                keys = slice(j * block, (j + 1) * block)
                score = dot_t(key[keys], query)
                score = score + bias_ref[j - i + blocks - 1]
                position = lax.broadcasted_iota(jnp.int32, (block, 1), 0) + j * block
                score = jnp.where(position < length, score, MASKED)
                prob = jnp.exp(score - log_norm)
                d_prob = dot_t(value[keys], grad)
                spread = spread + jnp.sum(prob * d_prob, axis=0, keepdims=True)
                dvalue_ref[keys, :] += dot(prob.astype(BF16), grad)
                probs.append(prob)
                d_probs.append(d_prob)
            d_query = jnp.zeros((head_width, block), F32)
            for j in range(blocks):
                keys = slice(j * block, (j + 1) * block)
                d_score = probs[j] * (d_probs[j] - spread)
                dbias_ref[j - i + blocks - 1] += d_score
                low_score = d_score.astype(BF16)
                dkey_ref[keys, :] += dot(low_score, query)
                d_query = d_query + t_dot(key[keys], low_score)
            dqkv_ref[rows, cols] = d_query.T.astype(BF16)

        dqkv_ref[:, part + h * head_width : part + (h + 1) * head_width] = dkey_ref[...].astype(BF16)
        dqkv_ref[:, 2 * part + h * head_width : 2 * part + (h + 1) * head_width] = dvalue_ref[...].astype(BF16)
        table_row = jnp.zeros((1, hot_ref.shape[1]), F32)
        for a in range(dbias_ref.shape[0]):
            wide = jnp.concatenate([dbias_ref[a], jnp.zeros((block, block), F32)], axis=1)
            half = block // 2
            while half:
                wide = wide[:half] + pltpu.roll(wide[half:], 2 * block - half, 1)
                half //= 2
            table_row = table_row + lax.dot_general(
                wide, hot_ref[a], (((1,), (1,)), ((), ())),
                precision=lax.Precision.HIGHEST, preferred_element_type=F32,
            )
        for m in range(quad):
            row = 12 + m * heads + h
            small_send[0, row : row + 1, : hot_ref.shape[1]] = jnp.where(mine == m, table_row, 0.0)
        if h < 2:
            relay(2 + h)

    mine_copies = []
    for n, (device, member) in enumerate(quad_others):
        mine_copies.append(
            send(dqkv_ref.at[my_rows(member)], dmine_ref.at[mine], mine_sems, (n,), device)
        )
    dmine_ref[mine] = dqkv_ref[my_rows(mine), :]

    d_parts = t_dot(normed_ref[...], dqkv_ref[...])
    d_gain = lax.dot_general(
        jnp.ones((8, 3 * part), F32), d_parts * w_quad_ref[mine].astype(F32), (((1,), (1,)), ((), ())),
        precision=lax.Precision.HIGHEST, preferred_element_type=F32,
    )
    load_ref[:, : 3 * part] = d_parts.astype(BF16)
    gain = gain_ref[...]
    small_send[0, 0:1, :] = d_gain[0:1] / gain
    for copy in low_copies:
        copy.wait()
    d_output = t_dot(attended_ref[...], low_ref[...]).astype(BF16)
    for m in range(quad):
        load_ref[m * part : (m + 1) * part, 3 * part :] = d_output[:, m * part : (m + 1) * part]

    core, x = place.core, place.x
    quarter = load_ref.shape[0] // 4

    def chunk(c, b):
        return pl.ds(pl.multiple_of((c * 2 + b) * quarter, quarter), quarter)

    core_device, x_device, z_device = place.flip("core"), place.flip("x"), place.flip("z_hi")
    one = [
        send(load_ref.at[chunk(1 - core, 1 - x)], first_ref.at[0], first_sems, (0,), core_device),
        send(load_ref.at[chunk(1 - core, x)], first_ref.at[1], first_sems, (1,), core_device),
    ]
    small_devices = [core_device, x_device, z_device, quad_others[0][0], quad_others[1][0]]
    small_copies = []

    def small_start(n):
        small_copies.append(
            send(small_send.at[n], small_recv.at[n], small_sems, (n,), small_devices[n])
        )

    def small_end(n):
        small_copies[n].wait()
        total = small_send[n] + small_recv[n]
        if n + 1 < len(small_devices):
            small_send[n + 1] = total
        else:
            total_ref[...] = total

    small_start(0)

    for copy in mine_copies:
        copy.wait()
    d_normed = dot_t(dmine_ref[0], w_quad_ref[0])
    for m in range(1, quad):
        d_normed = d_normed + dot_t(dmine_ref[m], w_quad_ref[m])

    one[0].wait()
    sum_one_ref[...] = (load_ref[chunk(core, 1 - x), :].astype(F32) + first_ref[0].astype(F32)).astype(BF16)
    two = send(sum_one_ref, second_ref, second_sems, (), x_device)
    small_end(0)
    small_start(1)
    token = token_ref[...].astype(F32)
    inverse = lax.rsqrt(jnp.mean(token * token, axis=-1, keepdims=True) + 1e-06)
    scaled = d_normed * gain
    cubed = inverse * inverse * inverse
    d_tokens_ref[...] = d_residual_ref[...] + inverse * scaled - token * cubed * jnp.mean(
        token * scaled, axis=-1, keepdims=True
    )
    one[1].wait()
    two.wait()
    sum_two_ref[...] = (
        load_ref[chunk(core, x), :].astype(F32) + first_ref[1].astype(F32) + second_ref[...].astype(F32)
    ).astype(BF16)
    three = send(sum_two_ref, third_ref, third_sems, (), z_device)
    small_end(1)
    small_start(2)

    relay_end()
    groups = rows_ref.shape[0]
    d_in_copies = []

    def hidden_gradients(e):
        for copy in block_copies(e):
            copy.wait()
        for g in range(groups):
            rows = rows_ref[g, e, :, :width]
            d_rows = rows_ref[g, e, :, width:]
            active, slope = gelu_parts(dot(rows, in_buf[e, :, :hidden]))
            inner_ref[g] = (dot_t(d_rows, out_buf[e, :hidden, :]) * slope).astype(BF16)
            active_ref[g] = active.astype(BF16)
        all_rows = rows_ref[:, e].reshape(groups * capacity, 2 * width)
        d_in = t_dot(all_rows[:, :width], inner_ref[...].reshape(groups * capacity, hidden))
        d_in_send[:, e] = d_in.astype(BF16).reshape(groups, width // groups, hidden)
        for n, device in enumerate(dp_others):
            d_in_copies.append(
                send(d_in_send.at[device[0], e], d_in_ref.at[dp, e], d_in_sems, (e, n), device)
            )
        d_in_ref[dp, e] = d_in_send[dp, e]
        d_out_ref[e] = t_dot(active_ref[...].reshape(groups * capacity, hidden), all_rows[:, width:])

    hidden_gradients(0)
    three.wait()

    d_weights_ref[mine, chunk(core, x), :] = (
        sum_two_ref[...].astype(F32) + third_ref[...].astype(F32)
    ).astype(BF16)
    thirds = 3
    third = quarter // thirds
    steps = {"x": x_device, "y": quad_others[0][0], "z": quad_others[1][0]}

    def spot(axes, t):
        y = 1 - place.y if "y" in axes else place.y
        z_lo = 1 - place.z_lo if "z" in axes else place.z_lo
        xx = 1 - x if "x" in axes else x
        row = pl.multiple_of((core * 2 + xx) * quarter + t * third, third)
        return d_weights_ref.at[z_lo * 2 + y, pl.ds(row, third)]

    orders = ("xyz", "yzx", "zxy")
    passed = []

    def to_core(axes, t, n):
        where = spot(axes, t)
        passed.append(send(where, where, core_sems, (t, n), core_device))

    rings = {}

    def forward(axes, t, axis, n):
        where = spot(axes, t)
        rings[t, n] = send(where, where, ring_sems, (t, n), steps[axis])

    for t, (a, b, c) in enumerate(orders):
        forward("", t, a, 0)
        forward("", t, b, 1)
        forward("", t, c, 3)
        to_core("", t, 0)
    small_end(2)
    small_start(3)
    hidden_gradients(1)
    for t, (a, b, c) in enumerate(orders):
        rings[t, 0].wait_recv()
        forward(a, t, b, 2)
        forward(a, t, c, 4)
        to_core(a, t, 1)
    small_end(3)
    small_start(4)
    for t, (a, b, c) in enumerate(orders):
        rings[t, 1].wait_recv()
        forward(b, t, c, 5)
        to_core(b, t, 2)
        rings[t, 2].wait_recv()
        forward(a + b, t, c, 6)
        to_core(a + b, t, 3)
    small_end(4)
    for t, (a, b, c) in enumerate(orders):
        for n, axes in ((3, c), (4, a + c), (5, b + c), (6, a + b + c)):
            rings[t, n].wait_recv()
            to_core(axes, t, n + 1)
    for t in range(thirds):
        for n in range(7):
            rings[t, n].wait_send()
    for copy in passed:
        copy.wait()
    for copy in d_in_copies:
        copy.wait()


def rest(length, sending, pack, placing, columns, residual, routed, cotangent, gain_two, w_router,
         window, hot, qkv, log_norm, attended, normed, tokens, gain, w_output, w_quad, w_in, w_out):
    heads, count, double = window.shape
    block = double // 2
    rows, triple = qkv.shape
    part = triple // 3
    full = normed.shape[1]
    head_width = part // heads
    quad = rows // block
    quarter = full // 4
    experts_count, slots, wide = sending.shape
    local, capacity, _ = pack.shape
    sources = experts_count // local
    groups = lax.axis_size("dp")
    hidden = w_in.shape[2] // groups
    piece = 512
    depth = 3
    small = (24, full)
    vmem = pl.BlockSpec(memory_space=pltpu.VMEM)
    hbm = pl.BlockSpec(memory_space=pl.ANY)
    dma = pltpu.SemaphoreType.DMA
    return pl.pallas_call(
        rest_kernel,
        in_specs=[pl.BlockSpec(memory_space=pltpu.SMEM)] + [vmem] * 19 + [hbm] * 2,
        out_specs=[vmem] * 6,
        out_shape=[
            jax.ShapeDtypeStruct((block, full), BF16),
            jax.ShapeDtypeStruct((block, full), F32),
            jax.ShapeDtypeStruct((quad, full, full), BF16),
            jax.ShapeDtypeStruct(small, F32),
            jax.ShapeDtypeStruct((local, hidden, full), F32),
            jax.ShapeDtypeStruct((groups, local, full // groups, hidden), BF16),
        ],
        scratch_shapes=[
            pltpu.VMEM((sources, local, slots, wide), BF16),
            pltpu.VMEM((groups, local, capacity, wide), BF16),
            pltpu.VMEM((depth, full, piece), BF16),
            pltpu.VMEM((depth, piece, full), BF16),
            pltpu.VMEM((capacity, wide), F32),
            pltpu.VMEM((sources, local, slots, wide), BF16),
            pltpu.VMEM((experts_count, slots, wide), BF16),
            pltpu.VMEM((rows, part), BF16),
            pltpu.VMEM((quad, block, part), BF16),
            pltpu.VMEM((rows, full), BF16),
            pltpu.VMEM((count, block, block), F32),
            pltpu.VMEM((count, block, block), F32),
            pltpu.VMEM((rows, head_width), F32),
            pltpu.VMEM((rows, head_width), F32),
            pltpu.VMEM((rows, triple), BF16),
            pltpu.VMEM((quad, block, triple), BF16),
            pltpu.VMEM((full, full), BF16),
            pltpu.VMEM((2, quarter, full), BF16),
            pltpu.VMEM((quarter, full), BF16),
            pltpu.VMEM((quarter, full), BF16),
            pltpu.VMEM((quarter, full), BF16),
            pltpu.VMEM((quarter, full), BF16),
            pltpu.VMEM((5,) + small, F32),
            pltpu.VMEM((5,) + small, F32),
            pltpu.VMEM((groups, capacity, hidden), BF16),
            pltpu.VMEM((groups, capacity, hidden), BF16),
            pltpu.VMEM((groups, local, full // groups, hidden), BF16),
            pltpu.VMEM((block, full), F32),
            dma((2, 3)), dma((2, depth)), dma((2, 2, 3)), dma((2, 7)), dma((2, 2, 3)),
            dma((2, 3)), dma((2, 3)), dma((2, 3)), dma((2, 2)), dma((2,)), dma((2,)),
            dma((2, 3, 7)), dma((2, 3, 8)), dma((2, 5)), dma((2, 2, 7)), dma((2, 2)),
        ],
        compiler_params=pltpu.CompilerParams(
            vmem_limit_bytes=61 * 1024 * 1024, collective_id=0, has_side_effects=True
        ),
        name="rest",
    )(length, sending, pack, placing, columns, residual, routed, cotangent, gain_two, w_router,
      window, hot, qkv, log_norm, attended, normed, tokens, gain, w_output, w_quad, w_in, w_out)


def finish_kernel(all_ref, d_in_ref, d_query_ref, d_key_ref, d_value_ref, d_output_ref, d_in_out_ref):
    quad, rows, full = all_ref.shape
    part = full // 4
    for kind, ref in enumerate((d_query_ref, d_key_ref, d_value_ref)):
        for i in range(rows // part):
            span = slice(i * part, (i + 1) * part)
            ref[span, :] = jnp.concatenate(
                [all_ref[m, span, kind * part : (kind + 1) * part].astype(F32) for m in range(quad)], axis=1
            )
    for m in range(quad):
        d_output_ref[m * part : (m + 1) * part, :] = jnp.concatenate(
            [all_ref[m, n * part : (n + 1) * part, 3 * part :].astype(F32) for n in range(quad)], axis=1
        )
    groups, local, count, hidden = d_in_ref.shape
    for g in range(groups):
        for e in range(local):
            d_in_out_ref[e, :, g * hidden : (g + 1) * hidden] = d_in_ref[g, e].astype(F32)


def finish(gathered, d_in):
    quad, rows, full = gathered.shape
    groups, local, count, hidden = d_in.shape
    vmem = pl.BlockSpec(memory_space=pltpu.VMEM)
    return pl.pallas_call(
        finish_kernel,
        in_specs=[vmem] * 2,
        out_specs=[vmem] * 5,
        out_shape=[jax.ShapeDtypeStruct((rows, full), F32)] * 4
        + [jax.ShapeDtypeStruct((local, count, groups * hidden), F32)],
        compiler_params=pltpu.CompilerParams(vmem_limit_bytes=VMEM_BYTES),
        name="finish",
    )(gathered, d_in)


def all_to_all(array, axis, groups=None):
    return lax.all_to_all(
        array, axis, split_axis=0, concat_axis=0, tiled=True, axis_index_groups=groups
    )


def to_experts(received, local):
    total, slots, width = received.shape
    shaped = received.reshape(total // local, local, slots, width)
    return jnp.swapaxes(shaped, 0, 1).reshape(local, total // local * slots, width)


def to_sources(by_expert, sources):
    local, total, width = by_expert.shape
    shaped = by_expert.reshape(local, sources, total // sources, width)
    return jnp.swapaxes(shaped, 0, 1).reshape(sources * local, total // sources, width)


def per_device(
    tokens, lengths, expert_ids, gain_one, w_query, w_key, w_value, w_output,
    bias_table, gain_two, w_router, w_in, w_out, cotangent,
):
    tok_rows, width = tokens.shape
    head_count = bias_table.shape[1]
    head_width = width // head_count
    expert_count = w_router.shape[1]
    local = w_in.shape[0]
    hidden = w_in.shape[2]
    dp_count, ex_count = lax.axis_size("dp"), lax.axis_size("expert")
    dp_index, ex_index = lax.axis_index("dp"), lax.axis_index("expert")
    span = dp_count // 2
    quad = math.gcd(span, head_count)
    heads = head_count // quad
    part = heads * head_width
    q_rows = quad * tok_rows
    q_parts = span // quad
    place = dp_index % span
    mine, q_part = place % quad, place // quad
    quads = [[i * quad + j for j in range(quad)] for i in range(dp_count // quad)]
    spans = [[i * span + j for j in range(span)] for i in range(dp_count // span)]
    seq_id = ex_index * (dp_count // span) + dp_index // span
    start_row = place * tok_rows

    length = jnp.sum(jnp.where(jnp.arange(lengths.shape[0], dtype=jnp.int32) == seq_id, lengths, 0))
    valid_mask = start_row + jnp.arange(tok_rows, dtype=jnp.int32) < length
    valid_f = valid_mask.astype(F32)
    length_arg = length.reshape(1)

    if q_parts == 1:
        tokens_all = all_to_all(
            jnp.broadcast_to(tokens[None], (quad, tok_rows, width)), "dp", quads
        ).reshape(q_rows, width)
        tokens_q = tokens_all
    else:
        tokens_all = lax.all_gather(tokens, "dp", axis_index_groups=spans, tiled=True)
        tokens_q = lax.dynamic_slice_in_dim(tokens_all, q_part * q_rows, q_rows, 0)
    gain_a = gain_one.astype(F32)
    normed_all = normalize(tokens_all.astype(F32), gain_a)[0].astype(BF16)
    normed_q = normalize(tokens_q.astype(F32), gain_a)[0].astype(BF16)

    table = lax.dynamic_slice_in_dim(bias_table.astype(F32), mine * heads, heads, 1)
    counts = span * tok_rows // tok_rows + quad - 1
    offset = jnp.arange(2 * tok_rows, dtype=jnp.int32)
    offset = jnp.where(offset < tok_rows, offset, offset - 2 * tok_rows)
    codes = (
        jnp.arange(counts, dtype=jnp.int32)[:, None] * tok_rows
        - offset[None, :]
        - (q_rows - tok_rows)
        - q_part * q_rows
    )
    window_hot = (
        bucket_of(codes)[:, :, None] == jnp.arange(table.shape[0], dtype=jnp.int32)
    ).astype(BF16)
    window = jnp.einsum("amb,bh->ham", window_hot, table.astype(BF16), preferred_element_type=F32)

    def my_columns(weight):
        return lax.dynamic_slice_in_dim(weight, mine * part, part, 1).reshape(
            width, heads, head_width
        )

    def project(rows, weight):
        return jnp.einsum(
            "sd,dhc->hsc", rows, my_columns(weight), preferred_element_type=F32
        ).astype(BF16)

    query = project(normed_q, w_query)
    key = project(normed_all, w_key)
    value = project(normed_all, w_value)
    attended_heads, log_norm = attend(length_arg, window, query, key, value)
    attended = all_to_all(
        jnp.transpose(
            attended_heads.reshape(heads, quad, tok_rows, head_width), (1, 2, 0, 3)
        ).reshape(quad, tok_rows, part),
        "dp",
        quads,
    )
    attended = jnp.swapaxes(attended, 0, 1).reshape(tok_rows, width)

    token_f = tokens.astype(F32)
    residual = token_f + dot(attended, w_output)
    gain_b = gain_two.astype(F32)
    routed_f, inverse_two = normalize(residual, gain_b)
    routed = routed_f.astype(BF16)
    router = jax.nn.softmax(dot(routed, w_router), axis=-1)

    chosen = expert_ids[:, 0]
    chosen_hot = chosen[:, None] == jnp.arange(expert_count, dtype=jnp.int32)[None, :]
    valid_hits = (chosen_hot & valid_mask[:, None]).astype(jnp.int32)
    per_source = lax.all_gather(jnp.sum(valid_hits, axis=0), "expert")
    earlier = jnp.arange(ex_count, dtype=jnp.int32)[:, None] < ex_index
    offsets = jnp.sum(jnp.where(earlier, per_source, 0), axis=0)
    local_rank = jnp.sum((jnp.cumsum(valid_hits, axis=0) - valid_hits) * valid_hits, axis=1)
    group_rank = local_rank + jnp.sum(valid_hits * offsets[None, :], axis=1)
    capacity = 5 * tok_rows // (4 * local)
    slots = 3 * tok_rows // (2 * expert_count)
    kept_mask = valid_mask & (group_rank < capacity)
    kept_f = kept_mask.astype(F32)
    target = jnp.where(kept_mask, chosen * slots + local_rank, -1)
    placing = (
        jnp.arange(expert_count * slots, dtype=jnp.int32)[:, None] == target[None, :]
    ).astype(BF16)
    chosen_f = chosen_hot.astype(F32)
    chosen_prob = jnp.sum(router * chosen_f, axis=1)
    gate = chosen_prob * kept_f
    upstream = cotangent.astype(F32) * valid_f[:, None]
    d_expert = (gate[:, None] * upstream).astype(BF16)

    sending = dot(placing, jnp.concatenate([routed, d_expert], axis=1)).astype(BF16)
    expert_rows = to_experts(
        all_to_all(sending.reshape(expert_count, slots, 2 * width), "expert"), local
    )
    group_rows = lax.all_gather(expert_rows, "dp")
    results = experts(expert_rows, w_in, w_out)
    returned = all_to_all(to_sources(results, ex_count), "expert")
    gathered = t_dot(placing, returned.reshape(expert_count * slots, 2 * width))
    expert_out, d_routed = gathered[:, :width], gathered[:, width:]

    output = (valid_f[:, None] * (residual + gate[:, None] * expert_out)).astype(BF16)
    d_gate = jnp.sum(upstream * expert_out, axis=1) * kept_f
    d_logits = router * (chosen_f - chosen_prob[:, None]) * d_gate[:, None]
    d_router = t_dot(routed, d_logits.astype(BF16))
    d_routed = d_routed + dot_t(d_logits.astype(BF16), w_router)
    d_norm_two, d_gain_two = norm_back(residual, inverse_two, gain_b, d_routed)
    d_residual = upstream + d_norm_two
    low_residual = d_residual.astype(BF16)
    d_attended = dot_t(low_residual, w_output).astype(BF16)
    d_output = t_dot(attended, low_residual)

    grad = all_to_all(
        jnp.swapaxes(d_attended.reshape(tok_rows, quad, part), 0, 1), "dp", quads
    ).reshape(q_rows, heads, head_width)
    grad = jnp.swapaxes(grad, 0, 1)
    d_query_rows, d_key_rows, d_value_rows, d_window = attend_back(
        length_arg, window, query, key, value, grad, log_norm
    )
    if q_parts > 1:
        strided = [
            [i * span + j + quad * n for n in range(q_parts)]
            for i in range(dp_count // span)
            for j in range(quad)
        ]
        d_key_rows, d_value_rows = [
            lax.psum_scatter(
                rows, "dp", scatter_dimension=1, axis_index_groups=strided, tiled=True
            )
            for rows in (d_key_rows, d_value_rows)
        ]
    d_rows = jnp.stack([d_query_rows, d_key_rows.astype(BF16), d_value_rows.astype(BF16)])
    d_parts = jnp.einsum("sd,khsc->dkhc", normed_q, d_rows, preferred_element_type=F32)
    d_table = jnp.einsum("amb,ham->bh", window_hot.astype(F32), d_window, precision="highest")
    d_mine = all_to_all(
        jnp.transpose(
            d_rows.reshape(3, heads, quad, tok_rows, head_width), (2, 3, 0, 1, 4)
        ).reshape(quad, tok_rows, 3 * part),
        "dp",
        quads,
    ).reshape(quad, tok_rows, 3, part)
    d_mine = jnp.transpose(d_mine, (2, 1, 0, 3)).reshape(3, tok_rows, width)
    d_normed = dot_t(d_mine[0], w_query) + dot_t(d_mine[1], w_key) + dot_t(d_mine[2], w_value)
    inverse_one = normalize(token_f, gain_a)[1]
    d_norm_one, d_gain_one = norm_back(token_f, inverse_one, gain_a, d_normed)
    d_tokens = d_residual + d_norm_one

    piece = hidden // dp_count
    my_in = lax.dynamic_slice_in_dim(w_in, dp_index * piece, piece, 2)
    my_out = lax.dynamic_slice_in_dim(w_out, dp_index * piece, piece, 1)
    d_in_piece, d_out = weight_grads(group_rows, my_in, my_out)
    d_in = all_to_all(
        jnp.swapaxes(d_in_piece.reshape(local, dp_count, width // dp_count, piece), 0, 1), "dp"
    )
    d_in = (
        jnp.transpose(d_in, (1, 2, 0, 3)).reshape(local, width // dp_count, hidden).astype(F32)
    )

    def spread(array, axis):
        wide = jnp.zeros(array.shape[:axis] + (array.shape[axis] * quad,) + array.shape[axis + 1 :], F32)
        return lax.dynamic_update_slice_in_dim(wide, array, mine * array.shape[axis], axis)

    d_parts = d_parts.reshape(width, 3, part)
    big = jnp.stack([spread(d_parts[:, n], 1) for n in range(3)] + [d_output])
    summed = lax.psum(big.astype(BF16), ("dp", "expert")).astype(F32)
    small = lax.psum(
        (d_gain_one, spread(d_table, 1), d_gain_two, d_router), ("dp", "expert")
    )
    return (
        output, d_tokens, small[0], summed[0], summed[1], summed[2], summed[3],
        small[1], small[2], small[3], d_in, d_out,
    )


def per_device_quad(
    tokens, lengths, expert_ids, gain_one, w_query, w_key, w_value, w_output,
    bias_table, gain_two, w_router, w_in, w_out, cotangent,
):
    tok_rows, width = tokens.shape
    head_count = bias_table.shape[1]
    expert_count = w_router.shape[1]
    local = w_in.shape[0]
    hidden = w_in.shape[2]
    dp_count, ex_count = lax.axis_size("dp"), lax.axis_size("expert")
    dp_index, ex_index = lax.axis_index("dp"), lax.axis_index("expert")
    quad = dp_count // 2
    heads = head_count // quad
    part = width // quad
    q_rows = quad * tok_rows
    mine = dp_index % quad
    quads = [[i * quad + j for j in range(quad)] for i in range(dp_count // quad)]
    seq_id = ex_index * 2 + dp_index // quad
    start_row = mine * tok_rows

    length = jnp.sum(jnp.where(jnp.arange(lengths.shape[0], dtype=jnp.int32) == seq_id, lengths, 0))
    valid_mask = start_row + jnp.arange(tok_rows, dtype=jnp.int32) < length
    valid_f = valid_mask.astype(F32)
    length_arg = length.reshape(1)

    tokens_all = all_to_all(
        jnp.broadcast_to(tokens[None], (quad, tok_rows, width)), "dp", quads
    ).reshape(q_rows, width)
    gain_a = gain_one.astype(F32)
    normed = normalize(tokens_all.astype(F32), gain_a)[0].astype(BF16)

    table = lax.dynamic_slice_in_dim(bias_table, mine * heads, heads, 1)
    counts = 2 * quad - 1
    offset = jnp.arange(2 * tok_rows, dtype=jnp.int32)
    offset = jnp.where(offset < tok_rows, offset, offset - 2 * tok_rows)
    codes = (
        jnp.arange(counts, dtype=jnp.int32)[:, None] * tok_rows
        - offset[None, :]
        - (q_rows - tok_rows)
    )
    window_hot = (
        bucket_of(codes)[:, :, None] == jnp.arange(table.shape[0], dtype=jnp.int32)
    ).astype(F32)
    window = jnp.einsum(
        "amb,bh->ham", window_hot.astype(BF16), table, preferred_element_type=F32
    )

    w_quad = jnp.transpose(
        jnp.stack([w.reshape(width, quad, part) for w in (w_query, w_key, w_value)], axis=1),
        (2, 0, 1, 3),
    ).reshape(quad, width, 3 * part)
    w_mine = lax.dynamic_index_in_dim(w_quad, mine, 0, keepdims=False)
    qkv = dot(normed, w_mine).astype(BF16)
    attended_heads, log_norm = attend_quad(length_arg, window, qkv)
    attended = all_to_all(attended_heads.reshape(quad, tok_rows, part), "dp", quads)
    attended = jnp.swapaxes(attended, 0, 1).reshape(tok_rows, width)

    token_f = tokens.astype(F32)
    residual = token_f + dot(attended, w_output)
    gain_b = gain_two.astype(F32)
    routed_f, inverse_two = normalize(residual, gain_b)
    routed = routed_f.astype(BF16)
    router = jax.nn.softmax(dot(routed, w_router), axis=-1)

    chosen = expert_ids[:, 0]
    chosen_hot = chosen[:, None] == jnp.arange(expert_count, dtype=jnp.int32)[None, :]
    valid_hits = (chosen_hot & valid_mask[:, None]).astype(jnp.int32)
    per_source = lax.all_gather(jnp.sum(valid_hits, axis=0), "expert")
    earlier = jnp.arange(ex_count, dtype=jnp.int32)[:, None] < ex_index
    offsets = jnp.sum(jnp.where(earlier, per_source, 0), axis=0)
    local_rank = jnp.sum((jnp.cumsum(valid_hits, axis=0) - valid_hits) * valid_hits, axis=1)
    group_rank = local_rank + jnp.sum(valid_hits * offsets[None, :], axis=1)
    capacity = 5 * tok_rows // (4 * local)
    slots = 3 * tok_rows // (2 * expert_count)
    kept_mask = valid_mask & (group_rank < capacity)
    kept_f = kept_mask.astype(F32)
    target = jnp.where(kept_mask, chosen * slots + local_rank, -1)
    placing = (
        jnp.arange(expert_count * slots, dtype=jnp.int32)[:, None] == target[None, :]
    ).astype(BF16)
    chosen_f = chosen_hot.astype(F32)
    chosen_prob = jnp.sum(router * chosen_f, axis=1)
    gate = chosen_prob * kept_f
    upstream = cotangent.astype(F32) * valid_f[:, None]
    d_expert = (gate[:, None] * upstream).astype(BF16)

    source = jnp.arange(ex_count * slots, dtype=jnp.int32) // slots
    turn = jnp.arange(ex_count * slots, dtype=jnp.int32) % slots
    my_counts = lax.dynamic_slice_in_dim(per_source, ex_index * local, local, 1)
    my_before = jnp.cumsum(my_counts, axis=0) - my_counts
    at = jnp.where(turn[:, None] < my_counts[source], my_before[source] + turn[:, None], -1)
    pack = (
        jnp.arange(capacity, dtype=jnp.int32)[None, :, None] == at.T[:, None, :]
    ).astype(BF16)

    sending = dot(placing, jnp.concatenate([routed, d_expert], axis=1)).astype(BF16)
    columns = jnp.concatenate(
        [
            router * (chosen_f - chosen_prob[:, None]), gate[:, None], valid_f[:, None], kept_f[:, None],
            jnp.zeros((tok_rows, 5), F32),
        ],
        axis=1,
    )
    output, d_tokens, d_weights, total, d_out, d_in_parts = rest(
        length_arg, sending.reshape(expert_count, slots, 2 * width), pack, placing, columns, residual,
        routed, cotangent, gain_b[None], w_router, window, jnp.swapaxes(window_hot, 1, 2), qkv, log_norm, attended_heads,
        normed, tokens, gain_a[None], w_output, w_quad, w_in, w_out,
    )
    d_query, d_key, d_value, d_output, d_in = finish(d_weights, d_in_parts)
    return (
        output, d_tokens, total[0], d_query, d_key, d_value, d_output,
        total[12:, : table.shape[0]].T, total[1], total[2 : 2 + expert_count].T, d_in, d_out,
    )


def solution(mesh):
    rows = P(("expert", "dp"), None)
    owned = P("expert", None, None)
    return jax.shard_map(
        per_device_quad if dict(mesh.shape) == {"dp": 8, "expert": 4} else per_device,
        mesh=mesh,
        in_specs=(
            rows, P(), rows, P(), P(), P(), P(), P(), P(), P(), P(), owned, owned, rows,
        ),
        out_specs=(
            rows, rows, P(), P(), P(), P(), P(), P(), P(), P(),
            P("expert", "dp", None), P("expert", "dp", None),
        ),
        check_vma=False,
    )
```

```python
import functools
import math

import jax
import jax.numpy as jnp
from jax import lax
from jax.experimental import pallas as pl
from jax.experimental.pallas import tpu as pltpu
from jax.sharding import PartitionSpec as P

BUCKETS = 32
EXACT = 8
MASKED = -1000000000.0
F32 = jnp.float32
BF16 = jnp.bfloat16
VMEM_BYTES = 56 * 1024 * 1024


def bucket_of(relative):
    distance = jnp.abs(relative)
    beyond = jnp.full(relative.shape, EXACT, jnp.int32)
    for level_step in range(1, BUCKETS // 2 - EXACT):
        boundary = math.isqrt(EXACT * EXACT * (1 << level_step) - 1) + 1
        beyond = beyond + (distance >= boundary).astype(jnp.int32)
    nearby = jnp.where(distance < EXACT, distance, beyond)
    return nearby + jnp.where(relative > 0, BUCKETS // 2, 0).astype(jnp.int32)


def normalize(values, gain):
    inverse = lax.rsqrt(jnp.mean(values * values, axis=-1, keepdims=True) + 1e-06)
    return (values * inverse * gain, inverse)


def norm_back(values, inverse, gain, upstream):
    scaled_up = upstream * gain
    d_gain = jnp.sum(upstream * values * inverse, axis=0)
    cubed = inverse * inverse * inverse
    d_values = inverse * scaled_up - values * cubed * jnp.mean(
        values * scaled_up, axis=-1, keepdims=True
    )
    return (d_values, d_gain)


def dot(left_side, right_side):
    return jnp.dot(left_side, right_side, preferred_element_type=F32)


def dot_t(left_side, right_side):
    return lax.dot_general(
        left_side, right_side, (((1,), (1,)), ((), ())), preferred_element_type=F32
    )


def t_dot(left_side, right_side):
    return lax.dot_general(
        left_side, right_side, (((0,), (0,)), ((), ())), preferred_element_type=F32
    )


def gelu_parts(value):
    scale = math.sqrt(2.0 / math.pi)
    square = value * value
    tanh = jnp.tanh(scale * (value + 0.044715 * value * square))
    half = 0.5 * (1.0 + tanh)
    slope = half + 0.5 * value * (1.0 - tanh * tanh) * scale * (1.0 + 3 * 0.044715 * square)
    return (value * half, slope)


def build_bias(win_ref, bias_ref):
    count, block, _ = bias_ref.shape

    @pl.loop(0, count)
    def _(index):
        row = win_ref[0, pl.ds(index, 1), :]
        wide = jnp.broadcast_to(row, (block, 2 * block))
        bias_ref[index] = pltpu.roll(wide, 0, 1, stride=1, stride_axis=0)[:, :block]


def attend_kernel(length_ref, win_ref, q_ref, k_ref, v_ref, o_ref, lse_ref, bias_ref):
    block = bias_ref.shape[1]
    q_blocks = q_ref.shape[1] // block
    k_blocks = k_ref.shape[1] // block
    build_bias(win_ref, bias_ref)
    length = length_ref[0]

    @pl.loop(0, q_blocks)
    def _(i):
        rows = pl.ds(pl.multiple_of(i * block, block), block)
        query = q_ref[0, rows, :]
        scores = []
        for j in range(k_blocks):
            part = dot_t(k_ref[0, j * block : (j + 1) * block, :], query)
            part = part + bias_ref[j - i + q_blocks - 1]
            position = lax.broadcasted_iota(jnp.int32, (block, 1), 0) + j * block
            scores.append(jnp.where(position < length, part, MASKED))
        top = functools.reduce(jnp.maximum, [jnp.max(s, axis=0, keepdims=True) for s in scores])
        total = jnp.zeros((1, block), F32)
        out = jnp.zeros((v_ref.shape[2], block), F32)
        for j in range(k_blocks):
            scaled = jnp.exp(scores[j] - top)
            total = total + jnp.sum(scaled, axis=0, keepdims=True)
            out = out + t_dot(v_ref[0, j * block : (j + 1) * block, :], scaled.astype(BF16))
        out = out * (1.0 / total)
        o_ref[0, rows, :] = out.T.astype(BF16)
        lse_ref[0, pl.ds(i, 1), :] = top + jnp.log(total)


def attend_back_kernel(
    length_ref, win_ref, q_ref, k_ref, v_ref, g_ref, lse_ref,
    dq_ref, dk_ref, dv_ref, dwin_ref, bias_ref, dbias_ref,
):
    block = bias_ref.shape[1]
    q_blocks = q_ref.shape[1] // block
    k_blocks = k_ref.shape[1] // block
    build_bias(win_ref, bias_ref)
    length = length_ref[0]
    dk_ref[...] = jnp.zeros_like(dk_ref)
    dv_ref[...] = jnp.zeros_like(dv_ref)
    dbias_ref[...] = jnp.zeros_like(dbias_ref)

    @pl.loop(0, q_blocks)
    def _(i):
        rows = pl.ds(pl.multiple_of(i * block, block), block)
        query = q_ref[0, rows, :]
        grad = g_ref[0, rows, :]
        log_norm = lse_ref[0, pl.ds(i, 1), :]
        probs, d_probs = [], []
        spread = jnp.zeros((1, block), F32)
        for j in range(k_blocks):
            keys = slice(j * block, (j + 1) * block)
            part = dot_t(k_ref[0, keys, :], query)
            part = part + bias_ref[j - i + q_blocks - 1]
            position = lax.broadcasted_iota(jnp.int32, (block, 1), 0) + j * block
            part = jnp.where(position < length, part, MASKED)
            prob = jnp.exp(part - log_norm)
            d_prob = dot_t(v_ref[0, keys, :], grad)
            spread = spread + jnp.sum(prob * d_prob, axis=0, keepdims=True)
            dv_ref[0, keys, :] += dot(prob.astype(BF16), grad)
            probs.append(prob)
            d_probs.append(d_prob)
        d_query = jnp.zeros((q_ref.shape[2], block), F32)
        for j in range(k_blocks):
            keys = slice(j * block, (j + 1) * block)
            d_score = probs[j] * (d_probs[j] - spread)
            dbias_ref[j - i + q_blocks - 1] += d_score
            low = d_score.astype(BF16)
            dk_ref[0, keys, :] += dot(low, query)
            d_query = d_query + t_dot(k_ref[0, keys, :], low)
        dq_ref[0, rows, :] = d_query.T.astype(BF16)

    @pl.loop(0, dbias_ref.shape[0])
    def _(index):
        wide = jnp.concatenate([dbias_ref[index], jnp.zeros((block, block), F32)], axis=1)
        half = block // 2
        while half:
            wide = wide[:half] + pltpu.roll(wide[half:], 2 * block - half, 1)
            half //= 2
        dwin_ref[0, pl.ds(index, 1), :] = wide


def head_block(rows, width):
    return pl.BlockSpec((1, rows, width), lambda h: (h, 0, 0))


def attend(length, window, query, key, value):
    heads, q_rows, width = query.shape
    k_rows = key.shape[1]
    count, block = window.shape[1], window.shape[2] // 2
    return pl.pallas_call(
        attend_kernel,
        grid=(heads,),
        in_specs=[
            pl.BlockSpec(memory_space=pltpu.SMEM),
            head_block(count, 2 * block),
            head_block(q_rows, width),
            head_block(k_rows, width),
            head_block(k_rows, width),
        ],
        out_specs=[head_block(q_rows, width), head_block(q_rows // block, block)],
        out_shape=[
            jax.ShapeDtypeStruct((heads, q_rows, width), BF16),
            jax.ShapeDtypeStruct((heads, q_rows // block, block), F32),
        ],
        scratch_shapes=[pltpu.VMEM((count, block, block), F32)],
        compiler_params=pltpu.CompilerParams(vmem_limit_bytes=VMEM_BYTES),
        name="attend",
    )(length, window, query, key, value)


def attend_back(length, window, query, key, value, grad, log_norm):
    heads, q_rows, width = query.shape
    k_rows = key.shape[1]
    count, block = window.shape[1], window.shape[2] // 2
    return pl.pallas_call(
        attend_back_kernel,
        grid=(heads,),
        in_specs=[
            pl.BlockSpec(memory_space=pltpu.SMEM),
            head_block(count, 2 * block),
            head_block(q_rows, width),
            head_block(k_rows, width),
            head_block(k_rows, width),
            head_block(q_rows, width),
            head_block(q_rows // block, block),
        ],
        out_specs=[
            head_block(q_rows, width),
            head_block(k_rows, width),
            head_block(k_rows, width),
            head_block(count, 2 * block),
        ],
        out_shape=[
            jax.ShapeDtypeStruct((heads, q_rows, width), BF16),
            jax.ShapeDtypeStruct((heads, k_rows, width), F32),
            jax.ShapeDtypeStruct((heads, k_rows, width), F32),
            jax.ShapeDtypeStruct((heads, count, 2 * block), F32),
        ],
        scratch_shapes=[pltpu.VMEM((count, block, block), F32) for _ in range(2)],
        compiler_params=pltpu.CompilerParams(vmem_limit_bytes=VMEM_BYTES),
        name="attend_back",
    )(length, window, query, key, value, grad, log_norm)


def experts_kernel(rows_ref, w_in_ref, w_out_ref, out_ref, acc_ref, back_ref):
    width = w_in_ref.shape[1]
    step = pl.program_id(1)

    @pl.when(step == 0)
    def _():
        acc_ref[...] = jnp.zeros_like(acc_ref)
        back_ref[...] = jnp.zeros_like(back_ref)

    inner = dot(rows_ref[0, :, :width], w_in_ref[0])
    active, slope = gelu_parts(inner)
    acc_ref[...] += dot(active.astype(BF16), w_out_ref[0])
    d_active = dot_t(rows_ref[0, :, width:], w_out_ref[0])
    d_inner = (d_active * slope).astype(BF16)
    back_ref[...] += dot_t(d_inner, w_in_ref[0])

    @pl.when(step == pl.num_programs(1) - 1)
    def _():
        out_ref[0, :, :width] = acc_ref[...].astype(BF16)
        out_ref[0, :, width:] = back_ref[...].astype(BF16)


def experts(rows, w_in, w_out):
    local, count, double = rows.shape
    width, hidden = w_in.shape[1:]
    piece = 512
    return pl.pallas_call(
        experts_kernel,
        grid=(local, hidden // piece),
        in_specs=[
            pl.BlockSpec((1, count, double), lambda e, f: (e, 0, 0)),
            pl.BlockSpec((1, width, piece), lambda e, f: (e, 0, f)),
            pl.BlockSpec((1, piece, width), lambda e, f: (e, f, 0)),
        ],
        out_specs=pl.BlockSpec((1, count, double), lambda e, f: (e, 0, 0)),
        out_shape=jax.ShapeDtypeStruct((local, count, double), BF16),
        scratch_shapes=[pltpu.VMEM((count, width), F32) for _ in range(2)],
        compiler_params=pltpu.CompilerParams(vmem_limit_bytes=VMEM_BYTES),
        name="experts",
    )(rows, w_in, w_out)


def weight_grads_kernel(rows_ref, w_in_ref, w_out_ref, d_in_ref, d_out_ref, acc_ref):
    width = w_in_ref.shape[1]
    step = pl.program_id(1)
    rows = rows_ref[...].reshape(rows_ref.shape[0] * rows_ref.shape[2], 2 * width)

    @pl.when(step == 0)
    def _():
        acc_ref[...] = jnp.zeros_like(acc_ref)
        d_out_ref[...] = jnp.zeros_like(d_out_ref)

    inner = dot(rows[:, :width], w_in_ref[0])
    active, slope = gelu_parts(inner)
    d_active = dot_t(rows[:, width:], w_out_ref[0])
    d_inner = (d_active * slope).astype(BF16)
    d_out_ref[0] += t_dot(active.astype(BF16), rows[:, width:])
    acc_ref[...] += t_dot(rows[:, :width], d_inner)

    @pl.when(step == pl.num_programs(1) - 1)
    def _():
        d_in_ref[0] = acc_ref[...].astype(BF16)


def weight_grads(rows, w_in, w_out):
    groups, local, count, double = rows.shape
    width, piece = w_in.shape[1:]
    together = 4
    return pl.pallas_call(
        weight_grads_kernel,
        grid=(local, groups // together),
        in_specs=[
            pl.BlockSpec((together, 1, count, double), lambda e, g: (g, e, 0, 0)),
            pl.BlockSpec((1, width, piece), lambda e, g: (e, 0, 0)),
            pl.BlockSpec((1, piece, width), lambda e, g: (e, 0, 0)),
        ],
        out_specs=[
            pl.BlockSpec((1, width, piece), lambda e, g: (e, 0, 0)),
            pl.BlockSpec((1, piece, width), lambda e, g: (e, 0, 0)),
        ],
        out_shape=[
            jax.ShapeDtypeStruct((local, width, piece), BF16),
            jax.ShapeDtypeStruct((local, piece, width), F32),
        ],
        scratch_shapes=[pltpu.VMEM((width, piece), F32)],
        compiler_params=pltpu.CompilerParams(vmem_limit_bytes=VMEM_BYTES),
        name="weight_grads",
    )(rows, w_in, w_out)


class Place:
    def __init__(self):
        self.dp, self.ex = lax.axis_index("dp"), lax.axis_index("expert")
        self.y = lax.rem(self.dp, 2)
        self.z = lax.div(self.dp, 2)
        self.z_lo = lax.rem(self.z, 2)
        self.z_hi = lax.div(self.dp, 4)
        self.core = lax.rem(self.ex, 2)
        self.x = lax.div(self.ex, 2)
        self.member = self.z_lo * 2 + self.y

    def flip(self, *names):
        c = {n: getattr(self, n) for n in ("y", "z_lo", "z_hi", "core", "x")}
        for name in names:
            c[name] = 1 - c[name]
        return (c["z_hi"] * 4 + c["z_lo"] * 2 + c["y"], c["x"] * 2 + c["core"])

    def quad_others(self):
        found = []
        for names in (("y",), ("z_lo",), ("y", "z_lo")):
            device = self.flip(*names)
            found.append((device, lax.rem(device[0], 4)))
        return found

    def expert_others(self):
        return [self.flip(*names) for names in (("core",), ("x",), ("core", "x"))]

    def dp_others(self):
        names = (("y",), ("z_lo",), ("y", "z_lo"), ("z_hi",), ("z_hi", "y"), ("z_hi", "z_lo"), ("z_hi", "y", "z_lo"))
        return [self.flip(*n) for n in names]


def remote(src, dst, sems, index, device):
    return pltpu.make_async_remote_copy(
        src_ref=src, dst_ref=dst, send_sem=sems.at[(0,) + index], recv_sem=sems.at[(1,) + index],
        device_id=device, device_id_type=pl.DeviceIdType.MESH,
    )


def send(src, dst, sems, index, device):
    copy = remote(src, dst, sems, index, device)
    copy.start()
    return copy


def greet(devices):
    barrier = pltpu.get_barrier_semaphore()
    for device in devices:
        pl.semaphore_signal(barrier, inc=1, device_id=device, device_id_type=pl.DeviceIdType.MESH)
    pl.semaphore_wait(barrier, len(devices))


class Relay:
    def __init__(self, place, ref, line_sems, cross_sems):
        self.ref, self.line_sems, self.cross_sems = ref, line_sems, cross_sems
        self.dp, self.ex, self.z = place.dp, place.ex, place.z
        self.across = place.flip("y")

    def block(self, offset):
        return self.ref.at[self.dp + 2 * offset]

    def along(self, direction, step, offset):
        neighbour = (self.dp + 2, self.ex) if direction else (self.dp - 2, self.ex)
        return remote(self.block(offset), self.block(offset), self.line_sems, (direction, step), neighbour)

    def over(self, index, offset):
        return remote(self.block(offset), self.block(offset), self.cross_sems, (index,), self.across)

    def begin(self):
        self.over(0, 0).start()

        @pl.when(self.z < 3)
        def _():
            self.along(1, 0, 0).start()

        @pl.when(self.z > 0)
        def _():
            self.along(0, 0, 0).start()

    def step(self, k):
        @pl.when(self.z >= k)
        def _():
            self.along(1, k - 1, -k).wait_recv()
            self.over(k, -k).start()
            if k < 3:

                @pl.when(self.z < 3)
                def _():
                    self.along(1, k, -k).start()

        @pl.when(self.z + k <= 3)
        def _():
            self.along(0, k - 1, k).wait_recv()
            self.over(3 + k, k).start()
            if k < 3:

                @pl.when(self.z > 0)
                def _():
                    self.along(0, k, k).start()

    def end(self):
        self.over(0, 0).wait()
        for k in (1, 2, 3):

            @pl.when(self.z >= k)
            def _():
                self.over(k, -k).wait()

            @pl.when(self.z + k <= 3)
            def _():
                self.over(3 + k, k).wait()

        for k in (0, 1, 2):

            @pl.when((self.z >= k) & (self.z < 3))
            def _():
                self.along(1, k, -k).wait_send()

            @pl.when((self.z + k <= 3) & (self.z > 0))
            def _():
                self.along(0, k, k).wait_send()


def exact_dot(left_side, right_side, left_dim, right_dim):
    return lax.dot_general(
        left_side, right_side, (((left_dim,), (right_dim,)), ((), ())),
        precision=lax.Precision.HIGHEST, preferred_element_type=F32,
    )


def layer_kernel(
    lengths_ref, token_ref, ids_ref, cotangent_ref, gain_one_ref, gain_two_ref, w_query_ref, w_key_ref,
    w_value_ref, w_output_ref, w_router_ref, table_ref, hot_ref, w_in_ref, w_out_ref,
    output_ref, d_tokens_ref, d_weights_ref, total_ref, d_out_ref, d_in_ref,
    w_mine_ref, normed_ref, qkv_ref, win_ref, lse_ref, attended_ref, attended_recv,
    count_send, count_ref, slot_send, up_arrive, rows_arrive, gate_send, gate_arrive, place_ref, pack_ref,
    up_ref, rows_ref, in_buf, out_buf, result_ref, back_send, back_ref, residual_ref,
    grad_ref, grad_send, low_ref, bias_ref, dbias_ref, dkey_ref, dvalue_ref, dqkv_ref,
    dmine_ref, load_ref, first_ref, second_ref, third_ref, sum_one_ref, sum_two_ref,
    small_send, small_recv, active_ref, inner_ref, d_in_send, d_residual_ref,
    token_sems, count_sems, up_sems, attended_sems, go_sems, gate_sems, weight_sems,
    up_line_sems, up_cross_sems, line_sems, cross_sems, back_sems,
    grad_sems, low_sems, mine_sems, first_sems, second_sems, third_sems, ring_sems, core_sems,
    small_sems, d_in_sems, block_sems,
):
    place = Place()
    mine, ex, dp, z = place.member, place.ex, place.dp, place.z
    block = bias_ref.shape[1]
    part = qkv_ref.shape[1] // 3
    head_width = dkey_ref.shape[1]
    heads = part // head_width
    blocks = quad = qkv_ref.shape[0] // block
    width = normed_ref.shape[1]
    sources, local, slots = rows_arrive.shape[:3]
    groups, _, capacity = up_ref.shape[:3]
    experts_count = local * sources
    length = lengths_ref[ex * 2 + place.z_hi]
    piece = in_buf.shape[2]
    pieces = w_in_ref.shape[2] // piece
    depth = in_buf.shape[0]
    hidden = active_ref.shape[2]
    my_hidden = pl.ds(pl.multiple_of(dp * hidden, hidden), hidden)
    diagonal = lax.broadcasted_iota(jnp.int32, (capacity, capacity), 0) == lax.broadcasted_iota(
        jnp.int32, (capacity, capacity), 1
    )

    def my_rows(index):
        return pl.ds(pl.multiple_of(index * block, block), block)

    def fill_bias(h):
        @pl.loop(0, bias_ref.shape[0])
        def _(index):
            wide = jnp.broadcast_to(win_ref[index, pl.ds(mine * heads + h, 1), :], (block, 2 * block))
            bias_ref[index] = pltpu.roll(wide, 0, 1, stride=1, stride_axis=0)[:, :block]

    quad_others = place.quad_others()
    expert_others = place.expert_others()
    dp_others = place.dp_others()
    up_relay = Relay(place, up_ref, up_line_sems, up_cross_sems)
    rows_relay = Relay(place, rows_ref, line_sems, cross_sems)

    def weight_copies(n):
        e, f, slot = n // pieces, n % pieces, n % depth
        return (
            pltpu.make_async_copy(
                w_in_ref.at[e, :, f * piece : (f + 1) * piece], in_buf.at[slot], weight_sems.at[0, slot]
            ),
            pltpu.make_async_copy(
                w_out_ref.at[e, f * piece : (f + 1) * piece, :], out_buf.at[slot], weight_sems.at[1, slot]
            ),
        )

    def block_copies(e):
        return (
            pltpu.make_async_copy(w_in_ref.at[e, :, my_hidden], in_buf.at[e, :, :hidden], block_sems.at[0, e]),
            pltpu.make_async_copy(w_out_ref.at[e, my_hidden, :], out_buf.at[e, :hidden, :], block_sems.at[1, e]),
        )

    for n in range(depth):
        for copy in weight_copies(n):
            copy.start()

    greet(dp_others + expert_others)

    tokens_going = [
        send(token_ref, low_ref.at[my_rows(mine)], token_sems, (n,), device)
        for n, (device, _) in enumerate(quad_others)
    ]
    low_ref[my_rows(mine), :] = token_ref[...]

    ids = ids_ref[...]
    position = lax.broadcasted_iota(jnp.int32, (block, 1), 0)
    valid = (position + mine * block < length).astype(F32)
    chosen = (lax.broadcasted_iota(jnp.int32, (block, experts_count), 1) == ids).astype(F32)
    hits = chosen * valid
    below = (
        lax.broadcasted_iota(jnp.int32, (block, block), 1) < lax.broadcasted_iota(jnp.int32, (block, block), 0)
    ).astype(BF16)
    rank = jnp.sum(dot(below, hits.astype(BF16)) * hits, axis=1, keepdims=True)
    count_send[...] = jnp.zeros_like(count_send)
    count_send[0:1, :experts_count] = jnp.sum(hits, axis=0, keepdims=True)
    counts_going = [
        send(count_send, count_ref.at[ex], count_sems, (n,), device) for n, device in enumerate(expert_others)
    ]
    count_ref[ex] = count_send[...]
    target = jnp.where(valid > 0, ids.astype(F32) * slots + rank, -1.0).astype(jnp.int32)
    place_ref[...] = (
        lax.broadcasted_iota(jnp.int32, place_ref.shape, 1) == target
    ).astype(BF16)

    slot_send[...] = t_dot(place_ref[...], cotangent_ref[...]).astype(BF16).reshape(slot_send.shape)

    def scatter(arrive, sems):
        going = [
            send(slot_send.at[pl.ds(device[1] * local, local)], arrive.at[ex], sems, (n,), device)
            for n, device in enumerate(expert_others)
        ]
        arrive[ex] = slot_send[pl.ds(ex * local, local)]
        return going

    ups_going = scatter(up_arrive, up_sems)

    for m in range(quad):

        @pl.when(mine == m)
        def _():
            for kind, weight_ref in enumerate((w_query_ref, w_key_ref, w_value_ref)):
                w_mine_ref[:, kind * part : (kind + 1) * part] = weight_ref[:, m * part : (m + 1) * part]

    for a in range(win_ref.shape[0]):
        win_ref[a] = dot(table_ref[...], hot_ref[a])
    fill_bias(0)

    for copy in counts_going:
        copy.wait()
    before = jnp.zeros((1, experts_count), F32)
    for s in range(sources):
        before = before + count_ref[s, 0:1, :experts_count] * (s < ex).astype(F32)
    kept = valid * (rank + jnp.sum(hits * before, axis=1, keepdims=True) < capacity).astype(F32)
    lane = lax.broadcasted_iota(jnp.int32, (1, sources * slots), 1)
    expert_lane = lax.broadcasted_iota(jnp.int32, (1, count_ref.shape[2]), 1)
    for e in range(local):
        at = jnp.full((1, sources * slots), -1, jnp.int32)
        start = jnp.zeros((1, 1), F32)
        for s in range(sources):
            count = jnp.sum(
                jnp.where(expert_lane == ex * local + e, count_ref[s, 0:1, :], 0.0), axis=1, keepdims=True
            )
            turn = lane - s * slots
            here = (turn >= 0) & (turn < slots) & (turn < count.astype(jnp.int32))
            at = jnp.where(here, start.astype(jnp.int32) + turn, at)
            start = start + count
        pack_ref[e] = (lax.broadcasted_iota(jnp.int32, (capacity, sources * slots), 0) == at).astype(BF16)

    for copy in tokens_going:
        copy.wait()
    gain = gain_one_ref[...].astype(F32)

    @pl.loop(0, blocks)
    def _(i):
        token = low_ref[my_rows(i), :].astype(F32)
        inverse = lax.rsqrt(jnp.mean(token * token, axis=-1, keepdims=True) + 1e-06)
        normed = (token * inverse * gain).astype(BF16)
        normed_ref[my_rows(i), :] = normed
        qkv_ref[my_rows(i), :] = dot(normed, w_mine_ref[...]).astype(BF16)

    for copy in ups_going:
        copy.wait()
    for e in range(local):
        up_ref[dp, e] = dot(pack_ref[e], up_arrive[:, e].reshape(sources * slots, width)).astype(BF16)
    up_relay.begin()

    for h in range(heads):
        if h:
            fill_bias(h)
        cols = slice(h * head_width, (h + 1) * head_width)
        key = qkv_ref[:, part + h * head_width : part + (h + 1) * head_width]
        value = qkv_ref[:, 2 * part + h * head_width : 2 * part + (h + 1) * head_width]

        @pl.loop(0, blocks)
        def _(i):
            rows = my_rows(i)
            query = qkv_ref[rows, cols]
            scores = []
            for j in range(blocks):
                score = dot_t(key[j * block : (j + 1) * block], query)
                score = score + bias_ref[j - i + blocks - 1]
                scores.append(jnp.where(position + j * block < length, score, MASKED))
            top = functools.reduce(
                jnp.maximum, [jnp.max(s, axis=0, keepdims=True) for s in scores]
            )
            total = jnp.zeros((1, block), F32)
            out = jnp.zeros((head_width, block), F32)
            for j in range(blocks):
                scaled = jnp.exp(scores[j] - top)
                total = total + jnp.sum(scaled, axis=0, keepdims=True)
                out = out + t_dot(value[j * block : (j + 1) * block], scaled.astype(BF16))
            out = out * (1.0 / total)
            attended_ref[rows, cols] = out.T.astype(BF16)
            lse_ref[h, pl.ds(i, 1), :] = top + jnp.log(total)

        if h == 1:
            up_relay.step(1)

    attended_going = [
        send(attended_ref.at[my_rows(member)], attended_recv.at[mine], attended_sems, (n,), device)
        for n, (device, member) in enumerate(quad_others)
    ]
    attended_recv[mine] = attended_ref[my_rows(mine), :]
    for copy in attended_going:
        copy.wait()
    attended = jnp.concatenate([attended_recv[m] for m in range(quad)], axis=1)
    residual = token_ref[...].astype(F32) + dot(attended, w_output_ref[...])
    residual_ref[...] = residual
    inverse = lax.rsqrt(jnp.mean(residual * residual, axis=-1, keepdims=True) + 1e-06)
    gain_two = gain_two_ref[...].astype(F32)
    routed = (residual * inverse * gain_two).astype(BF16)

    slot_send[...] = t_dot(place_ref[...], routed).astype(BF16).reshape(slot_send.shape)
    rows_going = scatter(rows_arrive, go_sems)
    logits = dot(routed, w_router_ref[...])
    router = jnp.exp(logits - jnp.max(logits, axis=1, keepdims=True))
    router = router / jnp.sum(router, axis=1, keepdims=True)
    chosen_prob = jnp.sum(router * chosen, axis=1, keepdims=True)
    gate = chosen_prob * kept
    slopes = router * (chosen - chosen_prob)
    gate_slots = exact_dot(jnp.broadcast_to(gate, (block, 8)), place_ref[...].astype(F32), 0, 0)
    gate_send[...] = jnp.zeros_like(gate_send)
    for e in range(experts_count):
        gate_send[e, :, :slots] = gate_slots[:, e * slots : (e + 1) * slots]
    gates_going = [
        send(gate_send.at[pl.ds(device[1] * local, local)], gate_arrive.at[ex], gate_sems, (n,), device)
        for n, device in enumerate(expert_others)
    ]
    gate_arrive[ex] = gate_send[pl.ds(ex * local, local)]
    up_relay.step(2)
    for copy in rows_going:
        copy.wait()
    for e in range(local):
        rows_ref[dp, e * capacity : (e + 1) * capacity, :] = dot(
            pack_ref[e], rows_arrive[:, e].reshape(sources * slots, width)
        ).astype(BF16)
    for copy in gates_going:
        copy.wait()
    rows_ref[dp, local * capacity :, :] = jnp.zeros((rows_ref.shape[1] - local * capacity, width), BF16)
    gate_lines = jnp.zeros((rows_ref.shape[1] - local * capacity, capacity), F32)
    line = lax.broadcasted_iota(jnp.int32, gate_lines.shape, 0)
    gate_columns = []
    for e in range(local):
        arrived = jnp.concatenate([gate_arrive[s, e, :, :slots] for s in range(sources)], axis=1)
        pack = pack_ref[e].astype(F32)
        gate_columns.append(exact_dot(pack, arrived, 1, 1)[:, 0:1])
        rest = exact_dot(arrived, pack, 1, 1)[0:1]
        for n in range(3):
            high = rest.astype(BF16).astype(F32)
            gate_lines = jnp.where(line == 3 * e + n, high, gate_lines)
            rest = rest - high
    rows_ref[dp, local * capacity :, :capacity] = gate_lines.astype(BF16)
    rows_relay.begin()

    backs = []
    for e in range(local):
        rows = rows_ref[dp, e * capacity : (e + 1) * capacity, :]
        d_rows = (gate_columns[e] * up_ref[dp, e].astype(F32)).astype(BF16)
        for f in range(pieces):
            n = e * pieces + f
            for copy in weight_copies(n):
                copy.wait()
            weight_in = in_buf[n % depth]
            weight_out = out_buf[n % depth]
            active, slope = gelu_parts(dot(rows, weight_in))
            forward = dot(active.astype(BF16), weight_out)
            d_inner = (dot_t(d_rows, weight_out) * slope).astype(BF16)
            backward = dot_t(d_inner, weight_in)
            if f == 0:
                result_ref[:, :width] = forward
                result_ref[:, width:] = backward
            else:
                result_ref[:, :width] += forward
                result_ref[:, width:] += backward
            if n + depth < local * pieces:
                for copy in weight_copies(n + depth):
                    copy.start()
        spread_rows = t_dot(pack_ref[e], result_ref[...].astype(BF16)).astype(BF16)
        back_send[:, e] = spread_rows.reshape(sources, slots, 2 * width)
        for n, device in enumerate(expert_others):
            backs.append(
                send(back_send.at[device[1], e], back_ref.at[ex * local + e], back_sems, (e, n), device)
            )
        back_ref[ex * local + e] = back_send[ex, e]
        if e == 0:
            up_relay.step(3)
    for e in range(local):
        for copy in block_copies(e):
            copy.start()
    fill_bias(0)
    for copy in backs:
        copy.wait()

    gathered = dot(place_ref[...], back_ref[...].reshape(experts_count * slots, 2 * width))
    expert_out = gathered[:, :width]
    residual = residual_ref[...]
    output_ref[...] = (valid * (residual + gate * expert_out)).astype(BF16)
    upstream = cotangent_ref[...].astype(F32) * valid
    d_gate = jnp.sum(upstream * expert_out, axis=1, keepdims=True) * kept
    d_logits = (slopes * d_gate).astype(BF16)
    small_send[0] = jnp.zeros(small_send.shape[1:], F32)
    inverse = lax.rsqrt(jnp.mean(residual * residual, axis=-1, keepdims=True) + 1e-06)
    routed = (residual * inverse * gain_two).astype(BF16)
    small_send[0, 2:10, :] = t_dot(d_logits, routed)
    d_routed = gathered[:, width:] + dot_t(d_logits, w_router_ref[...])
    small_send[0, 1:2, :] = jnp.sum(d_routed * residual * inverse, axis=0, keepdims=True)
    scaled = d_routed * gain_two
    cubed = inverse * inverse * inverse
    d_residual = upstream + inverse * scaled - residual * cubed * jnp.mean(
        residual * scaled, axis=-1, keepdims=True
    )
    d_residual_ref[...] = d_residual

    low = d_residual.astype(BF16)
    low_ref[my_rows(mine), :] = low
    d_attended = dot_t(low, w_output_ref[...]).astype(BF16)
    for m in range(quad):
        grad_send[m] = d_attended[:, m * part : (m + 1) * part]
    copies = []
    for n, (device, member) in enumerate(quad_others):
        copies.append(
            send(grad_send.at[member], grad_ref.at[my_rows(mine)], grad_sems, (n,), device)
        )
    low_copies = []
    for n, (device, member) in enumerate(quad_others):
        low_copies.append(
            send(low_ref.at[my_rows(mine)], low_ref.at[my_rows(mine)], low_sems, (n,), device)
        )
    grad_ref[my_rows(mine), :] = grad_send[mine]
    rows_relay.step(1)
    for copy in copies:
        copy.wait()

    for h in range(heads):
        if h:
            fill_bias(h)
        cols = slice(h * head_width, (h + 1) * head_width)
        key = qkv_ref[:, part + h * head_width : part + (h + 1) * head_width]
        value = qkv_ref[:, 2 * part + h * head_width : 2 * part + (h + 1) * head_width]
        dkey_ref[...] = jnp.zeros_like(dkey_ref)
        dvalue_ref[...] = jnp.zeros_like(dvalue_ref)
        dbias_ref[...] = jnp.zeros_like(dbias_ref)

        @pl.loop(0, blocks)
        def _(i):
            rows = my_rows(i)
            query = qkv_ref[rows, cols]
            grad = grad_ref[rows, cols]
            log_norm = lse_ref[h, pl.ds(i, 1), :]
            probs, d_probs = [], []
            spread = jnp.zeros((1, block), F32)
            for j in range(blocks):
                keys = slice(j * block, (j + 1) * block)
                score = dot_t(key[keys], query)
                score = score + bias_ref[j - i + blocks - 1]
                position = lax.broadcasted_iota(jnp.int32, (block, 1), 0) + j * block
                score = jnp.where(position < length, score, MASKED)
                prob = jnp.exp(score - log_norm)
                d_prob = dot_t(value[keys], grad)
                spread = spread + jnp.sum(prob * d_prob, axis=0, keepdims=True)
                dvalue_ref[keys, :] += dot(prob.astype(BF16), grad)
                probs.append(prob)
                d_probs.append(d_prob)
            d_query = jnp.zeros((head_width, block), F32)
            for j in range(blocks):
                keys = slice(j * block, (j + 1) * block)
                d_score = probs[j] * (d_probs[j] - spread)
                dbias_ref[j - i + blocks - 1] += d_score
                low_score = d_score.astype(BF16)
                dkey_ref[keys, :] += dot(low_score, query)
                d_query = d_query + t_dot(key[keys], low_score)
            dqkv_ref[rows, cols] = d_query.T.astype(BF16)

        dqkv_ref[:, part + h * head_width : part + (h + 1) * head_width] = dkey_ref[...].astype(BF16)
        dqkv_ref[:, 2 * part + h * head_width : 2 * part + (h + 1) * head_width] = dvalue_ref[...].astype(BF16)
        table_row = jnp.zeros((1, hot_ref.shape[1]), F32)
        for a in range(dbias_ref.shape[0]):
            wide = jnp.concatenate([dbias_ref[a], jnp.zeros((block, block), F32)], axis=1)
            half = block // 2
            while half:
                wide = wide[:half] + pltpu.roll(wide[half:], 2 * block - half, 1)
                half //= 2
            table_row = table_row + lax.dot_general(
                wide, hot_ref[a].astype(F32), (((1,), (1,)), ((), ())),
                precision=lax.Precision.HIGHEST, preferred_element_type=F32,
            )
        for m in range(quad):
            row = 12 + m * heads + h
            small_send[0, row : row + 1, : hot_ref.shape[1]] = jnp.where(mine == m, table_row, 0.0)
        if h < 2:
            rows_relay.step(2 + h)

    mine_copies = []
    for n, (device, member) in enumerate(quad_others):
        mine_copies.append(
            send(dqkv_ref.at[my_rows(member)], dmine_ref.at[mine], mine_sems, (n,), device)
        )
    dmine_ref[mine] = dqkv_ref[my_rows(mine), :]

    d_parts = t_dot(normed_ref[...], dqkv_ref[...])
    d_gain = lax.dot_general(
        jnp.ones((8, 3 * part), F32), d_parts * w_mine_ref[...].astype(F32), (((1,), (1,)), ((), ())),
        precision=lax.Precision.HIGHEST, preferred_element_type=F32,
    )
    load_ref[:, : 3 * part] = d_parts.astype(BF16)
    small_send[0, 0:1, :] = d_gain[0:1] / gain
    for copy in low_copies:
        copy.wait()
    d_output = t_dot(attended_ref[...], low_ref[...]).astype(BF16)
    for m in range(quad):
        load_ref[m * part : (m + 1) * part, 3 * part :] = d_output[:, m * part : (m + 1) * part]

    core, x = place.core, place.x
    quarter = load_ref.shape[0] // 4

    def chunk(c, b):
        return pl.ds(pl.multiple_of((c * 2 + b) * quarter, quarter), quarter)

    core_device, x_device, z_device = place.flip("core"), place.flip("x"), place.flip("z_hi")
    one = [
        send(load_ref.at[chunk(1 - core, 1 - x)], first_ref.at[0], first_sems, (0,), core_device),
        send(load_ref.at[chunk(1 - core, x)], first_ref.at[1], first_sems, (1,), core_device),
    ]
    small_devices = [core_device, x_device, z_device, quad_others[0][0], quad_others[1][0]]
    small_copies = []

    def small_start(n):
        small_copies.append(
            send(small_send.at[n], small_recv.at[n], small_sems, (n,), small_devices[n])
        )

    def small_end(n):
        small_copies[n].wait()
        total = small_send[n] + small_recv[n]
        if n + 1 < len(small_devices):
            small_send[n + 1] = total
        else:
            total_ref[...] = total

    small_start(0)

    for copy in mine_copies:
        copy.wait()
    d_normed = jnp.zeros((block, width), F32)
    for kind, weight_ref in enumerate((w_query_ref, w_key_ref, w_value_ref)):
        d_kind = [dmine_ref[m, :, kind * part : (kind + 1) * part] for m in range(quad)]
        d_normed = d_normed + dot_t(jnp.concatenate(d_kind, axis=1), weight_ref[...])

    one[0].wait()
    sum_one_ref[...] = (load_ref[chunk(core, 1 - x), :].astype(F32) + first_ref[0].astype(F32)).astype(BF16)
    two = send(sum_one_ref, second_ref, second_sems, (), x_device)
    small_end(0)
    small_start(1)
    token = token_ref[...].astype(F32)
    inverse = lax.rsqrt(jnp.mean(token * token, axis=-1, keepdims=True) + 1e-06)
    scaled = d_normed * gain
    cubed = inverse * inverse * inverse
    d_tokens_ref[...] = d_residual_ref[...] + inverse * scaled - token * cubed * jnp.mean(
        token * scaled, axis=-1, keepdims=True
    )
    one[1].wait()
    two.wait()
    sum_two_ref[...] = (
        load_ref[chunk(core, x), :].astype(F32) + first_ref[1].astype(F32) + second_ref[...].astype(F32)
    ).astype(BF16)
    three = send(sum_two_ref, third_ref, third_sems, (), z_device)
    small_end(1)
    small_start(2)

    up_relay.end()
    rows_relay.end()
    d_in_copies = []

    def hidden_gradients(e):
        for copy in block_copies(e):
            copy.wait()
        for g in range(groups):
            rows = rows_ref[g, e * capacity : (e + 1) * capacity, :]
            gates = rows_ref[g, local * capacity :, :capacity].astype(F32)
            gate_row = gates[3 * e : 3 * e + 1] + gates[3 * e + 1 : 3 * e + 2] + gates[3 * e + 2 : 3 * e + 3]
            gate_column = jnp.sum(jnp.where(diagonal, gate_row, 0.0), axis=1, keepdims=True)
            d_rows = (gate_column * up_ref[g, e].astype(F32)).astype(BF16)
            up_ref[g, e] = d_rows
            active, slope = gelu_parts(dot(rows, in_buf[e, :, :hidden]))
            inner_ref[g] = (dot_t(d_rows, out_buf[e, :hidden, :]) * slope).astype(BF16)
            active_ref[g] = active.astype(BF16)
        all_rows = rows_ref[:, e * capacity : (e + 1) * capacity, :].reshape(groups * capacity, width)
        all_d_rows = up_ref[:, e].reshape(groups * capacity, width)
        d_in = t_dot(all_rows, inner_ref[...].reshape(groups * capacity, hidden))
        d_in_send[:, e] = d_in.astype(BF16).reshape(groups, width // groups, hidden)
        for n, device in enumerate(dp_others):
            d_in_copies.append(
                send(d_in_send.at[device[0], e], d_in_ref.at[dp, e], d_in_sems, (e, n), device)
            )
        d_in_ref[dp, e] = d_in_send[dp, e]
        d_out_ref[e] = t_dot(active_ref[...].reshape(groups * capacity, hidden), all_d_rows)

    hidden_gradients(0)
    three.wait()

    d_weights_ref[mine, chunk(core, x), :] = (
        sum_two_ref[...].astype(F32) + third_ref[...].astype(F32)
    ).astype(BF16)
    thirds = 3
    third = quarter // thirds
    steps = {"x": x_device, "y": quad_others[0][0], "z": quad_others[1][0]}

    def spot(axes, t):
        y = 1 - place.y if "y" in axes else place.y
        z_lo = 1 - place.z_lo if "z" in axes else place.z_lo
        xx = 1 - x if "x" in axes else x
        row = pl.multiple_of((core * 2 + xx) * quarter + t * third, third)
        return d_weights_ref.at[z_lo * 2 + y, pl.ds(row, third)]

    orders = ("xyz", "yzx", "zxy")
    passed = []

    def to_core(axes, t, n):
        where = spot(axes, t)
        passed.append(send(where, where, core_sems, (t, n), core_device))

    rings = {}

    def forward(axes, t, axis, n):
        where = spot(axes, t)
        rings[t, n] = send(where, where, ring_sems, (t, n), steps[axis])

    for t, (a, b, c) in enumerate(orders):
        forward("", t, a, 0)
        forward("", t, b, 1)
        forward("", t, c, 3)
        to_core("", t, 0)
    small_end(2)
    small_start(3)
    hidden_gradients(1)
    for t, (a, b, c) in enumerate(orders):
        rings[t, 0].wait_recv()
        forward(a, t, b, 2)
        forward(a, t, c, 4)
        to_core(a, t, 1)
    small_end(3)
    small_start(4)
    for t, (a, b, c) in enumerate(orders):
        rings[t, 1].wait_recv()
        forward(b, t, c, 5)
        to_core(b, t, 2)
        rings[t, 2].wait_recv()
        forward(a + b, t, c, 6)
        to_core(a + b, t, 3)
    small_end(4)
    for t, (a, b, c) in enumerate(orders):
        for n, axes in ((3, c), (4, a + c), (5, b + c), (6, a + b + c)):
            rings[t, n].wait_recv()
            to_core(axes, t, n + 1)
    for t in range(thirds):
        for n in range(7):
            rings[t, n].wait_send()
    for copy in passed:
        copy.wait()
    for copy in d_in_copies:
        copy.wait()


def layer(lengths, tokens, ids, cotangent, gain_one, gain_two, w_query, w_key, w_value, w_output, w_router, table, hot, w_in, w_out, head_count):
    block, full = tokens.shape
    count, _, double = hot.shape
    quad = (count + 1) // 2
    rows = quad * block
    part = full // quad
    triple = 3 * part
    heads = head_count // quad
    head_width = part // heads
    quarter = full // 4
    experts_count = w_router.shape[1]
    local = w_in.shape[0]
    sources = experts_count // local
    capacity = 5 * block // (4 * local)
    slots = 3 * block // (2 * experts_count)
    groups = lax.axis_size("dp")
    hidden = w_in.shape[2] // groups
    piece = 512
    depth = 3
    small = (24, full)
    extra = 16
    vmem = pl.BlockSpec(memory_space=pltpu.VMEM)
    hbm = pl.BlockSpec(memory_space=pl.ANY)
    dma = pltpu.SemaphoreType.DMA
    return pl.pallas_call(
        layer_kernel,
        in_specs=[pl.BlockSpec(memory_space=pltpu.SMEM)] + [vmem] * 12 + [hbm] * 2,
        out_specs=[vmem] * 6,
        out_shape=[
            jax.ShapeDtypeStruct((block, full), BF16),
            jax.ShapeDtypeStruct((block, full), F32),
            jax.ShapeDtypeStruct((quad, full, full), BF16),
            jax.ShapeDtypeStruct(small, F32),
            jax.ShapeDtypeStruct((local, hidden, full), F32),
            jax.ShapeDtypeStruct((groups, local, full // groups, hidden), BF16),
        ],
        scratch_shapes=[
            pltpu.VMEM((full, triple), BF16),
            pltpu.VMEM((rows, full), BF16),
            pltpu.VMEM((rows, triple), BF16),
            pltpu.VMEM((count, table.shape[0], double), F32),
            pltpu.VMEM((heads, quad, block), F32),
            pltpu.VMEM((rows, part), BF16),
            pltpu.VMEM((quad, block, part), BF16),
            pltpu.VMEM((8, 128), F32),
            pltpu.VMEM((sources, 8, 128), F32),
            pltpu.VMEM((experts_count, slots, full), BF16),
            pltpu.VMEM((sources, local, slots, full), BF16),
            pltpu.VMEM((sources, local, slots, full), BF16),
            pltpu.VMEM((experts_count, 8, 128), F32),
            pltpu.VMEM((sources, local, 8, 128), F32),
            pltpu.VMEM((block, experts_count * slots), BF16),
            pltpu.VMEM((local, capacity, sources * slots), BF16),
            pltpu.VMEM((groups, local, capacity, full), BF16),
            pltpu.VMEM((groups, local * capacity + extra, full), BF16),
            pltpu.VMEM((depth, full, piece), BF16),
            pltpu.VMEM((depth, piece, full), BF16),
            pltpu.VMEM((capacity, 2 * full), F32),
            pltpu.VMEM((sources, local, slots, 2 * full), BF16),
            pltpu.VMEM((experts_count, slots, 2 * full), BF16),
            pltpu.VMEM((block, full), F32),
            pltpu.VMEM((rows, part), BF16),
            pltpu.VMEM((quad, block, part), BF16),
            pltpu.VMEM((rows, full), BF16),
            pltpu.VMEM((count, block, block), F32),
            pltpu.VMEM((count, block, block), F32),
            pltpu.VMEM((rows, head_width), F32),
            pltpu.VMEM((rows, head_width), F32),
            pltpu.VMEM((rows, triple), BF16),
            pltpu.VMEM((quad, block, triple), BF16),
            pltpu.VMEM((full, full), BF16),
            pltpu.VMEM((2, quarter, full), BF16),
            pltpu.VMEM((quarter, full), BF16),
            pltpu.VMEM((quarter, full), BF16),
            pltpu.VMEM((quarter, full), BF16),
            pltpu.VMEM((quarter, full), BF16),
            pltpu.VMEM((5,) + small, F32),
            pltpu.VMEM((5,) + small, F32),
            pltpu.VMEM((groups, capacity, hidden), BF16),
            pltpu.VMEM((groups, capacity, hidden), BF16),
            pltpu.VMEM((groups, local, full // groups, hidden), BF16),
            pltpu.VMEM((block, full), F32),
            dma((2, 3)), dma((2, 3)), dma((2, 3)), dma((2, 3)), dma((2, 3)), dma((2, 3)), dma((2, depth)),
            dma((2, 2, 3)), dma((2, 7)), dma((2, 2, 3)), dma((2, 7)), dma((2, 2, 3)),
            dma((2, 3)), dma((2, 3)), dma((2, 3)), dma((2, 2)), dma((2,)), dma((2,)),
            dma((2, 3, 7)), dma((2, 3, 8)), dma((2, 5)), dma((2, 2, 7)), dma((2, 2)),
        ],
        compiler_params=pltpu.CompilerParams(
            vmem_limit_bytes=62 * 1024 * 1024, collective_id=0, has_side_effects=True
        ),
        name="layer",
    )(lengths, tokens, ids, cotangent, gain_one, gain_two, w_query, w_key, w_value, w_output, w_router, table, hot,
      w_in, w_out)


def finish_kernel(all_ref, d_in_ref, d_query_ref, d_key_ref, d_value_ref, d_output_ref, d_in_out_ref):
    quad, rows, full = all_ref.shape
    part = full // 4
    for kind, ref in enumerate((d_query_ref, d_key_ref, d_value_ref)):
        for i in range(rows // part):
            span = slice(i * part, (i + 1) * part)
            ref[span, :] = jnp.concatenate(
                [all_ref[m, span, kind * part : (kind + 1) * part].astype(F32) for m in range(quad)], axis=1
            )
    for m in range(quad):
        d_output_ref[m * part : (m + 1) * part, :] = jnp.concatenate(
            [all_ref[m, n * part : (n + 1) * part, 3 * part :].astype(F32) for n in range(quad)], axis=1
        )
    groups, local, count, hidden = d_in_ref.shape
    for g in range(groups):
        for e in range(local):
            d_in_out_ref[e, :, g * hidden : (g + 1) * hidden] = d_in_ref[g, e].astype(F32)


def finish(gathered, d_in):
    quad, rows, full = gathered.shape
    groups, local, count, hidden = d_in.shape
    vmem = pl.BlockSpec(memory_space=pltpu.VMEM)
    return pl.pallas_call(
        finish_kernel,
        in_specs=[vmem] * 2,
        out_specs=[vmem] * 5,
        out_shape=[jax.ShapeDtypeStruct((rows, full), F32)] * 4
        + [jax.ShapeDtypeStruct((local, count, groups * hidden), F32)],
        compiler_params=pltpu.CompilerParams(vmem_limit_bytes=VMEM_BYTES),
        name="finish",
    )(gathered, d_in)


def all_to_all(array, axis, groups=None):
    return lax.all_to_all(
        array, axis, split_axis=0, concat_axis=0, tiled=True, axis_index_groups=groups
    )


def to_experts(received, local):
    total, slots, width = received.shape
    shaped = received.reshape(total // local, local, slots, width)
    return jnp.swapaxes(shaped, 0, 1).reshape(local, total // local * slots, width)


def to_sources(by_expert, sources):
    local, total, width = by_expert.shape
    shaped = by_expert.reshape(local, sources, total // sources, width)
    return jnp.swapaxes(shaped, 0, 1).reshape(sources * local, total // sources, width)


def per_device(
    tokens, lengths, expert_ids, gain_one, w_query, w_key, w_value, w_output,
    bias_table, gain_two, w_router, w_in, w_out, cotangent,
):
    tok_rows, width = tokens.shape
    head_count = bias_table.shape[1]
    head_width = width // head_count
    expert_count = w_router.shape[1]
    local = w_in.shape[0]
    hidden = w_in.shape[2]
    dp_count, ex_count = lax.axis_size("dp"), lax.axis_size("expert")
    dp_index, ex_index = lax.axis_index("dp"), lax.axis_index("expert")
    span = dp_count // 2
    quad = math.gcd(span, head_count)
    heads = head_count // quad
    part = heads * head_width
    q_rows = quad * tok_rows
    q_parts = span // quad
    place = dp_index % span
    mine, q_part = place % quad, place // quad
    quads = [[i * quad + j for j in range(quad)] for i in range(dp_count // quad)]
    spans = [[i * span + j for j in range(span)] for i in range(dp_count // span)]
    seq_id = ex_index * (dp_count // span) + dp_index // span
    start_row = place * tok_rows

    length = jnp.sum(jnp.where(jnp.arange(lengths.shape[0], dtype=jnp.int32) == seq_id, lengths, 0))
    valid_mask = start_row + jnp.arange(tok_rows, dtype=jnp.int32) < length
    valid_f = valid_mask.astype(F32)
    length_arg = length.reshape(1)

    if q_parts == 1:
        tokens_all = all_to_all(
            jnp.broadcast_to(tokens[None], (quad, tok_rows, width)), "dp", quads
        ).reshape(q_rows, width)
        tokens_q = tokens_all
    else:
        tokens_all = lax.all_gather(tokens, "dp", axis_index_groups=spans, tiled=True)
        tokens_q = lax.dynamic_slice_in_dim(tokens_all, q_part * q_rows, q_rows, 0)
    gain_a = gain_one.astype(F32)
    normed_all = normalize(tokens_all.astype(F32), gain_a)[0].astype(BF16)
    normed_q = normalize(tokens_q.astype(F32), gain_a)[0].astype(BF16)

    table = lax.dynamic_slice_in_dim(bias_table.astype(F32), mine * heads, heads, 1)
    counts = span * tok_rows // tok_rows + quad - 1
    offset = jnp.arange(2 * tok_rows, dtype=jnp.int32)
    offset = jnp.where(offset < tok_rows, offset, offset - 2 * tok_rows)
    codes = (
        jnp.arange(counts, dtype=jnp.int32)[:, None] * tok_rows
        - offset[None, :]
        - (q_rows - tok_rows)
        - q_part * q_rows
    )
    window_hot = (
        bucket_of(codes)[:, :, None] == jnp.arange(table.shape[0], dtype=jnp.int32)
    ).astype(BF16)
    window = jnp.einsum("amb,bh->ham", window_hot, table.astype(BF16), preferred_element_type=F32)

    def my_columns(weight):
        return lax.dynamic_slice_in_dim(weight, mine * part, part, 1).reshape(
            width, heads, head_width
        )

    def project(rows, weight):
        return jnp.einsum(
            "sd,dhc->hsc", rows, my_columns(weight), preferred_element_type=F32
        ).astype(BF16)

    query = project(normed_q, w_query)
    key = project(normed_all, w_key)
    value = project(normed_all, w_value)
    attended_heads, log_norm = attend(length_arg, window, query, key, value)
    attended = all_to_all(
        jnp.transpose(
            attended_heads.reshape(heads, quad, tok_rows, head_width), (1, 2, 0, 3)
        ).reshape(quad, tok_rows, part),
        "dp",
        quads,
    )
    attended = jnp.swapaxes(attended, 0, 1).reshape(tok_rows, width)

    token_f = tokens.astype(F32)
    residual = token_f + dot(attended, w_output)
    gain_b = gain_two.astype(F32)
    routed_f, inverse_two = normalize(residual, gain_b)
    routed = routed_f.astype(BF16)
    router = jax.nn.softmax(dot(routed, w_router), axis=-1)

    chosen = expert_ids[:, 0]
    chosen_hot = chosen[:, None] == jnp.arange(expert_count, dtype=jnp.int32)[None, :]
    valid_hits = (chosen_hot & valid_mask[:, None]).astype(jnp.int32)
    per_source = lax.all_gather(jnp.sum(valid_hits, axis=0), "expert")
    earlier = jnp.arange(ex_count, dtype=jnp.int32)[:, None] < ex_index
    offsets = jnp.sum(jnp.where(earlier, per_source, 0), axis=0)
    local_rank = jnp.sum((jnp.cumsum(valid_hits, axis=0) - valid_hits) * valid_hits, axis=1)
    group_rank = local_rank + jnp.sum(valid_hits * offsets[None, :], axis=1)
    capacity = 5 * tok_rows // (4 * local)
    slots = 3 * tok_rows // (2 * expert_count)
    kept_mask = valid_mask & (group_rank < capacity)
    kept_f = kept_mask.astype(F32)
    target = jnp.where(kept_mask, chosen * slots + local_rank, -1)
    placing = (
        jnp.arange(expert_count * slots, dtype=jnp.int32)[:, None] == target[None, :]
    ).astype(BF16)
    chosen_f = chosen_hot.astype(F32)
    chosen_prob = jnp.sum(router * chosen_f, axis=1)
    gate = chosen_prob * kept_f
    upstream = cotangent.astype(F32) * valid_f[:, None]
    d_expert = (gate[:, None] * upstream).astype(BF16)

    sending = dot(placing, jnp.concatenate([routed, d_expert], axis=1)).astype(BF16)
    expert_rows = to_experts(
        all_to_all(sending.reshape(expert_count, slots, 2 * width), "expert"), local
    )
    group_rows = lax.all_gather(expert_rows, "dp")
    results = experts(expert_rows, w_in, w_out)
    returned = all_to_all(to_sources(results, ex_count), "expert")
    gathered = t_dot(placing, returned.reshape(expert_count * slots, 2 * width))
    expert_out, d_routed = gathered[:, :width], gathered[:, width:]

    output = (valid_f[:, None] * (residual + gate[:, None] * expert_out)).astype(BF16)
    d_gate = jnp.sum(upstream * expert_out, axis=1) * kept_f
    d_logits = router * (chosen_f - chosen_prob[:, None]) * d_gate[:, None]
    d_router = t_dot(routed, d_logits.astype(BF16))
    d_routed = d_routed + dot_t(d_logits.astype(BF16), w_router)
    d_norm_two, d_gain_two = norm_back(residual, inverse_two, gain_b, d_routed)
    d_residual = upstream + d_norm_two
    low_residual = d_residual.astype(BF16)
    d_attended = dot_t(low_residual, w_output).astype(BF16)
    d_output = t_dot(attended, low_residual)

    grad = all_to_all(
        jnp.swapaxes(d_attended.reshape(tok_rows, quad, part), 0, 1), "dp", quads
    ).reshape(q_rows, heads, head_width)
    grad = jnp.swapaxes(grad, 0, 1)
    d_query_rows, d_key_rows, d_value_rows, d_window = attend_back(
        length_arg, window, query, key, value, grad, log_norm
    )
    if q_parts > 1:
        strided = [
            [i * span + j + quad * n for n in range(q_parts)]
            for i in range(dp_count // span)
            for j in range(quad)
        ]
        d_key_rows, d_value_rows = [
            lax.psum_scatter(
                rows, "dp", scatter_dimension=1, axis_index_groups=strided, tiled=True
            )
            for rows in (d_key_rows, d_value_rows)
        ]
    d_rows = jnp.stack([d_query_rows, d_key_rows.astype(BF16), d_value_rows.astype(BF16)])
    d_parts = jnp.einsum("sd,khsc->dkhc", normed_q, d_rows, preferred_element_type=F32)
    d_table = jnp.einsum("amb,ham->bh", window_hot.astype(F32), d_window, precision="highest")
    d_mine = all_to_all(
        jnp.transpose(
            d_rows.reshape(3, heads, quad, tok_rows, head_width), (2, 3, 0, 1, 4)
        ).reshape(quad, tok_rows, 3 * part),
        "dp",
        quads,
    ).reshape(quad, tok_rows, 3, part)
    d_mine = jnp.transpose(d_mine, (2, 1, 0, 3)).reshape(3, tok_rows, width)
    d_normed = dot_t(d_mine[0], w_query) + dot_t(d_mine[1], w_key) + dot_t(d_mine[2], w_value)
    inverse_one = normalize(token_f, gain_a)[1]
    d_norm_one, d_gain_one = norm_back(token_f, inverse_one, gain_a, d_normed)
    d_tokens = d_residual + d_norm_one

    piece = hidden // dp_count
    my_in = lax.dynamic_slice_in_dim(w_in, dp_index * piece, piece, 2)
    my_out = lax.dynamic_slice_in_dim(w_out, dp_index * piece, piece, 1)
    d_in_piece, d_out = weight_grads(group_rows, my_in, my_out)
    d_in = all_to_all(
        jnp.swapaxes(d_in_piece.reshape(local, dp_count, width // dp_count, piece), 0, 1), "dp"
    )
    d_in = (
        jnp.transpose(d_in, (1, 2, 0, 3)).reshape(local, width // dp_count, hidden).astype(F32)
    )

    def spread(array, axis):
        wide = jnp.zeros(array.shape[:axis] + (array.shape[axis] * quad,) + array.shape[axis + 1 :], F32)
        return lax.dynamic_update_slice_in_dim(wide, array, mine * array.shape[axis], axis)

    d_parts = d_parts.reshape(width, 3, part)
    big = jnp.stack([spread(d_parts[:, n], 1) for n in range(3)] + [d_output])
    summed = lax.psum(big.astype(BF16), ("dp", "expert")).astype(F32)
    small = lax.psum(
        (d_gain_one, spread(d_table, 1), d_gain_two, d_router), ("dp", "expert")
    )
    return (
        output, d_tokens, small[0], summed[0], summed[1], summed[2], summed[3],
        small[1], small[2], small[3], d_in, d_out,
    )


def per_device_quad(
    tokens, lengths, expert_ids, gain_one, w_query, w_key, w_value, w_output,
    bias_table, gain_two, w_router, w_in, w_out, cotangent,
):
    tok_rows, width = tokens.shape
    buckets, head_count = bias_table.shape
    expert_count = w_router.shape[1]
    quad = lax.axis_size("dp") // 2
    counts = 2 * quad - 1
    offset = jnp.arange(2 * tok_rows, dtype=jnp.int32)
    offset = jnp.where(offset < tok_rows, offset, offset - 2 * tok_rows)
    codes = (
        jnp.arange(counts, dtype=jnp.int32)[:, None] * tok_rows
        - offset[None, :]
        - (quad - 1) * tok_rows
    )
    hot = (
        bucket_of(codes)[:, None, :] == jnp.arange(buckets, dtype=jnp.int32)[None, :, None]
    ).astype(BF16)
    table = jnp.pad(bias_table.T, ((0, 16 - head_count), (0, 0)))
    output, d_tokens, d_weights, total, d_out, d_in_parts = layer(
        lengths, tokens, expert_ids, cotangent, gain_one[None], gain_two[None], w_query, w_key, w_value,
        w_output, w_router, table, hot, w_in, w_out, head_count,
    )
    d_query, d_key, d_value, d_output, d_in = finish(d_weights, d_in_parts)
    return (
        output, d_tokens, total[0], d_query, d_key, d_value, d_output,
        total[12:, :buckets].T, total[1], total[2 : 2 + expert_count].T, d_in, d_out,
    )


def solution(mesh):
    rows = P(("expert", "dp"), None)
    owned = P("expert", None, None)
    return jax.shard_map(
        per_device_quad if dict(mesh.shape) == {"dp": 8, "expert": 4} else per_device,
        mesh=mesh,
        in_specs=(
            rows, P(), rows, P(), P(), P(), P(), P(), P(), P(), P(), owned, owned, rows,
        ),
        out_specs=(
            rows, rows, P(), P(), P(), P(), P(), P(), P(), P(),
            P("expert", "dp", None), P("expert", "dp", None),
        ),
        check_vma=False,
    )
```

```python
import functools
import math

import jax
import jax.numpy as jnp
from jax import lax
from jax.experimental import pallas as pl
from jax.experimental.pallas import tpu as pltpu
from jax.sharding import PartitionSpec as P

BUCKETS = 32
EXACT = 8
MASKED = -1000000000.0
F32 = jnp.float32
BF16 = jnp.bfloat16
VMEM_BYTES = 56 * 1024 * 1024


def bucket_of(relative):
    distance = jnp.abs(relative)
    beyond = jnp.full(relative.shape, EXACT, jnp.int32)
    for level_step in range(1, BUCKETS // 2 - EXACT):
        boundary = math.isqrt(EXACT * EXACT * (1 << level_step) - 1) + 1
        beyond = beyond + (distance >= boundary).astype(jnp.int32)
    nearby = jnp.where(distance < EXACT, distance, beyond)
    return nearby + jnp.where(relative > 0, BUCKETS // 2, 0).astype(jnp.int32)


def normalize(values, gain):
    inverse = lax.rsqrt(jnp.mean(values * values, axis=-1, keepdims=True) + 1e-06)
    return (values * inverse * gain, inverse)


def norm_back(values, inverse, gain, upstream):
    scaled_up = upstream * gain
    d_gain = jnp.sum(upstream * values * inverse, axis=0)
    cubed = inverse * inverse * inverse
    d_values = inverse * scaled_up - values * cubed * jnp.mean(
        values * scaled_up, axis=-1, keepdims=True
    )
    return (d_values, d_gain)


def dot(left_side, right_side):
    return jnp.dot(left_side, right_side, preferred_element_type=F32)


def dot_t(left_side, right_side):
    return lax.dot_general(
        left_side, right_side, (((1,), (1,)), ((), ())), preferred_element_type=F32
    )


def t_dot(left_side, right_side):
    return lax.dot_general(
        left_side, right_side, (((0,), (0,)), ((), ())), preferred_element_type=F32
    )


def gelu_parts(value):
    scale = math.sqrt(2.0 / math.pi)
    square = value * value
    tanh = jnp.tanh(scale * (value + 0.044715 * value * square))
    half = 0.5 * (1.0 + tanh)
    slope = half + 0.5 * value * (1.0 - tanh * tanh) * scale * (1.0 + 3 * 0.044715 * square)
    return (value * half, slope)


def build_bias(win_ref, bias_ref):
    count, block, _ = bias_ref.shape

    @pl.loop(0, count)
    def _(index):
        row = win_ref[0, pl.ds(index, 1), :]
        wide = jnp.broadcast_to(row, (block, 2 * block))
        bias_ref[index] = pltpu.roll(wide, 0, 1, stride=1, stride_axis=0)[:, :block]


def attend_kernel(length_ref, win_ref, q_ref, k_ref, v_ref, o_ref, lse_ref, bias_ref):
    block = bias_ref.shape[1]
    q_blocks = q_ref.shape[1] // block
    k_blocks = k_ref.shape[1] // block
    build_bias(win_ref, bias_ref)
    length = length_ref[0]

    @pl.loop(0, q_blocks)
    def _(i):
        rows = pl.ds(pl.multiple_of(i * block, block), block)
        query = q_ref[0, rows, :]
        scores = []
        for j in range(k_blocks):
            part = dot_t(k_ref[0, j * block : (j + 1) * block, :], query)
            part = part + bias_ref[j - i + q_blocks - 1]
            position = lax.broadcasted_iota(jnp.int32, (block, 1), 0) + j * block
            scores.append(jnp.where(position < length, part, MASKED))
        top = functools.reduce(jnp.maximum, [jnp.max(s, axis=0, keepdims=True) for s in scores])
        total = jnp.zeros((1, block), F32)
        out = jnp.zeros((v_ref.shape[2], block), F32)
        for j in range(k_blocks):
            scaled = jnp.exp(scores[j] - top)
            total = total + jnp.sum(scaled, axis=0, keepdims=True)
            out = out + t_dot(v_ref[0, j * block : (j + 1) * block, :], scaled.astype(BF16))
        out = out * (1.0 / total)
        o_ref[0, rows, :] = out.T.astype(BF16)
        lse_ref[0, pl.ds(i, 1), :] = top + jnp.log(total)


def attend_back_kernel(
    length_ref, win_ref, q_ref, k_ref, v_ref, g_ref, lse_ref,
    dq_ref, dk_ref, dv_ref, dwin_ref, bias_ref, dbias_ref,
):
    block = bias_ref.shape[1]
    q_blocks = q_ref.shape[1] // block
    k_blocks = k_ref.shape[1] // block
    build_bias(win_ref, bias_ref)
    length = length_ref[0]
    dk_ref[...] = jnp.zeros_like(dk_ref)
    dv_ref[...] = jnp.zeros_like(dv_ref)
    dbias_ref[...] = jnp.zeros_like(dbias_ref)

    @pl.loop(0, q_blocks)
    def _(i):
        rows = pl.ds(pl.multiple_of(i * block, block), block)
        query = q_ref[0, rows, :]
        grad = g_ref[0, rows, :]
        log_norm = lse_ref[0, pl.ds(i, 1), :]
        probs, d_probs = [], []
        spread = jnp.zeros((1, block), F32)
        for j in range(k_blocks):
            keys = slice(j * block, (j + 1) * block)
            part = dot_t(k_ref[0, keys, :], query)
            part = part + bias_ref[j - i + q_blocks - 1]
            position = lax.broadcasted_iota(jnp.int32, (block, 1), 0) + j * block
            part = jnp.where(position < length, part, MASKED)
            prob = jnp.exp(part - log_norm)
            d_prob = dot_t(v_ref[0, keys, :], grad)
            spread = spread + jnp.sum(prob * d_prob, axis=0, keepdims=True)
            dv_ref[0, keys, :] += dot(prob.astype(BF16), grad)
            probs.append(prob)
            d_probs.append(d_prob)
        d_query = jnp.zeros((q_ref.shape[2], block), F32)
        for j in range(k_blocks):
            keys = slice(j * block, (j + 1) * block)
            d_score = probs[j] * (d_probs[j] - spread)
            dbias_ref[j - i + q_blocks - 1] += d_score
            low = d_score.astype(BF16)
            dk_ref[0, keys, :] += dot(low, query)
            d_query = d_query + t_dot(k_ref[0, keys, :], low)
        dq_ref[0, rows, :] = d_query.T.astype(BF16)

    @pl.loop(0, dbias_ref.shape[0])
    def _(index):
        wide = jnp.concatenate([dbias_ref[index], jnp.zeros((block, block), F32)], axis=1)
        half = block // 2
        while half:
            wide = wide[:half] + pltpu.roll(wide[half:], 2 * block - half, 1)
            half //= 2
        dwin_ref[0, pl.ds(index, 1), :] = wide


def head_block(rows, width):
    return pl.BlockSpec((1, rows, width), lambda h: (h, 0, 0))


def attend(length, window, query, key, value):
    heads, q_rows, width = query.shape
    k_rows = key.shape[1]
    count, block = window.shape[1], window.shape[2] // 2
    return pl.pallas_call(
        attend_kernel,
        grid=(heads,),
        in_specs=[
            pl.BlockSpec(memory_space=pltpu.SMEM),
            head_block(count, 2 * block),
            head_block(q_rows, width),
            head_block(k_rows, width),
            head_block(k_rows, width),
        ],
        out_specs=[head_block(q_rows, width), head_block(q_rows // block, block)],
        out_shape=[
            jax.ShapeDtypeStruct((heads, q_rows, width), BF16),
            jax.ShapeDtypeStruct((heads, q_rows // block, block), F32),
        ],
        scratch_shapes=[pltpu.VMEM((count, block, block), F32)],
        compiler_params=pltpu.CompilerParams(vmem_limit_bytes=VMEM_BYTES),
        name="attend",
    )(length, window, query, key, value)


def attend_back(length, window, query, key, value, grad, log_norm):
    heads, q_rows, width = query.shape
    k_rows = key.shape[1]
    count, block = window.shape[1], window.shape[2] // 2
    return pl.pallas_call(
        attend_back_kernel,
        grid=(heads,),
        in_specs=[
            pl.BlockSpec(memory_space=pltpu.SMEM),
            head_block(count, 2 * block),
            head_block(q_rows, width),
            head_block(k_rows, width),
            head_block(k_rows, width),
            head_block(q_rows, width),
            head_block(q_rows // block, block),
        ],
        out_specs=[
            head_block(q_rows, width),
            head_block(k_rows, width),
            head_block(k_rows, width),
            head_block(count, 2 * block),
        ],
        out_shape=[
            jax.ShapeDtypeStruct((heads, q_rows, width), BF16),
            jax.ShapeDtypeStruct((heads, k_rows, width), F32),
            jax.ShapeDtypeStruct((heads, k_rows, width), F32),
            jax.ShapeDtypeStruct((heads, count, 2 * block), F32),
        ],
        scratch_shapes=[pltpu.VMEM((count, block, block), F32) for _ in range(2)],
        compiler_params=pltpu.CompilerParams(vmem_limit_bytes=VMEM_BYTES),
        name="attend_back",
    )(length, window, query, key, value, grad, log_norm)


def experts_kernel(rows_ref, w_in_ref, w_out_ref, out_ref, acc_ref, back_ref):
    width = w_in_ref.shape[1]
    step = pl.program_id(1)

    @pl.when(step == 0)
    def _():
        acc_ref[...] = jnp.zeros_like(acc_ref)
        back_ref[...] = jnp.zeros_like(back_ref)

    inner = dot(rows_ref[0, :, :width], w_in_ref[0])
    active, slope = gelu_parts(inner)
    acc_ref[...] += dot(active.astype(BF16), w_out_ref[0])
    d_active = dot_t(rows_ref[0, :, width:], w_out_ref[0])
    d_inner = (d_active * slope).astype(BF16)
    back_ref[...] += dot_t(d_inner, w_in_ref[0])

    @pl.when(step == pl.num_programs(1) - 1)
    def _():
        out_ref[0, :, :width] = acc_ref[...].astype(BF16)
        out_ref[0, :, width:] = back_ref[...].astype(BF16)


def experts(rows, w_in, w_out):
    local, count, double = rows.shape
    width, hidden = w_in.shape[1:]
    piece = 512
    return pl.pallas_call(
        experts_kernel,
        grid=(local, hidden // piece),
        in_specs=[
            pl.BlockSpec((1, count, double), lambda e, f: (e, 0, 0)),
            pl.BlockSpec((1, width, piece), lambda e, f: (e, 0, f)),
            pl.BlockSpec((1, piece, width), lambda e, f: (e, f, 0)),
        ],
        out_specs=pl.BlockSpec((1, count, double), lambda e, f: (e, 0, 0)),
        out_shape=jax.ShapeDtypeStruct((local, count, double), BF16),
        scratch_shapes=[pltpu.VMEM((count, width), F32) for _ in range(2)],
        compiler_params=pltpu.CompilerParams(vmem_limit_bytes=VMEM_BYTES),
        name="experts",
    )(rows, w_in, w_out)


def weight_grads_kernel(rows_ref, w_in_ref, w_out_ref, d_in_ref, d_out_ref, acc_ref):
    width = w_in_ref.shape[1]
    step = pl.program_id(1)
    rows = rows_ref[...].reshape(rows_ref.shape[0] * rows_ref.shape[2], 2 * width)

    @pl.when(step == 0)
    def _():
        acc_ref[...] = jnp.zeros_like(acc_ref)
        d_out_ref[...] = jnp.zeros_like(d_out_ref)

    inner = dot(rows[:, :width], w_in_ref[0])
    active, slope = gelu_parts(inner)
    d_active = dot_t(rows[:, width:], w_out_ref[0])
    d_inner = (d_active * slope).astype(BF16)
    d_out_ref[0] += t_dot(active.astype(BF16), rows[:, width:])
    acc_ref[...] += t_dot(rows[:, :width], d_inner)

    @pl.when(step == pl.num_programs(1) - 1)
    def _():
        d_in_ref[0] = acc_ref[...].astype(BF16)


def weight_grads(rows, w_in, w_out):
    groups, local, count, double = rows.shape
    width, piece = w_in.shape[1:]
    together = 4
    return pl.pallas_call(
        weight_grads_kernel,
        grid=(local, groups // together),
        in_specs=[
            pl.BlockSpec((together, 1, count, double), lambda e, g: (g, e, 0, 0)),
            pl.BlockSpec((1, width, piece), lambda e, g: (e, 0, 0)),
            pl.BlockSpec((1, piece, width), lambda e, g: (e, 0, 0)),
        ],
        out_specs=[
            pl.BlockSpec((1, width, piece), lambda e, g: (e, 0, 0)),
            pl.BlockSpec((1, piece, width), lambda e, g: (e, 0, 0)),
        ],
        out_shape=[
            jax.ShapeDtypeStruct((local, width, piece), BF16),
            jax.ShapeDtypeStruct((local, piece, width), F32),
        ],
        scratch_shapes=[pltpu.VMEM((width, piece), F32)],
        compiler_params=pltpu.CompilerParams(vmem_limit_bytes=VMEM_BYTES),
        name="weight_grads",
    )(rows, w_in, w_out)


class Place:
    def __init__(self):
        self.dp, self.ex = lax.axis_index("dp"), lax.axis_index("expert")
        self.y = lax.rem(self.dp, 2)
        self.z = lax.div(self.dp, 2)
        self.z_lo = lax.rem(self.z, 2)
        self.z_hi = lax.div(self.dp, 4)
        self.core = lax.rem(self.ex, 2)
        self.x = lax.div(self.ex, 2)
        self.member = self.z_lo * 2 + self.y

    def flip(self, *names):
        c = {n: getattr(self, n) for n in ("y", "z_lo", "z_hi", "core", "x")}
        for name in names:
            c[name] = 1 - c[name]
        return (c["z_hi"] * 4 + c["z_lo"] * 2 + c["y"], c["x"] * 2 + c["core"])

    def quad_others(self):
        found = []
        for names in (("y",), ("z_lo",), ("y", "z_lo")):
            device = self.flip(*names)
            found.append((device, lax.rem(device[0], 4)))
        return found

    def expert_others(self):
        return [self.flip(*names) for names in (("core",), ("x",), ("core", "x"))]

    def dp_others(self):
        names = (("y",), ("z_lo",), ("y", "z_lo"), ("z_hi",), ("z_hi", "y"), ("z_hi", "z_lo"), ("z_hi", "y", "z_lo"))
        return [self.flip(*n) for n in names]


def remote(src, dst, sems, index, device):
    return pltpu.make_async_remote_copy(
        src_ref=src, dst_ref=dst, send_sem=sems.at[(0,) + index], recv_sem=sems.at[(1,) + index],
        device_id=device, device_id_type=pl.DeviceIdType.MESH,
    )


def send(src, dst, sems, index, device):
    copy = remote(src, dst, sems, index, device)
    copy.start()
    return copy


def greet(devices):
    barrier = pltpu.get_barrier_semaphore()
    for device in devices:
        pl.semaphore_signal(barrier, inc=1, device_id=device, device_id_type=pl.DeviceIdType.MESH)
    pl.semaphore_wait(barrier, len(devices))


class Relay:
    def __init__(self, place, ref, sems):
        self.ref, self.sems = ref, sems
        self.dp, self.ex, self.z = place.dp, place.ex, place.z

    def along(self, direction, step, offset):
        neighbour = (self.dp + 2, self.ex) if direction else (self.dp - 2, self.ex)
        block = self.ref.at[self.z + offset]
        return remote(block, block, self.sems, (direction, step), neighbour)

    def begin(self):
        @pl.when(self.z < 3)
        def _():
            self.along(1, 0, 0).start()

        @pl.when(self.z > 0)
        def _():
            self.along(0, 0, 0).start()

    def step(self, k):
        @pl.when(self.z >= k)
        def _():
            self.along(1, k - 1, -k).wait_recv()
            if k < 3:

                @pl.when(self.z < 3)
                def _():
                    self.along(1, k, -k).start()

        @pl.when(self.z + k <= 3)
        def _():
            self.along(0, k - 1, k).wait_recv()
            if k < 3:

                @pl.when(self.z > 0)
                def _():
                    self.along(0, k, k).start()

    def end(self):
        for k in (0, 1, 2):

            @pl.when((self.z >= k) & (self.z < 3))
            def _():
                self.along(1, k, -k).wait_send()

            @pl.when((self.z + k <= 3) & (self.z > 0))
            def _():
                self.along(0, k, k).wait_send()


class QuadGather:
    def __init__(self, place, ref, sems, rows):
        self.ref, self.sems, self.rows = ref, sems, rows
        (self.y_device, self.y_member), (self.z_device, self.z_member), _ = place.quad_others()
        self.mine = place.member

    def part(self, member, start, size):
        return self.ref.at[pl.ds(pl.multiple_of(member * self.rows + start, size), size)]

    def begin(self):
        own = self.part(self.mine, 0, self.rows)
        self.first = [
            send(own, own, self.sems, (0,), self.y_device), send(own, own, self.sems, (1,), self.z_device),
        ]

    def forward(self):
        half = self.rows // 2
        self.first[0].wait_recv()
        upper = self.part(self.y_member, 0, half)
        self.second = [send(upper, upper, self.sems, (2,), self.z_device)]
        self.first[1].wait_recv()
        lower = self.part(self.z_member, half, half)
        self.second.append(send(lower, lower, self.sems, (3,), self.y_device))

    def end(self):
        for copy in self.second:
            copy.wait()
        for copy in self.first:
            copy.wait_send()


def exact_dot(left_side, right_side, left_dim, right_dim):
    return lax.dot_general(
        left_side, right_side, (((left_dim,), (right_dim,)), ((), ())),
        precision=lax.Precision.HIGHEST, preferred_element_type=F32,
    )


def layer_kernel(
    lengths_ref, token_ref, ids_ref, cotangent_ref, gain_one_ref, gain_two_ref, w_query_ref, w_key_ref,
    w_value_ref, w_output_ref, w_router_ref, table_ref, hot_ref, w_in_ref, w_out_ref,
    output_ref, d_tokens_ref, d_weights_ref, total_ref, d_out_ref, d_in_ref,
    w_mine_ref, normed_ref, qkv_ref, win_ref, lse_ref, attended_ref, attended_recv,
    count_send, count_ref, slot_send, up_arrive, rows_arrive, gate_send, gate_arrive, place_ref, pack_ref,
    up_ref, rows_ref, in_buf, out_buf, result_ref, back_send, back_ref, residual_ref,
    grad_ref, grad_send, low_ref, bias_ref, dbias_ref, dkey_ref, dvalue_ref, dqkv_ref,
    dmine_ref, load_ref, first_ref, second_ref, third_ref, sum_one_ref, sum_two_ref,
    small_send, small_recv, active_ref, inner_ref, half_send, half_recv, d_out_send, d_out_recv,
    token_sems, count_sems, up_sems, attended_sems, go_sems, gate_sems, weight_sems,
    up_line_sems, line_sems, back_sems,
    grad_sems, low_sems, mine_sems, first_sems, second_sems, third_sems, ring_sems, core_sems,
    small_sems, d_in_sems, half_sems, block_sems,
):
    place = Place()
    mine, ex, dp, z = place.member, place.ex, place.dp, place.z
    block = bias_ref.shape[1]
    part = qkv_ref.shape[1] // 3
    head_width = dkey_ref.shape[1]
    heads = part // head_width
    blocks = quad = qkv_ref.shape[0] // block
    width = normed_ref.shape[0]
    sources, local, slots = rows_arrive.shape[:3]
    groups, _, capacity = up_ref.shape[:3]
    experts_count = local * sources
    length = lengths_ref[ex * 2 + place.z_hi]
    piece = in_buf.shape[2]
    pieces = w_in_ref.shape[2] // piece
    depth = in_buf.shape[0]
    hidden = active_ref.shape[2]
    my_hidden = pl.ds(pl.multiple_of(z * hidden, hidden), hidden)
    diagonal = lax.broadcasted_iota(jnp.int32, (capacity, capacity), 0) == lax.broadcasted_iota(
        jnp.int32, (capacity, capacity), 1
    )

    def my_rows(index):
        return pl.ds(pl.multiple_of(index * block, block), block)

    def fill_bias(h):
        @pl.loop(0, bias_ref.shape[0])
        def _(index):
            wide = jnp.broadcast_to(win_ref[index, pl.ds(mine * heads + h, 1), :], (block, 2 * block))
            bias_ref[index] = pltpu.roll(wide, 0, 1, stride=1, stride_axis=0)[:, :block]

    quad_others = place.quad_others()
    expert_others = place.expert_others()
    dp_others = place.dp_others()
    up_relay = Relay(place, up_ref, up_line_sems)
    rows_relay = Relay(place, rows_ref, line_sems)

    def weight_copies(n):
        e, f, slot = n // pieces, n % pieces, n % depth
        return (
            pltpu.make_async_copy(
                w_in_ref.at[e, :, f * piece : (f + 1) * piece], in_buf.at[slot], weight_sems.at[0, slot]
            ),
            pltpu.make_async_copy(
                w_out_ref.at[e, f * piece : (f + 1) * piece, :], out_buf.at[slot], weight_sems.at[1, slot]
            ),
        )

    def block_copies(e):
        return (
            pltpu.make_async_copy(w_in_ref.at[e, :, my_hidden], in_buf.at[e], block_sems.at[0, e]),
            pltpu.make_async_copy(w_out_ref.at[e, my_hidden, :], out_buf.at[e], block_sems.at[1, e]),
        )

    for n in range(depth):
        for copy in weight_copies(n):
            copy.start()

    greet(dp_others + expert_others)

    low_ref[my_rows(mine), :] = token_ref[...]
    token_gather = QuadGather(place, low_ref, token_sems, block)
    token_gather.begin()

    ids = ids_ref[...]
    position = lax.broadcasted_iota(jnp.int32, (block, 1), 0)
    valid = (position + mine * block < length).astype(F32)
    chosen = (lax.broadcasted_iota(jnp.int32, (block, experts_count), 1) == ids).astype(F32)
    hits = chosen * valid
    below = (
        lax.broadcasted_iota(jnp.int32, (block, block), 1) < lax.broadcasted_iota(jnp.int32, (block, block), 0)
    ).astype(BF16)
    rank = jnp.sum(dot(below, hits.astype(BF16)) * hits, axis=1, keepdims=True)
    count_send[...] = jnp.zeros_like(count_send)
    count_send[0:1, :experts_count] = jnp.sum(hits, axis=0, keepdims=True)
    counts_going = [
        send(count_send, count_ref.at[ex], count_sems, (n,), device) for n, device in enumerate(expert_others)
    ]
    count_ref[ex] = count_send[...]
    target = jnp.where(valid > 0, ids.astype(F32) * slots + rank, -1.0).astype(jnp.int32)
    place_ref[...] = (
        lax.broadcasted_iota(jnp.int32, place_ref.shape, 1) == target
    ).astype(BF16)

    slot_send[...] = t_dot(place_ref[...], cotangent_ref[...]).astype(BF16).reshape(slot_send.shape)

    def scatter(arrive, sems):
        going = [
            send(slot_send.at[pl.ds(device[1] * local, local)], arrive.at[ex], sems, (n,), device)
            for n, device in enumerate(expert_others)
        ]
        arrive[ex] = slot_send[pl.ds(ex * local, local)]
        return going

    ups_going = scatter(up_arrive, up_sems)

    for m in range(quad):

        @pl.when(mine == m)
        def _():
            for kind, weight_ref in enumerate((w_query_ref, w_key_ref, w_value_ref)):
                w_mine_ref[:, kind * part : (kind + 1) * part] = weight_ref[:, m * part : (m + 1) * part]

    for a in range(win_ref.shape[0]):
        win_ref[a] = dot(table_ref[...], hot_ref[a])
    fill_bias(0)

    for copy in counts_going:
        copy.wait()
    before = jnp.zeros((1, experts_count), F32)
    for s in range(sources):
        before = before + count_ref[s, 0:1, :experts_count] * (s < ex).astype(F32)
    kept = valid * (rank + jnp.sum(hits * before, axis=1, keepdims=True) < capacity).astype(F32)
    lane = lax.broadcasted_iota(jnp.int32, (1, sources * slots), 1)
    expert_lane = lax.broadcasted_iota(jnp.int32, (1, count_ref.shape[2]), 1)
    for e in range(local):
        at = jnp.full((1, sources * slots), -1, jnp.int32)
        start = jnp.zeros((1, 1), F32)
        for s in range(sources):
            count = jnp.sum(
                jnp.where(expert_lane == ex * local + e, count_ref[s, 0:1, :], 0.0), axis=1, keepdims=True
            )
            turn = lane - s * slots
            here = (turn >= 0) & (turn < slots) & (turn < count.astype(jnp.int32))
            at = jnp.where(here, start.astype(jnp.int32) + turn, at)
            start = start + count
        pack_ref[e] = (lax.broadcasted_iota(jnp.int32, (capacity, sources * slots), 0) == at).astype(BF16)

    gain = gain_one_ref[...].astype(F32)

    def project(i):
        token = low_ref[my_rows(i), :].astype(F32)
        inverse = lax.rsqrt(jnp.mean(token * token, axis=-1, keepdims=True) + 1e-06)
        normed = token * inverse * gain
        normed_ref[:, my_rows(i)] = normed.T.astype(BF16)
        qkv_ref[my_rows(i), :] = dot(normed.astype(BF16), w_mine_ref[...]).astype(BF16)

    project(mine)
    token_gather.forward()
    project(quad_others[0][1])
    project(quad_others[1][1])
    token_gather.end()
    project(quad_others[2][1])

    for copy in ups_going:
        copy.wait()
    for e in range(local):
        up_ref[z, e] = dot(pack_ref[e], up_arrive[:, e].reshape(sources * slots, width)).astype(BF16)
    up_relay.begin()

    for h in range(heads):
        if h:
            fill_bias(h)
        cols = slice(h * head_width, (h + 1) * head_width)
        key = qkv_ref[:, part + h * head_width : part + (h + 1) * head_width]
        value = qkv_ref[:, 2 * part + h * head_width : 2 * part + (h + 1) * head_width]

        @pl.loop(0, blocks)
        def _(i):
            rows = my_rows(i)
            query = qkv_ref[rows, cols]
            scores = []
            for j in range(blocks):
                score = dot_t(key[j * block : (j + 1) * block], query)
                score = score + bias_ref[j - i + blocks - 1]
                scores.append(jnp.where(position + j * block < length, score, MASKED))
            top = functools.reduce(
                jnp.maximum, [jnp.max(s, axis=0, keepdims=True) for s in scores]
            )
            total = jnp.zeros((1, block), F32)
            out = jnp.zeros((head_width, block), F32)
            for j in range(blocks):
                scaled = jnp.exp(scores[j] - top)
                total = total + jnp.sum(scaled, axis=0, keepdims=True)
                out = out + t_dot(value[j * block : (j + 1) * block], scaled.astype(BF16))
            out = out * (1.0 / total)
            attended_ref[rows, cols] = out.T.astype(BF16)
            lse_ref[h, pl.ds(i, 1), :] = top + jnp.log(total)

        if h == 1:
            up_relay.step(1)

    attended_going = [
        send(attended_ref.at[my_rows(member)], attended_recv.at[mine], attended_sems, (n,), device)
        for n, (device, member) in enumerate(quad_others)
    ]
    attended_recv[mine] = attended_ref[my_rows(mine), :]
    for copy in attended_going:
        copy.wait()
    attended = jnp.concatenate([attended_recv[m] for m in range(quad)], axis=1)
    residual = token_ref[...].astype(F32) + dot(attended, w_output_ref[...])
    residual_ref[...] = residual
    inverse = lax.rsqrt(jnp.mean(residual * residual, axis=-1, keepdims=True) + 1e-06)
    gain_two = gain_two_ref[...].astype(F32)
    routed = (residual * inverse * gain_two).astype(BF16)

    slot_send[...] = t_dot(place_ref[...], routed).astype(BF16).reshape(slot_send.shape)
    rows_going = scatter(rows_arrive, go_sems)
    logits = dot(routed, w_router_ref[...])
    router = jnp.exp(logits - jnp.max(logits, axis=1, keepdims=True))
    router = router / jnp.sum(router, axis=1, keepdims=True)
    chosen_prob = jnp.sum(router * chosen, axis=1, keepdims=True)
    gate = chosen_prob * kept
    slopes = router * (chosen - chosen_prob)
    gate_slots = exact_dot(jnp.broadcast_to(gate, (block, 8)), place_ref[...].astype(F32), 0, 0)
    gate_send[...] = jnp.zeros_like(gate_send)
    for e in range(experts_count):
        gate_send[e, :, :slots] = gate_slots[:, e * slots : (e + 1) * slots]
    gates_going = [
        send(gate_send.at[pl.ds(device[1] * local, local)], gate_arrive.at[ex], gate_sems, (n,), device)
        for n, device in enumerate(expert_others)
    ]
    gate_arrive[ex] = gate_send[pl.ds(ex * local, local)]
    up_relay.step(2)
    for copy in rows_going:
        copy.wait()
    for e in range(local):
        rows_ref[z, e * capacity : (e + 1) * capacity, :] = dot(
            pack_ref[e], rows_arrive[:, e].reshape(sources * slots, width)
        ).astype(BF16)
    for copy in gates_going:
        copy.wait()
    rows_ref[z, local * capacity :, :] = jnp.zeros((rows_ref.shape[1] - local * capacity, width), BF16)
    gate_lines = jnp.zeros((rows_ref.shape[1] - local * capacity, capacity), F32)
    line = lax.broadcasted_iota(jnp.int32, gate_lines.shape, 0)
    gate_columns = []
    for e in range(local):
        arrived = jnp.concatenate([gate_arrive[s, e, :, :slots] for s in range(sources)], axis=1)
        pack = pack_ref[e].astype(F32)
        gate_columns.append(exact_dot(pack, arrived, 1, 1)[:, 0:1])
        rest = exact_dot(arrived, pack, 1, 1)[0:1]
        for n in range(3):
            high = rest.astype(BF16).astype(F32)
            gate_lines = jnp.where(line == 3 * e + n, high, gate_lines)
            rest = rest - high
    rows_ref[z, local * capacity :, :capacity] = gate_lines.astype(BF16)
    rows_relay.begin()

    backs = []
    for e in range(local):
        rows = rows_ref[z, e * capacity : (e + 1) * capacity, :]
        d_rows = (gate_columns[e] * up_ref[z, e].astype(F32)).astype(BF16)
        for f in range(pieces):
            n = e * pieces + f
            for copy in weight_copies(n):
                copy.wait()
            weight_in = in_buf[n % depth]
            weight_out = out_buf[n % depth]
            active, slope = gelu_parts(dot(rows, weight_in))
            forward = dot(active.astype(BF16), weight_out)
            d_inner = (dot_t(d_rows, weight_out) * slope).astype(BF16)
            backward = dot_t(d_inner, weight_in)
            if f == 0:
                result_ref[:, :width] = forward
                result_ref[:, width:] = backward
            else:
                result_ref[:, :width] += forward
                result_ref[:, width:] += backward
            if n + depth < local * pieces:
                for copy in weight_copies(n + depth):
                    copy.start()
        spread_rows = t_dot(pack_ref[e], result_ref[...].astype(BF16)).astype(BF16)
        back_send[:, e] = spread_rows.reshape(sources, slots, 2 * width)
        for n, device in enumerate(expert_others):
            backs.append(
                send(back_send.at[device[1], e], back_ref.at[ex * local + e], back_sems, (e, n), device)
            )
        back_ref[ex * local + e] = back_send[ex, e]
        if e == 0:
            up_relay.step(3)
        else:
            rows_relay.step(1)
    for e in range(local):
        for copy in block_copies(e):
            copy.start()
    fill_bias(0)
    for copy in backs:
        copy.wait()

    gathered = dot(place_ref[...], back_ref[...].reshape(experts_count * slots, 2 * width))
    expert_out = gathered[:, :width]
    residual = residual_ref[...]
    output_ref[...] = (valid * (residual + gate * expert_out)).astype(BF16)
    upstream = cotangent_ref[...].astype(F32) * valid
    d_gate = jnp.sum(upstream * expert_out, axis=1, keepdims=True) * kept
    d_logits = (slopes * d_gate).astype(BF16)
    small_send[0] = jnp.zeros(small_send.shape[1:], F32)
    inverse = lax.rsqrt(jnp.mean(residual * residual, axis=-1, keepdims=True) + 1e-06)
    routed = (residual * inverse * gain_two).astype(BF16)
    small_send[0, 2:10, :] = t_dot(d_logits, routed)
    d_routed = gathered[:, width:] + dot_t(d_logits, w_router_ref[...])
    small_send[0, 1:2, :] = jnp.sum(d_routed * residual * inverse, axis=0, keepdims=True)
    scaled = d_routed * gain_two
    cubed = inverse * inverse * inverse
    d_residual = upstream + inverse * scaled - residual * cubed * jnp.mean(
        residual * scaled, axis=-1, keepdims=True
    )
    residual_ref[...] = d_residual

    low = d_residual.astype(BF16)
    low_ref[my_rows(mine), :] = low
    d_attended = dot_t(low, w_output_ref[...]).astype(BF16)
    for m in range(quad):
        grad_send[m] = d_attended[:, m * part : (m + 1) * part]
    copies = []
    for n, (device, member) in enumerate(quad_others):
        copies.append(
            send(grad_send.at[member], grad_ref.at[my_rows(mine)], grad_sems, (n,), device)
        )
    grad_ref[my_rows(mine), :] = grad_send[mine]
    rows_relay.step(2)
    for copy in copies:
        copy.wait()
    low_gather = QuadGather(place, low_ref, low_sems, block)
    low_gather.begin()

    table_count = hot_ref.shape[1]
    core, x = place.core, place.x
    quarter = width // 4
    core_device, x_device, z_device = place.flip("core"), place.flip("x"), place.flip("z_hi")
    thirds = 3
    third = quarter // thirds
    axes_devices = {"x": x_device, "y": quad_others[0][0], "z": quad_others[1][0]}
    orders = ("xyz", "yzx", "zxy")

    def chunk(c, b):
        return pl.ds(pl.multiple_of((c * 2 + b) * quarter, quarter), quarter)

    class Sum:
        def __init__(self, u):
            self.u = u
            self.rings, self.passed = {}, []

        def begin(self):
            u = self.u
            self.one = [
                send(load_ref.at[u, chunk(1 - core, 1 - x)], first_ref.at[u, 0], first_sems, (u, 0), core_device),
                send(load_ref.at[u, chunk(1 - core, x)], first_ref.at[u, 1], first_sems, (u, 1), core_device),
            ]

        def over_x(self):
            u = self.u
            self.one[0].wait()
            sum_one_ref[u] = (
                load_ref[u, chunk(core, 1 - x), :].astype(F32) + first_ref[u, 0].astype(F32)
            ).astype(BF16)
            self.two = send(sum_one_ref.at[u], second_ref.at[u], second_sems, (u,), x_device)

        def over_z(self):
            u = self.u
            self.one[1].wait()
            self.two.wait()
            sum_two_ref[u] = (
                load_ref[u, chunk(core, x), :].astype(F32) + first_ref[u, 1].astype(F32) + second_ref[u].astype(F32)
            ).astype(BF16)
            self.three = send(sum_two_ref.at[u], third_ref.at[u], third_sems, (u,), z_device)

        def spot(self, axes, t):
            y = 1 - place.y if "y" in axes else place.y
            z_lo = 1 - place.z_lo if "z" in axes else place.z_lo
            xx = 1 - x if "x" in axes else x
            row = pl.multiple_of((core * 2 + xx) * quarter + t * third, third)
            return d_weights_ref.at[self.u, z_lo * 2 + y, pl.ds(row, third)]

        def to_core(self, axes, t, n):
            where = self.spot(axes, t)
            self.passed.append(send(where, where, core_sems, (self.u, t, n), core_device))

        def forward(self, axes, t, axis, n):
            where = self.spot(axes, t)
            self.rings[t, n] = send(where, where, ring_sems, (self.u, t, n), axes_devices[axis])

        def gather_one(self):
            u = self.u
            self.three.wait()
            d_weights_ref[u, mine, chunk(core, x), :] = (
                sum_two_ref[u].astype(F32) + third_ref[u].astype(F32)
            ).astype(BF16)
            for t, (a, b, c) in enumerate(orders):
                self.forward("", t, a, 0)
                self.forward("", t, b, 1)
                self.forward("", t, c, 3)
                self.to_core("", t, 0)

        def gather_two(self):
            for t, (a, b, c) in enumerate(orders):
                self.rings[t, 0].wait_recv()
                self.forward(a, t, b, 2)
                self.forward(a, t, c, 4)
                self.to_core(a, t, 1)

        def gather_three(self):
            for t, (a, b, c) in enumerate(orders):
                self.rings[t, 1].wait_recv()
                self.forward(b, t, c, 5)
                self.to_core(b, t, 2)
                self.rings[t, 2].wait_recv()
                self.forward(a + b, t, c, 6)
                self.to_core(a + b, t, 3)

        def gather_last(self):
            for t, (a, b, c) in enumerate(orders):
                for n, axes in ((3, c), (4, a + c), (5, b + c), (6, a + b + c)):
                    self.rings[t, n].wait_recv()
                    self.to_core(axes, t, n + 1)

        def end(self):
            for t in range(thirds):
                for n in range(7):
                    self.rings[t, n].wait_send()
            for copy in self.passed:
                copy.wait()

    sums = [Sum(h) for h in range(heads)]
    small_devices = [core_device, x_device, z_device, quad_others[0][0], quad_others[1][0]]
    small_copies = []

    def small_start(n):
        small_copies.append(
            send(small_send.at[n], small_recv.at[n], small_sems, (n,), small_devices[n])
        )

    def small_end(n):
        small_copies[n].wait()
        total = small_send[n] + small_recv[n]
        if n + 1 < len(small_devices):
            small_send[n + 1] = total
        else:
            total_ref[...] = total

    y = place.y
    y_device = quad_others[0][0]
    z_devices = [
        place.flip("z_lo"), place.flip("z_hi"), place.flip("z_lo", "z_hi"),
    ]
    share = width // (2 * groups)
    half_copies, d_out_copies, d_in_copies = [], [], []

    def hidden_gradients(e):
        for copy in block_copies(e):
            copy.wait()
        for g in range(groups):
            rows = rows_ref[g, e * capacity : (e + 1) * capacity, :]
            gates = rows_ref[g, local * capacity :, :capacity].astype(F32)
            gate_row = gates[3 * e : 3 * e + 1] + gates[3 * e + 1 : 3 * e + 2] + gates[3 * e + 2 : 3 * e + 3]
            gate_column = jnp.sum(jnp.where(diagonal, gate_row, 0.0), axis=1, keepdims=True)
            d_rows = (gate_column * up_ref[g, e].astype(F32)).astype(BF16)
            up_ref[g, e] = d_rows
            active, slope = gelu_parts(dot(rows, in_buf[e]))
            inner_ref[g] = (dot_t(d_rows, out_buf[e]) * slope).astype(BF16)
            active_ref[g] = active.astype(BF16)
        all_rows = rows_ref[:, e * capacity : (e + 1) * capacity, :].reshape(groups * capacity, width)
        all_d_rows = up_ref[:, e].reshape(groups * capacity, width)
        d_in = t_dot(all_rows, inner_ref[...].reshape(groups * capacity, hidden)).astype(BF16)
        for n in range(2 * groups):
            half_send[e, n % 2, n // 2] = d_in[n * share : (n + 1) * share]
        half_copies.append(send(half_send.at[e, 1 - y], half_recv.at[e], half_sems, (0, e), y_device))
        d_out = t_dot(active_ref[...].reshape(groups * capacity, hidden), all_d_rows).astype(BF16)
        d_out_send[e] = d_out.reshape(d_out_send.shape[1:])

    def hidden_d_out(e):
        d_out_copies.append(send(d_out_send.at[e, 1 - y], d_out_recv.at[e], half_sems, (1, e), y_device))

    def hidden_d_in(e):
        half_copies[e].wait()
        half_send[e, y] = (half_send[e, y].astype(F32) + half_recv[e].astype(F32)).astype(BF16)
        for n, device in enumerate(z_devices):
            d_in_copies.append(
                send(half_send.at[e, y, lax.div(device[0], 2)], d_in_ref.at[z, e], d_in_sems, (e, n), device)
            )
        d_in_ref[z, e] = half_send[e, y, z]

    def hidden_end(e):
        d_out_copies[e].wait()
        d_out_ref[e] = (d_out_send[e, y].astype(F32) + d_out_recv[e].astype(F32)).astype(BF16)

    for h in range(heads):
        if h:
            fill_bias(h)
        cols = slice(h * head_width, (h + 1) * head_width)
        key_cols = slice(part + h * head_width, part + (h + 1) * head_width)
        value_cols = slice(2 * part + h * head_width, 2 * part + (h + 1) * head_width)
        key = qkv_ref[:, key_cols]
        value = qkv_ref[:, value_cols]
        dkey_ref[...] = jnp.zeros_like(dkey_ref)
        dvalue_ref[...] = jnp.zeros_like(dvalue_ref)
        dbias_ref[...] = jnp.zeros_like(dbias_ref)

        def query_block(i):
            rows = my_rows(i)
            query = qkv_ref[rows, cols]
            grad = grad_ref[rows, cols]
            log_norm = lse_ref[h, pl.ds(i, 1), :]
            probs, d_probs = [], []
            spread = jnp.zeros((1, block), F32)
            for j in range(blocks):
                keys = slice(j * block, (j + 1) * block)
                score = dot_t(key[keys], query)
                score = score + bias_ref[j - i + blocks - 1]
                score = jnp.where(position + j * block < length, score, MASKED)
                prob = jnp.exp(score - log_norm)
                d_prob = dot_t(value[keys], grad)
                spread = spread + jnp.sum(prob * d_prob, axis=0, keepdims=True)
                dvalue_ref[keys, :] += dot(prob.astype(BF16), grad)
                probs.append(prob)
                d_probs.append(d_prob)
            d_query = jnp.zeros((head_width, block), F32)
            for j in range(blocks):
                keys = slice(j * block, (j + 1) * block)
                d_score = probs[j] * (d_probs[j] - spread)
                dbias_ref[j - i + blocks - 1] += d_score
                low_score = d_score.astype(BF16)
                dkey_ref[keys, :] += dot(low_score, query)
                d_query = d_query + t_dot(key[keys], low_score)
            dqkv_ref[rows, cols] = d_query.T.astype(BF16)

        pl.loop(0, blocks // 2)(query_block)
        if h == 0:
            rows_relay.step(3)
        elif h == 1:
            sums[0].over_x()
        else:
            sums[0].gather_one()
            sums[1].over_x()
        pl.loop(blocks // 2, blocks)(query_block)

        dqkv_ref[:, key_cols] = dkey_ref[...].astype(BF16)
        dqkv_ref[:, value_cols] = dvalue_ref[...].astype(BF16)

        terms = jnp.concatenate([dqkv_ref[:, cols], dqkv_ref[:, key_cols], dqkv_ref[:, value_cols]], axis=1)
        d_parts = dot(normed_ref[...], terms)
        w_head = jnp.concatenate([w_mine_ref[:, cols], w_mine_ref[:, key_cols], w_mine_ref[:, value_cols]], axis=1)
        d_gain = exact_dot(jnp.ones((8, part), F32), d_parts * w_head.astype(F32), 1, 1)[0:1] / gain
        if h == 0:
            small_send[0, 0:1, :] = d_gain
            low_gather.forward()
            up_relay.end()
            rows_relay.end()
            hidden_gradients(0)
            hidden_gradients(1)
            low_gather.end()
            d_output = t_dot(attended_ref[...], low_ref[...]).astype(BF16)
            for u in range(heads):
                for m in range(quad):
                    load_ref[u, m * part : (m + 1) * part, part:] = d_output[
                        :, m * part + u * head_width : m * part + (u + 1) * head_width
                    ]
        else:
            small_send[0, 0:1, :] += d_gain
        load_ref[h, :, :part] = d_parts.astype(BF16)
        sums[h].begin()
        if h == 1:
            sums[0].over_z()
        elif h == 2:
            sums[0].gather_two()
            sums[1].over_z()
            hidden_d_in(0)
            hidden_d_in(1)
            hidden_d_out(0)
            hidden_d_out(1)

            mine_copies = []
            for n, (device, member) in enumerate(quad_others):
                mine_copies.append(
                    send(dqkv_ref.at[my_rows(member)], dmine_ref.at[mine], mine_sems, (n,), device)
                )
            dmine_ref[mine] = dqkv_ref[my_rows(mine), :]
        table_row = jnp.zeros((1, table_count), F32)
        for a in range(dbias_ref.shape[0]):
            wide = jnp.concatenate([dbias_ref[a], jnp.zeros((block, block), F32)], axis=1)
            half = block // 2
            while half:
                wide = wide[:half] + pltpu.roll(wide[half:], 2 * block - half, 1)
                half //= 2
            table_row = table_row + exact_dot(wide, hot_ref[a].astype(F32), 1, 1)
        for m in range(quad):
            row = 12 + m * heads + h
            small_send[0, row : row + 1, :table_count] = jnp.where(mine == m, table_row, 0.0)

    small_start(0)
    sums[2].over_x()
    sums[0].gather_three()
    sums[2].over_z()
    sums[1].gather_one()
    small_end(0)
    small_start(1)
    sums[0].gather_last()
    sums[2].gather_one()
    sums[1].gather_two()
    small_end(1)
    small_start(2)

    for copy in mine_copies:
        copy.wait()
    d_normed = jnp.zeros((block, width), F32)
    for kind, weight_ref in enumerate((w_query_ref, w_key_ref, w_value_ref)):
        d_kind = [dmine_ref[m, :, kind * part : (kind + 1) * part] for m in range(quad)]
        d_normed = d_normed + dot_t(jnp.concatenate(d_kind, axis=1), weight_ref[...])
    sums[2].gather_two()
    sums[1].gather_three()
    small_end(2)
    small_start(3)
    token = token_ref[...].astype(F32)
    inverse = lax.rsqrt(jnp.mean(token * token, axis=-1, keepdims=True) + 1e-06)
    scaled = d_normed * gain
    cubed = inverse * inverse * inverse
    d_tokens_ref[...] = residual_ref[...] + inverse * scaled - token * cubed * jnp.mean(
        token * scaled, axis=-1, keepdims=True
    )
    sums[2].gather_three()
    sums[1].gather_last()
    small_end(3)
    small_start(4)
    sums[2].gather_last()
    small_end(4)
    for e in range(local):
        hidden_end(e)
    for total in sums:
        total.end()
    for copy in d_in_copies:
        copy.wait()


def layer(lengths, tokens, ids, cotangent, gain_one, gain_two, w_query, w_key, w_value, w_output, w_router, table, hot, w_in, w_out, head_count):
    block, full = tokens.shape
    count, _, double = hot.shape
    quad = (count + 1) // 2
    rows = quad * block
    part = full // quad
    triple = 3 * part
    heads = head_count // quad
    head_width = part // heads
    quarter = full // 4
    experts_count = w_router.shape[1]
    local = w_in.shape[0]
    sources = experts_count // local
    capacity = 5 * block // (4 * local)
    slots = 3 * block // (2 * experts_count)
    groups = lax.axis_size("dp") // 2
    hidden = w_in.shape[2] // groups
    share = full // (2 * groups)
    piece = hidden
    depth = 2
    small = (24, full)
    extra = 16
    vmem = pl.BlockSpec(memory_space=pltpu.VMEM)
    hbm = pl.BlockSpec(memory_space=pl.ANY)
    dma = pltpu.SemaphoreType.DMA
    return pl.pallas_call(
        layer_kernel,
        in_specs=[pl.BlockSpec(memory_space=pltpu.SMEM)] + [vmem] * 12 + [hbm] * 2,
        out_specs=[vmem] * 6,
        out_shape=[
            jax.ShapeDtypeStruct((block, full), BF16),
            jax.ShapeDtypeStruct((block, full), F32),
            jax.ShapeDtypeStruct((heads, quad, full, part + head_width), BF16),
            jax.ShapeDtypeStruct(small, F32),
            jax.ShapeDtypeStruct((local, hidden // 2, full), BF16),
            jax.ShapeDtypeStruct((groups, local, share, hidden), BF16),
        ],
        scratch_shapes=[
            pltpu.VMEM((full, triple), BF16),
            pltpu.VMEM((full, rows), BF16),
            pltpu.VMEM((rows, triple), BF16),
            pltpu.VMEM((count, table.shape[0], double), F32),
            pltpu.VMEM((heads, quad, block), F32),
            pltpu.VMEM((rows, part), BF16),
            pltpu.VMEM((quad, block, part), BF16),
            pltpu.VMEM((8, 128), F32),
            pltpu.VMEM((sources, 8, 128), F32),
            pltpu.VMEM((experts_count, slots, full), BF16),
            pltpu.VMEM((sources, local, slots, full), BF16),
            pltpu.VMEM((sources, local, slots, full), BF16),
            pltpu.VMEM((experts_count, 8, 128), F32),
            pltpu.VMEM((sources, local, 8, 128), F32),
            pltpu.VMEM((block, experts_count * slots), BF16),
            pltpu.VMEM((local, capacity, sources * slots), BF16),
            pltpu.VMEM((groups, local, capacity, full), BF16),
            pltpu.VMEM((groups, local * capacity + extra, full), BF16),
            pltpu.VMEM((depth, full, piece), BF16),
            pltpu.VMEM((depth, piece, full), BF16),
            pltpu.VMEM((capacity, 2 * full), F32),
            pltpu.VMEM((sources, local, slots, 2 * full), BF16),
            pltpu.VMEM((experts_count, slots, 2 * full), BF16),
            pltpu.VMEM((block, full), F32),
            pltpu.VMEM((rows, part), BF16),
            pltpu.VMEM((quad, block, part), BF16),
            pltpu.VMEM((rows, full), BF16),
            pltpu.VMEM((count, block, block), F32),
            pltpu.VMEM((count, block, block), F32),
            pltpu.VMEM((rows, head_width), F32),
            pltpu.VMEM((rows, head_width), F32),
            pltpu.VMEM((rows, triple), BF16),
            pltpu.VMEM((quad, block, triple), BF16),
            pltpu.VMEM((heads, full, part + head_width), BF16),
            pltpu.VMEM((heads, 2, quarter, part + head_width), BF16),
            pltpu.VMEM((heads, quarter, part + head_width), BF16),
            pltpu.VMEM((heads, quarter, part + head_width), BF16),
            pltpu.VMEM((heads, quarter, part + head_width), BF16),
            pltpu.VMEM((heads, quarter, part + head_width), BF16),
            pltpu.VMEM((5,) + small, F32),
            pltpu.VMEM((5,) + small, F32),
            pltpu.VMEM((groups, capacity, hidden), BF16),
            pltpu.VMEM((groups, capacity, hidden), BF16),
            pltpu.VMEM((local, 2, groups, share, hidden), BF16),
            pltpu.VMEM((local, groups, share, hidden), BF16),
            pltpu.VMEM((local, 2, hidden // 2, full), BF16),
            pltpu.VMEM((local, hidden // 2, full), BF16),
            dma((2, 4)), dma((2, 3)), dma((2, 3)), dma((2, 3)), dma((2, 3)), dma((2, 3)), dma((2, depth)),
            dma((2, 2, 3)), dma((2, 2, 3)), dma((2, 2, 3)),
            dma((2, 3)), dma((2, 4)), dma((2, 3)), dma((2, 3, 2)), dma((2, 3)), dma((2, 3)),
            dma((2, 3, 3, 7)), dma((2, 3, 3, 8)), dma((2, 5)), dma((2, 2, 3)), dma((2, 2, 2)), dma((2, 2)),
        ],
        compiler_params=pltpu.CompilerParams(
            vmem_limit_bytes=62 * 1024 * 1024, collective_id=0, has_side_effects=True
        ),
        name="layer",
    )(lengths, tokens, ids, cotangent, gain_one, gain_two, w_query, w_key, w_value, w_output, w_router, table, hot,
      w_in, w_out)


def finish_kernel(all_ref, d_in_ref, d_out_ref, d_query_ref, d_key_ref, d_value_ref, d_output_ref, d_in_out_ref, d_out_out_ref):
    heads, quad, rows, wide = all_ref.shape
    full = d_query_ref.shape[1]
    part = full // quad
    width = wide - part
    for kind, ref in enumerate((d_query_ref, d_key_ref, d_value_ref)):
        for i in range(rows // part):
            span = slice(i * part, (i + 1) * part)
            ref[span, :] = jnp.concatenate(
                [
                    all_ref[h, m, span, kind * width : (kind + 1) * width].astype(F32)
                    for m in range(quad)
                    for h in range(heads)
                ],
                axis=1,
            )
    for m in range(quad):
        d_output_ref[m * part : (m + 1) * part, :] = jnp.concatenate(
            [
                all_ref[h, m, n * part : (n + 1) * part, part:].astype(F32)
                for n in range(quad)
                for h in range(heads)
            ],
            axis=1,
        )
    groups, local, count, hidden = d_in_ref.shape
    for g in range(groups):
        for e in range(local):
            d_in_out_ref[e, :, g * hidden : (g + 1) * hidden] = d_in_ref[g, e].astype(F32)
    d_out_out_ref[...] = d_out_ref[...].astype(F32)


def finish(gathered, d_in, d_out):
    heads, quad, rows, wide = gathered.shape
    groups, local, count, hidden = d_in.shape
    full = rows
    vmem = pl.BlockSpec(memory_space=pltpu.VMEM)
    return pl.pallas_call(
        finish_kernel,
        in_specs=[vmem] * 3,
        out_specs=[vmem] * 6,
        out_shape=[jax.ShapeDtypeStruct((rows, full), F32)] * 4
        + [jax.ShapeDtypeStruct((local, count, groups * hidden), F32), jax.ShapeDtypeStruct(d_out.shape, F32)],
        compiler_params=pltpu.CompilerParams(vmem_limit_bytes=VMEM_BYTES),
        name="finish",
    )(gathered, d_in, d_out)


def all_to_all(array, axis, groups=None):
    return lax.all_to_all(
        array, axis, split_axis=0, concat_axis=0, tiled=True, axis_index_groups=groups
    )


def to_experts(received, local):
    total, slots, width = received.shape
    shaped = received.reshape(total // local, local, slots, width)
    return jnp.swapaxes(shaped, 0, 1).reshape(local, total // local * slots, width)


def to_sources(by_expert, sources):
    local, total, width = by_expert.shape
    shaped = by_expert.reshape(local, sources, total // sources, width)
    return jnp.swapaxes(shaped, 0, 1).reshape(sources * local, total // sources, width)


def per_device(
    tokens, lengths, expert_ids, gain_one, w_query, w_key, w_value, w_output,
    bias_table, gain_two, w_router, w_in, w_out, cotangent,
):
    tok_rows, width = tokens.shape
    head_count = bias_table.shape[1]
    head_width = width // head_count
    expert_count = w_router.shape[1]
    local = w_in.shape[0]
    hidden = w_in.shape[2]
    dp_count, ex_count = lax.axis_size("dp"), lax.axis_size("expert")
    dp_index, ex_index = lax.axis_index("dp"), lax.axis_index("expert")
    span = dp_count // 2
    quad = math.gcd(span, head_count)
    heads = head_count // quad
    part = heads * head_width
    q_rows = quad * tok_rows
    q_parts = span // quad
    place = dp_index % span
    mine, q_part = place % quad, place // quad
    quads = [[i * quad + j for j in range(quad)] for i in range(dp_count // quad)]
    spans = [[i * span + j for j in range(span)] for i in range(dp_count // span)]
    seq_id = ex_index * (dp_count // span) + dp_index // span
    start_row = place * tok_rows

    length = jnp.sum(jnp.where(jnp.arange(lengths.shape[0], dtype=jnp.int32) == seq_id, lengths, 0))
    valid_mask = start_row + jnp.arange(tok_rows, dtype=jnp.int32) < length
    valid_f = valid_mask.astype(F32)
    length_arg = length.reshape(1)

    if q_parts == 1:
        tokens_all = all_to_all(
            jnp.broadcast_to(tokens[None], (quad, tok_rows, width)), "dp", quads
        ).reshape(q_rows, width)
        tokens_q = tokens_all
    else:
        tokens_all = lax.all_gather(tokens, "dp", axis_index_groups=spans, tiled=True)
        tokens_q = lax.dynamic_slice_in_dim(tokens_all, q_part * q_rows, q_rows, 0)
    gain_a = gain_one.astype(F32)
    normed_all = normalize(tokens_all.astype(F32), gain_a)[0].astype(BF16)
    normed_q = normalize(tokens_q.astype(F32), gain_a)[0].astype(BF16)

    table = lax.dynamic_slice_in_dim(bias_table.astype(F32), mine * heads, heads, 1)
    counts = span * tok_rows // tok_rows + quad - 1
    offset = jnp.arange(2 * tok_rows, dtype=jnp.int32)
    offset = jnp.where(offset < tok_rows, offset, offset - 2 * tok_rows)
    codes = (
        jnp.arange(counts, dtype=jnp.int32)[:, None] * tok_rows
        - offset[None, :]
        - (q_rows - tok_rows)
        - q_part * q_rows
    )
    window_hot = (
        bucket_of(codes)[:, :, None] == jnp.arange(table.shape[0], dtype=jnp.int32)
    ).astype(BF16)
    window = jnp.einsum("amb,bh->ham", window_hot, table.astype(BF16), preferred_element_type=F32)

    def my_columns(weight):
        return lax.dynamic_slice_in_dim(weight, mine * part, part, 1).reshape(
            width, heads, head_width
        )

    def project(rows, weight):
        return jnp.einsum(
            "sd,dhc->hsc", rows, my_columns(weight), preferred_element_type=F32
        ).astype(BF16)

    query = project(normed_q, w_query)
    key = project(normed_all, w_key)
    value = project(normed_all, w_value)
    attended_heads, log_norm = attend(length_arg, window, query, key, value)
    attended = all_to_all(
        jnp.transpose(
            attended_heads.reshape(heads, quad, tok_rows, head_width), (1, 2, 0, 3)
        ).reshape(quad, tok_rows, part),
        "dp",
        quads,
    )
    attended = jnp.swapaxes(attended, 0, 1).reshape(tok_rows, width)

    token_f = tokens.astype(F32)
    residual = token_f + dot(attended, w_output)
    gain_b = gain_two.astype(F32)
    routed_f, inverse_two = normalize(residual, gain_b)
    routed = routed_f.astype(BF16)
    router = jax.nn.softmax(dot(routed, w_router), axis=-1)

    chosen = expert_ids[:, 0]
    chosen_hot = chosen[:, None] == jnp.arange(expert_count, dtype=jnp.int32)[None, :]
    valid_hits = (chosen_hot & valid_mask[:, None]).astype(jnp.int32)
    per_source = lax.all_gather(jnp.sum(valid_hits, axis=0), "expert")
    earlier = jnp.arange(ex_count, dtype=jnp.int32)[:, None] < ex_index
    offsets = jnp.sum(jnp.where(earlier, per_source, 0), axis=0)
    local_rank = jnp.sum((jnp.cumsum(valid_hits, axis=0) - valid_hits) * valid_hits, axis=1)
    group_rank = local_rank + jnp.sum(valid_hits * offsets[None, :], axis=1)
    capacity = 5 * tok_rows // (4 * local)
    slots = 3 * tok_rows // (2 * expert_count)
    kept_mask = valid_mask & (group_rank < capacity)
    kept_f = kept_mask.astype(F32)
    target = jnp.where(kept_mask, chosen * slots + local_rank, -1)
    placing = (
        jnp.arange(expert_count * slots, dtype=jnp.int32)[:, None] == target[None, :]
    ).astype(BF16)
    chosen_f = chosen_hot.astype(F32)
    chosen_prob = jnp.sum(router * chosen_f, axis=1)
    gate = chosen_prob * kept_f
    upstream = cotangent.astype(F32) * valid_f[:, None]
    d_expert = (gate[:, None] * upstream).astype(BF16)

    sending = dot(placing, jnp.concatenate([routed, d_expert], axis=1)).astype(BF16)
    expert_rows = to_experts(
        all_to_all(sending.reshape(expert_count, slots, 2 * width), "expert"), local
    )
    group_rows = lax.all_gather(expert_rows, "dp")
    results = experts(expert_rows, w_in, w_out)
    returned = all_to_all(to_sources(results, ex_count), "expert")
    gathered = t_dot(placing, returned.reshape(expert_count * slots, 2 * width))
    expert_out, d_routed = gathered[:, :width], gathered[:, width:]

    output = (valid_f[:, None] * (residual + gate[:, None] * expert_out)).astype(BF16)
    d_gate = jnp.sum(upstream * expert_out, axis=1) * kept_f
    d_logits = router * (chosen_f - chosen_prob[:, None]) * d_gate[:, None]
    d_router = t_dot(routed, d_logits.astype(BF16))
    d_routed = d_routed + dot_t(d_logits.astype(BF16), w_router)
    d_norm_two, d_gain_two = norm_back(residual, inverse_two, gain_b, d_routed)
    d_residual = upstream + d_norm_two
    low_residual = d_residual.astype(BF16)
    d_attended = dot_t(low_residual, w_output).astype(BF16)
    d_output = t_dot(attended, low_residual)

    grad = all_to_all(
        jnp.swapaxes(d_attended.reshape(tok_rows, quad, part), 0, 1), "dp", quads
    ).reshape(q_rows, heads, head_width)
    grad = jnp.swapaxes(grad, 0, 1)
    d_query_rows, d_key_rows, d_value_rows, d_window = attend_back(
        length_arg, window, query, key, value, grad, log_norm
    )
    if q_parts > 1:
        strided = [
            [i * span + j + quad * n for n in range(q_parts)]
            for i in range(dp_count // span)
            for j in range(quad)
        ]
        d_key_rows, d_value_rows = [
            lax.psum_scatter(
                rows, "dp", scatter_dimension=1, axis_index_groups=strided, tiled=True
            )
            for rows in (d_key_rows, d_value_rows)
        ]
    d_rows = jnp.stack([d_query_rows, d_key_rows.astype(BF16), d_value_rows.astype(BF16)])
    d_parts = jnp.einsum("sd,khsc->dkhc", normed_q, d_rows, preferred_element_type=F32)
    d_table = jnp.einsum("amb,ham->bh", window_hot.astype(F32), d_window, precision="highest")
    d_mine = all_to_all(
        jnp.transpose(
            d_rows.reshape(3, heads, quad, tok_rows, head_width), (2, 3, 0, 1, 4)
        ).reshape(quad, tok_rows, 3 * part),
        "dp",
        quads,
    ).reshape(quad, tok_rows, 3, part)
    d_mine = jnp.transpose(d_mine, (2, 1, 0, 3)).reshape(3, tok_rows, width)
    d_normed = dot_t(d_mine[0], w_query) + dot_t(d_mine[1], w_key) + dot_t(d_mine[2], w_value)
    inverse_one = normalize(token_f, gain_a)[1]
    d_norm_one, d_gain_one = norm_back(token_f, inverse_one, gain_a, d_normed)
    d_tokens = d_residual + d_norm_one

    piece = hidden // dp_count
    my_in = lax.dynamic_slice_in_dim(w_in, dp_index * piece, piece, 2)
    my_out = lax.dynamic_slice_in_dim(w_out, dp_index * piece, piece, 1)
    d_in_piece, d_out = weight_grads(group_rows, my_in, my_out)
    d_in = all_to_all(
        jnp.swapaxes(d_in_piece.reshape(local, dp_count, width // dp_count, piece), 0, 1), "dp"
    )
    d_in = (
        jnp.transpose(d_in, (1, 2, 0, 3)).reshape(local, width // dp_count, hidden).astype(F32)
    )

    def spread(array, axis):
        wide = jnp.zeros(array.shape[:axis] + (array.shape[axis] * quad,) + array.shape[axis + 1 :], F32)
        return lax.dynamic_update_slice_in_dim(wide, array, mine * array.shape[axis], axis)

    d_parts = d_parts.reshape(width, 3, part)
    big = jnp.stack([spread(d_parts[:, n], 1) for n in range(3)] + [d_output])
    summed = lax.psum(big.astype(BF16), ("dp", "expert")).astype(F32)
    small = lax.psum(
        (d_gain_one, spread(d_table, 1), d_gain_two, d_router), ("dp", "expert")
    )
    return (
        output, d_tokens, small[0], summed[0], summed[1], summed[2], summed[3],
        small[1], small[2], small[3], d_in, d_out,
    )


def per_device_quad(
    tokens, lengths, expert_ids, gain_one, w_query, w_key, w_value, w_output,
    bias_table, gain_two, w_router, w_in, w_out, cotangent,
):
    tok_rows, width = tokens.shape
    buckets, head_count = bias_table.shape
    expert_count = w_router.shape[1]
    quad = lax.axis_size("dp") // 2
    counts = 2 * quad - 1
    offset = jnp.arange(2 * tok_rows, dtype=jnp.int32)
    offset = jnp.where(offset < tok_rows, offset, offset - 2 * tok_rows)
    codes = (
        jnp.arange(counts, dtype=jnp.int32)[:, None] * tok_rows
        - offset[None, :]
        - (quad - 1) * tok_rows
    )
    hot = (
        bucket_of(codes)[:, None, :] == jnp.arange(buckets, dtype=jnp.int32)[None, :, None]
    ).astype(BF16)
    table = jnp.pad(bias_table.T, ((0, 16 - head_count), (0, 0)))
    output, d_tokens, d_weights, total, d_out_parts, d_in_parts = layer(
        lengths, tokens, expert_ids, cotangent, gain_one[None], gain_two[None], w_query, w_key, w_value,
        w_output, w_router, table, hot, w_in, w_out, head_count,
    )
    d_query, d_key, d_value, d_output, d_in, d_out = finish(d_weights, d_in_parts, d_out_parts)
    return (
        output, d_tokens, total[0], d_query, d_key, d_value, d_output,
        total[12:, :buckets].T, total[1], total[2 : 2 + expert_count].T, d_in, d_out,
    )


def solution(mesh):
    rows = P(("expert", "dp"), None)
    owned = P("expert", None, None)
    return jax.shard_map(
        per_device_quad if dict(mesh.shape) == {"dp": 8, "expert": 4} else per_device,
        mesh=mesh,
        in_specs=(
            rows, P(), rows, P(), P(), P(), P(), P(), P(), P(), P(), owned, owned, rows,
        ),
        out_specs=(
            rows, rows, P(), P(), P(), P(), P(), P(), P(), P(),
            P("expert", "dp", None), P("expert", "dp", None),
        ),
        check_vma=False,
    )
```

```python
import functools
import math

import jax
import jax.numpy as jnp
from jax import lax
from jax.experimental import pallas as pl
from jax.experimental.pallas import tpu as pltpu
from jax.sharding import PartitionSpec as P

BUCKETS = 32
EXACT = 8
MASKED = -1000000000.0
F32 = jnp.float32
BF16 = jnp.bfloat16
VMEM_BYTES = 56 * 1024 * 1024


def bucket_of(relative):
    distance = jnp.abs(relative)
    beyond = jnp.full(relative.shape, EXACT, jnp.int32)
    for level_step in range(1, BUCKETS // 2 - EXACT):
        boundary = math.isqrt(EXACT * EXACT * (1 << level_step) - 1) + 1
        beyond = beyond + (distance >= boundary).astype(jnp.int32)
    nearby = jnp.where(distance < EXACT, distance, beyond)
    return nearby + jnp.where(relative > 0, BUCKETS // 2, 0).astype(jnp.int32)


def normalize(values, gain):
    inverse = lax.rsqrt(jnp.mean(values * values, axis=-1, keepdims=True) + 1e-06)
    return (values * inverse * gain, inverse)


def norm_back(values, inverse, gain, upstream):
    scaled_up = upstream * gain
    d_gain = jnp.sum(upstream * values * inverse, axis=0)
    cubed = inverse * inverse * inverse
    d_values = inverse * scaled_up - values * cubed * jnp.mean(
        values * scaled_up, axis=-1, keepdims=True
    )
    return (d_values, d_gain)


def dot(left_side, right_side):
    return jnp.dot(left_side, right_side, preferred_element_type=F32)


def dot_t(left_side, right_side):
    return lax.dot_general(
        left_side, right_side, (((1,), (1,)), ((), ())), preferred_element_type=F32
    )


def t_dot(left_side, right_side):
    return lax.dot_general(
        left_side, right_side, (((0,), (0,)), ((), ())), preferred_element_type=F32
    )


def gelu_parts(value):
    scale = math.sqrt(2.0 / math.pi)
    square = value * value
    tanh = jnp.tanh(scale * (value + 0.044715 * value * square))
    half = 0.5 * (1.0 + tanh)
    slope = half + 0.5 * value * (1.0 - tanh * tanh) * scale * (1.0 + 3 * 0.044715 * square)
    return (value * half, slope)


def build_bias(win_ref, bias_ref):
    count, block, _ = bias_ref.shape

    @pl.loop(0, count)
    def _(index):
        row = win_ref[0, pl.ds(index, 1), :]
        wide = jnp.broadcast_to(row, (block, 2 * block))
        bias_ref[index] = pltpu.roll(wide, 0, 1, stride=1, stride_axis=0)[:, :block]


def attend_kernel(length_ref, win_ref, q_ref, k_ref, v_ref, o_ref, lse_ref, bias_ref):
    block = bias_ref.shape[1]
    q_blocks = q_ref.shape[1] // block
    k_blocks = k_ref.shape[1] // block
    build_bias(win_ref, bias_ref)
    length = length_ref[0]

    @pl.loop(0, q_blocks)
    def _(i):
        rows = pl.ds(pl.multiple_of(i * block, block), block)
        query = q_ref[0, rows, :]
        scores = []
        for j in range(k_blocks):
            part = dot_t(k_ref[0, j * block : (j + 1) * block, :], query)
            part = part + bias_ref[j - i + q_blocks - 1]
            position = lax.broadcasted_iota(jnp.int32, (block, 1), 0) + j * block
            scores.append(jnp.where(position < length, part, MASKED))
        top = functools.reduce(jnp.maximum, [jnp.max(s, axis=0, keepdims=True) for s in scores])
        total = jnp.zeros((1, block), F32)
        out = jnp.zeros((v_ref.shape[2], block), F32)
        for j in range(k_blocks):
            scaled = jnp.exp(scores[j] - top)
            total = total + jnp.sum(scaled, axis=0, keepdims=True)
            out = out + t_dot(v_ref[0, j * block : (j + 1) * block, :], scaled.astype(BF16))
        out = out * (1.0 / total)
        o_ref[0, rows, :] = out.T.astype(BF16)
        lse_ref[0, pl.ds(i, 1), :] = top + jnp.log(total)


def attend_back_kernel(
    length_ref, win_ref, q_ref, k_ref, v_ref, g_ref, lse_ref,
    dq_ref, dk_ref, dv_ref, dwin_ref, bias_ref, dbias_ref,
):
    block = bias_ref.shape[1]
    q_blocks = q_ref.shape[1] // block
    k_blocks = k_ref.shape[1] // block
    build_bias(win_ref, bias_ref)
    length = length_ref[0]
    dk_ref[...] = jnp.zeros_like(dk_ref)
    dv_ref[...] = jnp.zeros_like(dv_ref)
    dbias_ref[...] = jnp.zeros_like(dbias_ref)

    @pl.loop(0, q_blocks)
    def _(i):
        rows = pl.ds(pl.multiple_of(i * block, block), block)
        query = q_ref[0, rows, :]
        grad = g_ref[0, rows, :]
        log_norm = lse_ref[0, pl.ds(i, 1), :]
        probs, d_probs = [], []
        spread = jnp.zeros((1, block), F32)
        for j in range(k_blocks):
            keys = slice(j * block, (j + 1) * block)
            part = dot_t(k_ref[0, keys, :], query)
            part = part + bias_ref[j - i + q_blocks - 1]
            position = lax.broadcasted_iota(jnp.int32, (block, 1), 0) + j * block
            part = jnp.where(position < length, part, MASKED)
            prob = jnp.exp(part - log_norm)
            d_prob = dot_t(v_ref[0, keys, :], grad)
            spread = spread + jnp.sum(prob * d_prob, axis=0, keepdims=True)
            dv_ref[0, keys, :] += dot(prob.astype(BF16), grad)
            probs.append(prob)
            d_probs.append(d_prob)
        d_query = jnp.zeros((q_ref.shape[2], block), F32)
        for j in range(k_blocks):
            keys = slice(j * block, (j + 1) * block)
            d_score = probs[j] * (d_probs[j] - spread)
            dbias_ref[j - i + q_blocks - 1] += d_score
            low = d_score.astype(BF16)
            dk_ref[0, keys, :] += dot(low, query)
            d_query = d_query + t_dot(k_ref[0, keys, :], low)
        dq_ref[0, rows, :] = d_query.T.astype(BF16)

    @pl.loop(0, dbias_ref.shape[0])
    def _(index):
        wide = jnp.concatenate([dbias_ref[index], jnp.zeros((block, block), F32)], axis=1)
        half = block // 2
        while half:
            wide = wide[:half] + pltpu.roll(wide[half:], 2 * block - half, 1)
            half //= 2
        dwin_ref[0, pl.ds(index, 1), :] = wide


def head_block(rows, width):
    return pl.BlockSpec((1, rows, width), lambda h: (h, 0, 0))


def attend(length, window, query, key, value):
    heads, q_rows, width = query.shape
    k_rows = key.shape[1]
    count, block = window.shape[1], window.shape[2] // 2
    return pl.pallas_call(
        attend_kernel,
        grid=(heads,),
        in_specs=[
            pl.BlockSpec(memory_space=pltpu.SMEM),
            head_block(count, 2 * block),
            head_block(q_rows, width),
            head_block(k_rows, width),
            head_block(k_rows, width),
        ],
        out_specs=[head_block(q_rows, width), head_block(q_rows // block, block)],
        out_shape=[
            jax.ShapeDtypeStruct((heads, q_rows, width), BF16),
            jax.ShapeDtypeStruct((heads, q_rows // block, block), F32),
        ],
        scratch_shapes=[pltpu.VMEM((count, block, block), F32)],
        compiler_params=pltpu.CompilerParams(vmem_limit_bytes=VMEM_BYTES),
        name="attend",
    )(length, window, query, key, value)


def attend_back(length, window, query, key, value, grad, log_norm):
    heads, q_rows, width = query.shape
    k_rows = key.shape[1]
    count, block = window.shape[1], window.shape[2] // 2
    return pl.pallas_call(
        attend_back_kernel,
        grid=(heads,),
        in_specs=[
            pl.BlockSpec(memory_space=pltpu.SMEM),
            head_block(count, 2 * block),
            head_block(q_rows, width),
            head_block(k_rows, width),
            head_block(k_rows, width),
            head_block(q_rows, width),
            head_block(q_rows // block, block),
        ],
        out_specs=[
            head_block(q_rows, width),
            head_block(k_rows, width),
            head_block(k_rows, width),
            head_block(count, 2 * block),
        ],
        out_shape=[
            jax.ShapeDtypeStruct((heads, q_rows, width), BF16),
            jax.ShapeDtypeStruct((heads, k_rows, width), F32),
            jax.ShapeDtypeStruct((heads, k_rows, width), F32),
            jax.ShapeDtypeStruct((heads, count, 2 * block), F32),
        ],
        scratch_shapes=[pltpu.VMEM((count, block, block), F32) for _ in range(2)],
        compiler_params=pltpu.CompilerParams(vmem_limit_bytes=VMEM_BYTES),
        name="attend_back",
    )(length, window, query, key, value, grad, log_norm)


def experts_kernel(rows_ref, w_in_ref, w_out_ref, out_ref, acc_ref, back_ref):
    width = w_in_ref.shape[1]
    step = pl.program_id(1)

    @pl.when(step == 0)
    def _():
        acc_ref[...] = jnp.zeros_like(acc_ref)
        back_ref[...] = jnp.zeros_like(back_ref)

    inner = dot(rows_ref[0, :, :width], w_in_ref[0])
    active, slope = gelu_parts(inner)
    acc_ref[...] += dot(active.astype(BF16), w_out_ref[0])
    d_active = dot_t(rows_ref[0, :, width:], w_out_ref[0])
    d_inner = (d_active * slope).astype(BF16)
    back_ref[...] += dot_t(d_inner, w_in_ref[0])

    @pl.when(step == pl.num_programs(1) - 1)
    def _():
        out_ref[0, :, :width] = acc_ref[...].astype(BF16)
        out_ref[0, :, width:] = back_ref[...].astype(BF16)


def experts(rows, w_in, w_out):
    local, count, double = rows.shape
    width, hidden = w_in.shape[1:]
    piece = 512
    return pl.pallas_call(
        experts_kernel,
        grid=(local, hidden // piece),
        in_specs=[
            pl.BlockSpec((1, count, double), lambda e, f: (e, 0, 0)),
            pl.BlockSpec((1, width, piece), lambda e, f: (e, 0, f)),
            pl.BlockSpec((1, piece, width), lambda e, f: (e, f, 0)),
        ],
        out_specs=pl.BlockSpec((1, count, double), lambda e, f: (e, 0, 0)),
        out_shape=jax.ShapeDtypeStruct((local, count, double), BF16),
        scratch_shapes=[pltpu.VMEM((count, width), F32) for _ in range(2)],
        compiler_params=pltpu.CompilerParams(vmem_limit_bytes=VMEM_BYTES),
        name="experts",
    )(rows, w_in, w_out)


def weight_grads_kernel(rows_ref, w_in_ref, w_out_ref, d_in_ref, d_out_ref, acc_ref):
    width = w_in_ref.shape[1]
    step = pl.program_id(1)
    rows = rows_ref[...].reshape(rows_ref.shape[0] * rows_ref.shape[2], 2 * width)

    @pl.when(step == 0)
    def _():
        acc_ref[...] = jnp.zeros_like(acc_ref)
        d_out_ref[...] = jnp.zeros_like(d_out_ref)

    inner = dot(rows[:, :width], w_in_ref[0])
    active, slope = gelu_parts(inner)
    d_active = dot_t(rows[:, width:], w_out_ref[0])
    d_inner = (d_active * slope).astype(BF16)
    d_out_ref[0] += t_dot(active.astype(BF16), rows[:, width:])
    acc_ref[...] += t_dot(rows[:, :width], d_inner)

    @pl.when(step == pl.num_programs(1) - 1)
    def _():
        d_in_ref[0] = acc_ref[...].astype(BF16)


def weight_grads(rows, w_in, w_out):
    groups, local, count, double = rows.shape
    width, piece = w_in.shape[1:]
    together = 4
    return pl.pallas_call(
        weight_grads_kernel,
        grid=(local, groups // together),
        in_specs=[
            pl.BlockSpec((together, 1, count, double), lambda e, g: (g, e, 0, 0)),
            pl.BlockSpec((1, width, piece), lambda e, g: (e, 0, 0)),
            pl.BlockSpec((1, piece, width), lambda e, g: (e, 0, 0)),
        ],
        out_specs=[
            pl.BlockSpec((1, width, piece), lambda e, g: (e, 0, 0)),
            pl.BlockSpec((1, piece, width), lambda e, g: (e, 0, 0)),
        ],
        out_shape=[
            jax.ShapeDtypeStruct((local, width, piece), BF16),
            jax.ShapeDtypeStruct((local, piece, width), F32),
        ],
        scratch_shapes=[pltpu.VMEM((width, piece), F32)],
        compiler_params=pltpu.CompilerParams(vmem_limit_bytes=VMEM_BYTES),
        name="weight_grads",
    )(rows, w_in, w_out)


class Place:
    def __init__(self):
        self.dp, self.ex = lax.axis_index("dp"), lax.axis_index("expert")
        self.y = lax.rem(self.dp, 2)
        self.z = lax.div(self.dp, 2)
        self.z_lo = lax.rem(self.z, 2)
        self.z_hi = lax.div(self.dp, 4)
        self.core = lax.rem(self.ex, 2)
        self.x = lax.div(self.ex, 2)
        self.member = self.z_lo * 2 + self.y

    def flip(self, *names):
        c = {n: getattr(self, n) for n in ("y", "z_lo", "z_hi", "core", "x")}
        for name in names:
            c[name] = 1 - c[name]
        return (c["z_hi"] * 4 + c["z_lo"] * 2 + c["y"], c["x"] * 2 + c["core"])

    def quad_others(self):
        found = []
        for names in (("y",), ("z_lo",), ("y", "z_lo")):
            device = self.flip(*names)
            found.append((device, lax.rem(device[0], 4)))
        return found

    def expert_others(self):
        return [self.flip(*names) for names in (("core",), ("x",), ("core", "x"))]

    def dp_others(self):
        names = (("y",), ("z_lo",), ("y", "z_lo"), ("z_hi",), ("z_hi", "y"), ("z_hi", "z_lo"), ("z_hi", "y", "z_lo"))
        return [self.flip(*n) for n in names]


def remote(src, dst, sems, index, device):
    return pltpu.make_async_remote_copy(
        src_ref=src, dst_ref=dst, send_sem=sems.at[(0,) + index], recv_sem=sems.at[(1,) + index],
        device_id=device, device_id_type=pl.DeviceIdType.MESH,
    )


def send(src, dst, sems, index, device):
    copy = remote(src, dst, sems, index, device)
    copy.start()
    return copy


def greet(devices):
    barrier = pltpu.get_barrier_semaphore()
    for device in devices:
        pl.semaphore_signal(barrier, inc=1, device_id=device, device_id_type=pl.DeviceIdType.MESH)
    pl.semaphore_wait(barrier, len(devices))


class Relay:
    def __init__(self, place, ref, sems):
        self.ref, self.sems = ref, sems
        self.dp, self.ex, self.z = place.dp, place.ex, place.z

    def along(self, direction, step, offset):
        neighbour = (self.dp + 2, self.ex) if direction else (self.dp - 2, self.ex)
        block = self.ref.at[self.z + offset]
        return remote(block, block, self.sems, (direction, step), neighbour)

    def begin(self):
        @pl.when(self.z < 3)
        def _():
            self.along(1, 0, 0).start()

        @pl.when(self.z > 0)
        def _():
            self.along(0, 0, 0).start()

    def step(self, k):
        @pl.when(self.z >= k)
        def _():
            self.along(1, k - 1, -k).wait_recv()
            if k < 3:

                @pl.when(self.z < 3)
                def _():
                    self.along(1, k, -k).start()

        @pl.when(self.z + k <= 3)
        def _():
            self.along(0, k - 1, k).wait_recv()
            if k < 3:

                @pl.when(self.z > 0)
                def _():
                    self.along(0, k, k).start()

    def end(self):
        for k in (0, 1, 2):

            @pl.when((self.z >= k) & (self.z < 3))
            def _():
                self.along(1, k, -k).wait_send()

            @pl.when((self.z + k <= 3) & (self.z > 0))
            def _():
                self.along(0, k, k).wait_send()


def with_mask(key, length):
    rows, width = key.shape
    lane = lax.broadcasted_iota(jnp.int32, (rows, width), 1)
    row = lax.broadcasted_iota(jnp.int32, (rows, width), 0)
    return jnp.concatenate(
        [key, jnp.where((lane == 0) & (row >= length), MASKED, 0.0).astype(BF16)], axis=1
    )


def with_one(query):
    lane = lax.broadcasted_iota(jnp.int32, query.shape, 1)
    return jnp.concatenate([query, (lane == 0).astype(BF16)], axis=1)


class QuadGather:
    def __init__(self, place, ref, sems, rows):
        self.ref, self.sems, self.rows = ref, sems, rows
        (self.y_device, self.y_member), (self.z_device, self.z_member), _ = place.quad_others()
        self.mine = place.member

    def part(self, member, start, size):
        return self.ref.at[pl.ds(pl.multiple_of(member * self.rows + start, size), size)]

    def begin(self):
        own = self.part(self.mine, 0, self.rows)
        self.first = [
            send(own, own, self.sems, (0,), self.y_device), send(own, own, self.sems, (1,), self.z_device),
        ]

    def forward(self):
        half = self.rows // 2
        self.first[0].wait_recv()
        upper = self.part(self.y_member, 0, half)
        self.second = [send(upper, upper, self.sems, (2,), self.z_device)]
        self.first[1].wait_recv()
        lower = self.part(self.z_member, half, half)
        self.second.append(send(lower, lower, self.sems, (3,), self.y_device))

    def end(self):
        for copy in self.second:
            copy.wait()
        for copy in self.first:
            copy.wait_send()


def exact_dot(left_side, right_side, left_dim, right_dim):
    return lax.dot_general(
        left_side, right_side, (((left_dim,), (right_dim,)), ((), ())),
        precision=lax.Precision.HIGHEST, preferred_element_type=F32,
    )


def layer_kernel(
    lengths_ref, token_ref, ids_ref, cotangent_ref, gains_ref, w_query_ref, w_key_ref,
    w_value_ref, w_output_ref, w_router_ref, table_ref, hot_ref, w_in_ref, w_out_ref,
    output_ref, d_tokens_ref, d_weights_ref, total_ref, d_out_ref, d_in_ref,
    w_mine_ref, normed_ref, qkv_ref, win_ref, lse_ref, attended_ref, attended_recv,
    count_send, count_ref, slot_send, up_arrive, rows_arrive, gate_send, gate_arrive, place_ref, pack_ref,
    up_ref, rows_ref, in_buf, out_buf, result_ref, back_send, back_ref, residual_ref,
    grad_ref, grad_send, low_ref, bias_ref, dbias_ref, dkey_ref, dvalue_ref, dqkv_ref,
    dmine_ref, load_ref, first_ref, second_ref, third_ref, sum_one_ref, sum_two_ref,
    small_send, small_recv, active_ref, inner_ref, half_send, half_recv, d_out_send, d_out_recv,
    token_sems, count_sems, up_sems, attended_sems, go_sems, gate_sems, weight_sems,
    up_line_sems, line_sems, back_sems,
    grad_sems, low_sems, mine_sems, first_sems, second_sems, third_sems, ring_sems, core_sems,
    small_sems, d_in_sems, half_sems, block_sems,
):
    place = Place()
    mine, ex, dp, z = place.member, place.ex, place.dp, place.z
    block = bias_ref.shape[1]
    part = qkv_ref.shape[1] // 3
    head_width = dkey_ref.shape[1]
    heads = part // head_width
    blocks = quad = qkv_ref.shape[0] // block
    width = normed_ref.shape[0]
    sources, local, slots = rows_arrive.shape[:3]
    groups, _, capacity = up_ref.shape[:3]
    experts_count = local * sources
    length = lengths_ref[ex * 2 + place.z_hi]
    piece = in_buf.shape[2]
    pieces = w_in_ref.shape[2] // piece
    depth = in_buf.shape[0]
    hidden = active_ref.shape[2]
    my_hidden = pl.ds(pl.multiple_of(z * hidden, hidden), hidden)
    diagonal = lax.broadcasted_iota(jnp.int32, (capacity, capacity), 0) == lax.broadcasted_iota(
        jnp.int32, (capacity, capacity), 1
    )

    def my_rows(index):
        return pl.ds(pl.multiple_of(index * block, block), block)

    def fill_bias(h):
        @pl.loop(0, bias_ref.shape[0])
        def _(index):
            wide = jnp.broadcast_to(win_ref[index, pl.ds(mine * heads + h, 1), :], (block, 2 * block))
            bias_ref[index] = pltpu.roll(wide, 0, 1, stride=1, stride_axis=0)[:, :block]

    quad_others = place.quad_others()
    expert_others = place.expert_others()
    dp_others = place.dp_others()
    up_relay = Relay(place, up_ref, up_line_sems)
    rows_relay = Relay(place, rows_ref, line_sems)

    def weight_copies(n):
        e, f, slot = n // pieces, n % pieces, n % depth
        return (
            pltpu.make_async_copy(
                w_in_ref.at[e, :, f * piece : (f + 1) * piece], in_buf.at[slot], weight_sems.at[0, slot]
            ),
            pltpu.make_async_copy(
                w_out_ref.at[e, f * piece : (f + 1) * piece, :], out_buf.at[slot], weight_sems.at[1, slot]
            ),
        )

    def block_copies(e):
        return (
            pltpu.make_async_copy(w_in_ref.at[e, :, my_hidden], in_buf.at[e], block_sems.at[0, e]),
            pltpu.make_async_copy(w_out_ref.at[e, my_hidden, :], out_buf.at[e], block_sems.at[1, e]),
        )

    for n in range(depth):
        for copy in weight_copies(n):
            copy.start()

    greet(dp_others + expert_others)

    low_ref[my_rows(mine), :] = token_ref[...]
    token_gather = QuadGather(place, low_ref, token_sems, block)
    token_gather.begin()

    square = (block, block)
    ids = jnp.sum(
        jnp.where(
            lax.broadcasted_iota(jnp.int32, square, 0) == lax.broadcasted_iota(jnp.int32, square, 1),
            ids_ref[...].astype(F32), 0.0,
        ),
        axis=1, keepdims=True,
    ).astype(jnp.int32)
    position = lax.broadcasted_iota(jnp.int32, (block, 1), 0)
    valid = (position + mine * block < length).astype(F32)
    chosen = (lax.broadcasted_iota(jnp.int32, (block, experts_count), 1) == ids).astype(F32)
    hits = chosen * valid
    below = (
        lax.broadcasted_iota(jnp.int32, (block, block), 1) < lax.broadcasted_iota(jnp.int32, (block, block), 0)
    ).astype(BF16)
    rank = jnp.sum(dot(below, hits.astype(BF16)) * hits, axis=1, keepdims=True)
    count_send[...] = jnp.zeros_like(count_send)
    count_send[0:1, :experts_count] = jnp.sum(hits, axis=0, keepdims=True)
    counts_going = [
        send(count_send, count_ref.at[ex], count_sems, (n,), device) for n, device in enumerate(expert_others)
    ]
    count_ref[ex] = count_send[...]
    target = jnp.where(valid > 0, ids.astype(F32) * slots + rank, -1.0).astype(jnp.int32)
    place_ref[...] = (
        lax.broadcasted_iota(jnp.int32, place_ref.shape, 1) == target
    ).astype(BF16)

    slot_send[...] = t_dot(place_ref[...], cotangent_ref[...]).astype(BF16).reshape(slot_send.shape)

    def scatter(arrive, sems):
        going = [
            send(slot_send.at[pl.ds(device[1] * local, local)], arrive.at[ex], sems, (n,), device)
            for n, device in enumerate(expert_others)
        ]
        arrive[ex] = slot_send[pl.ds(ex * local, local)]
        return going

    ups_going = scatter(up_arrive, up_sems)

    for m in range(quad):

        @pl.when(mine == m)
        def _():
            for kind, weight_ref in enumerate((w_query_ref, w_key_ref, w_value_ref)):
                w_mine_ref[:, kind * part : (kind + 1) * part] = weight_ref[:, m * part : (m + 1) * part]

    for a in range(win_ref.shape[0]):
        win_ref[a, : table_ref.shape[0], :] = dot(table_ref[...], hot_ref[a])
    fill_bias(0)

    for copy in counts_going:
        copy.wait()
    before = jnp.zeros((1, experts_count), F32)
    for s in range(sources):
        before = before + count_ref[s, 0:1, :experts_count] * (s < ex).astype(F32)
    kept = valid * (rank + jnp.sum(hits * before, axis=1, keepdims=True) < capacity).astype(F32)
    lane = lax.broadcasted_iota(jnp.int32, (1, sources * slots), 1)
    expert_lane = lax.broadcasted_iota(jnp.int32, (1, count_ref.shape[2]), 1)
    for e in range(local):
        at = jnp.full((1, sources * slots), -1, jnp.int32)
        start = jnp.zeros((1, 1), F32)
        for s in range(sources):
            count = jnp.sum(
                jnp.where(expert_lane == ex * local + e, count_ref[s, 0:1, :], 0.0), axis=1, keepdims=True
            )
            turn = lane - s * slots
            here = (turn >= 0) & (turn < slots) & (turn < count.astype(jnp.int32))
            at = jnp.where(here, start.astype(jnp.int32) + turn, at)
            start = start + count
        pack_ref[e] = (lax.broadcasted_iota(jnp.int32, (capacity, sources * slots), 0) == at).astype(BF16)

    gain = gains_ref[0:1, :].astype(F32)

    def project(i):
        token = low_ref[my_rows(i), :].astype(F32)
        inverse = lax.rsqrt(jnp.mean(token * token, axis=-1, keepdims=True) + 1e-06)
        normed = token * inverse * gain
        normed_ref[:, my_rows(i)] = normed.T.astype(BF16)
        qkv_ref[my_rows(i), :] = dot(normed.astype(BF16), w_mine_ref[...]).astype(BF16)

    project(mine)
    token_gather.forward()
    project(quad_others[0][1])
    project(quad_others[1][1])
    token_gather.end()
    project(quad_others[2][1])

    for copy in ups_going:
        copy.wait()
    for e in range(local):
        up_ref[z, e] = dot(pack_ref[e], up_arrive[:, e].reshape(sources * slots, width)).astype(BF16)
    up_relay.begin()

    for h in range(heads):
        if h:
            fill_bias(h)
        cols = slice(h * head_width, (h + 1) * head_width)
        key = with_mask(qkv_ref[:, part + h * head_width : part + (h + 1) * head_width], length)
        value = qkv_ref[:, 2 * part + h * head_width : 2 * part + (h + 1) * head_width]

        @pl.loop(0, blocks)
        def _(i):
            rows = my_rows(i)
            query = with_one(qkv_ref[rows, cols])
            scores = []
            for j in range(blocks):
                score = dot_t(key[j * block : (j + 1) * block], query)
                scores.append(score + bias_ref[j - i + blocks - 1])
            top = functools.reduce(
                jnp.maximum, [jnp.max(s, axis=0, keepdims=True) for s in scores]
            )
            total = jnp.zeros((1, block), F32)
            out = jnp.zeros((head_width, block), F32)
            for j in range(blocks):
                scaled = jnp.exp(scores[j] - top)
                total = total + jnp.sum(scaled, axis=0, keepdims=True)
                out = out + t_dot(value[j * block : (j + 1) * block], scaled.astype(BF16))
            out = out * (1.0 / total)
            attended_ref[rows, cols] = out.T.astype(BF16)
            lse_ref[h, pl.ds(i, 1), :] = top + jnp.log(total)

        if h == 1:
            up_relay.step(1)

    attended_going = [
        send(attended_ref.at[my_rows(member)], attended_recv.at[mine], attended_sems, (n,), device)
        for n, (device, member) in enumerate(quad_others)
    ]
    attended_recv[mine] = attended_ref[my_rows(mine), :]
    for copy in attended_going:
        copy.wait()
    attended = jnp.concatenate([attended_recv[m] for m in range(quad)], axis=1)
    residual = token_ref[...].astype(F32) + dot(attended, w_output_ref[...])
    residual_ref[...] = residual
    inverse = lax.rsqrt(jnp.mean(residual * residual, axis=-1, keepdims=True) + 1e-06)
    gain_two = gains_ref[1:2, :].astype(F32)
    routed = (residual * inverse * gain_two).astype(BF16)

    slot_send[...] = t_dot(place_ref[...], routed).astype(BF16).reshape(slot_send.shape)
    rows_going = scatter(rows_arrive, go_sems)
    logits = dot_t(routed, w_router_ref[...])
    router = jnp.exp(logits - jnp.max(logits, axis=1, keepdims=True))
    router = router / jnp.sum(router, axis=1, keepdims=True)
    chosen_prob = jnp.sum(router * chosen, axis=1, keepdims=True)
    gate = chosen_prob * kept
    slopes = router * (chosen - chosen_prob)
    gate_slots = exact_dot(jnp.broadcast_to(gate, (block, 8)), place_ref[...].astype(F32), 0, 0)
    gate_send[...] = jnp.zeros_like(gate_send)
    for e in range(experts_count):
        gate_send[e, :, :slots] = gate_slots[:, e * slots : (e + 1) * slots]
    gates_going = [
        send(gate_send.at[pl.ds(device[1] * local, local)], gate_arrive.at[ex], gate_sems, (n,), device)
        for n, device in enumerate(expert_others)
    ]
    gate_arrive[ex] = gate_send[pl.ds(ex * local, local)]
    up_relay.step(2)
    for copy in rows_going:
        copy.wait()
    for e in range(local):
        rows_ref[z, e * capacity : (e + 1) * capacity, :] = dot(
            pack_ref[e], rows_arrive[:, e].reshape(sources * slots, width)
        ).astype(BF16)
    for copy in gates_going:
        copy.wait()
    rows_ref[z, local * capacity :, :] = jnp.zeros((rows_ref.shape[1] - local * capacity, width), BF16)
    gate_lines = jnp.zeros((rows_ref.shape[1] - local * capacity, capacity), F32)
    line = lax.broadcasted_iota(jnp.int32, gate_lines.shape, 0)
    gate_columns = []
    for e in range(local):
        arrived = jnp.concatenate([gate_arrive[s, e, :, :slots] for s in range(sources)], axis=1)
        pack = pack_ref[e].astype(F32)
        gate_columns.append(exact_dot(pack, arrived, 1, 1)[:, 0:1])
        rest = exact_dot(arrived, pack, 1, 1)[0:1]
        for n in range(3):
            high = rest.astype(BF16).astype(F32)
            gate_lines = jnp.where(line == 3 * e + n, high, gate_lines)
            rest = rest - high
    rows_ref[z, local * capacity :, :capacity] = gate_lines.astype(BF16)
    rows_relay.begin()

    backs = []
    for e in range(local):
        rows = rows_ref[z, e * capacity : (e + 1) * capacity, :]
        d_rows = (gate_columns[e] * up_ref[z, e].astype(F32)).astype(BF16)
        for f in range(pieces):
            n = e * pieces + f
            for copy in weight_copies(n):
                copy.wait()
            weight_in = in_buf[n % depth]
            weight_out = out_buf[n % depth]
            active, slope = gelu_parts(dot(rows, weight_in))
            forward = dot(active.astype(BF16), weight_out)
            d_inner = (dot_t(d_rows, weight_out) * slope).astype(BF16)
            backward = dot_t(d_inner, weight_in)
            if f == 0:
                result_ref[:, :width] = forward
                result_ref[:, width:] = backward
            else:
                result_ref[:, :width] += forward
                result_ref[:, width:] += backward
            if n + depth < local * pieces:
                for copy in weight_copies(n + depth):
                    copy.start()
        spread_rows = t_dot(pack_ref[e], result_ref[...].astype(BF16)).astype(BF16)
        back_send[:, e] = spread_rows.reshape(sources, slots, 2 * width)
        for n, device in enumerate(expert_others):
            backs.append(
                send(back_send.at[device[1], e], back_ref.at[ex * local + e], back_sems, (e, n), device)
            )
        back_ref[ex * local + e] = back_send[ex, e]
        if e == 0:
            up_relay.step(3)
        else:
            rows_relay.step(1)
    for e in range(local):
        for copy in block_copies(e):
            copy.start()
    fill_bias(0)
    for copy in backs:
        copy.wait()

    gathered = dot(place_ref[...], back_ref[...].reshape(experts_count * slots, 2 * width))
    expert_out = gathered[:, :width]
    residual = residual_ref[...]
    output_ref[...] = (valid * (residual + gate * expert_out)).astype(BF16)
    upstream = cotangent_ref[...].astype(F32) * valid
    d_gate = jnp.sum(upstream * expert_out, axis=1, keepdims=True) * kept
    d_logits = (slopes * d_gate).astype(BF16)
    small_send[0] = jnp.zeros(small_send.shape[1:], F32)
    inverse = lax.rsqrt(jnp.mean(residual * residual, axis=-1, keepdims=True) + 1e-06)
    routed = (residual * inverse * gain_two).astype(BF16)
    small_send[0, 2:10, :] = t_dot(d_logits, routed)
    d_routed = gathered[:, width:] + dot(d_logits, w_router_ref[...])
    small_send[0, 1:2, :] = jnp.sum(d_routed * residual * inverse, axis=0, keepdims=True)
    scaled = d_routed * gain_two
    cubed = inverse * inverse * inverse
    d_residual = upstream + inverse * scaled - residual * cubed * jnp.mean(
        residual * scaled, axis=-1, keepdims=True
    )
    residual_ref[...] = d_residual

    low = d_residual.astype(BF16)
    low_ref[my_rows(mine), :] = low
    d_attended = dot_t(low, w_output_ref[...]).astype(BF16)
    for m in range(quad):
        grad_send[m] = d_attended[:, m * part : (m + 1) * part]
    copies = []
    for n, (device, member) in enumerate(quad_others):
        copies.append(
            send(grad_send.at[member], grad_ref.at[my_rows(mine)], grad_sems, (n,), device)
        )
    grad_ref[my_rows(mine), :] = grad_send[mine]
    rows_relay.step(2)
    for copy in copies:
        copy.wait()
    low_gather = QuadGather(place, low_ref, low_sems, block)
    low_gather.begin()

    table_count = hot_ref.shape[1]
    core, x = place.core, place.x
    quarter = width // 4
    core_device, x_device, z_device = place.flip("core"), place.flip("x"), place.flip("z_hi")
    thirds = 3
    third = quarter // thirds
    axes_devices = {"x": x_device, "y": quad_others[0][0], "z": quad_others[1][0]}
    orders = ("yzx", "yzx", "yzx")

    def chunk(c, b):
        return pl.ds(pl.multiple_of((c * 2 + b) * quarter, quarter), quarter)

    class Sum:
        def __init__(self, u):
            self.u = u
            self.rings, self.passed = {}, []

        def begin(self):
            u = self.u
            self.one = [
                send(load_ref.at[u, chunk(1 - core, 1 - x)], first_ref.at[u, 0], first_sems, (u, 0), core_device),
                send(load_ref.at[u, chunk(1 - core, x)], first_ref.at[u, 1], first_sems, (u, 1), core_device),
            ]

        def over_x(self):
            u = self.u
            self.one[0].wait()
            sum_one_ref[u] = (
                load_ref[u, chunk(core, 1 - x), :].astype(F32) + first_ref[u, 0].astype(F32)
            ).astype(BF16)
            self.two = send(sum_one_ref.at[u], second_ref.at[u], second_sems, (u,), x_device)

        def over_z(self):
            u = self.u
            self.one[1].wait()
            self.two.wait()
            sum_two_ref[u] = (
                load_ref[u, chunk(core, x), :].astype(F32) + first_ref[u, 1].astype(F32) + second_ref[u].astype(F32)
            ).astype(BF16)
            self.three = send(sum_two_ref.at[u], third_ref.at[u], third_sems, (u,), z_device)

        def spot(self, axes, t):
            y = 1 - place.y if "y" in axes else place.y
            z_lo = 1 - place.z_lo if "z" in axes else place.z_lo
            xx = 1 - x if "x" in axes else x
            row = pl.multiple_of((core * 2 + xx) * quarter + t * third, third)
            return d_weights_ref.at[self.u, z_lo * 2 + y, pl.ds(row, third)]

        def to_core(self, axes, t, n):
            where = self.spot(axes, t)
            self.passed.append(send(where, where, core_sems, (self.u, t, n), core_device))

        def forward(self, axes, t, axis, n):
            where = self.spot(axes, t)
            self.rings[t, n] = send(where, where, ring_sems, (self.u, t, n), axes_devices[axis])

        def gather_one(self):
            u = self.u
            self.three.wait()
            d_weights_ref[u, mine, chunk(core, x), :] = (
                sum_two_ref[u].astype(F32) + third_ref[u].astype(F32)
            ).astype(BF16)
            for t, (a, b, c) in enumerate(orders):
                self.forward("", t, a, 0)
                self.forward("", t, b, 1)
                self.forward("", t, c, 3)
                self.to_core("", t, 0)

        def gather_two(self):
            for t, (a, b, c) in enumerate(orders):
                self.rings[t, 0].wait_recv()
                self.forward(a, t, b, 2)
                self.forward(a, t, c, 4)
                self.to_core(a, t, 1)

        def gather_three(self):
            for t, (a, b, c) in enumerate(orders):
                self.rings[t, 1].wait_recv()
                self.forward(b, t, c, 5)
                self.to_core(b, t, 2)
                self.rings[t, 2].wait_recv()
                self.forward(a + b, t, c, 6)
                self.to_core(a + b, t, 3)

        def gather_last(self):
            for t, (a, b, c) in enumerate(orders):
                for n, axes in ((3, c), (4, a + c), (5, b + c), (6, a + b + c)):
                    self.rings[t, n].wait_recv()
                    self.to_core(axes, t, n + 1)

        def end(self):
            for t in range(thirds):
                for n in range(7):
                    self.rings[t, n].wait_send()
            for copy in self.passed:
                copy.wait()

    sums = [Sum(h) for h in range(heads)]
    small_devices = [core_device, x_device, z_device, quad_others[0][0], quad_others[1][0]]
    small_copies = []

    def small_start(n):
        small_copies.append(
            send(small_send.at[n], small_recv.at[n], small_sems, (n,), small_devices[n])
        )

    def small_end(n):
        small_copies[n].wait()
        total = small_send[n] + small_recv[n]
        if n + 1 < len(small_devices):
            small_send[n + 1] = total
        else:
            total_ref[...] = total

    y = place.y
    y_device = quad_others[0][0]
    z_devices = [
        place.flip("z_lo"), place.flip("z_hi"), place.flip("z_lo", "z_hi"),
    ]
    share = width // (2 * groups)
    half_copies, d_out_copies, d_in_copies = [], [], []

    def hidden_gradients(e):
        for copy in block_copies(e):
            copy.wait()
        for g in range(groups):
            rows = rows_ref[g, e * capacity : (e + 1) * capacity, :]
            gates = rows_ref[g, local * capacity :, :capacity].astype(F32)
            gate_row = gates[3 * e : 3 * e + 1] + gates[3 * e + 1 : 3 * e + 2] + gates[3 * e + 2 : 3 * e + 3]
            gate_column = jnp.sum(jnp.where(diagonal, gate_row, 0.0), axis=1, keepdims=True)
            d_rows = (gate_column * up_ref[g, e].astype(F32)).astype(BF16)
            up_ref[g, e] = d_rows
            active, slope = gelu_parts(dot(rows, in_buf[e]))
            inner_ref[g] = (dot_t(d_rows, out_buf[e]) * slope).astype(BF16)
            active_ref[g] = active.astype(BF16)
        all_rows = rows_ref[:, e * capacity : (e + 1) * capacity, :].reshape(groups * capacity, width)
        all_d_rows = up_ref[:, e].reshape(groups * capacity, width)
        d_in = t_dot(all_rows, inner_ref[...].reshape(groups * capacity, hidden)).astype(BF16)
        for n in range(2 * groups):
            half_send[e, n % 2, n // 2] = d_in[n * share : (n + 1) * share]
        half_copies.append(send(half_send.at[e, 1 - y], half_recv.at[e], half_sems, (0, e), y_device))
        d_out = t_dot(active_ref[...].reshape(groups * capacity, hidden), all_d_rows).astype(BF16)
        d_out_send[e] = d_out.reshape(d_out_send.shape[1:])

    def hidden_d_out(e):
        d_out_copies.append(send(d_out_send.at[e, 1 - y], d_out_recv.at[e], half_sems, (1, e), y_device))

    def hidden_d_in(e):
        half_copies[e].wait()
        half_send[e, y] = (half_send[e, y].astype(F32) + half_recv[e].astype(F32)).astype(BF16)
        for n, device in enumerate(z_devices):
            d_in_copies.append(
                send(half_send.at[e, y, lax.div(device[0], 2)], d_in_ref.at[z, e], d_in_sems, (e, n), device)
            )
        d_in_ref[z, e] = half_send[e, y, z]

    def hidden_end(e):
        d_out_copies[e].wait()
        d_out_ref[e] = (d_out_send[e, y].astype(F32) + d_out_recv[e].astype(F32)).astype(BF16)

    for h in range(heads):
        if h:
            fill_bias(h)
        cols = slice(h * head_width, (h + 1) * head_width)
        key_cols = slice(part + h * head_width, part + (h + 1) * head_width)
        value_cols = slice(2 * part + h * head_width, 2 * part + (h + 1) * head_width)
        key = qkv_ref[:, key_cols]
        masked_key = with_mask(key, length)
        value = qkv_ref[:, value_cols]
        dkey_ref[...] = jnp.zeros_like(dkey_ref)
        dvalue_ref[...] = jnp.zeros_like(dvalue_ref)
        dbias_ref[...] = jnp.zeros_like(dbias_ref)

        def query_block(i):
            rows = my_rows(i)
            query = qkv_ref[rows, cols]
            masked_query = with_one(query)
            grad = grad_ref[rows, cols]
            log_norm = lse_ref[h, pl.ds(i, 1), :]
            probs, d_probs = [], []
            spread = jnp.zeros((1, block), F32)
            for j in range(blocks):
                keys = slice(j * block, (j + 1) * block)
                score = dot_t(masked_key[keys], masked_query)
                score = score + bias_ref[j - i + blocks - 1]
                prob = jnp.exp(score - log_norm)
                d_prob = dot_t(value[keys], grad)
                spread = spread + jnp.sum(prob * d_prob, axis=0, keepdims=True)
                dvalue_ref[keys, :] += dot(prob.astype(BF16), grad)
                probs.append(prob)
                d_probs.append(d_prob)
            d_query = jnp.zeros((head_width, block), F32)
            for j in range(blocks):
                keys = slice(j * block, (j + 1) * block)
                d_score = probs[j] * (d_probs[j] - spread)
                dbias_ref[j - i + blocks - 1] += d_score
                low_score = d_score.astype(BF16)
                dkey_ref[keys, :] += dot(low_score, query)
                d_query = d_query + t_dot(key[keys], low_score)
            dqkv_ref[rows, cols] = d_query.T.astype(BF16)

        pl.loop(0, blocks // 2)(query_block)
        if h == 0:
            rows_relay.step(3)
        elif h == 1:
            sums[0].over_x()
        else:
            sums[0].gather_one()
            sums[1].over_x()
        pl.loop(blocks // 2, blocks)(query_block)

        dqkv_ref[:, key_cols] = dkey_ref[...].astype(BF16)
        dqkv_ref[:, value_cols] = dvalue_ref[...].astype(BF16)

        terms = jnp.concatenate([dqkv_ref[:, cols], dqkv_ref[:, key_cols], dqkv_ref[:, value_cols]], axis=1)
        d_parts = dot(normed_ref[...], terms)
        w_head = jnp.concatenate([w_mine_ref[:, cols], w_mine_ref[:, key_cols], w_mine_ref[:, value_cols]], axis=1)
        d_gain = exact_dot(jnp.ones((8, part), F32), d_parts * w_head.astype(F32), 1, 1)[0:1] / gain
        if h == 0:
            small_send[0, 0:1, :] = d_gain
            low_gather.forward()
            up_relay.end()
            rows_relay.end()
            hidden_gradients(0)
            hidden_gradients(1)
            low_gather.end()
            d_output = t_dot(attended_ref[...], low_ref[...]).astype(BF16)
            for u in range(heads):
                for m in range(quad):
                    load_ref[u, m * part : (m + 1) * part, part:] = d_output[
                        :, m * part + u * head_width : m * part + (u + 1) * head_width
                    ]
        else:
            small_send[0, 0:1, :] += d_gain
        load_ref[h, :, :part] = d_parts.astype(BF16)
        sums[h].begin()
        if h == 1:
            sums[0].over_z()
        elif h == 2:
            sums[0].gather_two()
            sums[1].over_z()

            mine_copies = []
            for n, (device, member) in enumerate(quad_others):
                mine_copies.append(
                    send(dqkv_ref.at[my_rows(member)], dmine_ref.at[mine], mine_sems, (n,), device)
                )
            dmine_ref[mine] = dqkv_ref[my_rows(mine), :]
        table_row = jnp.zeros((1, table_count), F32)
        for a in range(dbias_ref.shape[0]):
            wide = jnp.concatenate([dbias_ref[a], jnp.zeros((block, block), F32)], axis=1)
            half = block // 2
            while half:
                wide = wide[:half] + pltpu.roll(wide[half:], 2 * block - half, 1)
                half //= 2
            table_row = table_row + exact_dot(wide, hot_ref[a].astype(F32), 1, 1)
        for m in range(quad):
            row = 12 + m * heads + h
            small_send[0, row : row + 1, :table_count] = jnp.where(mine == m, table_row, 0.0)

    small_start(0)
    sums[2].over_x()
    sums[0].gather_three()
    hidden_d_in(0)
    hidden_d_in(1)
    hidden_d_out(0)
    hidden_d_out(1)
    sums[2].over_z()
    sums[1].gather_one()
    small_end(0)
    small_start(1)
    sums[0].gather_last()
    sums[2].gather_one()
    sums[1].gather_two()
    small_end(1)
    small_start(2)

    for copy in mine_copies:
        copy.wait()
    d_normed = jnp.zeros((block, width), F32)
    for kind, weight_ref in enumerate((w_query_ref, w_key_ref, w_value_ref)):
        d_kind = [dmine_ref[m, :, kind * part : (kind + 1) * part] for m in range(quad)]
        d_normed = d_normed + dot_t(jnp.concatenate(d_kind, axis=1), weight_ref[...])
    sums[2].gather_two()
    sums[1].gather_three()
    small_end(2)
    small_start(3)
    token = token_ref[...].astype(F32)
    inverse = lax.rsqrt(jnp.mean(token * token, axis=-1, keepdims=True) + 1e-06)
    scaled = d_normed * gain
    cubed = inverse * inverse * inverse
    d_tokens_ref[...] = residual_ref[...] + inverse * scaled - token * cubed * jnp.mean(
        token * scaled, axis=-1, keepdims=True
    )
    sums[2].gather_three()
    sums[1].gather_last()
    small_end(3)
    small_start(4)
    sums[2].gather_last()
    small_end(4)
    for e in range(local):
        hidden_end(e)
    for total in sums:
        total.end()
    for copy in d_in_copies:
        copy.wait()


def layer(lengths, tokens, ids, cotangent, gains, w_query, w_key, w_value, w_output, w_router, table, hot, w_in, w_out, head_count):
    block, full = tokens.shape
    count, _, double = hot.shape
    quad = (count + 1) // 2
    rows = quad * block
    part = full // quad
    triple = 3 * part
    heads = head_count // quad
    head_width = part // heads
    quarter = full // 4
    experts_count = w_router.shape[0]
    local = w_in.shape[0]
    sources = experts_count // local
    capacity = 5 * block // (4 * local)
    slots = 3 * block // (2 * experts_count)
    groups = lax.axis_size("dp") // 2
    hidden = w_in.shape[2] // groups
    share = full // (2 * groups)
    piece = hidden
    depth = 2
    small = (24, full)
    extra = 16
    vmem = pl.BlockSpec(memory_space=pltpu.VMEM)
    hbm = pl.BlockSpec(memory_space=pl.ANY)
    dma = pltpu.SemaphoreType.DMA
    return pl.pallas_call(
        layer_kernel,
        in_specs=[pl.BlockSpec(memory_space=pltpu.SMEM)] + [vmem] * 11 + [hbm] * 2,
        out_specs=[vmem] * 6,
        out_shape=[
            jax.ShapeDtypeStruct((block, full), BF16),
            jax.ShapeDtypeStruct((block, full), F32),
            jax.ShapeDtypeStruct((heads, quad, full, part + head_width), BF16),
            jax.ShapeDtypeStruct(small, F32),
            jax.ShapeDtypeStruct((local, hidden // 2, full), BF16),
            jax.ShapeDtypeStruct((groups, local, share, hidden), BF16),
        ],
        scratch_shapes=[
            pltpu.VMEM((full, triple), BF16),
            pltpu.VMEM((full, rows), BF16),
            pltpu.VMEM((rows, triple), BF16),
            pltpu.VMEM((count, 16, double), F32),
            pltpu.VMEM((heads, quad, block), F32),
            pltpu.VMEM((rows, part), BF16),
            pltpu.VMEM((quad, block, part), BF16),
            pltpu.VMEM((8, 128), F32),
            pltpu.VMEM((sources, 8, 128), F32),
            pltpu.VMEM((experts_count, slots, full), BF16),
            pltpu.VMEM((sources, local, slots, full), BF16),
            pltpu.VMEM((sources, local, slots, full), BF16),
            pltpu.VMEM((experts_count, 8, 128), F32),
            pltpu.VMEM((sources, local, 8, 128), F32),
            pltpu.VMEM((block, experts_count * slots), BF16),
            pltpu.VMEM((local, capacity, sources * slots), BF16),
            pltpu.VMEM((groups, local, capacity, full), BF16),
            pltpu.VMEM((groups, local * capacity + extra, full), BF16),
            pltpu.VMEM((depth, full, piece), BF16),
            pltpu.VMEM((depth, piece, full), BF16),
            pltpu.VMEM((capacity, 2 * full), F32),
            pltpu.VMEM((sources, local, slots, 2 * full), BF16),
            pltpu.VMEM((experts_count, slots, 2 * full), BF16),
            pltpu.VMEM((block, full), F32),
            pltpu.VMEM((rows, part), BF16),
            pltpu.VMEM((quad, block, part), BF16),
            pltpu.VMEM((rows, full), BF16),
            pltpu.VMEM((count, block, block), F32),
            pltpu.VMEM((count, block, block), F32),
            pltpu.VMEM((rows, head_width), F32),
            pltpu.VMEM((rows, head_width), F32),
            pltpu.VMEM((rows, triple), BF16),
            pltpu.VMEM((quad, block, triple), BF16),
            pltpu.VMEM((heads, full, part + head_width), BF16),
            pltpu.VMEM((heads, 2, quarter, part + head_width), BF16),
            pltpu.VMEM((heads, quarter, part + head_width), BF16),
            pltpu.VMEM((heads, quarter, part + head_width), BF16),
            pltpu.VMEM((heads, quarter, part + head_width), BF16),
            pltpu.VMEM((heads, quarter, part + head_width), BF16),
            pltpu.VMEM((5,) + small, F32),
            pltpu.VMEM((5,) + small, F32),
            pltpu.VMEM((groups, capacity, hidden), BF16),
            pltpu.VMEM((groups, capacity, hidden), BF16),
            pltpu.VMEM((local, 2, groups, share, hidden), BF16),
            pltpu.VMEM((local, groups, share, hidden), BF16),
            pltpu.VMEM((local, 2, hidden // 2, full), BF16),
            pltpu.VMEM((local, hidden // 2, full), BF16),
            dma((2, 4)), dma((2, 3)), dma((2, 3)), dma((2, 3)), dma((2, 3)), dma((2, 3)), dma((2, depth)),
            dma((2, 2, 3)), dma((2, 2, 3)), dma((2, 2, 3)),
            dma((2, 3)), dma((2, 4)), dma((2, 3)), dma((2, 3, 2)), dma((2, 3)), dma((2, 3)),
            dma((2, 3, 3, 7)), dma((2, 3, 3, 8)), dma((2, 5)), dma((2, 2, 3)), dma((2, 2, 2)), dma((2, 2)),
        ],
        compiler_params=pltpu.CompilerParams(
            vmem_limit_bytes=62 * 1024 * 1024, collective_id=0, has_side_effects=True
        ),
        name="layer",
    )(lengths, tokens, ids, cotangent, gains, w_query, w_key, w_value, w_output, w_router, table, hot,
      w_in, w_out)


def finish_kernel(
    all_ref, d_in_ref, d_out_ref, total_ref,
    d_query_ref, d_key_ref, d_value_ref, d_output_ref, d_in_out_ref, d_out_out_ref,
    gain_one_ref, gain_two_ref, router_ref, table_ref,
):
    heads, quad, rows, wide = all_ref.shape
    part = d_query_ref.shape[1] // quad
    width = wide - part
    i = pl.program_id(0)
    span = pl.ds(pl.multiple_of(i * part, part), part)
    for kind, ref in enumerate((d_query_ref, d_key_ref, d_value_ref)):
        ref[...] = jnp.concatenate(
            [
                all_ref[h, m, span, kind * width : (kind + 1) * width].astype(F32)
                for m in range(quad)
                for h in range(heads)
            ],
            axis=1,
        )
    d_output_ref[...] = jnp.concatenate(
        [
            all_ref[h, i, n * part : (n + 1) * part, part:].astype(F32)
            for n in range(quad)
            for h in range(heads)
        ],
        axis=1,
    )
    d_in_out_ref[...] = d_in_ref[0].astype(F32)
    d_out_out_ref[...] = d_out_ref[...].astype(F32)

    @pl.when(i == 0)
    def _():
        gain_one_ref[...] = total_ref[0:1, :]
        gain_two_ref[...] = total_ref[1:2, :]
        router_ref[...] = total_ref[2 : 2 + router_ref.shape[0], :]
        first = total_ref.shape[0] - table_ref.shape[0]
        table_ref[...] = total_ref[first:, : table_ref.shape[1]]


def finish(gathered, d_in, d_out, total, experts_count, head_count, buckets):
    heads, quad, rows, wide = gathered.shape
    groups, local, count, hidden = d_in.shape
    full = rows
    part = full // quad
    out_rows = d_out.shape[1] // groups
    weight = pl.BlockSpec((part, full), lambda i: (i, 0))

    def whole(*shape):
        return pl.BlockSpec(shape, lambda i: (0,) * len(shape))

    d_out_spec = pl.BlockSpec((local, out_rows, full), lambda i: (0, i, 0))
    small = [(1, full), (1, full), (experts_count, full), (head_count, buckets)]
    return pl.pallas_call(
        finish_kernel,
        grid=(groups,),
        in_specs=[
            whole(*gathered.shape),
            pl.BlockSpec((1, local, count, hidden), lambda i: (i, 0, 0, 0)),
            d_out_spec,
            whole(*total.shape),
        ],
        out_specs=[weight] * 4
        + [pl.BlockSpec((local, count, hidden), lambda i: (0, 0, i)), d_out_spec]
        + [whole(*shape) for shape in small],
        out_shape=[jax.ShapeDtypeStruct((rows, full), F32)] * 4
        + [jax.ShapeDtypeStruct((local, count, groups * hidden), F32), jax.ShapeDtypeStruct(d_out.shape, F32)]
        + [jax.ShapeDtypeStruct(shape, F32) for shape in small],
        compiler_params=pltpu.CompilerParams(vmem_limit_bytes=VMEM_BYTES),
        name="finish",
    )(gathered, d_in, d_out, total)


def all_to_all(array, axis, groups=None):
    return lax.all_to_all(
        array, axis, split_axis=0, concat_axis=0, tiled=True, axis_index_groups=groups
    )


def to_experts(received, local):
    total, slots, width = received.shape
    shaped = received.reshape(total // local, local, slots, width)
    return jnp.swapaxes(shaped, 0, 1).reshape(local, total // local * slots, width)


def to_sources(by_expert, sources):
    local, total, width = by_expert.shape
    shaped = by_expert.reshape(local, sources, total // sources, width)
    return jnp.swapaxes(shaped, 0, 1).reshape(sources * local, total // sources, width)


def per_device(
    tokens, lengths, expert_ids, gain_one, w_query, w_key, w_value, w_output,
    bias_table, gain_two, w_router, w_in, w_out, cotangent,
):
    tok_rows, width = tokens.shape
    head_count = bias_table.shape[1]
    head_width = width // head_count
    expert_count = w_router.shape[1]
    local = w_in.shape[0]
    hidden = w_in.shape[2]
    dp_count, ex_count = lax.axis_size("dp"), lax.axis_size("expert")
    dp_index, ex_index = lax.axis_index("dp"), lax.axis_index("expert")
    span = dp_count // 2
    quad = math.gcd(span, head_count)
    heads = head_count // quad
    part = heads * head_width
    q_rows = quad * tok_rows
    q_parts = span // quad
    place = dp_index % span
    mine, q_part = place % quad, place // quad
    quads = [[i * quad + j for j in range(quad)] for i in range(dp_count // quad)]
    spans = [[i * span + j for j in range(span)] for i in range(dp_count // span)]
    seq_id = ex_index * (dp_count // span) + dp_index // span
    start_row = place * tok_rows

    length = jnp.sum(jnp.where(jnp.arange(lengths.shape[0], dtype=jnp.int32) == seq_id, lengths, 0))
    valid_mask = start_row + jnp.arange(tok_rows, dtype=jnp.int32) < length
    valid_f = valid_mask.astype(F32)
    length_arg = length.reshape(1)

    if q_parts == 1:
        tokens_all = all_to_all(
            jnp.broadcast_to(tokens[None], (quad, tok_rows, width)), "dp", quads
        ).reshape(q_rows, width)
        tokens_q = tokens_all
    else:
        tokens_all = lax.all_gather(tokens, "dp", axis_index_groups=spans, tiled=True)
        tokens_q = lax.dynamic_slice_in_dim(tokens_all, q_part * q_rows, q_rows, 0)
    gain_a = gain_one.astype(F32)
    normed_all = normalize(tokens_all.astype(F32), gain_a)[0].astype(BF16)
    normed_q = normalize(tokens_q.astype(F32), gain_a)[0].astype(BF16)

    table = lax.dynamic_slice_in_dim(bias_table.astype(F32), mine * heads, heads, 1)
    counts = span * tok_rows // tok_rows + quad - 1
    offset = jnp.arange(2 * tok_rows, dtype=jnp.int32)
    offset = jnp.where(offset < tok_rows, offset, offset - 2 * tok_rows)
    codes = (
        jnp.arange(counts, dtype=jnp.int32)[:, None] * tok_rows
        - offset[None, :]
        - (q_rows - tok_rows)
        - q_part * q_rows
    )
    window_hot = (
        bucket_of(codes)[:, :, None] == jnp.arange(table.shape[0], dtype=jnp.int32)
    ).astype(BF16)
    window = jnp.einsum("amb,bh->ham", window_hot, table.astype(BF16), preferred_element_type=F32)

    def my_columns(weight):
        return lax.dynamic_slice_in_dim(weight, mine * part, part, 1).reshape(
            width, heads, head_width
        )

    def project(rows, weight):
        return jnp.einsum(
            "sd,dhc->hsc", rows, my_columns(weight), preferred_element_type=F32
        ).astype(BF16)

    query = project(normed_q, w_query)
    key = project(normed_all, w_key)
    value = project(normed_all, w_value)
    attended_heads, log_norm = attend(length_arg, window, query, key, value)
    attended = all_to_all(
        jnp.transpose(
            attended_heads.reshape(heads, quad, tok_rows, head_width), (1, 2, 0, 3)
        ).reshape(quad, tok_rows, part),
        "dp",
        quads,
    )
    attended = jnp.swapaxes(attended, 0, 1).reshape(tok_rows, width)

    token_f = tokens.astype(F32)
    residual = token_f + dot(attended, w_output)
    gain_b = gain_two.astype(F32)
    routed_f, inverse_two = normalize(residual, gain_b)
    routed = routed_f.astype(BF16)
    router = jax.nn.softmax(dot(routed, w_router), axis=-1)

    chosen = expert_ids[:, 0]
    chosen_hot = chosen[:, None] == jnp.arange(expert_count, dtype=jnp.int32)[None, :]
    valid_hits = (chosen_hot & valid_mask[:, None]).astype(jnp.int32)
    per_source = lax.all_gather(jnp.sum(valid_hits, axis=0), "expert")
    earlier = jnp.arange(ex_count, dtype=jnp.int32)[:, None] < ex_index
    offsets = jnp.sum(jnp.where(earlier, per_source, 0), axis=0)
    local_rank = jnp.sum((jnp.cumsum(valid_hits, axis=0) - valid_hits) * valid_hits, axis=1)
    group_rank = local_rank + jnp.sum(valid_hits * offsets[None, :], axis=1)
    capacity = 5 * tok_rows // (4 * local)
    slots = 3 * tok_rows // (2 * expert_count)
    kept_mask = valid_mask & (group_rank < capacity)
    kept_f = kept_mask.astype(F32)
    target = jnp.where(kept_mask, chosen * slots + local_rank, -1)
    placing = (
        jnp.arange(expert_count * slots, dtype=jnp.int32)[:, None] == target[None, :]
    ).astype(BF16)
    chosen_f = chosen_hot.astype(F32)
    chosen_prob = jnp.sum(router * chosen_f, axis=1)
    gate = chosen_prob * kept_f
    upstream = cotangent.astype(F32) * valid_f[:, None]
    d_expert = (gate[:, None] * upstream).astype(BF16)

    sending = dot(placing, jnp.concatenate([routed, d_expert], axis=1)).astype(BF16)
    expert_rows = to_experts(
        all_to_all(sending.reshape(expert_count, slots, 2 * width), "expert"), local
    )
    group_rows = lax.all_gather(expert_rows, "dp")
    results = experts(expert_rows, w_in, w_out)
    returned = all_to_all(to_sources(results, ex_count), "expert")
    gathered = t_dot(placing, returned.reshape(expert_count * slots, 2 * width))
    expert_out, d_routed = gathered[:, :width], gathered[:, width:]

    output = (valid_f[:, None] * (residual + gate[:, None] * expert_out)).astype(BF16)
    d_gate = jnp.sum(upstream * expert_out, axis=1) * kept_f
    d_logits = router * (chosen_f - chosen_prob[:, None]) * d_gate[:, None]
    d_router = t_dot(routed, d_logits.astype(BF16))
    d_routed = d_routed + dot_t(d_logits.astype(BF16), w_router)
    d_norm_two, d_gain_two = norm_back(residual, inverse_two, gain_b, d_routed)
    d_residual = upstream + d_norm_two
    low_residual = d_residual.astype(BF16)
    d_attended = dot_t(low_residual, w_output).astype(BF16)
    d_output = t_dot(attended, low_residual)

    grad = all_to_all(
        jnp.swapaxes(d_attended.reshape(tok_rows, quad, part), 0, 1), "dp", quads
    ).reshape(q_rows, heads, head_width)
    grad = jnp.swapaxes(grad, 0, 1)
    d_query_rows, d_key_rows, d_value_rows, d_window = attend_back(
        length_arg, window, query, key, value, grad, log_norm
    )
    if q_parts > 1:
        strided = [
            [i * span + j + quad * n for n in range(q_parts)]
            for i in range(dp_count // span)
            for j in range(quad)
        ]
        d_key_rows, d_value_rows = [
            lax.psum_scatter(
                rows, "dp", scatter_dimension=1, axis_index_groups=strided, tiled=True
            )
            for rows in (d_key_rows, d_value_rows)
        ]
    d_rows = jnp.stack([d_query_rows, d_key_rows.astype(BF16), d_value_rows.astype(BF16)])
    d_parts = jnp.einsum("sd,khsc->dkhc", normed_q, d_rows, preferred_element_type=F32)
    d_table = jnp.einsum("amb,ham->bh", window_hot.astype(F32), d_window, precision="highest")
    d_mine = all_to_all(
        jnp.transpose(
            d_rows.reshape(3, heads, quad, tok_rows, head_width), (2, 3, 0, 1, 4)
        ).reshape(quad, tok_rows, 3 * part),
        "dp",
        quads,
    ).reshape(quad, tok_rows, 3, part)
    d_mine = jnp.transpose(d_mine, (2, 1, 0, 3)).reshape(3, tok_rows, width)
    d_normed = dot_t(d_mine[0], w_query) + dot_t(d_mine[1], w_key) + dot_t(d_mine[2], w_value)
    inverse_one = normalize(token_f, gain_a)[1]
    d_norm_one, d_gain_one = norm_back(token_f, inverse_one, gain_a, d_normed)
    d_tokens = d_residual + d_norm_one

    piece = hidden // dp_count
    my_in = lax.dynamic_slice_in_dim(w_in, dp_index * piece, piece, 2)
    my_out = lax.dynamic_slice_in_dim(w_out, dp_index * piece, piece, 1)
    d_in_piece, d_out = weight_grads(group_rows, my_in, my_out)
    d_in = all_to_all(
        jnp.swapaxes(d_in_piece.reshape(local, dp_count, width // dp_count, piece), 0, 1), "dp"
    )
    d_in = (
        jnp.transpose(d_in, (1, 2, 0, 3)).reshape(local, width // dp_count, hidden).astype(F32)
    )

    def spread(array, axis):
        wide = jnp.zeros(array.shape[:axis] + (array.shape[axis] * quad,) + array.shape[axis + 1 :], F32)
        return lax.dynamic_update_slice_in_dim(wide, array, mine * array.shape[axis], axis)

    d_parts = d_parts.reshape(width, 3, part)
    big = jnp.stack([spread(d_parts[:, n], 1) for n in range(3)] + [d_output])
    summed = lax.psum(big.astype(BF16), ("dp", "expert")).astype(F32)
    small = lax.psum(
        (d_gain_one, spread(d_table, 1), d_gain_two, d_router), ("dp", "expert")
    )
    return (
        output, d_tokens, small[0], summed[0], summed[1], summed[2], summed[3],
        small[1], small[2], small[3], d_in, d_out,
    )


def per_device_quad(
    tokens, lengths, expert_ids, gain_one, w_query, w_key, w_value, w_output,
    bias_table, gain_two, w_router, w_in, w_out, cotangent,
):
    tok_rows, width = tokens.shape
    buckets, head_count = bias_table.shape
    expert_count = w_router.shape[1]
    quad = lax.axis_size("dp") // 2
    counts = 2 * quad - 1
    offset = jnp.arange(2 * tok_rows, dtype=jnp.int32)
    offset = jnp.where(offset < tok_rows, offset, offset - 2 * tok_rows)
    codes = (
        jnp.arange(counts, dtype=jnp.int32)[:, None] * tok_rows
        - offset[None, :]
        - (quad - 1) * tok_rows
    )
    hot = (
        bucket_of(codes)[:, None, :] == jnp.arange(buckets, dtype=jnp.int32)[None, :, None]
    ).astype(BF16)
    output, d_tokens, d_weights, total, d_out_parts, d_in_parts = layer(
        lengths, tokens, expert_ids.reshape(1, tok_rows), cotangent, jnp.stack([gain_one, gain_two]), w_query,
        w_key, w_value, w_output, w_router.T, bias_table.T, hot, w_in, w_out, head_count,
    )
    d_query, d_key, d_value, d_output, d_in, d_out, d_gain_one, d_gain_two, d_router, d_table = finish(
        d_weights, d_in_parts, d_out_parts, total, expert_count, head_count, buckets
    )
    return (
        output, d_tokens, d_gain_one.reshape(width), d_query, d_key, d_value, d_output,
        d_table.T, d_gain_two.reshape(width), d_router.T, d_in, d_out,
    )


def solution(mesh):
    rows = P(("expert", "dp"), None)
    owned = P("expert", None, None)
    return jax.shard_map(
        per_device_quad if dict(mesh.shape) == {"dp": 8, "expert": 4} else per_device,
        mesh=mesh,
        in_specs=(
            rows, P(), rows, P(), P(), P(), P(), P(), P(), P(), P(), owned, owned, rows,
        ),
        out_specs=(
            rows, rows, P(), P(), P(), P(), P(), P(), P(), P(),
            P("expert", "dp", None), P("expert", "dp", None),
        ),
        check_vma=False,
    )
```

```python
import functools
import math

import jax
import jax.numpy as jnp
from jax import lax
from jax.experimental import pallas as pl
from jax.experimental.pallas import tpu as pltpu
from jax.sharding import PartitionSpec as P

BUCKETS = 32
EXACT = 8
MASKED = -1000000000.0
F32 = jnp.float32
BF16 = jnp.bfloat16
VMEM_BYTES = 56 * 1024 * 1024


def bucket_of(relative):
    distance = jnp.abs(relative)
    beyond = jnp.full(relative.shape, EXACT, jnp.int32)
    for level_step in range(1, BUCKETS // 2 - EXACT):
        boundary = math.isqrt(EXACT * EXACT * (1 << level_step) - 1) + 1
        beyond = beyond + (distance >= boundary).astype(jnp.int32)
    nearby = jnp.where(distance < EXACT, distance, beyond)
    return nearby + jnp.where(relative > 0, BUCKETS // 2, 0).astype(jnp.int32)


def normalize(values, gain):
    inverse = lax.rsqrt(jnp.mean(values * values, axis=-1, keepdims=True) + 1e-06)
    return (values * inverse * gain, inverse)


def norm_back(values, inverse, gain, upstream):
    scaled_up = upstream * gain
    d_gain = jnp.sum(upstream * values * inverse, axis=0)
    cubed = inverse * inverse * inverse
    d_values = inverse * scaled_up - values * cubed * jnp.mean(
        values * scaled_up, axis=-1, keepdims=True
    )
    return (d_values, d_gain)


def dot(left_side, right_side):
    return jnp.dot(left_side, right_side, preferred_element_type=F32)


def dot_t(left_side, right_side):
    return lax.dot_general(
        left_side, right_side, (((1,), (1,)), ((), ())), preferred_element_type=F32
    )


def t_dot(left_side, right_side):
    return lax.dot_general(
        left_side, right_side, (((0,), (0,)), ((), ())), preferred_element_type=F32
    )


def gelu_parts(value):
    scale = math.sqrt(2.0 / math.pi)
    square = value * value
    tanh = jnp.tanh(scale * (value + 0.044715 * value * square))
    half = 0.5 * (1.0 + tanh)
    slope = half + 0.5 * value * (1.0 - tanh * tanh) * scale * (1.0 + 3 * 0.044715 * square)
    return (value * half, slope)


def build_bias(win_ref, bias_ref):
    count, block, _ = bias_ref.shape

    @pl.loop(0, count)
    def _(index):
        row = win_ref[0, pl.ds(index, 1), :]
        wide = jnp.broadcast_to(row, (block, 2 * block))
        bias_ref[index] = pltpu.roll(wide, 0, 1, stride=1, stride_axis=0)[:, :block]


def attend_kernel(length_ref, win_ref, q_ref, k_ref, v_ref, o_ref, lse_ref, bias_ref):
    block = bias_ref.shape[1]
    q_blocks = q_ref.shape[1] // block
    k_blocks = k_ref.shape[1] // block
    build_bias(win_ref, bias_ref)
    length = length_ref[0]

    @pl.loop(0, q_blocks)
    def _(i):
        rows = pl.ds(pl.multiple_of(i * block, block), block)
        query = q_ref[0, rows, :]
        scores = []
        for j in range(k_blocks):
            part = dot_t(k_ref[0, j * block : (j + 1) * block, :], query)
            part = part + bias_ref[j - i + q_blocks - 1]
            position = lax.broadcasted_iota(jnp.int32, (block, 1), 0) + j * block
            scores.append(jnp.where(position < length, part, MASKED))
        top = functools.reduce(jnp.maximum, [jnp.max(s, axis=0, keepdims=True) for s in scores])
        total = jnp.zeros((1, block), F32)
        out = jnp.zeros((v_ref.shape[2], block), F32)
        for j in range(k_blocks):
            scaled = jnp.exp(scores[j] - top)
            total = total + jnp.sum(scaled, axis=0, keepdims=True)
            out = out + t_dot(v_ref[0, j * block : (j + 1) * block, :], scaled.astype(BF16))
        out = out * (1.0 / total)
        o_ref[0, rows, :] = out.T.astype(BF16)
        lse_ref[0, pl.ds(i, 1), :] = top + jnp.log(total)


def attend_back_kernel(
    length_ref, win_ref, q_ref, k_ref, v_ref, g_ref, lse_ref,
    dq_ref, dk_ref, dv_ref, dwin_ref, bias_ref, dbias_ref,
):
    block = bias_ref.shape[1]
    q_blocks = q_ref.shape[1] // block
    k_blocks = k_ref.shape[1] // block
    build_bias(win_ref, bias_ref)
    length = length_ref[0]
    dk_ref[...] = jnp.zeros_like(dk_ref)
    dv_ref[...] = jnp.zeros_like(dv_ref)
    dbias_ref[...] = jnp.zeros_like(dbias_ref)

    @pl.loop(0, q_blocks)
    def _(i):
        rows = pl.ds(pl.multiple_of(i * block, block), block)
        query = q_ref[0, rows, :]
        grad = g_ref[0, rows, :]
        log_norm = lse_ref[0, pl.ds(i, 1), :]
        probs, d_probs = [], []
        spread = jnp.zeros((1, block), F32)
        for j in range(k_blocks):
            keys = slice(j * block, (j + 1) * block)
            part = dot_t(k_ref[0, keys, :], query)
            part = part + bias_ref[j - i + q_blocks - 1]
            position = lax.broadcasted_iota(jnp.int32, (block, 1), 0) + j * block
            part = jnp.where(position < length, part, MASKED)
            prob = jnp.exp(part - log_norm)
            d_prob = dot_t(v_ref[0, keys, :], grad)
            spread = spread + jnp.sum(prob * d_prob, axis=0, keepdims=True)
            dv_ref[0, keys, :] += dot(prob.astype(BF16), grad)
            probs.append(prob)
            d_probs.append(d_prob)
        d_query = jnp.zeros((q_ref.shape[2], block), F32)
        for j in range(k_blocks):
            keys = slice(j * block, (j + 1) * block)
            d_score = probs[j] * (d_probs[j] - spread)
            dbias_ref[j - i + q_blocks - 1] += d_score
            low = d_score.astype(BF16)
            dk_ref[0, keys, :] += dot(low, query)
            d_query = d_query + t_dot(k_ref[0, keys, :], low)
        dq_ref[0, rows, :] = d_query.T.astype(BF16)

    @pl.loop(0, dbias_ref.shape[0])
    def _(index):
        wide = jnp.concatenate([dbias_ref[index], jnp.zeros((block, block), F32)], axis=1)
        half = block // 2
        while half:
            wide = wide[:half] + pltpu.roll(wide[half:], 2 * block - half, 1)
            half //= 2
        dwin_ref[0, pl.ds(index, 1), :] = wide


def head_block(rows, width):
    return pl.BlockSpec((1, rows, width), lambda h: (h, 0, 0))


def attend(length, window, query, key, value):
    heads, q_rows, width = query.shape
    k_rows = key.shape[1]
    count, block = window.shape[1], window.shape[2] // 2
    return pl.pallas_call(
        attend_kernel,
        grid=(heads,),
        in_specs=[
            pl.BlockSpec(memory_space=pltpu.SMEM),
            head_block(count, 2 * block),
            head_block(q_rows, width),
            head_block(k_rows, width),
            head_block(k_rows, width),
        ],
        out_specs=[head_block(q_rows, width), head_block(q_rows // block, block)],
        out_shape=[
            jax.ShapeDtypeStruct((heads, q_rows, width), BF16),
            jax.ShapeDtypeStruct((heads, q_rows // block, block), F32),
        ],
        scratch_shapes=[pltpu.VMEM((count, block, block), F32)],
        compiler_params=pltpu.CompilerParams(vmem_limit_bytes=VMEM_BYTES),
        name="attend",
    )(length, window, query, key, value)


def attend_back(length, window, query, key, value, grad, log_norm):
    heads, q_rows, width = query.shape
    k_rows = key.shape[1]
    count, block = window.shape[1], window.shape[2] // 2
    return pl.pallas_call(
        attend_back_kernel,
        grid=(heads,),
        in_specs=[
            pl.BlockSpec(memory_space=pltpu.SMEM),
            head_block(count, 2 * block),
            head_block(q_rows, width),
            head_block(k_rows, width),
            head_block(k_rows, width),
            head_block(q_rows, width),
            head_block(q_rows // block, block),
        ],
        out_specs=[
            head_block(q_rows, width),
            head_block(k_rows, width),
            head_block(k_rows, width),
            head_block(count, 2 * block),
        ],
        out_shape=[
            jax.ShapeDtypeStruct((heads, q_rows, width), BF16),
            jax.ShapeDtypeStruct((heads, k_rows, width), F32),
            jax.ShapeDtypeStruct((heads, k_rows, width), F32),
            jax.ShapeDtypeStruct((heads, count, 2 * block), F32),
        ],
        scratch_shapes=[pltpu.VMEM((count, block, block), F32) for _ in range(2)],
        compiler_params=pltpu.CompilerParams(vmem_limit_bytes=VMEM_BYTES),
        name="attend_back",
    )(length, window, query, key, value, grad, log_norm)


def experts_kernel(rows_ref, w_in_ref, w_out_ref, out_ref, acc_ref, back_ref):
    width = w_in_ref.shape[1]
    step = pl.program_id(1)

    @pl.when(step == 0)
    def _():
        acc_ref[...] = jnp.zeros_like(acc_ref)
        back_ref[...] = jnp.zeros_like(back_ref)

    inner = dot(rows_ref[0, :, :width], w_in_ref[0])
    active, slope = gelu_parts(inner)
    acc_ref[...] += dot(active.astype(BF16), w_out_ref[0])
    d_active = dot_t(rows_ref[0, :, width:], w_out_ref[0])
    d_inner = (d_active * slope).astype(BF16)
    back_ref[...] += dot_t(d_inner, w_in_ref[0])

    @pl.when(step == pl.num_programs(1) - 1)
    def _():
        out_ref[0, :, :width] = acc_ref[...].astype(BF16)
        out_ref[0, :, width:] = back_ref[...].astype(BF16)


def experts(rows, w_in, w_out):
    local, count, double = rows.shape
    width, hidden = w_in.shape[1:]
    piece = 512
    return pl.pallas_call(
        experts_kernel,
        grid=(local, hidden // piece),
        in_specs=[
            pl.BlockSpec((1, count, double), lambda e, f: (e, 0, 0)),
            pl.BlockSpec((1, width, piece), lambda e, f: (e, 0, f)),
            pl.BlockSpec((1, piece, width), lambda e, f: (e, f, 0)),
        ],
        out_specs=pl.BlockSpec((1, count, double), lambda e, f: (e, 0, 0)),
        out_shape=jax.ShapeDtypeStruct((local, count, double), BF16),
        scratch_shapes=[pltpu.VMEM((count, width), F32) for _ in range(2)],
        compiler_params=pltpu.CompilerParams(vmem_limit_bytes=VMEM_BYTES),
        name="experts",
    )(rows, w_in, w_out)


def weight_grads_kernel(rows_ref, w_in_ref, w_out_ref, d_in_ref, d_out_ref, acc_ref):
    width = w_in_ref.shape[1]
    step = pl.program_id(1)
    rows = rows_ref[...].reshape(rows_ref.shape[0] * rows_ref.shape[2], 2 * width)

    @pl.when(step == 0)
    def _():
        acc_ref[...] = jnp.zeros_like(acc_ref)
        d_out_ref[...] = jnp.zeros_like(d_out_ref)

    inner = dot(rows[:, :width], w_in_ref[0])
    active, slope = gelu_parts(inner)
    d_active = dot_t(rows[:, width:], w_out_ref[0])
    d_inner = (d_active * slope).astype(BF16)
    d_out_ref[0] += t_dot(active.astype(BF16), rows[:, width:])
    acc_ref[...] += t_dot(rows[:, :width], d_inner)

    @pl.when(step == pl.num_programs(1) - 1)
    def _():
        d_in_ref[0] = acc_ref[...].astype(BF16)


def weight_grads(rows, w_in, w_out):
    groups, local, count, double = rows.shape
    width, piece = w_in.shape[1:]
    together = 4
    return pl.pallas_call(
        weight_grads_kernel,
        grid=(local, groups // together),
        in_specs=[
            pl.BlockSpec((together, 1, count, double), lambda e, g: (g, e, 0, 0)),
            pl.BlockSpec((1, width, piece), lambda e, g: (e, 0, 0)),
            pl.BlockSpec((1, piece, width), lambda e, g: (e, 0, 0)),
        ],
        out_specs=[
            pl.BlockSpec((1, width, piece), lambda e, g: (e, 0, 0)),
            pl.BlockSpec((1, piece, width), lambda e, g: (e, 0, 0)),
        ],
        out_shape=[
            jax.ShapeDtypeStruct((local, width, piece), BF16),
            jax.ShapeDtypeStruct((local, piece, width), F32),
        ],
        scratch_shapes=[pltpu.VMEM((width, piece), F32)],
        compiler_params=pltpu.CompilerParams(vmem_limit_bytes=VMEM_BYTES),
        name="weight_grads",
    )(rows, w_in, w_out)


class Place:
    def __init__(self):
        self.dp, self.ex = lax.axis_index("dp"), lax.axis_index("expert")
        self.y = lax.rem(self.dp, 2)
        self.z = lax.div(self.dp, 2)
        self.z_lo = lax.rem(self.z, 2)
        self.z_hi = lax.div(self.dp, 4)
        self.core = lax.rem(self.ex, 2)
        self.x = lax.div(self.ex, 2)
        self.member = self.z_lo * 2 + self.y

    def flip(self, *names):
        c = {n: getattr(self, n) for n in ("y", "z_lo", "z_hi", "core", "x")}
        for name in names:
            c[name] = 1 - c[name]
        return (c["z_hi"] * 4 + c["z_lo"] * 2 + c["y"], c["x"] * 2 + c["core"])

    def quad_others(self):
        found = []
        for names in (("y",), ("z_lo",), ("y", "z_lo")):
            device = self.flip(*names)
            found.append((device, lax.rem(device[0], 4)))
        return found

    def expert_others(self):
        return [self.flip(*names) for names in (("core",), ("x",), ("core", "x"))]

    def dp_others(self):
        names = (("y",), ("z_lo",), ("y", "z_lo"), ("z_hi",), ("z_hi", "y"), ("z_hi", "z_lo"), ("z_hi", "y", "z_lo"))
        return [self.flip(*n) for n in names]


def remote(src, dst, sems, index, device):
    return pltpu.make_async_remote_copy(
        src_ref=src, dst_ref=dst, send_sem=sems.at[(0,) + index], recv_sem=sems.at[(1,) + index],
        device_id=device, device_id_type=pl.DeviceIdType.MESH,
    )


def send(src, dst, sems, index, device):
    copy = remote(src, dst, sems, index, device)
    copy.start()
    return copy


def greet(devices):
    barrier = pltpu.get_barrier_semaphore()
    for device in devices:
        pl.semaphore_signal(barrier, inc=1, device_id=device, device_id_type=pl.DeviceIdType.MESH)
    pl.semaphore_wait(barrier, len(devices))


class Relay:
    def __init__(self, place, ref, sems):
        self.ref, self.sems = ref, sems
        self.dp, self.ex, self.z = place.dp, place.ex, place.z

    def along(self, direction, step, offset):
        neighbour = (self.dp + 2, self.ex) if direction else (self.dp - 2, self.ex)
        block = self.ref.at[self.z + offset]
        return remote(block, block, self.sems, (direction, step), neighbour)

    def begin(self):
        @pl.when(self.z < 3)
        def _():
            self.along(1, 0, 0).start()

        @pl.when(self.z > 0)
        def _():
            self.along(0, 0, 0).start()

    def step(self, k):
        @pl.when(self.z >= k)
        def _():
            self.along(1, k - 1, -k).wait_recv()
            if k < 3:

                @pl.when(self.z < 3)
                def _():
                    self.along(1, k, -k).start()

        @pl.when(self.z + k <= 3)
        def _():
            self.along(0, k - 1, k).wait_recv()
            if k < 3:

                @pl.when(self.z > 0)
                def _():
                    self.along(0, k, k).start()

    def end(self):
        for k in (0, 1, 2):

            @pl.when((self.z >= k) & (self.z < 3))
            def _():
                self.along(1, k, -k).wait_send()

            @pl.when((self.z + k <= 3) & (self.z > 0))
            def _():
                self.along(0, k, k).wait_send()


def with_mask(key, length):
    rows, width = key.shape
    lane = lax.broadcasted_iota(jnp.int32, (rows, width), 1)
    row = lax.broadcasted_iota(jnp.int32, (rows, width), 0)
    return jnp.concatenate(
        [key, jnp.where((lane == 0) & (row >= length), MASKED, 0.0).astype(BF16)], axis=1
    )


def with_one(query):
    lane = lax.broadcasted_iota(jnp.int32, query.shape, 1)
    return jnp.concatenate([query, (lane == 0).astype(BF16)], axis=1)


class QuadGather:
    def __init__(self, place, ref, sems, rows):
        self.ref, self.sems, self.rows = ref, sems, rows
        (self.y_device, self.y_member), (self.z_device, self.z_member), _ = place.quad_others()
        self.mine = place.member

    def part(self, member, start, size):
        return self.ref.at[pl.ds(pl.multiple_of(member * self.rows + start, size), size)]

    def begin(self):
        own = self.part(self.mine, 0, self.rows)
        self.first = [
            send(own, own, self.sems, (0,), self.y_device), send(own, own, self.sems, (1,), self.z_device),
        ]

    def forward(self):
        half = self.rows // 2
        self.first[0].wait_recv()
        upper = self.part(self.y_member, 0, half)
        self.second = [send(upper, upper, self.sems, (2,), self.z_device)]
        self.first[1].wait_recv()
        lower = self.part(self.z_member, half, half)
        self.second.append(send(lower, lower, self.sems, (3,), self.y_device))

    def end(self):
        for copy in self.second:
            copy.wait()
        for copy in self.first:
            copy.wait_send()


def exact_dot(left_side, right_side, left_dim, right_dim):
    return lax.dot_general(
        left_side, right_side, (((left_dim,), (right_dim,)), ((), ())),
        precision=lax.Precision.HIGHEST, preferred_element_type=F32,
    )


def layer_kernel(
    lengths_ref, token_ref, ids_ref, cotangent_ref, gains_ref, w_query_ref, w_key_ref,
    w_value_ref, w_output_ref, w_router_ref, table_ref, hot_ref, w_in_ref, w_out_ref,
    output_ref, d_tokens_ref, d_weights_ref, total_ref, d_out_ref, d_in_ref,
    w_mine_ref, normed_ref, qkv_ref, win_ref, lse_ref, attended_ref, attended_recv,
    count_send, count_ref, slot_send, up_arrive, rows_arrive, gate_send, gate_arrive, place_ref, pack_ref,
    up_ref, rows_ref, in_buf, out_buf, result_ref, back_send, back_ref, residual_ref,
    grad_ref, grad_send, low_ref, bias_ref, dbias_ref, dkey_ref, dvalue_ref, dqkv_ref,
    dmine_ref, load_ref, first_ref, second_ref, third_ref, sum_one_ref, sum_two_ref,
    small_send, small_recv, active_ref, inner_ref, half_send, half_recv, d_out_send, d_out_recv,
    token_sems, count_sems, up_sems, attended_sems, go_sems, gate_sems, weight_sems,
    up_line_sems, line_sems, back_sems,
    grad_sems, low_sems, mine_sems, first_sems, second_sems, third_sems, ring_sems, core_sems,
    small_sems, d_in_sems, half_sems, block_sems,
):
    place = Place()
    mine, ex, dp, z = place.member, place.ex, place.dp, place.z
    block = bias_ref.shape[1]
    part = qkv_ref.shape[1] // 3
    head_width = dkey_ref.shape[1]
    heads = part // head_width
    blocks = quad = qkv_ref.shape[0] // block
    width = normed_ref.shape[0]
    sources, local, slots = rows_arrive.shape[:3]
    groups, _, capacity = up_ref.shape[:3]
    experts_count = local * sources
    length = lengths_ref[ex * 2 + place.z_hi]
    piece = in_buf.shape[2]
    pieces = w_in_ref.shape[2] // piece
    depth = in_buf.shape[0]
    hidden = active_ref.shape[2]
    my_hidden = pl.ds(pl.multiple_of(z * hidden, hidden), hidden)
    diagonal = lax.broadcasted_iota(jnp.int32, (capacity, capacity), 0) == lax.broadcasted_iota(
        jnp.int32, (capacity, capacity), 1
    )

    def my_rows(index):
        return pl.ds(pl.multiple_of(index * block, block), block)

    def fill_bias(h):
        @pl.loop(0, bias_ref.shape[0])
        def _(index):
            wide = jnp.broadcast_to(win_ref[index, pl.ds(mine * heads + h, 1), :], (block, 2 * block))
            bias_ref[index] = pltpu.roll(wide, 0, 1, stride=1, stride_axis=0)[:, :block]

    quad_others = place.quad_others()
    expert_others = place.expert_others()
    dp_others = place.dp_others()
    up_relay = Relay(place, up_ref, up_line_sems)
    rows_relay = Relay(place, rows_ref, line_sems)

    def weight_copies(n):
        e, f, slot = n // pieces, n % pieces, n % depth
        return (
            pltpu.make_async_copy(
                w_in_ref.at[e, :, f * piece : (f + 1) * piece], in_buf.at[slot], weight_sems.at[0, slot]
            ),
            pltpu.make_async_copy(
                w_out_ref.at[e, f * piece : (f + 1) * piece, :], out_buf.at[slot], weight_sems.at[1, slot]
            ),
        )

    def block_copies(e):
        return (
            pltpu.make_async_copy(w_in_ref.at[e, :, my_hidden], in_buf.at[e], block_sems.at[0, e]),
            pltpu.make_async_copy(w_out_ref.at[e, my_hidden, :], out_buf.at[e], block_sems.at[1, e]),
        )

    for n in range(depth):
        for copy in weight_copies(n):
            copy.start()

    greet(dp_others + expert_others)

    low_ref[my_rows(mine), :] = token_ref[...]
    token_gather = QuadGather(place, low_ref, token_sems, block)
    token_gather.begin()

    square = (block, block)
    ids = jnp.sum(
        jnp.where(
            lax.broadcasted_iota(jnp.int32, square, 0) == lax.broadcasted_iota(jnp.int32, square, 1),
            ids_ref[...].astype(F32), 0.0,
        ),
        axis=1, keepdims=True,
    ).astype(jnp.int32)
    position = lax.broadcasted_iota(jnp.int32, (block, 1), 0)
    valid = (position + mine * block < length).astype(F32)
    chosen = (lax.broadcasted_iota(jnp.int32, (block, experts_count), 1) == ids).astype(F32)
    hits = chosen * valid
    below = (
        lax.broadcasted_iota(jnp.int32, (block, block), 1) < lax.broadcasted_iota(jnp.int32, (block, block), 0)
    ).astype(BF16)
    rank = jnp.sum(dot(below, hits.astype(BF16)) * hits, axis=1, keepdims=True)
    count_send[...] = jnp.zeros_like(count_send)
    count_send[0:1, :experts_count] = jnp.sum(hits, axis=0, keepdims=True)
    counts_going = [
        send(count_send, count_ref.at[ex], count_sems, (n,), device) for n, device in enumerate(expert_others)
    ]
    count_ref[ex] = count_send[...]
    target = jnp.where(valid > 0, ids.astype(F32) * slots + rank, -1.0).astype(jnp.int32)
    place_ref[...] = (
        lax.broadcasted_iota(jnp.int32, place_ref.shape, 1) == target
    ).astype(BF16)

    slot_send[...] = t_dot(place_ref[...], cotangent_ref[...]).astype(BF16).reshape(slot_send.shape)

    def scatter(arrive, sems):
        going = [
            send(slot_send.at[pl.ds(device[1] * local, local)], arrive.at[ex], sems, (n,), device)
            for n, device in enumerate(expert_others)
        ]
        arrive[ex] = slot_send[pl.ds(ex * local, local)]
        return going

    ups_going = scatter(up_arrive, up_sems)

    for m in range(quad):

        @pl.when(mine == m)
        def _():
            for kind, weight_ref in enumerate((w_query_ref, w_key_ref, w_value_ref)):
                w_mine_ref[:, kind * part : (kind + 1) * part] = weight_ref[:, m * part : (m + 1) * part]

    for a in range(win_ref.shape[0]):
        win_ref[a, : table_ref.shape[0], :] = dot(table_ref[...], hot_ref[a])
    fill_bias(0)

    for copy in counts_going:
        copy.wait()
    before = jnp.zeros((1, experts_count), F32)
    for s in range(sources):
        before = before + count_ref[s, 0:1, :experts_count] * (s < ex).astype(F32)
    kept = valid * (rank + jnp.sum(hits * before, axis=1, keepdims=True) < capacity).astype(F32)
    lane = lax.broadcasted_iota(jnp.int32, (1, sources * slots), 1)
    expert_lane = lax.broadcasted_iota(jnp.int32, (1, count_ref.shape[2]), 1)
    for e in range(local):
        at = jnp.full((1, sources * slots), -1, jnp.int32)
        start = jnp.zeros((1, 1), F32)
        for s in range(sources):
            count = jnp.sum(
                jnp.where(expert_lane == ex * local + e, count_ref[s, 0:1, :], 0.0), axis=1, keepdims=True
            )
            turn = lane - s * slots
            here = (turn >= 0) & (turn < slots) & (turn < count.astype(jnp.int32))
            at = jnp.where(here, start.astype(jnp.int32) + turn, at)
            start = start + count
        pack_ref[e] = (lax.broadcasted_iota(jnp.int32, (capacity, sources * slots), 0) == at).astype(BF16)

    gain = gains_ref[0:1, :].astype(F32)

    def project(i):
        token = low_ref[my_rows(i), :].astype(F32)
        inverse = lax.rsqrt(jnp.mean(token * token, axis=-1, keepdims=True) + 1e-06)
        normed = token * inverse * gain
        normed_ref[:, my_rows(i)] = normed.T.astype(BF16)
        qkv_ref[my_rows(i), :] = dot(normed.astype(BF16), w_mine_ref[...]).astype(BF16)

    project(mine)
    token_gather.forward()
    project(quad_others[0][1])
    project(quad_others[1][1])
    token_gather.end()
    project(quad_others[2][1])

    for copy in ups_going:
        copy.wait()
    for e in range(local):
        up_ref[z, e] = dot(pack_ref[e], up_arrive[:, e].reshape(sources * slots, width)).astype(BF16)
    up_relay.begin()

    for h in range(heads):
        if h:
            fill_bias(h)
        cols = slice(h * head_width, (h + 1) * head_width)
        key = with_mask(qkv_ref[:, part + h * head_width : part + (h + 1) * head_width], length)
        value = qkv_ref[:, 2 * part + h * head_width : 2 * part + (h + 1) * head_width]

        @pl.loop(0, blocks)
        def _(i):
            rows = my_rows(i)
            query = with_one(qkv_ref[rows, cols])
            scores = []
            for j in range(blocks):
                score = dot_t(key[j * block : (j + 1) * block], query)
                scores.append(score + bias_ref[j - i + blocks - 1])
            top = functools.reduce(
                jnp.maximum, [jnp.max(s, axis=0, keepdims=True) for s in scores]
            )
            total = jnp.zeros((1, block), F32)
            out = jnp.zeros((head_width, block), F32)
            for j in range(blocks):
                scaled = jnp.exp(scores[j] - top)
                total = total + jnp.sum(scaled, axis=0, keepdims=True)
                out = out + t_dot(value[j * block : (j + 1) * block], scaled.astype(BF16))
            out = out * (1.0 / total)
            attended_ref[rows, cols] = out.T.astype(BF16)
            lse_ref[h, pl.ds(i, 1), :] = top + jnp.log(total)

        if h == 1:
            up_relay.step(1)

    attended_going = [
        send(attended_ref.at[my_rows(member)], attended_recv.at[mine], attended_sems, (n,), device)
        for n, (device, member) in enumerate(quad_others)
    ]
    attended_recv[mine] = attended_ref[my_rows(mine), :]
    for copy in attended_going:
        copy.wait()
    attended = jnp.concatenate([attended_recv[m] for m in range(quad)], axis=1)
    residual = token_ref[...].astype(F32) + dot(attended, w_output_ref[...])
    residual_ref[...] = residual
    inverse = lax.rsqrt(jnp.mean(residual * residual, axis=-1, keepdims=True) + 1e-06)
    gain_two = gains_ref[1:2, :].astype(F32)
    routed = (residual * inverse * gain_two).astype(BF16)

    slot_send[...] = t_dot(place_ref[...], routed).astype(BF16).reshape(slot_send.shape)
    rows_going = scatter(rows_arrive, go_sems)
    logits = dot_t(routed, w_router_ref[...])
    router = jnp.exp(logits - jnp.max(logits, axis=1, keepdims=True))
    router = router / jnp.sum(router, axis=1, keepdims=True)
    chosen_prob = jnp.sum(router * chosen, axis=1, keepdims=True)
    gate = chosen_prob * kept
    slopes = router * (chosen - chosen_prob)
    gate_slots = exact_dot(jnp.broadcast_to(gate, (block, 8)), place_ref[...].astype(F32), 0, 0)
    gate_send[...] = jnp.zeros_like(gate_send)
    for e in range(experts_count):
        gate_send[e, :, :slots] = gate_slots[:, e * slots : (e + 1) * slots]
    gates_going = [
        send(gate_send.at[pl.ds(device[1] * local, local)], gate_arrive.at[ex], gate_sems, (n,), device)
        for n, device in enumerate(expert_others)
    ]
    gate_arrive[ex] = gate_send[pl.ds(ex * local, local)]
    up_relay.step(2)
    for copy in rows_going:
        copy.wait()
    for e in range(local):
        rows_ref[z, e * capacity : (e + 1) * capacity, :] = dot(
            pack_ref[e], rows_arrive[:, e].reshape(sources * slots, width)
        ).astype(BF16)
    for copy in gates_going:
        copy.wait()
    rows_ref[z, local * capacity :, :] = jnp.zeros((rows_ref.shape[1] - local * capacity, width), BF16)
    gate_lines = jnp.zeros((rows_ref.shape[1] - local * capacity, capacity), F32)
    line = lax.broadcasted_iota(jnp.int32, gate_lines.shape, 0)
    gate_columns = []
    for e in range(local):
        arrived = jnp.concatenate([gate_arrive[s, e, :, :slots] for s in range(sources)], axis=1)
        pack = pack_ref[e].astype(F32)
        gate_columns.append(exact_dot(pack, arrived, 1, 1)[:, 0:1])
        rest = exact_dot(arrived, pack, 1, 1)[0:1]
        for n in range(3):
            high = rest.astype(BF16).astype(F32)
            gate_lines = jnp.where(line == 3 * e + n, high, gate_lines)
            rest = rest - high
    rows_ref[z, local * capacity :, :capacity] = gate_lines.astype(BF16)
    rows_relay.begin()

    backs = []
    for e in range(local):
        rows = rows_ref[z, e * capacity : (e + 1) * capacity, :]
        d_rows = (gate_columns[e] * up_ref[z, e].astype(F32)).astype(BF16)
        for f in range(pieces):
            n = e * pieces + f
            for copy in weight_copies(n):
                copy.wait()
            weight_in = in_buf[n % depth]
            weight_out = out_buf[n % depth]
            active, slope = gelu_parts(dot(rows, weight_in))
            forward = dot(active.astype(BF16), weight_out)
            d_inner = (dot_t(d_rows, weight_out) * slope).astype(BF16)
            backward = dot_t(d_inner, weight_in)
            if f == 0:
                result_ref[:, :width] = forward
                result_ref[:, width:] = backward
            else:
                result_ref[:, :width] += forward
                result_ref[:, width:] += backward
            if n + depth < local * pieces:
                for copy in weight_copies(n + depth):
                    copy.start()
        spread_rows = t_dot(pack_ref[e], result_ref[...].astype(BF16)).astype(BF16)
        back_send[:, e] = spread_rows.reshape(sources, slots, 2 * width)
        for n, device in enumerate(expert_others):
            backs.append(
                send(back_send.at[device[1], e], back_ref.at[ex * local + e], back_sems, (e, n), device)
            )
        back_ref[ex * local + e] = back_send[ex, e]
        if e == 0:
            up_relay.step(3)
        else:
            rows_relay.step(1)
    for e in range(local):
        for copy in block_copies(e):
            copy.start()
    fill_bias(0)
    for copy in backs:
        copy.wait()

    gathered = dot(place_ref[...], back_ref[...].reshape(experts_count * slots, 2 * width))
    expert_out = gathered[:, :width]
    residual = residual_ref[...]
    output_ref[...] = (valid * (residual + gate * expert_out)).astype(BF16)
    upstream = cotangent_ref[...].astype(F32) * valid
    d_gate = jnp.sum(upstream * expert_out, axis=1, keepdims=True) * kept
    d_logits = (slopes * d_gate).astype(BF16)
    small_send[0] = jnp.zeros(small_send.shape[1:], F32)
    inverse = lax.rsqrt(jnp.mean(residual * residual, axis=-1, keepdims=True) + 1e-06)
    routed = (residual * inverse * gain_two).astype(BF16)
    small_send[0, 2:10, :] = t_dot(d_logits, routed)
    d_routed = gathered[:, width:] + dot(d_logits, w_router_ref[...])
    small_send[0, 1:2, :] = jnp.sum(d_routed * residual * inverse, axis=0, keepdims=True)
    scaled = d_routed * gain_two
    cubed = inverse * inverse * inverse
    d_residual = upstream + inverse * scaled - residual * cubed * jnp.mean(
        residual * scaled, axis=-1, keepdims=True
    )
    residual_ref[...] = d_residual

    low = d_residual.astype(BF16)
    low_ref[my_rows(mine), :] = low
    d_attended = dot_t(low, w_output_ref[...]).astype(BF16)
    for m in range(quad):
        grad_send[m] = d_attended[:, m * part : (m + 1) * part]
    copies = []
    for n, (device, member) in enumerate(quad_others):
        copies.append(
            send(grad_send.at[member], grad_ref.at[my_rows(mine)], grad_sems, (n,), device)
        )
    grad_ref[my_rows(mine), :] = grad_send[mine]
    rows_relay.step(2)
    for copy in copies:
        copy.wait()
    low_gather = QuadGather(place, low_ref, low_sems, block)
    low_gather.begin()

    table_count = hot_ref.shape[1]
    core, x = place.core, place.x
    quarter = width // 4
    core_device, x_device, z_device = place.flip("core"), place.flip("x"), place.flip("z_hi")
    thirds = 3
    third = quarter // thirds
    axes_devices = {"x": x_device, "y": quad_others[0][0], "z": quad_others[1][0]}
    orders = ("yzx", "yzx", "yzx")

    def chunk(c, b):
        return pl.ds(pl.multiple_of((c * 2 + b) * quarter, quarter), quarter)

    class Sum:
        def __init__(self, u):
            self.u = u
            self.rings, self.passed = {}, []

        def begin(self):
            u = self.u
            self.one = [
                send(load_ref.at[u, chunk(1 - core, 1 - x)], first_ref.at[u, 0], first_sems, (u, 0), core_device),
                send(load_ref.at[u, chunk(1 - core, x)], first_ref.at[u, 1], first_sems, (u, 1), core_device),
            ]

        def over_x(self):
            u = self.u
            self.one[0].wait()
            sum_one_ref[u] = (
                load_ref[u, chunk(core, 1 - x), :].astype(F32) + first_ref[u, 0].astype(F32)
            ).astype(BF16)
            self.two = send(sum_one_ref.at[u], second_ref.at[u], second_sems, (u,), x_device)

        def over_z(self):
            u = self.u
            self.one[1].wait()
            self.two.wait()
            sum_two_ref[u] = (
                load_ref[u, chunk(core, x), :].astype(F32) + first_ref[u, 1].astype(F32) + second_ref[u].astype(F32)
            ).astype(BF16)
            self.three = send(sum_two_ref.at[u], third_ref.at[u], third_sems, (u,), z_device)

        def spot(self, axes, t):
            y = 1 - place.y if "y" in axes else place.y
            z_lo = 1 - place.z_lo if "z" in axes else place.z_lo
            xx = 1 - x if "x" in axes else x
            row = pl.multiple_of((core * 2 + xx) * quarter + t * third, third)
            return d_weights_ref.at[self.u, z_lo * 2 + y, pl.ds(row, third)]

        def to_core(self, axes, t, n):
            where = self.spot(axes, t)
            self.passed.append(send(where, where, core_sems, (self.u, t, n), core_device))

        def forward(self, axes, t, axis, n):
            where = self.spot(axes, t)
            self.rings[t, n] = send(where, where, ring_sems, (self.u, t, n), axes_devices[axis])

        def gather_one(self):
            u = self.u
            self.three.wait()
            d_weights_ref[u, mine, chunk(core, x), :] = (
                sum_two_ref[u].astype(F32) + third_ref[u].astype(F32)
            ).astype(BF16)
            for t, (a, b, c) in enumerate(orders):
                self.forward("", t, a, 0)
                self.forward("", t, b, 1)
                self.forward("", t, c, 3)
                self.to_core("", t, 0)

        def gather_two(self):
            for t, (a, b, c) in enumerate(orders):
                self.rings[t, 0].wait_recv()
                self.forward(a, t, b, 2)
                self.forward(a, t, c, 4)
                self.to_core(a, t, 1)

        def gather_three(self):
            for t, (a, b, c) in enumerate(orders):
                self.rings[t, 1].wait_recv()
                self.forward(b, t, c, 5)
                self.to_core(b, t, 2)
                self.rings[t, 2].wait_recv()
                self.forward(a + b, t, c, 6)
                self.to_core(a + b, t, 3)

        def gather_last(self):
            for t, (a, b, c) in enumerate(orders):
                for n, axes in ((3, c), (4, a + c), (5, b + c), (6, a + b + c)):
                    self.rings[t, n].wait_recv()
                    self.to_core(axes, t, n + 1)

        def end(self):
            for t in range(thirds):
                for n in range(7):
                    self.rings[t, n].wait_send()
            for copy in self.passed:
                copy.wait()

    sums = [Sum(h) for h in range(heads)]
    small_devices = [core_device, x_device, z_device, quad_others[0][0], quad_others[1][0]]
    small_copies = []

    def small_start(n):
        small_copies.append(
            send(small_send.at[n], small_recv.at[n], small_sems, (n,), small_devices[n])
        )

    def small_end(n):
        small_copies[n].wait()
        total = small_send[n] + small_recv[n]
        if n + 1 < len(small_devices):
            small_send[n + 1] = total
        else:
            total_ref[...] = total

    y = place.y
    y_device = quad_others[0][0]
    z_devices = [
        place.flip("z_lo"), place.flip("z_hi"), place.flip("z_lo", "z_hi"),
    ]
    share = width // (2 * groups)
    half_copies, d_out_copies, d_in_copies = [], [], []

    def hidden_gradients(e):
        for copy in block_copies(e):
            copy.wait()
        for g in range(groups):
            rows = rows_ref[g, e * capacity : (e + 1) * capacity, :]
            gates = rows_ref[g, local * capacity :, :capacity].astype(F32)
            gate_row = gates[3 * e : 3 * e + 1] + gates[3 * e + 1 : 3 * e + 2] + gates[3 * e + 2 : 3 * e + 3]
            gate_column = jnp.sum(jnp.where(diagonal, gate_row, 0.0), axis=1, keepdims=True)
            d_rows = (gate_column * up_ref[g, e].astype(F32)).astype(BF16)
            up_ref[g, e] = d_rows
            active, slope = gelu_parts(dot(rows, in_buf[e]))
            inner_ref[g] = (dot_t(d_rows, out_buf[e]) * slope).astype(BF16)
            active_ref[g] = active.astype(BF16)
        all_rows = rows_ref[:, e * capacity : (e + 1) * capacity, :].reshape(groups * capacity, width)
        all_d_rows = up_ref[:, e].reshape(groups * capacity, width)
        d_in = t_dot(all_rows, inner_ref[...].reshape(groups * capacity, hidden)).astype(BF16)
        for n in range(2 * groups):
            half_send[e, n % 2, n // 2] = d_in[n * share : (n + 1) * share]
        half_copies.append(send(half_send.at[e, 1 - y], half_recv.at[e], half_sems, (0, e), y_device))
        d_out = t_dot(active_ref[...].reshape(groups * capacity, hidden), all_d_rows).astype(BF16)
        d_out_send[e] = d_out.reshape(d_out_send.shape[1:])

    def hidden_d_out(e):
        d_out_copies.append(send(d_out_send.at[e, 1 - y], d_out_recv.at[e], half_sems, (1, e), y_device))

    def hidden_d_in(e):
        half_copies[e].wait()
        half_send[e, y] = (half_send[e, y].astype(F32) + half_recv[e].astype(F32)).astype(BF16)
        for n, device in enumerate(z_devices):
            d_in_copies.append(
                send(half_send.at[e, y, lax.div(device[0], 2)], d_in_ref.at[z, e], d_in_sems, (e, n), device)
            )
        d_in_ref[z, e] = half_send[e, y, z]

    def hidden_end(e):
        d_out_copies[e].wait()
        d_out_ref[e] = (d_out_send[e, y].astype(F32) + d_out_recv[e].astype(F32)).astype(BF16)

    for h in range(heads):
        if h:
            fill_bias(h)
        cols = slice(h * head_width, (h + 1) * head_width)
        key_cols = slice(part + h * head_width, part + (h + 1) * head_width)
        value_cols = slice(2 * part + h * head_width, 2 * part + (h + 1) * head_width)
        key = qkv_ref[:, key_cols]
        masked_key = with_mask(key, length)
        value = qkv_ref[:, value_cols]
        dkey_ref[...] = jnp.zeros_like(dkey_ref)
        dvalue_ref[...] = jnp.zeros_like(dvalue_ref)
        dbias_ref[...] = jnp.zeros_like(dbias_ref)

        def query_block(i):
            rows = my_rows(i)
            query = qkv_ref[rows, cols]
            masked_query = with_one(query)
            grad = grad_ref[rows, cols]
            log_norm = lse_ref[h, pl.ds(i, 1), :]
            probs, d_probs = [], []
            spread = jnp.zeros((1, block), F32)
            for j in range(blocks):
                keys = slice(j * block, (j + 1) * block)
                score = dot_t(masked_key[keys], masked_query)
                score = score + bias_ref[j - i + blocks - 1]
                prob = jnp.exp(score - log_norm)
                d_prob = dot_t(value[keys], grad)
                spread = spread + jnp.sum(prob * d_prob, axis=0, keepdims=True)
                dvalue_ref[keys, :] += dot(prob.astype(BF16), grad)
                probs.append(prob)
                d_probs.append(d_prob)
            d_query = jnp.zeros((head_width, block), F32)
            for j in range(blocks):
                keys = slice(j * block, (j + 1) * block)
                d_score = probs[j] * (d_probs[j] - spread)
                dbias_ref[j - i + blocks - 1] += d_score
                low_score = d_score.astype(BF16)
                dkey_ref[keys, :] += dot(low_score, query)
                d_query = d_query + t_dot(key[keys], low_score)
            dqkv_ref[rows, cols] = d_query.T.astype(BF16)

        pl.loop(0, blocks // 2)(query_block)
        if h == 0:
            rows_relay.step(3)
        elif h == 1:
            sums[0].over_x()
        else:
            sums[0].gather_one()
            sums[1].over_x()
        pl.loop(blocks // 2, blocks)(query_block)

        dqkv_ref[:, key_cols] = dkey_ref[...].astype(BF16)
        dqkv_ref[:, value_cols] = dvalue_ref[...].astype(BF16)

        terms = jnp.concatenate([dqkv_ref[:, cols], dqkv_ref[:, key_cols], dqkv_ref[:, value_cols]], axis=1)
        d_parts = dot(normed_ref[...], terms)
        w_head = jnp.concatenate([w_mine_ref[:, cols], w_mine_ref[:, key_cols], w_mine_ref[:, value_cols]], axis=1)
        d_gain = exact_dot(jnp.ones((8, part), F32), d_parts * w_head.astype(F32), 1, 1)[0:1] / gain
        if h == 0:
            small_send[0, 0:1, :] = d_gain
            low_gather.forward()
            up_relay.end()
            rows_relay.end()
            hidden_gradients(0)
            hidden_gradients(1)
            low_gather.end()
            d_output = t_dot(attended_ref[...], low_ref[...]).astype(BF16)
            for u in range(heads):
                for m in range(quad):
                    load_ref[u, m * part : (m + 1) * part, part:] = d_output[
                        :, m * part + u * head_width : m * part + (u + 1) * head_width
                    ]
        else:
            small_send[0, 0:1, :] += d_gain
        load_ref[h, :, :part] = d_parts.astype(BF16)
        sums[h].begin()
        if h == 1:
            sums[0].over_z()
        elif h == 2:
            sums[0].gather_two()
            sums[1].over_z()

            mine_copies = []
            for n, (device, member) in enumerate(quad_others):
                mine_copies.append(
                    send(dqkv_ref.at[my_rows(member)], dmine_ref.at[mine], mine_sems, (n,), device)
                )
            dmine_ref[mine] = dqkv_ref[my_rows(mine), :]
        table_row = jnp.zeros((1, table_count), F32)
        for a in range(dbias_ref.shape[0]):
            wide = jnp.concatenate([dbias_ref[a], jnp.zeros((block, block), F32)], axis=1)
            half = block // 2
            while half:
                wide = wide[:half] + pltpu.roll(wide[half:], 2 * block - half, 1)
                half //= 2
            table_row = table_row + exact_dot(wide, hot_ref[a].astype(F32), 1, 1)
        for m in range(quad):
            row = 12 + m * heads + h
            small_send[0, row : row + 1, :table_count] = jnp.where(mine == m, table_row, 0.0)

    small_start(0)
    sums[2].over_x()
    sums[0].gather_three()
    hidden_d_in(0)
    sums[2].over_z()
    hidden_d_in(1)
    sums[1].gather_one()
    hidden_d_out(0)
    hidden_d_out(1)
    small_end(0)
    small_start(1)
    sums[0].gather_last()
    sums[2].gather_one()
    sums[1].gather_two()
    small_end(1)
    small_start(2)

    for copy in mine_copies:
        copy.wait()
    d_normed = jnp.zeros((block, width), F32)
    for kind, weight_ref in enumerate((w_query_ref, w_key_ref, w_value_ref)):
        d_kind = [dmine_ref[m, :, kind * part : (kind + 1) * part] for m in range(quad)]
        d_normed = d_normed + dot_t(jnp.concatenate(d_kind, axis=1), weight_ref[...])
    sums[2].gather_two()
    sums[1].gather_three()
    small_end(2)
    small_start(3)
    token = token_ref[...].astype(F32)
    inverse = lax.rsqrt(jnp.mean(token * token, axis=-1, keepdims=True) + 1e-06)
    scaled = d_normed * gain
    cubed = inverse * inverse * inverse
    d_tokens_ref[...] = residual_ref[...] + inverse * scaled - token * cubed * jnp.mean(
        token * scaled, axis=-1, keepdims=True
    )
    sums[2].gather_three()
    sums[1].gather_last()
    small_end(3)
    small_start(4)
    sums[2].gather_last()
    small_end(4)
    for e in range(local):
        hidden_end(e)
    for total in sums:
        total.end()
    for copy in d_in_copies:
        copy.wait()


def layer(lengths, tokens, ids, cotangent, gains, w_query, w_key, w_value, w_output, w_router, table, hot, w_in, w_out, head_count):
    block, full = tokens.shape
    count, _, double = hot.shape
    quad = (count + 1) // 2
    rows = quad * block
    part = full // quad
    triple = 3 * part
    heads = head_count // quad
    head_width = part // heads
    quarter = full // 4
    experts_count = w_router.shape[0]
    local = w_in.shape[0]
    sources = experts_count // local
    capacity = 5 * block // (4 * local)
    slots = 3 * block // (2 * experts_count)
    groups = lax.axis_size("dp") // 2
    hidden = w_in.shape[2] // groups
    share = full // (2 * groups)
    piece = hidden
    depth = 2
    small = (24, full)
    extra = 16
    vmem = pl.BlockSpec(memory_space=pltpu.VMEM)
    hbm = pl.BlockSpec(memory_space=pl.ANY)
    dma = pltpu.SemaphoreType.DMA
    return pl.pallas_call(
        layer_kernel,
        in_specs=[pl.BlockSpec(memory_space=pltpu.SMEM)] + [vmem] * 11 + [hbm] * 2,
        out_specs=[vmem] * 6,
        out_shape=[
            jax.ShapeDtypeStruct((block, full), BF16),
            jax.ShapeDtypeStruct((block, full), F32),
            jax.ShapeDtypeStruct((heads, quad, full, part + head_width), BF16),
            jax.ShapeDtypeStruct(small, F32),
            jax.ShapeDtypeStruct((local, hidden // 2, full), BF16),
            jax.ShapeDtypeStruct((groups, local, share, hidden), BF16),
        ],
        scratch_shapes=[
            pltpu.VMEM((full, triple), BF16),
            pltpu.VMEM((full, rows), BF16),
            pltpu.VMEM((rows, triple), BF16),
            pltpu.VMEM((count, 16, double), F32),
            pltpu.VMEM((heads, quad, block), F32),
            pltpu.VMEM((rows, part), BF16),
            pltpu.VMEM((quad, block, part), BF16),
            pltpu.VMEM((8, 128), F32),
            pltpu.VMEM((sources, 8, 128), F32),
            pltpu.VMEM((experts_count, slots, full), BF16),
            pltpu.VMEM((sources, local, slots, full), BF16),
            pltpu.VMEM((sources, local, slots, full), BF16),
            pltpu.VMEM((experts_count, 8, 128), F32),
            pltpu.VMEM((sources, local, 8, 128), F32),
            pltpu.VMEM((block, experts_count * slots), BF16),
            pltpu.VMEM((local, capacity, sources * slots), BF16),
            pltpu.VMEM((groups, local, capacity, full), BF16),
            pltpu.VMEM((groups, local * capacity + extra, full), BF16),
            pltpu.VMEM((depth, full, piece), BF16),
            pltpu.VMEM((depth, piece, full), BF16),
            pltpu.VMEM((capacity, 2 * full), F32),
            pltpu.VMEM((sources, local, slots, 2 * full), BF16),
            pltpu.VMEM((experts_count, slots, 2 * full), BF16),
            pltpu.VMEM((block, full), F32),
            pltpu.VMEM((rows, part), BF16),
            pltpu.VMEM((quad, block, part), BF16),
            pltpu.VMEM((rows, full), BF16),
            pltpu.VMEM((count, block, block), F32),
            pltpu.VMEM((count, block, block), F32),
            pltpu.VMEM((rows, head_width), F32),
            pltpu.VMEM((rows, head_width), F32),
            pltpu.VMEM((rows, triple), BF16),
            pltpu.VMEM((quad, block, triple), BF16),
            pltpu.VMEM((heads, full, part + head_width), BF16),
            pltpu.VMEM((heads, 2, quarter, part + head_width), BF16),
            pltpu.VMEM((heads, quarter, part + head_width), BF16),
            pltpu.VMEM((heads, quarter, part + head_width), BF16),
            pltpu.VMEM((heads, quarter, part + head_width), BF16),
            pltpu.VMEM((heads, quarter, part + head_width), BF16),
            pltpu.VMEM((5,) + small, F32),
            pltpu.VMEM((5,) + small, F32),
            pltpu.VMEM((groups, capacity, hidden), BF16),
            pltpu.VMEM((groups, capacity, hidden), BF16),
            pltpu.VMEM((local, 2, groups, share, hidden), BF16),
            pltpu.VMEM((local, groups, share, hidden), BF16),
            pltpu.VMEM((local, 2, hidden // 2, full), BF16),
            pltpu.VMEM((local, hidden // 2, full), BF16),
            dma((2, 4)), dma((2, 3)), dma((2, 3)), dma((2, 3)), dma((2, 3)), dma((2, 3)), dma((2, depth)),
            dma((2, 2, 3)), dma((2, 2, 3)), dma((2, 2, 3)),
            dma((2, 3)), dma((2, 4)), dma((2, 3)), dma((2, 3, 2)), dma((2, 3)), dma((2, 3)),
            dma((2, 3, 3, 7)), dma((2, 3, 3, 8)), dma((2, 5)), dma((2, 2, 3)), dma((2, 2, 2)), dma((2, 2)),
        ],
        compiler_params=pltpu.CompilerParams(
            vmem_limit_bytes=62 * 1024 * 1024, collective_id=0, has_side_effects=True
        ),
        name="layer",
    )(lengths, tokens, ids, cotangent, gains, w_query, w_key, w_value, w_output, w_router, table, hot,
      w_in, w_out)


def finish_kernel(
    all_ref, d_in_ref, d_out_ref, total_ref,
    d_query_ref, d_key_ref, d_value_ref, d_output_ref, d_in_out_ref, d_out_out_ref,
    gain_one_ref, gain_two_ref, router_ref, table_ref,
):
    heads, quad, rows, wide = all_ref.shape
    part = d_query_ref.shape[1] // quad
    width = wide - part
    i = pl.program_id(0)
    span = pl.ds(pl.multiple_of(i * part, part), part)
    for kind, ref in enumerate((d_query_ref, d_key_ref, d_value_ref)):
        ref[...] = jnp.concatenate(
            [
                all_ref[h, m, span, kind * width : (kind + 1) * width].astype(F32)
                for m in range(quad)
                for h in range(heads)
            ],
            axis=1,
        )
    d_output_ref[...] = jnp.concatenate(
        [
            all_ref[h, i, n * part : (n + 1) * part, part:].astype(F32)
            for n in range(quad)
            for h in range(heads)
        ],
        axis=1,
    )
    d_in_out_ref[...] = d_in_ref[0].astype(F32)
    d_out_out_ref[...] = d_out_ref[...].astype(F32)

    @pl.when(i == 0)
    def _():
        gain_one_ref[...] = total_ref[0:1, :]
        gain_two_ref[...] = total_ref[1:2, :]
        router_ref[...] = total_ref[2 : 2 + router_ref.shape[0], :]
        first = total_ref.shape[0] - table_ref.shape[0]
        table_ref[...] = total_ref[first:, : table_ref.shape[1]]


def finish(gathered, d_in, d_out, total, experts_count, head_count, buckets):
    heads, quad, rows, wide = gathered.shape
    groups, local, count, hidden = d_in.shape
    full = rows
    part = full // quad
    out_rows = d_out.shape[1] // groups
    weight = pl.BlockSpec((part, full), lambda i: (i, 0))

    def whole(*shape):
        return pl.BlockSpec(shape, lambda i: (0,) * len(shape))

    d_out_spec = pl.BlockSpec((local, out_rows, full), lambda i: (0, i, 0))
    small = [(1, full), (1, full), (experts_count, full), (head_count, buckets)]
    return pl.pallas_call(
        finish_kernel,
        grid=(groups,),
        in_specs=[
            whole(*gathered.shape),
            pl.BlockSpec((1, local, count, hidden), lambda i: (i, 0, 0, 0)),
            d_out_spec,
            whole(*total.shape),
        ],
        out_specs=[weight] * 4
        + [pl.BlockSpec((local, count, hidden), lambda i: (0, 0, i)), d_out_spec]
        + [whole(*shape) for shape in small],
        out_shape=[jax.ShapeDtypeStruct((rows, full), F32)] * 4
        + [jax.ShapeDtypeStruct((local, count, groups * hidden), F32), jax.ShapeDtypeStruct(d_out.shape, F32)]
        + [jax.ShapeDtypeStruct(shape, F32) for shape in small],
        compiler_params=pltpu.CompilerParams(vmem_limit_bytes=VMEM_BYTES),
        name="finish",
    )(gathered, d_in, d_out, total)


def all_to_all(array, axis, groups=None):
    return lax.all_to_all(
        array, axis, split_axis=0, concat_axis=0, tiled=True, axis_index_groups=groups
    )


def to_experts(received, local):
    total, slots, width = received.shape
    shaped = received.reshape(total // local, local, slots, width)
    return jnp.swapaxes(shaped, 0, 1).reshape(local, total // local * slots, width)


def to_sources(by_expert, sources):
    local, total, width = by_expert.shape
    shaped = by_expert.reshape(local, sources, total // sources, width)
    return jnp.swapaxes(shaped, 0, 1).reshape(sources * local, total // sources, width)


def per_device(
    tokens, lengths, expert_ids, gain_one, w_query, w_key, w_value, w_output,
    bias_table, gain_two, w_router, w_in, w_out, cotangent,
):
    tok_rows, width = tokens.shape
    head_count = bias_table.shape[1]
    head_width = width // head_count
    expert_count = w_router.shape[1]
    local = w_in.shape[0]
    hidden = w_in.shape[2]
    dp_count, ex_count = lax.axis_size("dp"), lax.axis_size("expert")
    dp_index, ex_index = lax.axis_index("dp"), lax.axis_index("expert")
    span = dp_count // 2
    quad = math.gcd(span, head_count)
    heads = head_count // quad
    part = heads * head_width
    q_rows = quad * tok_rows
    q_parts = span // quad
    place = dp_index % span
    mine, q_part = place % quad, place // quad
    quads = [[i * quad + j for j in range(quad)] for i in range(dp_count // quad)]
    spans = [[i * span + j for j in range(span)] for i in range(dp_count // span)]
    seq_id = ex_index * (dp_count // span) + dp_index // span
    start_row = place * tok_rows

    length = jnp.sum(jnp.where(jnp.arange(lengths.shape[0], dtype=jnp.int32) == seq_id, lengths, 0))
    valid_mask = start_row + jnp.arange(tok_rows, dtype=jnp.int32) < length
    valid_f = valid_mask.astype(F32)
    length_arg = length.reshape(1)

    if q_parts == 1:
        tokens_all = all_to_all(
            jnp.broadcast_to(tokens[None], (quad, tok_rows, width)), "dp", quads
        ).reshape(q_rows, width)
        tokens_q = tokens_all
    else:
        tokens_all = lax.all_gather(tokens, "dp", axis_index_groups=spans, tiled=True)
        tokens_q = lax.dynamic_slice_in_dim(tokens_all, q_part * q_rows, q_rows, 0)
    gain_a = gain_one.astype(F32)
    normed_all = normalize(tokens_all.astype(F32), gain_a)[0].astype(BF16)
    normed_q = normalize(tokens_q.astype(F32), gain_a)[0].astype(BF16)

    table = lax.dynamic_slice_in_dim(bias_table.astype(F32), mine * heads, heads, 1)
    counts = span * tok_rows // tok_rows + quad - 1
    offset = jnp.arange(2 * tok_rows, dtype=jnp.int32)
    offset = jnp.where(offset < tok_rows, offset, offset - 2 * tok_rows)
    codes = (
        jnp.arange(counts, dtype=jnp.int32)[:, None] * tok_rows
        - offset[None, :]
        - (q_rows - tok_rows)
        - q_part * q_rows
    )
    window_hot = (
        bucket_of(codes)[:, :, None] == jnp.arange(table.shape[0], dtype=jnp.int32)
    ).astype(BF16)
    window = jnp.einsum("amb,bh->ham", window_hot, table.astype(BF16), preferred_element_type=F32)

    def my_columns(weight):
        return lax.dynamic_slice_in_dim(weight, mine * part, part, 1).reshape(
            width, heads, head_width
        )

    def project(rows, weight):
        return jnp.einsum(
            "sd,dhc->hsc", rows, my_columns(weight), preferred_element_type=F32
        ).astype(BF16)

    query = project(normed_q, w_query)
    key = project(normed_all, w_key)
    value = project(normed_all, w_value)
    attended_heads, log_norm = attend(length_arg, window, query, key, value)
    attended = all_to_all(
        jnp.transpose(
            attended_heads.reshape(heads, quad, tok_rows, head_width), (1, 2, 0, 3)
        ).reshape(quad, tok_rows, part),
        "dp",
        quads,
    )
    attended = jnp.swapaxes(attended, 0, 1).reshape(tok_rows, width)

    token_f = tokens.astype(F32)
    residual = token_f + dot(attended, w_output)
    gain_b = gain_two.astype(F32)
    routed_f, inverse_two = normalize(residual, gain_b)
    routed = routed_f.astype(BF16)
    router = jax.nn.softmax(dot(routed, w_router), axis=-1)

    chosen = expert_ids[:, 0]
    chosen_hot = chosen[:, None] == jnp.arange(expert_count, dtype=jnp.int32)[None, :]
    valid_hits = (chosen_hot & valid_mask[:, None]).astype(jnp.int32)
    per_source = lax.all_gather(jnp.sum(valid_hits, axis=0), "expert")
    earlier = jnp.arange(ex_count, dtype=jnp.int32)[:, None] < ex_index
    offsets = jnp.sum(jnp.where(earlier, per_source, 0), axis=0)
    local_rank = jnp.sum((jnp.cumsum(valid_hits, axis=0) - valid_hits) * valid_hits, axis=1)
    group_rank = local_rank + jnp.sum(valid_hits * offsets[None, :], axis=1)
    capacity = 5 * tok_rows // (4 * local)
    slots = 3 * tok_rows // (2 * expert_count)
    kept_mask = valid_mask & (group_rank < capacity)
    kept_f = kept_mask.astype(F32)
    target = jnp.where(kept_mask, chosen * slots + local_rank, -1)
    placing = (
        jnp.arange(expert_count * slots, dtype=jnp.int32)[:, None] == target[None, :]
    ).astype(BF16)
    chosen_f = chosen_hot.astype(F32)
    chosen_prob = jnp.sum(router * chosen_f, axis=1)
    gate = chosen_prob * kept_f
    upstream = cotangent.astype(F32) * valid_f[:, None]
    d_expert = (gate[:, None] * upstream).astype(BF16)

    sending = dot(placing, jnp.concatenate([routed, d_expert], axis=1)).astype(BF16)
    expert_rows = to_experts(
        all_to_all(sending.reshape(expert_count, slots, 2 * width), "expert"), local
    )
    group_rows = lax.all_gather(expert_rows, "dp")
    results = experts(expert_rows, w_in, w_out)
    returned = all_to_all(to_sources(results, ex_count), "expert")
    gathered = t_dot(placing, returned.reshape(expert_count * slots, 2 * width))
    expert_out, d_routed = gathered[:, :width], gathered[:, width:]

    output = (valid_f[:, None] * (residual + gate[:, None] * expert_out)).astype(BF16)
    d_gate = jnp.sum(upstream * expert_out, axis=1) * kept_f
    d_logits = router * (chosen_f - chosen_prob[:, None]) * d_gate[:, None]
    d_router = t_dot(routed, d_logits.astype(BF16))
    d_routed = d_routed + dot_t(d_logits.astype(BF16), w_router)
    d_norm_two, d_gain_two = norm_back(residual, inverse_two, gain_b, d_routed)
    d_residual = upstream + d_norm_two
    low_residual = d_residual.astype(BF16)
    d_attended = dot_t(low_residual, w_output).astype(BF16)
    d_output = t_dot(attended, low_residual)

    grad = all_to_all(
        jnp.swapaxes(d_attended.reshape(tok_rows, quad, part), 0, 1), "dp", quads
    ).reshape(q_rows, heads, head_width)
    grad = jnp.swapaxes(grad, 0, 1)
    d_query_rows, d_key_rows, d_value_rows, d_window = attend_back(
        length_arg, window, query, key, value, grad, log_norm
    )
    if q_parts > 1:
        strided = [
            [i * span + j + quad * n for n in range(q_parts)]
            for i in range(dp_count // span)
            for j in range(quad)
        ]
        d_key_rows, d_value_rows = [
            lax.psum_scatter(
                rows, "dp", scatter_dimension=1, axis_index_groups=strided, tiled=True
            )
            for rows in (d_key_rows, d_value_rows)
        ]
    d_rows = jnp.stack([d_query_rows, d_key_rows.astype(BF16), d_value_rows.astype(BF16)])
    d_parts = jnp.einsum("sd,khsc->dkhc", normed_q, d_rows, preferred_element_type=F32)
    d_table = jnp.einsum("amb,ham->bh", window_hot.astype(F32), d_window, precision="highest")
    d_mine = all_to_all(
        jnp.transpose(
            d_rows.reshape(3, heads, quad, tok_rows, head_width), (2, 3, 0, 1, 4)
        ).reshape(quad, tok_rows, 3 * part),
        "dp",
        quads,
    ).reshape(quad, tok_rows, 3, part)
    d_mine = jnp.transpose(d_mine, (2, 1, 0, 3)).reshape(3, tok_rows, width)
    d_normed = dot_t(d_mine[0], w_query) + dot_t(d_mine[1], w_key) + dot_t(d_mine[2], w_value)
    inverse_one = normalize(token_f, gain_a)[1]
    d_norm_one, d_gain_one = norm_back(token_f, inverse_one, gain_a, d_normed)
    d_tokens = d_residual + d_norm_one

    piece = hidden // dp_count
    my_in = lax.dynamic_slice_in_dim(w_in, dp_index * piece, piece, 2)
    my_out = lax.dynamic_slice_in_dim(w_out, dp_index * piece, piece, 1)
    d_in_piece, d_out = weight_grads(group_rows, my_in, my_out)
    d_in = all_to_all(
        jnp.swapaxes(d_in_piece.reshape(local, dp_count, width // dp_count, piece), 0, 1), "dp"
    )
    d_in = (
        jnp.transpose(d_in, (1, 2, 0, 3)).reshape(local, width // dp_count, hidden).astype(F32)
    )

    def spread(array, axis):
        wide = jnp.zeros(array.shape[:axis] + (array.shape[axis] * quad,) + array.shape[axis + 1 :], F32)
        return lax.dynamic_update_slice_in_dim(wide, array, mine * array.shape[axis], axis)

    d_parts = d_parts.reshape(width, 3, part)
    big = jnp.stack([spread(d_parts[:, n], 1) for n in range(3)] + [d_output])
    summed = lax.psum(big.astype(BF16), ("dp", "expert")).astype(F32)
    small = lax.psum(
        (d_gain_one, spread(d_table, 1), d_gain_two, d_router), ("dp", "expert")
    )
    return (
        output, d_tokens, small[0], summed[0], summed[1], summed[2], summed[3],
        small[1], small[2], small[3], d_in, d_out,
    )


def per_device_quad(
    tokens, lengths, expert_ids, gain_one, w_query, w_key, w_value, w_output,
    bias_table, gain_two, w_router, w_in, w_out, cotangent,
):
    tok_rows, width = tokens.shape
    buckets, head_count = bias_table.shape
    expert_count = w_router.shape[1]
    quad = lax.axis_size("dp") // 2
    counts = 2 * quad - 1
    offset = jnp.arange(2 * tok_rows, dtype=jnp.int32)
    offset = jnp.where(offset < tok_rows, offset, offset - 2 * tok_rows)
    codes = (
        jnp.arange(counts, dtype=jnp.int32)[:, None] * tok_rows
        - offset[None, :]
        - (quad - 1) * tok_rows
    )
    hot = (
        bucket_of(codes)[:, None, :] == jnp.arange(buckets, dtype=jnp.int32)[None, :, None]
    ).astype(BF16)
    output, d_tokens, d_weights, total, d_out_parts, d_in_parts = layer(
        lengths, tokens, expert_ids.reshape(1, tok_rows), cotangent, jnp.stack([gain_one, gain_two]), w_query,
        w_key, w_value, w_output, w_router.T, bias_table.T, hot, w_in, w_out, head_count,
    )
    d_query, d_key, d_value, d_output, d_in, d_out, d_gain_one, d_gain_two, d_router, d_table = finish(
        d_weights, d_in_parts, d_out_parts, total, expert_count, head_count, buckets
    )
    return (
        output, d_tokens, d_gain_one.reshape(width), d_query, d_key, d_value, d_output,
        d_table.T, d_gain_two.reshape(width), d_router.T, d_in, d_out,
    )


def solution(mesh):
    rows = P(("expert", "dp"), None)
    owned = P("expert", None, None)
    return jax.shard_map(
        per_device_quad if dict(mesh.shape) == {"dp": 8, "expert": 4} else per_device,
        mesh=mesh,
        in_specs=(
            rows, P(), rows, P(), P(), P(), P(), P(), P(), P(), P(), owned, owned, rows,
        ),
        out_specs=(
            rows, rows, P(), P(), P(), P(), P(), P(), P(), P(),
            P("expert", "dp", None), P("expert", "dp", None),
        ),
        check_vma=False,
    )
```
